32 devices in a mesh: seq: 8 (over z, y), head: 2 (over x), batch: 2 (over core).
Axes of the slice: x: 2, y: 2, z: 4, core: 2. Of those that a mesh axis runs over, the one named last changes fastest.
Arguments:
- tokens: float32 [2, 8192, 1024], P('batch', ('seq', 'head')), may hold values from -6 to 6
- cotangent: float32 [2, 8192, 1024], P('batch', ('seq', 'head')), may hold values from -6 to 6
- doc_lengths: int32 [2, 8], P('batch'), may hold values from 0 to 8192, as said below
- adapter_ids: int32 [2], P('batch'), may hold values from 0 to 7
- query_weight: bfloat16 [1024, 1024], replicated, may hold values from -0.25 to 0.25
- key_weight: bfloat16 [1024, 1024], replicated, may hold values from -0.25 to 0.25
- value_weight: bfloat16 [1024, 1024], replicated, may hold values from -0.1875 to 0.1875
- output_weight: bfloat16 [1024, 1024], replicated, may hold values from -0.75 to 0.75
- up_weight: bfloat16 [1024, 4096], replicated, may hold values from -0.1875 to 0.1875
- down_weight: bfloat16 [4096, 1024], replicated, may hold values from -0.09375 to 0.09375
- attention_gain: float32 [1024], replicated, may hold values from 0.1 to 1.9
- feedforward_gain: float32 [1024], replicated, may hold values from 0.1 to 1.9
- position_gain: float32 [1024], replicated, may hold values from 0.1 to 1.9
- position_table: float32 [512, 1024], replicated, may hold values from -6 to 6
- attention_down: float32 [4, 8, 1024, 16], replicated, may hold values from -0.1875 to 0.1875
- attention_up: float32 [4, 8, 16, 1024], replicated, may hold values from -0.375 to 0.375
- expand_down: float32 [8, 1024, 16], replicated, may hold values from -0.1875 to 0.1875
- expand_up: float32 [8, 16, 4096], replicated, may hold values from -0.375 to 0.375
- reduce_down: float32 [8, 4096, 16], replicated, may hold values from -0.09375 to 0.09375
- reduce_up: float32 [8, 16, 1024], replicated, may hold values from -0.375 to 0.375
Outputs:
- layer_output: float32 [2, 8192, 1024], P('batch', ('seq', 'head'))
- input_grad: float32 [2, 8192, 1024], P('batch', ('seq', 'head'))
- table_grad: float32 [512, 1024], P('head')
- attention_down_grad: float32 [4, 8, 1024, 16], P(None, 'head')
- attention_up_grad: float32 [4, 8, 16, 1024], P(None, 'head')
- expand_down_grad: float32 [8, 1024, 16], P('head')
- expand_up_grad: float32 [8, 16, 4096], P('head')
- reduce_down_grad: float32 [8, 4096, 16], P('head')
- reduce_up_grad: float32 [8, 16, 1024], P('head')
The draws below stay inside these ranges and needn't reach their ends.
Inputs may be any that keep to these rules, and one draw needn't show every extreme that they name: `doc_lengths`: each row holds 8 document lengths whose sum is at most 8192; positions past the sum are padding. In each group of 1 row one row, drawn from the seed, holds a first document that ends within the last block of positions of one device (in the first group at the sequence's last position, so that it is 8192 long), then a second document of at most the remaining positions (possibly empty), then zeros; every other row holds lengths from 512 to 1024.
All inputs are finite; a program needn't handle non-finite values.
Results may differ from the reference program's by a relative error of at most 0.015.
The reference program's roundings to bfloat16 on the way count: a program that leaves them out, or rounds other values in their place, can miss the bound.
Values may be sent and summed in bfloat16 or wider, within the bound.
A program may use at most 704 MiB of HBM per device.

```python
import math
import jax
import jax.numpy as jnp
import numpy as np
from jax import lax

D = 1024
HEADS = 16
HEAD_DIM = 64
FF = 4096
BUCK = 256
SPAN = 512
RANK = 16
ADAPTERS = 8
HALF = 512
LEN = 8192
DOCS = 8
SEQS = 1
BATCH_SEQS = 2
N_SEQ = 8
N_HEAD = 2
N_BATCH = 2


def draw_doc_lengths(key, part):
    key = jax.random.fold_in(key, 7)
    length_key = jax.random.fold_in(key, 1)
    row_key = jax.random.fold_in(key, 2)
    tail_key = jax.random.fold_in(key, 3)
    second_key = jax.random.fold_in(key, 4)
    lengths = jax.random.randint(length_key, (BATCH_SEQS, DOCS), LEN // (2 * DOCS), LEN // DOCS + 1, dtype=jnp.int32)
    chosen = jnp.arange(N_BATCH, dtype=jnp.int32) * SEQS + jax.random.randint(row_key, (N_BATCH,), 0, SEQS, dtype=jnp.int32)
    whole_row = jnp.any(jnp.arange(BATCH_SEQS, dtype=jnp.int32)[:, None] == chosen[None, :], axis=1)
    tail_most = max(2, min(LEN // DOCS, LEN // (N_SEQ * N_HEAD)))
    tail = jax.random.randint(tail_key, (N_BATCH,), 1, tail_most, dtype=jnp.int32)
    tail = jnp.where(jnp.arange(N_BATCH, dtype=jnp.int32) == 0, 0, tail).astype(jnp.int32)
    second = jnp.floor(jax.random.uniform(second_key, (N_BATCH,)) * (tail + 1).astype(jnp.float32)).astype(jnp.int32)
    second = jnp.minimum(second, tail)
    tail_rows = jnp.repeat(tail, SEQS)
    second_rows = jnp.repeat(second, SEQS)
    slots = jnp.arange(DOCS, dtype=jnp.int32)[None, :]
    single = jnp.where(slots == 0, LEN - tail_rows[:, None], jnp.where(slots == 1, second_rows[:, None], 0)).astype(jnp.int32)
    return jnp.where(whole_row[:, None], single, lengths)


def shard_levels(key, dims, cuts, least, high):
    def one(dim, shards_of):
        heights = jax.random.uniform(jax.random.fold_in(jax.random.fold_in(key, 6), dim), (shards_of,), jnp.float32, least / len(cuts), high / len(cuts))
        return jnp.repeat(jnp.exp(heights), dims[dim] // shards_of).reshape((-1,) + (1,) * (len(dims) - dim - 1))

    loudness = one(*cuts[0])
    for cut in cuts[1:]:
        loudness = loudness * one(*cut)
    return loudness


def bell_draw(key, extent, deviation, bound, pieces=(), held_as=jnp.bfloat16):
    array = jax.random.normal(key, extent, jnp.float32) * deviation
    if len(pieces) > 0:
        array = shard_levels(key, extent, pieces, -0.22, 0.18) * array
    return jnp.clip(array, min=-bound, max=bound).astype(held_as)


def setup_inputs(seed: int = 0) -> dict:
    key_of = jax.random.split(jax.random.key(seed), 21)
    return {
        "tokens": bell_draw(key_of[0], (BATCH_SEQS, LEN, D), 1.0, 6.0, ((0, 2), (1, 16)), jnp.float32),
        "cotangent": bell_draw(key_of[1], (BATCH_SEQS, LEN, D), 1.0, 6.0, ((0, 2), (1, 16)), jnp.float32),
        "doc_lengths": draw_doc_lengths(jax.random.fold_in(key_of[20], 71), 0),
        "adapter_ids": jax.random.randint(key_of[3], (BATCH_SEQS,), 0, ADAPTERS).astype(jnp.int32),
        "query_weight": bell_draw(key_of[4], (D, D), (D // 2) ** -0.5, 0.25),
        "key_weight": bell_draw(key_of[5], (D, D), (D // 2) ** -0.5, 0.25),
        "value_weight": bell_draw(key_of[6], (D, D), D ** -0.5, 0.1875),
        "output_weight": bell_draw(key_of[7], (D, D), (D // 16) ** -0.5, 0.75),
        "up_weight": bell_draw(key_of[8], (D, FF), D ** -0.5, 0.1875),
        "down_weight": bell_draw(key_of[9], (FF, D), FF ** -0.5, 0.09375),
        "attention_gain": jnp.clip(1.0 + 0.18 * jax.random.normal(key_of[10], (D,), jnp.float32), 0.1, 1.9),
        "feedforward_gain": jnp.clip(1.0 + 0.18 * jax.random.normal(key_of[11], (D,), jnp.float32), 0.1, 1.9),
        "position_gain": jnp.clip(1.0 + 0.18 * jax.random.normal(key_of[12], (D,), jnp.float32), 0.1, 1.9),
        "position_table": bell_draw(key_of[13], (2 * BUCK, D), 1.0, 6.0, (), jnp.float32),
        "attention_down": bell_draw(key_of[14], (4, ADAPTERS, D, RANK), D ** -0.5, 0.1875, (), jnp.float32),
        "attention_up": bell_draw(key_of[15], (4, ADAPTERS, RANK, D), (16 * RANK) ** -0.5, 0.375, (), jnp.float32),
        "expand_down": bell_draw(key_of[16], (ADAPTERS, D, RANK), D ** -0.5, 0.1875, (), jnp.float32),
        "expand_up": bell_draw(key_of[17], (ADAPTERS, RANK, FF), (16 * RANK) ** -0.5, 0.375, (), jnp.float32),
        "reduce_down": bell_draw(key_of[18], (ADAPTERS, FF, RANK), FF ** -0.5, 0.09375, (), jnp.float32),
        "reduce_up": bell_draw(key_of[19], (ADAPTERS, RANK, D), (16 * RANK) ** -0.5, 0.375, (), jnp.float32),
    }


EPSILON = 1e-07
ADAPTER_SCALING = 2.0
NEGATIVE = -1e+30
PRECISE = lax.Precision.HIGHEST

@jax.custom_vjp
def low(v):
    return lax.optimization_barrier(v.astype(jnp.bfloat16)).astype(jnp.float32)

@jax.custom_vjp
def low_back(v):
    return v

def low_keep(v):
    return (low(v), None)

def low_pass(kept, grad):
    return (grad,)

def back_keep(v):
    return (v, None)

def back_low(kept, grad):
    return (low(grad),)
low.defvjp(low_keep, low_pass)
low_back.defvjp(back_keep, back_low)

def bucket_tables(query_rows, half_span, buckets, distance_cap):
    query_place = np.arange(query_rows)[:, None]
    key_place = np.arange(query_rows + 2 * half_span)[None, :]
    offset = np.clip(query_place + half_span - key_place, 1 - half_span, half_span - 1)
    middle = buckets // 2
    sign_of = np.sign(offset)
    magnitude = np.where((offset < middle) & (offset > -middle), middle - 1, np.abs(offset))
    log_place = np.ceil(np.log(magnitude / middle) / np.log((distance_cap - 1) / middle) * (middle - 1)) + middle
    bucket = np.where(np.abs(offset) <= middle, offset, log_place * sign_of).astype(np.int32)
    to_key = np.clip(bucket + buckets, 0, 2 * buckets - 1).astype(np.int32)
    to_query = np.clip(buckets - bucket, 0, 2 * buckets - 1).astype(np.int32)
    return (to_key, to_query)

def window_tables(query_rows, half_span):
    query_place = np.arange(query_rows)[:, None]
    key_place = np.arange(query_rows + 2 * half_span)[None, :]
    offset = query_place + half_span - key_place
    return (np.abs(offset) < half_span, offset == 0)

def segment_ids(lengths, positions):
    bounds = jnp.cumsum(lengths, axis=-1, dtype=jnp.int32)
    return lax.optimization_barrier(jnp.sum((bounds[..., None, :] <= positions[:, None]).astype(jnp.int32), axis=-1, dtype=jnp.int32))

def normalize(values, scale_gain):
    centered = values - lax.optimization_barrier(jnp.mean(values, axis=-1, keepdims=True))
    variance = lax.optimization_barrier(jnp.mean(centered * centered, axis=-1, keepdims=True))
    return centered * lax.rsqrt(variance + EPSILON) * scale_gain

def product_result(left_side, right_side):
    return jnp.dot(left_side, right_side, precision=PRECISE)

def adapted(input_rows, weight_matrix, down_map, up_factor_mapping, round_grad):
    inner_reduced = low(product_result(input_rows, down_map))
    if round_grad:
        inner_reduced = low_back(inner_reduced)
    return product_result(input_rows, weight_matrix) + ADAPTER_SCALING * product_result(inner_reduced, up_factor_mapping)

def attend(queries, key_rows, value_rows, pos_query, pos_key, lengths):
    query_count = min(512, LEN)
    to_key, to_query = bucket_tables(query_count, HALF, BUCK, SPAN)
    in_window, on_diagonal = window_tables(query_count, HALF)
    heads_shape = (LEN, HEADS, HEAD_DIM)
    queries = queries.reshape(heads_shape)
    key_pad = jnp.pad(key_rows.reshape(heads_shape), ((HALF, HALF), (0, 0), (0, 0)))
    value_pad = jnp.pad(value_rows.reshape(heads_shape), ((HALF, HALF), (0, 0), (0, 0)))
    pos_query = pos_query.reshape(2 * BUCK, HEADS, HEAD_DIM)
    pos_key = pos_key.reshape(2 * BUCK, HEADS, HEAD_DIM)
    segments = segment_ids(lengths, jnp.arange(LEN, dtype=jnp.int32))
    seg_pad = jnp.pad(segments, (HALF, HALF), constant_values=DOCS)
    score_scale = 1.0 / math.sqrt(3 * HEAD_DIM)

    def one_block(block_number):
        first_row = block_number * query_count
        block_query = lax.dynamic_slice_in_dim(queries, first_row, query_count, 0)
        block_key = lax.dynamic_slice_in_dim(key_pad, first_row, query_count + 2 * HALF, 0)
        block_value = lax.dynamic_slice_in_dim(value_pad, first_row, query_count + 2 * HALF, 0)
        seg_query = lax.dynamic_slice_in_dim(segments, first_row, query_count, 0)
        seg_key = lax.dynamic_slice_in_dim(seg_pad, first_row, query_count + 2 * HALF, 0)
        allowed = jnp.asarray(in_window) & (seg_query[:, None] == seg_key[None, :]) & (seg_query[:, None] < DOCS) | jnp.asarray(on_diagonal)
        direct = jnp.einsum('qhe,khe->hqk', block_query, block_key, precision=PRECISE)
        query_pos = jnp.einsum('qhe,bhe->hqb', block_query, pos_key, precision=PRECISE)
        key_pos = jnp.einsum('khe,bhe->hkb', block_key, pos_query, precision=PRECISE)
        near_key = jnp.take_along_axis(query_pos, jnp.asarray(to_key)[None], axis=2)
        near_query = jnp.swapaxes(jnp.take_along_axis(key_pos, jnp.asarray(to_query).T[None], axis=2), 1, 2)
        raw_score = low_back((direct + near_key + near_query) * score_scale)
        masked = jnp.where(allowed[None], raw_score, NEGATIVE)
        row_top = lax.optimization_barrier(jnp.max(masked, axis=2, keepdims=True))
        row_exp = jnp.exp(masked - row_top)
        attn_probs = row_exp / lax.optimization_barrier(jnp.sum(row_exp, axis=2, keepdims=True))
        return jnp.einsum('hqk,khe->qhe', low(attn_probs), block_value, precision=PRECISE)
    blocks = lax.map(jax.checkpoint(one_block), jnp.arange(LEN // query_count, dtype=jnp.int32))
    return blocks.reshape(LEN, D)

def layer_one(tokens, select, lengths, frozen, params):
    query_weight, key_weight, value_weight, output_weight, up_weight, down_weight, attention_gain, feedforward_gain, position_gain = frozen
    position_table, attention_down, attention_up, expand_down, expand_up, reduce_down, reduce_up = params
    attention_down_factor = low(jnp.tensordot(select, attention_down, axes=([0], [1]), precision=PRECISE))
    attention_up_factor = low(jnp.tensordot(select, attention_up, axes=([0], [1]), precision=PRECISE))
    exp_down = low(jnp.tensordot(select, expand_down, axes=1, precision=PRECISE))
    exp_up = low(jnp.tensordot(select, expand_up, axes=1, precision=PRECISE))
    red_down = low(jnp.tensordot(select, reduce_down, axes=1, precision=PRECISE))
    red_up = low(jnp.tensordot(select, reduce_up, axes=1, precision=PRECISE))
    token_low = low(tokens)
    queries = low_back(low(adapted(token_low, query_weight, attention_down_factor[0], attention_up_factor[0], True)))
    key_rows = low_back(low(adapted(token_low, key_weight, attention_down_factor[1], attention_up_factor[1], True)))
    value_rows = low_back(low(adapted(token_low, value_weight, attention_down_factor[2], attention_up_factor[2], True)))
    table_reduced = low(normalize(position_table, position_gain))
    pos_query = low(adapted(table_reduced, query_weight, attention_down_factor[0], attention_up_factor[0], False))
    pos_key = low(adapted(table_reduced, key_weight, attention_down_factor[1], attention_up_factor[1], False))
    context = low_back(low(attend(queries, key_rows, value_rows, pos_query, pos_key, lengths)))
    attended = low_back(adapted(context, output_weight, attention_down_factor[3], attention_up_factor[3], True))
    hidden = normalize(tokens + attended, attention_gain)
    hidden_low = low(hidden)
    pre_act = low_back(adapted(hidden_low, up_weight, exp_down, exp_up, True))
    act_low = low_back(low(jax.nn.gelu(pre_act, approximate=False)))
    branch = low_back(adapted(act_low, down_weight, red_down, red_up, True))
    return normalize(hidden + branch, feedforward_gain)

def reference(tokens, cotangent, doc_lengths, adapter_ids, query_weight, key_weight, value_weight, output_weight, up_weight, down_weight, attention_gain, feedforward_gain, position_gain, position_table, attention_down, attention_up, expand_down, expand_up, reduce_down, reduce_up):
    frozen = tuple((weight_matrix.astype(jnp.float32) for weight_matrix in (query_weight, key_weight, value_weight, output_weight, up_weight, down_weight))) + (attention_gain, feedforward_gain, position_gain)
    select = jax.nn.one_hot(adapter_ids, ADAPTERS, dtype=jnp.float32)

    def forward(input_rows, table, attention_down_factor, attention_up_factor, exp_down, exp_up, red_down, red_up):
        params = (table, attention_down_factor, attention_up_factor, exp_down, exp_up, red_down, red_up)

        def one_sequence(sequence_parts):
            return layer_one(sequence_parts[0], sequence_parts[1], sequence_parts[2], frozen, params)
        return lax.map(one_sequence, (input_rows, select, doc_lengths))
    output, pullback = jax.vjp(forward, tokens, position_table, attention_down, attention_up, expand_down, expand_up, reduce_down, reduce_up)
    gradients = pullback(cotangent)
    return (output, gradients[0], gradients[1], gradients[2], gradients[3], gradients[4], gradients[5], gradients[6], gradients[7])
```

```python
from functools import partial
import math

import jax
import jax.numpy as jnp
import numpy as np
from jax import lax
from jax.experimental import pallas as pl
from jax.experimental.pallas import tpu as pltpu
from jax.sharding import PartitionSpec as P

HEADS = 16
HEAD_DIM = 64
BUCK = 256
SPAN = 512
ADAPTERS = 8
HALF = 512
DOCS = 8

EPSILON = 1e-07
ADAPTER_SCALING = 2.0
NEGATIVE = -1e30
PRECISE = lax.Precision.HIGHEST
TILE = 128
BF = jnp.bfloat16
F32 = jnp.float32
NN = (((1,), (0,)), ((), ()))
NT = (((1,), (1,)), ((), ()))


def mm(a, b, dims=NN):
    return lax.dot_general(a, b, dims, preferred_element_type=F32)

def lanes(shape=(TILE, TILE)):
    return lax.broadcasted_iota(jnp.int32, shape, 1)

def rows(shape=(TILE, TILE)):
    return lax.broadcasted_iota(jnp.int32, shape, 0)

def skew(tile):
    return pltpu.roll(tile, 0, 1, stride=1, stride_axis=0)

def flip_matrix():
    return jnp.where(lanes() + rows() == TILE - 1, 1.0, 0.0).astype(BF)


def forward_kernel(q_ref, k_ref, v_ref, pk_ref, pq_ref, qhot_ref, kbias_ref,
                   ctx_ref, p_ref, ctxf_ref, inv_ref,
                   qs_ref, kz_ref, vz_ref, ks_ref, s_ref):
    rows_q = q_ref.shape[1]
    tiles = rows_q // TILE
    span = 2 * HALF // TILE
    width = (span + 1) * TILE
    flip = flip_matrix()
    factor = math.log2(math.e) / math.sqrt(3 * HEAD_DIM)
    k = k_ref[0]
    v = v_ref[0]
    kb = kbias_ref[0]
    kcol = lanes(k.shape) < HEAD_DIM
    below = lanes() + rows() < TILE
    place = lanes() + rows()
    qcol = lanes((rows_q, TILE)) < HEAD_DIM
    tcol = lanes() < HEAD_DIM
    for h in range(2):
        own = kcol if h == 0 else ~kcol
        kz_ref[h] = jnp.where(own, k, kb)
        vz_ref[h] = jnp.where(own, v, jnp.ones_like(v))
        km = jnp.where(own, k, jnp.zeros_like(k))
        for d in range(span + 1):
            lo = max(span - 1 - d, 0) * TILE
            hi = min(span + 1 - d, span) * TILE
            key_rel = mm(km[d * TILE:d * TILE + rows_q], pq_ref[0, lo:hi, :], NT).astype(BF)
            for t in range(tiles):
                part = key_rel[t * TILE:(t + 1) * TILE]
                if d == 0 or d == span:
                    picked = part
                else:
                    picked = jnp.where(below, part[:, TILE:], part[:, :TILE])
                ks_ref[h, t, d * TILE:(d + 1) * TILE, :] = skew(picked)
        q_masked = jnp.where(qcol if h == 0 else ~qcol, q_ref[0], jnp.zeros_like(q_ref[0]))
        query_rel = mm(q_masked, pk_ref[0], NT).astype(BF)
        for t in range(tiles):
            part = query_rel[t * TILE:(t + 1) * TILE]
            for d in range(span + 1):
                if d == 0:
                    picked = part[:, :TILE]
                elif d == span:
                    picked = part[:, (span - 1) * TILE:]
                else:
                    picked = jnp.where(below, part[:, d * TILE:(d + 1) * TILE], part[:, (d - 1) * TILE:d * TILE])
                qs_ref[h, t, :, d * TILE:(d + 1) * TILE] = skew(picked)

    def tile_step(t, carry):
        base = pl.multiple_of(t * TILE, TILE)
        q = q_ref[0, pl.ds(base, TILE), :]
        hot = qhot_ref[0, pl.ds(base, TILE), :]
        a = t % 2
        outs = []
        for h in range(2):
            own = tcol if h == 0 else ~tcol
            q_side = mm(flip, jnp.where(own, q, hot)).astype(BF)
            left = jnp.concatenate([q_side, flip], axis=1)
            right = jnp.concatenate([kz_ref[h, pl.ds(base, width), :], ks_ref[h, t]], axis=1)
            s_ref[h] = mm(left, right, NT) + mm(flip, qs_ref[h, t])
        for h in range(2):
            own = tcol if h == 0 else ~tcol
            first = s_ref[h, :, :TILE]
            s_ref[h, :, :TILE] = jnp.where(place > TILE - 1, first, NEGATIVE)
            last = s_ref[h, :, span * TILE:]
            s_ref[h, :, span * TILE:] = jnp.where(place < TILE - 1, last, NEGATIVE)
            mid = s_ref[h, :, (span // 2) * TILE:(span // 2 + 1) * TILE]
            s_ref[h, :, (span // 2) * TILE:(span // 2 + 1) * TILE] = jnp.where((place == TILE - 1) & (mid < 0.1 * NEGATIVE), 0.0, mid)
            top = s_ref[h, :, :TILE]
            for d in range(1, span + 1):
                top = jnp.maximum(top, s_ref[h, :, d * TILE:(d + 1) * TILE])
            peak = jnp.max(top, axis=1, keepdims=True)
            prob = jnp.exp2((s_ref[h] - peak) * factor).astype(BF)
            p_ref[0, h, t // 2, pl.ds(pl.multiple_of(a * TILE, TILE), TILE), pl.ds(pl.multiple_of(a * TILE, TILE), width)] = prob
            total = mm(prob, vz_ref[h, pl.ds(base, width), :])
            swapped = pltpu.roll(total, HEAD_DIM, 1)
            den = jnp.where(own, swapped, total)
            inv = 1.0 / den
            inv_ref[0, h, pl.ds(base, TILE), :] = inv
            p_ref[0, h, t // 2, pl.ds(pl.multiple_of(a * TILE, TILE), TILE), pl.ds(pl.multiple_of((1 - a) * width, TILE), TILE)] = jnp.zeros((TILE, TILE), BF)
            outs.append(total * inv)
        ctx = jnp.where(tcol, outs[0], outs[1])
        ctxf_ref[0, pl.ds(base, TILE), :] = ctx
        ctx_ref[0, pl.ds(base, TILE), :] = mm(flip, ctx.astype(BF)).astype(BF)
        return carry

    lax.fori_loop(0, tiles, tile_step, 0, unroll=True)


def attention_forward(q, kext, vext, pk, pq, qhot, kbias):
    n, rq, width = q.shape
    rk = kext.shape[1]
    pairs = width // TILE
    off = 2 * HALF
    def col(r):
        return pl.BlockSpec((1, r, TILE), lambda s, p: (s, 0, p))
    def whole(r):
        return pl.BlockSpec((1, r, TILE), lambda s, p: (s, 0, 0))
    wide = off + 2 * TILE
    return pl.pallas_call(
        forward_kernel,
        grid=(n, pairs),
        in_specs=[col(rq), col(rk), col(rk), col(off), col(off), whole(rq), whole(rk)],
        out_specs=[col(rq),
                   pl.BlockSpec((1, 2, rq // (2 * TILE), 2 * TILE, wide), lambda s, p: (s, p, 0, 0, 0)),
                   col(rq),
                   pl.BlockSpec((1, 2, rq, TILE), lambda s, p: (s, p, 0, 0))],
        out_shape=[jax.ShapeDtypeStruct((n, rq, width), BF),
                   jax.ShapeDtypeStruct((n, 2 * pairs, rq // (2 * TILE), 2 * TILE, wide), BF),
                   jax.ShapeDtypeStruct((n, rq, width), F32),
                   jax.ShapeDtypeStruct((n, 2 * pairs, rq, TILE), F32)],
        scratch_shapes=[pltpu.VMEM((2, rq // TILE, TILE, off + TILE), BF),
                        pltpu.VMEM((2, rk, TILE), BF), pltpu.VMEM((2, rk, TILE), BF),
                        pltpu.VMEM((2, rq // TILE, off + TILE, TILE), BF),
                        pltpu.VMEM((2, TILE, off + TILE), F32)],
        compiler_params=pltpu.CompilerParams(dimension_semantics=("arbitrary", "arbitrary"), vmem_limit_bytes=48 * 2**20),
        name="attention_forward",
    )(q, kext, vext, pk, pq, qhot, kbias)


def backward_kernel(q_ref, k_ref, v_ref, pk_ref, pq_ref, p_ref, g_ref, ctxf_ref, inv_ref,
                    dq_ref, dk_ref, dv_ref, dpk_ref, dpq_ref,
                    qr_ref, gr_ref, e_ref, gc_ref, gk_ref, dvt_ref):
    rows_q = q_ref.shape[1]
    rows_k = k_ref.shape[1]
    tiles = rows_q // TILE
    key_tiles = rows_k // TILE
    span = 2 * HALF // TILE
    wide = (span + 2) * TILE
    flip = flip_matrix()
    scale = 1.0 / math.sqrt(3 * HEAD_DIM)
    tcol = lanes() < HEAD_DIM
    qcol = lanes((rows_q, TILE)) < HEAD_DIM
    over = lanes() > rows()
    under = lanes() >= rows()

    @pl.when((pl.program_id(0) == 0) & (pl.program_id(1) == 0))
    def _():
        gk_ref[...] = jnp.zeros_like(gk_ref)

    for t in range(tiles):
        at = slice(t * TILE, (t + 1) * TILE)
        qr_ref[at] = mm(flip, q_ref[0, at]).astype(BF)
        gr_ref[at] = mm(flip, g_ref[0, at]).astype(BF)
    q_rev = qr_ref[...]
    g_rev = gr_ref[...]
    q_turned = q_rev.T
    k_turned = k_ref[0].T
    product = g_rev.astype(F32) * ctxf_ref[0]
    dvt_ref[...] = jnp.zeros_like(dvt_ref)
    dq_parts = []
    dk_parts = []
    for h in range(2):
        own = qcol if h == 0 else ~qcol
        part = slice(h * HEAD_DIM, (h + 1) * HEAD_DIM)
        g_masked = jnp.where(own, g_rev, jnp.zeros_like(g_rev))
        inv = inv_ref[0, h]
        delta = jnp.sum(jnp.where(own, product, 0.0), axis=1, keepdims=True) * inv
        g_turned = (g_rev.astype(F32) * inv).astype(BF).T[part]
        dq_main = []
        for u in range(tiles // 2):
            at = slice(u * 2 * TILE, (u + 1) * 2 * TILE)
            window = slice(u * 2 * TILE, u * 2 * TILE + wide)
            prob = p_ref[0, h, u]
            g_probs = mm(g_masked[at], v_ref[0, window], NT)
            inv_u = jnp.concatenate([inv[at]] * (span + 2), axis=1)
            delta_u = jnp.concatenate([delta[at]] * (span + 2), axis=1)
            e = (prob.astype(F32) * (g_probs * inv_u - delta_u)).astype(BF)
            e_ref[h, u] = e
            dvt_ref[part, window] += mm(g_turned[:, at], prob)
            dq_main.append(mm(e, k_ref[0, window]))
            for a in range(2):
                for t in range(span):
                    def turned(d):
                        return pltpu.roll(e_ref[h, u, a * TILE:(a + 1) * TILE, (a + d) * TILE:(a + d + 1) * TILE], 1, 1, stride=1, stride_axis=0)
                    here = turned(t) if t == 0 else after
                    after = turned(t + 1)
                    gc_ref[h, (2 * u + a) * TILE:(2 * u + a + 1) * TILE, t * TILE:(t + 1) * TILE] = jnp.where(over, after, here)
        dq_parts.append(jnp.concatenate(dq_main, axis=0) + mm(gc_ref[h], pk_ref[0]))
        dpk_ref[0, part, :] = mm(q_turned[part], gc_ref[h]) * scale
        dk_tiles = []
        for kt in range(key_tiles):
            dlow = max(0, kt - tiles + 1)
            dhigh = min(span, kt)
            flat = []
            spun = {}
            for d in range(dlow, dhigh + 1):
                qt = kt - d
                a = qt % 2
                et = e_ref[h, qt // 2, a * TILE:(a + 1) * TILE, (a + d) * TILE:(a + d + 1) * TILE].T
                flat.append((qt, et))
                spun[d] = skew(et)
            tlow = max(dlow - 1, 0)
            thigh = min(dhigh, span - 1)
            for t in range(tlow, thigh + 1):
                zero = jnp.zeros((TILE, TILE), BF)
                gk_ref[h, kt * TILE:(kt + 1) * TILE, t * TILE:(t + 1) * TILE] = jnp.where(under, spun.get(t + 1, zero), spun.get(t, zero))
            flat = flat[::-1]
            left = jnp.concatenate([et for _, et in flat] + [gk_ref[h, kt * TILE:(kt + 1) * TILE, tlow * TILE:(thigh + 1) * TILE]], axis=1)
            right = jnp.concatenate([q_rev[flat[0][0] * TILE:(flat[-1][0] + 1) * TILE], pq_ref[0, tlow * TILE:(thigh + 1) * TILE]], axis=0)
            dk_tiles.append(mm(left, right))
        dk_parts.append(jnp.concatenate(dk_tiles, axis=0))
        dpq_ref[0, part, :] = mm(k_turned[part], gk_ref[h]) * scale
    dq = (jnp.where(qcol, dq_parts[0], dq_parts[1]) * scale).astype(BF)
    for t in range(tiles):
        at = slice(t * TILE, (t + 1) * TILE)
        dq_ref[0, at] = mm(flip, dq[at]).astype(BF)
    kcol = lanes((rows_k, TILE)) < HEAD_DIM
    dk_ref[0] = (jnp.where(kcol, dk_parts[0], dk_parts[1]) * scale).astype(BF)
    dv_ref[0] = dvt_ref[...].astype(BF).T


def attention_backward(q, kext, vext, pk, pq, probs, g, ctxf, inv):
    n, rq, width = q.shape
    rk = kext.shape[1]
    pairs = width // TILE
    off = 2 * HALF
    wide = off + 2 * TILE
    def col(r):
        return pl.BlockSpec((1, r, TILE), lambda s, p: (s, 0, p))
    def row(r):
        return pl.BlockSpec((1, TILE, r), lambda s, p: (s, p, 0))
    return pl.pallas_call(
        backward_kernel,
        grid=(n, pairs),
        in_specs=[col(rq), col(rk), col(rk), col(off), col(off),
                  pl.BlockSpec((1, 2, rq // (2 * TILE), 2 * TILE, wide), lambda s, p: (s, p, 0, 0, 0)),
                  col(rq), col(rq),
                  pl.BlockSpec((1, 2, rq, TILE), lambda s, p: (s, p, 0, 0))],
        out_specs=[col(rq), col(rk), col(rk), row(off), row(off)],
        out_shape=[jax.ShapeDtypeStruct((n, rq, width), BF),
                   jax.ShapeDtypeStruct((n, rk, width), BF),
                   jax.ShapeDtypeStruct((n, rk, width), BF),
                   jax.ShapeDtypeStruct((n, width, off), F32),
                   jax.ShapeDtypeStruct((n, width, off), F32)],
        scratch_shapes=[pltpu.VMEM((rq, TILE), BF), pltpu.VMEM((rq, TILE), BF),
                        pltpu.VMEM((2, rq // (2 * TILE), 2 * TILE, wide), BF),
                        pltpu.VMEM((2, rq, off), BF),
                        pltpu.VMEM((2, rk, off), BF),
                        pltpu.VMEM((TILE, rk), F32)],
        compiler_params=pltpu.CompilerParams(dimension_semantics=("arbitrary", "arbitrary"), vmem_limit_bytes=56 * 2**20),
        name="attention_backward",
    )(q, kext, vext, pk, pq, probs, g, ctxf, inv)


def shifted(value, axes, steps):
    count = math.prod(lax.axis_size(axis) for axis in axes)
    initial, last = (max(0, -steps), min(count, count - steps))
    return lax.ppermute(value, axes, [(source, source + steps) for source in range(initial, last)])


def bucket_of(offset, buckets, distance_cap):
    middle = buckets // 2
    sign_of = np.sign(offset)
    magnitude = np.where((offset < middle) & (offset > -middle), middle - 1, np.abs(offset))
    log_place = (
        np.ceil(np.log(magnitude / middle) / np.log((distance_cap - 1) / middle) * (middle - 1))
        + middle
    )
    return np.where(np.abs(offset) <= middle, offset, log_place * sign_of).astype(np.int32)


def offset_tables():
    place = np.arange(2 * HALF)

    def hot(distance, sign):
        clipped = np.clip(distance, 1 - HALF, HALF - 1)
        bucket = np.clip(BUCK + sign * bucket_of(clipped, BUCK, SPAN), 0, 2 * BUCK - 1)
        return np.eye(2 * BUCK, dtype=np.float32)[bucket]

    return hot(HALF - place, 1), hot(place - HALF, -1), hot(HALF - 1 - place, -1)


def segment_ids(lengths, positions):
    bounds = jnp.cumsum(lengths, axis=-1, dtype=jnp.int32)
    return jnp.sum(
        (bounds[..., None, :] <= positions[:, None]).astype(jnp.int32), axis=-1, dtype=jnp.int32
    )


def product(pattern, left_side, right_side):
    return jnp.einsum(pattern, left_side, right_side, preferred_element_type=F32)


def split_product(pattern, exact, wide):
    high = wide.astype(BF)
    low = (wide - high.astype(F32)).astype(BF)
    return product(pattern, exact, high) + product(pattern, exact, low)


def norm_stats(values):
    centered = values - jnp.mean(values, axis=-1, keepdims=True)
    inverse = lax.rsqrt(jnp.mean(centered * centered, axis=-1, keepdims=True) + EPSILON)
    return (centered * inverse, inverse)


def norm_back(normed, inverse, scale_gain, upstream):
    scaled = upstream * scale_gain
    return inverse * (
        scaled
        - jnp.mean(scaled, axis=-1, keepdims=True)
        - normed * jnp.mean(scaled * normed, axis=-1, keepdims=True)
    )


def adapter_forward(rows_in, weight, down, up):
    inner = product("sti,sir->str", rows_in, down).astype(BF)
    mapped = product("sti,io->sto", rows_in, weight) + ADAPTER_SCALING * product(
        "str,sro->sto", inner, up
    )
    return (mapped, inner)


def adapter_back(rows_in, inner, weight, down, up, gradient):
    grad_up = ADAPTER_SCALING * product("str,sto->sro", inner, gradient)
    grad_inner = (ADAPTER_SCALING * product("sto,sro->str", gradient, up)).astype(BF)
    grad_down = product("sti,str->sir", rows_in, grad_inner)
    grad_in = product("sto,io->sti", gradient, weight) + product("str,sir->sti", grad_inner, down)
    return (grad_in, grad_down, grad_up)


def body(
    tokens,
    cotangent,
    doc_lengths,
    adapter_ids,
    query_weight,
    key_weight,
    value_weight,
    output_weight,
    up_weight,
    down_weight,
    attention_gain,
    feedforward_gain,
    position_gain,
    position_table,
    attention_down,
    attention_up,
    expand_down,
    expand_up,
    reduce_down,
    reduce_up,
):
    seqs, row_count, width = tokens.shape
    head_groups = lax.axis_size("head")
    head_index = lax.axis_index("head")
    seq_index = lax.axis_index("seq")
    by_rows = row_count >= HALF

    def chosen(stack, axis):
        return jnp.take(stack, adapter_ids, axis=axis).astype(BF)

    att_down = [chosen(attention_down[member], 0) for member in range(4)]
    att_up = [chosen(attention_up[member], 0) for member in range(4)]
    exp_down = chosen(expand_down, 0)
    exp_up = chosen(expand_up, 0)
    red_down = chosen(reduce_down, 0)
    red_up = chosen(reduce_up, 0)

    token_low = tokens.astype(BF)
    frozen = (query_weight, key_weight, value_weight)

    def columns(matrix):
        if by_rows:
            return matrix
        local = width // head_groups
        return lax.dynamic_slice_in_dim(matrix, head_index * local, local, matrix.ndim - 1)

    if by_rows:
        block_axes = ("seq", "head")
        block_index = seq_index * head_groups + head_index
        query_count = row_count
    else:
        block_axes = ("seq",)
        block_index = seq_index
        query_count = row_count * head_groups
    blocks = math.prod(lax.axis_size(axis) for axis in block_axes)

    def halo(array):
        before = shifted(array[:, query_count - HALF :], block_axes, 1)
        after = shifted(array[:, :HALF], block_axes, -1)
        return before, after

    if by_rows:
        before, after = halo(token_low)
        query_map, query_inner = adapter_forward(token_low, frozen[0], att_down[0], att_up[0])
        queries = query_map.astype(BF)
        rows_ext = jnp.concatenate([before, token_low, after], axis=1)
        inners = [query_inner]
        extended = []
        for member in (1, 2):
            mapped, inner = adapter_forward(rows_ext, frozen[member], att_down[member], att_up[member])
            extended.append(mapped.astype(BF))
            inners.append(inner)
        keys_ext, values_ext = extended
    else:
        projected = []
        inners = []
        for member in range(3):
            mapped, inner = adapter_forward(
                token_low, frozen[member], att_down[member], att_up[member]
            )
            projected.append(mapped.astype(BF))
            inners.append(inner)
        queries, keys, values = lax.all_to_all(
            jnp.stack(projected), "head", split_axis=3, concat_axis=2, tiled=True
        )
        keys_ext, values_ext = [
            jnp.concatenate([side[0], array, side[1]], axis=1)
            for array, side in ((keys, halo(keys)), (values, halo(values)))
        ]

    table_normed, table_inverse = norm_stats(position_table)
    table_low = (table_normed * position_gain).astype(BF)
    key_hot, query_hot, back_hot = (jnp.asarray(hot, BF) for hot in offset_tables())
    position_inners = []
    tables = []
    for member in range(2):
        inner = product("pi,sir->spr", table_low, att_down[member]).astype(BF)
        mapped = product("pi,io->po", table_low, columns(frozen[member]))[
            None
        ] + ADAPTER_SCALING * product("spr,sro->spo", inner, columns(att_up[member]))
        position_inners.append(inner)
        tables.append(mapped.astype(BF))
    key_rel = product("cp,spo->sco", key_hot, tables[1]).astype(BF)
    query_rel = product("cp,spo->sco", query_hot, tables[0]).astype(BF)
    query_back = product("cp,spo->sco", back_hot, tables[0]).astype(BF)

    key_places = block_index * query_count - HALF + jnp.arange(query_count + 2 * HALF, dtype=jnp.int32)
    key_segments = segment_ids(doc_lengths, key_places)
    inside = (key_places >= 0) & (key_places < query_count * blocks)
    key_segments = jnp.where(inside[None, :], key_segments, DOCS)
    query_segments = key_segments[:, HALF : HALF + query_count]
    slot = jnp.arange(TILE, dtype=jnp.int32) % HEAD_DIM
    query_seg = (slot == query_segments[..., None]).astype(BF)
    open_slot = (slot == key_segments[..., None]) & (key_segments[..., None] < DOCS)
    key_bias = jnp.where(open_slot | (slot > DOCS), 0.0, NEGATIVE).astype(BF)

    context, probs, context_wide, inverse_total = attention_forward(
        queries, keys_ext, values_ext, key_rel, query_rel, query_seg, key_bias
    )
    if by_rows:
        context_rows = context
    else:
        context_rows = lax.all_to_all(context, "head", split_axis=1, concat_axis=2, tiled=True)

    attended, inner_out = adapter_forward(context_rows, output_weight, att_down[3], att_up[3])
    normed_one, inverse_one = norm_stats(tokens + attended)
    hidden = normed_one * attention_gain
    hidden_low = hidden.astype(BF)
    pre_act, inner_up = adapter_forward(hidden_low, up_weight, exp_down, exp_up)
    act_low = jax.nn.gelu(pre_act, approximate=False).astype(BF)
    branch, inner_down = adapter_forward(act_low, down_weight, red_down, red_up)
    normed_two, inverse_two = norm_stats(hidden + branch)
    layer_output = normed_two * feedforward_gain
    grad_two = norm_back(normed_two, inverse_two, feedforward_gain, cotangent)
    grad_act, grad_red_down, grad_red_up = adapter_back(
        act_low, inner_down, down_weight, red_down, red_up, grad_two.astype(BF)
    )
    gelu_pull = jax.vjp(partial(jax.nn.gelu, approximate=False), pre_act)[1]
    grad_pre = gelu_pull(grad_act.astype(BF).astype(F32))[0].astype(BF)
    grad_hidden, grad_exp_down, grad_exp_up = adapter_back(
        hidden_low, inner_up, up_weight, exp_down, exp_up, grad_pre
    )
    grad_one = norm_back(normed_one, inverse_one, attention_gain, grad_hidden + grad_two)
    grad_context, grad_out_down, grad_out_up = adapter_back(
        context_rows, inner_out, output_weight, att_down[3], att_up[3], grad_one.astype(BF)
    )
    grad_context = grad_context.astype(BF)
    if not by_rows:
        grad_context = lax.all_to_all(grad_context, "head", split_axis=2, concat_axis=1, tiled=True)

    grad_q, grad_k, grad_v, grad_key_rel, grad_query_rel = attention_backward(
        queries,
        keys_ext,
        values_ext,
        key_rel,
        query_back,
        probs,
        grad_context,
        context_wide,
        inverse_total,
    )
    own = slice(HALF, HALF + query_count)

    def fold(array):
        from_above = shifted(array[:, :HALF].astype(BF), block_axes, -1).astype(F32)
        from_below = shifted(array[:, HALF + query_count :].astype(BF), block_axes, 1).astype(F32)
        total = array[:, own].astype(F32)
        if query_count == HALF:
            return total + from_above + from_below
        total = total.at[:, query_count - HALF :].add(from_above)
        return total.at[:, :HALF].add(from_below)

    down_grads = []
    up_grads = []
    if by_rows:
        grad_in, grad_dn, grad_upper = adapter_back(
            token_low, inners[0], frozen[0], att_down[0], att_up[0], grad_q
        )
        input_grad = grad_one + grad_in
        down_grads.append(grad_dn)
        up_grads.append(grad_upper)
        grad_rows = 0.0
        for member, gradient in ((1, grad_k), (2, grad_v)):
            grad_in, grad_dn, grad_upper = adapter_back(
                rows_ext, inners[member], frozen[member], att_down[member], att_up[member], gradient
            )
            grad_rows = grad_rows + grad_in
            down_grads.append(grad_dn)
            up_grads.append(grad_upper)
        input_grad = input_grad + fold(grad_rows)
    else:
        grad_qkv = jnp.stack([grad_q, fold(grad_k).astype(BF), fold(grad_v).astype(BF)])
        grad_qkv = lax.all_to_all(grad_qkv, "head", split_axis=2, concat_axis=3, tiled=True)
        input_grad = grad_one
        for member in range(3):
            grad_in, grad_dn, grad_upper = adapter_back(
                token_low,
                inners[member],
                frozen[member],
                att_down[member],
                att_up[member],
                grad_qkv[member],
            )
            input_grad = input_grad + grad_in
            down_grads.append(grad_dn)
            up_grads.append(grad_upper)
    down_grads.append(grad_out_down)
    up_grads.append(grad_out_up)

    position_grads = (
        split_product("cb,soc->sbo", back_hot, grad_query_rel),
        split_product("cb,soc->sbo", key_hot, grad_key_rel),
    )
    grad_table_low = jnp.zeros(position_table.shape, F32)
    for member in range(2):
        gradient = position_grads[member].astype(BF)
        up = columns(att_up[member])
        grad_columns = ADAPTER_SCALING * product("spr,spo->sro", position_inners[member], gradient)
        grad_inner = (ADAPTER_SCALING * product("spo,sro->spr", gradient, up)).astype(BF)
        grad_table_low = (
            grad_table_low
            + product("spo,io->pi", gradient, columns(frozen[member]))
            + product("spr,sir->pi", grad_inner, att_down[member])
        )
        down_grads[member] = down_grads[member] + product("pi,spr->sir", table_low, grad_inner)
        if not by_rows:
            grad_columns = lax.dynamic_update_slice_in_dim(
                jnp.zeros_like(up_grads[member]),
                grad_columns,
                head_index * (width // head_groups),
                2,
            )
        up_grads[member] = up_grads[member] + grad_columns
    table_grad = norm_back(table_normed, table_inverse, position_gain, grad_table_low)

    def reduced(parts):
        totals = lax.psum(parts, ("seq", "head"))
        totals = lax.all_gather(totals, "batch", axis=0, tiled=True)
        ids = lax.all_gather(adapter_ids, "batch", axis=0, tiled=True)
        count = ADAPTERS // head_groups
        slots = head_index * count + jnp.arange(count, dtype=jnp.int32)
        select = (ids[:, None] == slots[None, :]).astype(F32)

        def spread(array):
            shape = (array.shape[0], 1) + (1,) * (array.ndim - 1)
            return jnp.sum(
                select.reshape(select.shape + (1,) * (array.ndim - 1)) * array[:, None], axis=0
            )

        return [spread(array) for array in totals]

    early = reduced([grad_exp_down, grad_exp_up, grad_red_down, grad_red_up])
    late = reduced([jnp.stack(down_grads, axis=1), jnp.stack(up_grads, axis=1)])
    table_total = lax.psum(table_grad, ("seq", "batch"))
    table_total = lax.psum_scatter(table_total, "head", scatter_dimension=0, tiled=True)
    return (
        layer_output,
        input_grad,
        table_total,
        jnp.swapaxes(late[0], 0, 1),
        jnp.swapaxes(late[1], 0, 1),
        early[0],
        early[1],
        early[2],
        early[3],
    )


def solution(mesh):
    rows = P("batch", ("seq", "head"), None)
    return jax.shard_map(
        body,
        mesh=mesh,
        in_specs=(rows, rows, P("batch", None), P("batch")) + (P(),) * 16,
        out_specs=(
            rows,
            rows,
            P("head", None),
            P(None, "head", None, None),
            P(None, "head", None, None),
            P("head", None, None),
            P("head", None, None),
            P("head", None, None),
            P("head", None, None),
        ),
        check_vma=False,
    )
```

```python
from functools import partial
import math

import jax
import jax.numpy as jnp
import numpy as np
from jax import lax
from jax.experimental import pallas as pl
from jax.experimental.pallas import tpu as pltpu
from jax.sharding import PartitionSpec as P

HEADS = 16
HEAD_DIM = 64
BUCK = 256
SPAN = 512
ADAPTERS = 8
HALF = 512
DOCS = 8

EPSILON = 1e-07
ADAPTER_SCALING = 2.0
NEGATIVE = -1e30
PRECISE = lax.Precision.HIGHEST
TILE = 128
BF = jnp.bfloat16
F32 = jnp.float32
MESH = pl.DeviceIdType.MESH
NN = (((1,), (0,)), ((), ()))
NT = (((1,), (1,)), ((), ()))


def mm(a, b, dims=NN):
    return lax.dot_general(a, b, dims, preferred_element_type=F32)

def lanes(shape=(TILE, TILE)):
    return lax.broadcasted_iota(jnp.int32, shape, 1)

def rows(shape=(TILE, TILE)):
    return lax.broadcasted_iota(jnp.int32, shape, 0)

def skew(tile):
    return pltpu.roll(tile, 0, 1, stride=1, stride_axis=0)

def flip_matrix():
    return jnp.where(lanes() + rows() == TILE - 1, 1.0, 0.0).astype(BF)


def with_halo(own_ref, halo_ref):
    return jnp.concatenate([halo_ref[0, :HALF], own_ref[0], halo_ref[0, HALF:]], axis=0)


def forward_kernel(q_ref, k_ref, kh_ref, v_ref, vh_ref, pk_ref, pq_ref, qhot_ref, kbias_ref,
                   ctx_ref, p_ref, ctxf_ref, inv_ref,
                   qs_ref, kz_ref, vz_ref, ks_ref, s_ref):
    rows_q = q_ref.shape[1]
    tiles = rows_q // TILE
    span = 2 * HALF // TILE
    width = (span + 1) * TILE
    flip = flip_matrix()
    factor = math.log2(math.e) / math.sqrt(3 * HEAD_DIM)
    k = with_halo(k_ref, kh_ref)
    v = with_halo(v_ref, vh_ref)
    kb = kbias_ref[0]
    kcol = lanes(k.shape) < HEAD_DIM
    below = lanes() + rows() < TILE
    place = lanes() + rows()
    qcol = lanes((rows_q, TILE)) < HEAD_DIM
    tcol = lanes() < HEAD_DIM
    for h in range(2):
        own = kcol if h == 0 else ~kcol
        kz_ref[h] = jnp.where(own, k, kb)
        vz_ref[h] = jnp.where(own, v, jnp.ones_like(v))
        km = jnp.where(own, k, jnp.zeros_like(k))
        for d in range(span + 1):
            lo = max(span - 1 - d, 0) * TILE
            hi = min(span + 1 - d, span) * TILE
            key_rel = mm(km[d * TILE:d * TILE + rows_q], pq_ref[0, lo:hi, :], NT).astype(BF)
            for t in range(tiles):
                part = key_rel[t * TILE:(t + 1) * TILE]
                if d == 0 or d == span:
                    picked = part
                else:
                    picked = jnp.where(below, part[:, TILE:], part[:, :TILE])
                ks_ref[h, t, d * TILE:(d + 1) * TILE, :] = skew(picked)
        q_masked = jnp.where(qcol if h == 0 else ~qcol, q_ref[0], jnp.zeros_like(q_ref[0]))
        query_rel = mm(q_masked, pk_ref[0], NT).astype(BF)
        for t in range(tiles):
            part = query_rel[t * TILE:(t + 1) * TILE]
            for d in range(span + 1):
                if d == 0:
                    picked = part[:, :TILE]
                elif d == span:
                    picked = part[:, (span - 1) * TILE:]
                else:
                    picked = jnp.where(below, part[:, d * TILE:(d + 1) * TILE], part[:, (d - 1) * TILE:d * TILE])
                qs_ref[h, t, :, d * TILE:(d + 1) * TILE] = skew(picked)

    def tile_step(t, carry):
        base = pl.multiple_of(t * TILE, TILE)
        q = q_ref[0, pl.ds(base, TILE), :]
        hot = qhot_ref[0, pl.ds(base, TILE), :]
        a = t % 2
        outs = []
        for h in range(2):
            own = tcol if h == 0 else ~tcol
            q_side = mm(flip, jnp.where(own, q, hot)).astype(BF)
            left = jnp.concatenate([q_side, flip], axis=1)
            right = jnp.concatenate([kz_ref[h, pl.ds(base, width), :], ks_ref[h, t]], axis=1)
            s_ref[h] = mm(left, right, NT) + mm(flip, qs_ref[h, t])
        for h in range(2):
            own = tcol if h == 0 else ~tcol
            first = s_ref[h, :, :TILE]
            s_ref[h, :, :TILE] = jnp.where(place > TILE - 1, first, NEGATIVE)
            last = s_ref[h, :, span * TILE:]
            s_ref[h, :, span * TILE:] = jnp.where(place < TILE - 1, last, NEGATIVE)
            mid = s_ref[h, :, (span // 2) * TILE:(span // 2 + 1) * TILE]
            s_ref[h, :, (span // 2) * TILE:(span // 2 + 1) * TILE] = jnp.where((place == TILE - 1) & (mid < 0.1 * NEGATIVE), 0.0, mid)
            top = s_ref[h, :, :TILE]
            for d in range(1, span + 1):
                top = jnp.maximum(top, s_ref[h, :, d * TILE:(d + 1) * TILE])
            peak = jnp.max(top, axis=1, keepdims=True)
            prob = jnp.exp2((s_ref[h] - peak) * factor).astype(BF)
            p_ref[0, h, t // 2, pl.ds(pl.multiple_of(a * TILE, TILE), TILE), pl.ds(pl.multiple_of(a * TILE, TILE), width)] = prob
            total = mm(prob, vz_ref[h, pl.ds(base, width), :])
            swapped = pltpu.roll(total, HEAD_DIM, 1)
            den = jnp.where(own, swapped, total)
            inv = 1.0 / den
            inv_ref[0, h, pl.ds(base, TILE), :] = inv
            p_ref[0, h, t // 2, pl.ds(pl.multiple_of(a * TILE, TILE), TILE), pl.ds(pl.multiple_of((1 - a) * width, TILE), TILE)] = jnp.zeros((TILE, TILE), BF)
            outs.append(total * inv)
        ctx = jnp.where(tcol, outs[0], outs[1])
        ctxf_ref[0, pl.ds(base, TILE), :] = ctx
        ctx_ref[0, pl.ds(base, TILE), :] = mm(flip, ctx.astype(BF)).astype(BF)
        return carry

    lax.fori_loop(0, tiles, tile_step, 0, unroll=True)


def attention_forward(q, k, k_halo, v, v_halo, pk, pq, qhot, kbias):
    n, rq, width = q.shape
    off = 2 * HALF
    rk = rq + off
    pairs = width // TILE
    def col(r):
        return pl.BlockSpec((1, r, TILE), lambda s, p: (s, 0, p))
    def whole(r):
        return pl.BlockSpec((1, r, TILE), lambda s, p: (s, 0, 0))
    wide = off + 2 * TILE
    return pl.pallas_call(
        forward_kernel,
        grid=(n, pairs),
        in_specs=[col(rq), col(rq), col(off), col(rq), col(off), col(off), col(off), whole(rq), whole(rk)],
        out_specs=[col(rq),
                   pl.BlockSpec((1, 2, rq // (2 * TILE), 2 * TILE, wide), lambda s, p: (s, p, 0, 0, 0)),
                   col(rq),
                   pl.BlockSpec((1, 2, rq, TILE), lambda s, p: (s, p, 0, 0))],
        out_shape=[jax.ShapeDtypeStruct((n, rq, width), BF),
                   jax.ShapeDtypeStruct((n, 2 * pairs, rq // (2 * TILE), 2 * TILE, wide), BF),
                   jax.ShapeDtypeStruct((n, rq, width), F32),
                   jax.ShapeDtypeStruct((n, 2 * pairs, rq, TILE), F32)],
        scratch_shapes=[pltpu.VMEM((2, rq // TILE, TILE, off + TILE), BF),
                        pltpu.VMEM((2, rk, TILE), BF), pltpu.VMEM((2, rk, TILE), BF),
                        pltpu.VMEM((2, rq // TILE, off + TILE, TILE), BF),
                        pltpu.VMEM((2, TILE, off + TILE), F32)],
        compiler_params=pltpu.CompilerParams(dimension_semantics=("arbitrary", "arbitrary"), vmem_limit_bytes=48 * 2**20),
        name="attention_forward",
    )(q, k, k_halo, v, v_halo, pk, pq, qhot, kbias)


def backward_kernel(q_ref, k_ref, kh_ref, v_ref, vh_ref, pk_ref, pq_ref, p_ref, g_ref, ctxf_ref, inv_ref,
                    dq_ref, dk_ref, dkh_ref, dv_ref, dvh_ref, dpk_ref, dpq_ref,
                    kx_ref, vx_ref, qr_ref, gr_ref, e_ref, gc_ref, gk_ref, dvt_ref):
    rows_q = q_ref.shape[1]
    rows_k = kx_ref.shape[0]
    kx_ref[...] = with_halo(k_ref, kh_ref)
    vx_ref[...] = with_halo(v_ref, vh_ref)
    tiles = rows_q // TILE
    key_tiles = rows_k // TILE
    span = 2 * HALF // TILE
    wide = (span + 2) * TILE
    flip = flip_matrix()
    scale = 1.0 / math.sqrt(3 * HEAD_DIM)
    tcol = lanes() < HEAD_DIM
    qcol = lanes((rows_q, TILE)) < HEAD_DIM
    over = lanes() > rows()
    under = lanes() >= rows()

    @pl.when((pl.program_id(0) == 0) & (pl.program_id(1) == 0))
    def _():
        gk_ref[...] = jnp.zeros_like(gk_ref)

    for t in range(tiles):
        at = slice(t * TILE, (t + 1) * TILE)
        qr_ref[at] = mm(flip, q_ref[0, at]).astype(BF)
        gr_ref[at] = mm(flip, g_ref[0, at]).astype(BF)
    q_rev = qr_ref[...]
    g_rev = gr_ref[...]
    q_turned = q_rev.T
    k_turned = kx_ref[...].T
    product = g_rev.astype(F32) * ctxf_ref[0]
    dvt_ref[...] = jnp.zeros_like(dvt_ref)
    dq_parts = []
    dk_parts = []
    for h in range(2):
        own = qcol if h == 0 else ~qcol
        part = slice(h * HEAD_DIM, (h + 1) * HEAD_DIM)
        g_masked = jnp.where(own, g_rev, jnp.zeros_like(g_rev))
        inv = inv_ref[0, h]
        delta = jnp.sum(jnp.where(own, product, 0.0), axis=1, keepdims=True) * inv
        g_turned = (g_rev.astype(F32) * inv).astype(BF).T[part]
        dq_main = []
        for u in range(tiles // 2):
            at = slice(u * 2 * TILE, (u + 1) * 2 * TILE)
            window = slice(u * 2 * TILE, u * 2 * TILE + wide)
            prob = p_ref[0, h, u]
            g_probs = mm(g_masked[at], vx_ref[window], NT)
            inv_u = jnp.concatenate([inv[at]] * (span + 2), axis=1)
            delta_u = jnp.concatenate([delta[at]] * (span + 2), axis=1)
            e = (prob.astype(F32) * (g_probs * inv_u - delta_u)).astype(BF)
            e_ref[h, u] = e
            dvt_ref[part, window] += mm(g_turned[:, at], prob)
            dq_main.append(mm(e, kx_ref[window]))
            for a in range(2):
                for t in range(span):
                    def turned(d):
                        return pltpu.roll(e_ref[h, u, a * TILE:(a + 1) * TILE, (a + d) * TILE:(a + d + 1) * TILE], 1, 1, stride=1, stride_axis=0)
                    here = turned(t) if t == 0 else after
                    after = turned(t + 1)
                    gc_ref[h, (2 * u + a) * TILE:(2 * u + a + 1) * TILE, t * TILE:(t + 1) * TILE] = jnp.where(over, after, here)
        dq_parts.append(jnp.concatenate(dq_main, axis=0) + mm(gc_ref[h], pk_ref[0]))
        dpk_ref[0, part, :] = (mm(q_turned[part], gc_ref[h]) * scale).astype(BF)
        dk_tiles = []
        for kt in range(key_tiles):
            dlow = max(0, kt - tiles + 1)
            dhigh = min(span, kt)
            flat = []
            spun = {}
            for d in range(dlow, dhigh + 1):
                qt = kt - d
                a = qt % 2
                et = e_ref[h, qt // 2, a * TILE:(a + 1) * TILE, (a + d) * TILE:(a + d + 1) * TILE].T
                flat.append((qt, et))
                spun[d] = skew(et)
            tlow = max(dlow - 1, 0)
            thigh = min(dhigh, span - 1)
            for t in range(tlow, thigh + 1):
                zero = jnp.zeros((TILE, TILE), BF)
                gk_ref[h, kt * TILE:(kt + 1) * TILE, t * TILE:(t + 1) * TILE] = jnp.where(under, spun.get(t + 1, zero), spun.get(t, zero))
            flat = flat[::-1]
            left = jnp.concatenate([et for _, et in flat] + [gk_ref[h, kt * TILE:(kt + 1) * TILE, tlow * TILE:(thigh + 1) * TILE]], axis=1)
            right = jnp.concatenate([q_rev[flat[0][0] * TILE:(flat[-1][0] + 1) * TILE], pq_ref[0, tlow * TILE:(thigh + 1) * TILE]], axis=0)
            dk_tiles.append(mm(left, right))
        dk_parts.append(jnp.concatenate(dk_tiles, axis=0))
        dpq_ref[0, part, :] = (mm(k_turned[part], gk_ref[h]) * scale).astype(BF)
    dq = (jnp.where(qcol, dq_parts[0], dq_parts[1]) * scale).astype(BF)
    for t in range(tiles):
        at = slice(t * TILE, (t + 1) * TILE)
        dq_ref[0, at] = mm(flip, dq[at]).astype(BF)
    kcol = lanes((rows_k, TILE)) < HEAD_DIM
    dk = (jnp.where(kcol, dk_parts[0], dk_parts[1]) * scale).astype(BF)
    dv = dvt_ref[...].astype(BF).T
    for whole, own_ref, halo_ref in ((dk, dk_ref, dkh_ref), (dv, dv_ref, dvh_ref)):
        halo_ref[0, :HALF] = whole[:HALF]
        own_ref[0] = whole[HALF : HALF + rows_q]
        halo_ref[0, HALF:] = whole[HALF + rows_q :]


def attention_backward(q, k, k_halo, v, v_halo, pk, pq, probs, g, ctxf, inv):
    n, rq, width = q.shape
    off = 2 * HALF
    rk = rq + off
    pairs = width // TILE
    wide = off + 2 * TILE
    def col(r):
        return pl.BlockSpec((1, r, TILE), lambda s, p: (s, 0, p))
    def row(r):
        return pl.BlockSpec((1, TILE, r), lambda s, p: (s, p, 0))
    return pl.pallas_call(
        backward_kernel,
        grid=(n, pairs),
        in_specs=[col(rq), col(rq), col(off), col(rq), col(off), col(off), col(off),
                  pl.BlockSpec((1, 2, rq // (2 * TILE), 2 * TILE, wide), lambda s, p: (s, p, 0, 0, 0)),
                  col(rq), col(rq),
                  pl.BlockSpec((1, 2, rq, TILE), lambda s, p: (s, p, 0, 0))],
        out_specs=[col(rq), col(rq), col(off), col(rq), col(off), row(off), row(off)],
        out_shape=[jax.ShapeDtypeStruct((n, rq, width), BF),
                   jax.ShapeDtypeStruct((n, rq, width), BF),
                   jax.ShapeDtypeStruct((n, off, width), BF),
                   jax.ShapeDtypeStruct((n, rq, width), BF),
                   jax.ShapeDtypeStruct((n, off, width), BF),
                   jax.ShapeDtypeStruct((n, width, off), BF),
                   jax.ShapeDtypeStruct((n, width, off), BF)],
        scratch_shapes=[pltpu.VMEM((rk, TILE), BF), pltpu.VMEM((rk, TILE), BF), pltpu.VMEM((rq, TILE), BF), pltpu.VMEM((rq, TILE), BF),
                        pltpu.VMEM((2, rq // (2 * TILE), 2 * TILE, wide), BF),
                        pltpu.VMEM((2, rq, off), BF),
                        pltpu.VMEM((2, rk, off), BF),
                        pltpu.VMEM((TILE, rk), F32)],
        compiler_params=pltpu.CompilerParams(dimension_semantics=("arbitrary", "arbitrary"), vmem_limit_bytes=56 * 2**20),
        name="attention_backward",
    )(q, k, k_halo, v, v_halo, pk, pq, probs, g, ctxf, inv)

def reduce_kernel(halo_ref, table_ref, lora_ref, halo_out, table_out, lora_out, halo_sems, core_ref, stage_ref, recv_ref, sum_ref,
                  mine_t, mine_l, core_sems, send_sems, recv_sems, spread_l, spread_t,
                  arrive_l, arrive_t, pass_l, pass_t, other_l, other_t):
    blocks, heads = lax.axis_size("seq"), lax.axis_size("head")
    seq, head, core = lax.axis_index("seq"), lax.axis_index("head"), lax.axis_index("batch")
    peers = blocks * heads
    me = seq * heads + head
    width = table_ref.shape[3]
    partner = (seq, head, 1 - core)

    def place(p):
        return (p // heads, p % heads, core)

    def remote(src, dst, send, recv, device):
        return pltpu.make_async_remote_copy(
            src_ref=src, dst_ref=dst, send_sem=send, recv_sem=recv, device_id=device, device_id_type=MESH
        )

    def each(count, step):
        lax.fori_loop(1, count, lambda k, c: (step(k), c)[1], 0)

    barrier = pltpu.get_barrier_semaphore()
    pl.semaphore_signal(barrier, inc=1, device_id=partner, device_id_type=MESH)
    each(peers, lambda k: pl.semaphore_signal(barrier, inc=1, device_id=place((me + k) % peers), device_id_type=MESH))
    pl.semaphore_wait(barrier, peers)

    before = remote(halo_ref.at[0], halo_out.at[1], halo_sems.at[0], halo_sems.at[1], place(jnp.maximum(me - 1, 0)))
    after = remote(halo_ref.at[1], halo_out.at[0], halo_sems.at[2], halo_sems.at[3], place(jnp.minimum(me + 1, peers - 1)))

    @pl.when(me > 0)
    def _():
        before.start()

    @pl.when(me < peers - 1)
    def _():
        after.start()

    swap = remote(table_ref.at[1 - core], core_ref, core_sems.at[0], core_sems.at[1], partner)
    swap.start()
    swap.wait()

    def to_peer(p):
        return remote(stage_ref.at[p], recv_ref.at[me], send_sems.at[p], recv_sems.at[me], place(p))

    def send(k):
        p = (me + k) % peers
        stage_ref[p, :, :width] = (table_ref[core, p].astype(F32) + core_ref[p].astype(F32)).astype(BF)
        stage_ref[p, :, width:] = lora_ref[p]
        to_peer(p).start()

    each(peers, send)
    sum_ref[:, :width] = table_ref[core, me].astype(F32) + core_ref[me].astype(F32)
    sum_ref[:, width:] = lora_ref[me].astype(F32)

    def take(k):
        p = (me + peers - k) % peers
        remote(stage_ref.at[p], recv_ref.at[p], send_sems.at[p], recv_sems.at[p], place(p)).wait_recv()
        sum_ref[...] += recv_ref[p].astype(F32)

    each(peers, take)
    mine_t[...] = sum_ref[:, :width].astype(BF)
    mine_l[...] = sum_ref[:, width:].astype(BF)
    lora_out[core, me] = mine_l[...]
    table_out[seq, core] = mine_t[...]

    def give_l(p):
        return remote(mine_l, lora_out.at[core, me], spread_l.at[p], arrive_l.at[me], place(p))

    def give_t(s):
        return remote(mine_t, table_out.at[seq, core], spread_t.at[s], arrive_t.at[seq], (s, head, core))

    each(peers, lambda k: give_l((me + k) % peers).start())
    each(blocks, lambda k: give_t((seq + k) % blocks).start())

    def on_l(p):
        return remote(lora_out.at[core, p], lora_out.at[core, p], pass_l.at[p], other_l.at[p], partner)

    def on_t(s):
        return remote(table_out.at[s, core], table_out.at[s, core], pass_t.at[s], other_t.at[s], partner)

    on_l(me).start()
    on_t(seq).start()

    def got_l(k):
        p = (me + peers - k) % peers
        remote(mine_l, lora_out.at[core, p], spread_l.at[p], arrive_l.at[p], place(p)).wait_recv()
        on_l(p).start()

    def got_t(k):
        s = (seq + blocks - k) % blocks
        remote(mine_t, table_out.at[s, core], spread_t.at[s], arrive_t.at[s], (s, head, core)).wait_recv()
        on_t(s).start()

    each(peers, got_l)
    each(blocks, got_t)

    def end_l(k):
        p = k - 1
        remote(lora_out.at[1 - core, p], lora_out.at[1 - core, p], pass_l.at[p], other_l.at[p], partner).wait_recv()
        on_l(p).wait_send()

    def end_t(k):
        s = k - 1
        remote(table_out.at[s, 1 - core], table_out.at[s, 1 - core], pass_t.at[s], other_t.at[s], partner).wait_recv()
        on_t(s).wait_send()

    each(peers + 1, end_l)
    each(blocks + 1, end_t)

    def sent(k):
        p = (me + k) % peers
        to_peer(p).wait_send()
        give_l(p).wait_send()

    each(peers, sent)
    each(blocks, lambda k: give_t((seq + k) % blocks).wait_send())

    @pl.when(me > 0)
    def _():
        before.wait_send()
        after.wait_recv()

    @pl.when(me < peers - 1)
    def _():
        after.wait_send()
        before.wait_recv()


def reduce_late(halo, table, lora):
    cores, peers, rank, width = table.shape
    extra = lora.shape[2]
    blocks = lax.axis_size("seq")
    vm = pl.BlockSpec(memory_space=pltpu.VMEM)
    hbm = pl.BlockSpec(memory_space=pl.ANY)
    dma = pltpu.SemaphoreType.DMA
    return pl.pallas_call(
        reduce_kernel,
        in_specs=[hbm, vm, vm],
        out_specs=[hbm, vm, vm],
        out_shape=[jax.ShapeDtypeStruct(halo.shape, BF), jax.ShapeDtypeStruct((blocks, cores, rank, width), BF),
                   jax.ShapeDtypeStruct((cores, peers, rank, extra), BF)],
        scratch_shapes=[
            dma((4,)),
            pltpu.VMEM((peers, rank, width), BF),
            pltpu.VMEM((peers, rank, width + extra), BF),
            pltpu.VMEM((peers, rank, width + extra), BF),
            pltpu.VMEM((rank, width + extra), F32),
            pltpu.VMEM((rank, width), BF),
            pltpu.VMEM((rank, extra), BF),
            dma((2,)), dma((peers,)), dma((peers,)), dma((peers,)), dma((blocks,)),
            dma((peers,)), dma((blocks,)), dma((peers,)), dma((blocks,)), dma((peers,)), dma((blocks,)),
        ],
        compiler_params=pltpu.CompilerParams(collective_id=0, has_side_effects=True, vmem_limit_bytes=32 * 2**20),
        name="reduce_late",
    )(halo, table, lora)


def load_all(pairs, sems):
    copies = []
    for index, (source, target) in enumerate(pairs):
        copy = pltpu.make_async_copy(source, target, sems.at[index])
        copy.start()
        copies.append(copy)
    return copies


def gather_rows(left, right):
    return lax.dot_general(left, right, (((0,), (0,)), ((), ())), preferred_element_type=F32)


def maps_kernel(count, *refs):
    x_ref = refs[0]
    weights = refs[1 : 1 + count]
    downs = refs[1 + count : 1 + 2 * count]
    ups = refs[1 + 2 * count : 1 + 3 * count]
    results = refs[1 + 3 * count : 1 + 4 * count]
    inners = refs[1 + 4 * count : 1 + 5 * count]
    held, sems = refs[1 + 5 * count :]
    copies = load_all([(weights[i], held.at[i]) for i in range(count)], sems)
    x = x_ref[...]
    for i in range(count):
        inners[i][...] = mm(x, downs[i][...], NT).astype(BF)
    for i in range(count):
        copies[i].wait()
        results[i][...] = (
            mm(x, held[i]) + ADAPTER_SCALING * mm(inners[i][...], ups[i][...])
        ).astype(BF)


def maps(x, weights, downs, ups):
    rows, width = x.shape
    count = len(weights)
    rank = ups[0].shape[0]
    vm = pl.BlockSpec(memory_space=pltpu.VMEM)
    found = pl.pallas_call(
        partial(maps_kernel, count),
        in_specs=[vm] + [pl.BlockSpec(memory_space=pl.ANY)] * count + [vm] * (2 * count),
        out_specs=[vm] * (2 * count),
        out_shape=[jax.ShapeDtypeStruct((rows, width), BF)] * count
        + [jax.ShapeDtypeStruct((rows, rank), BF)] * count,
        scratch_shapes=[pltpu.VMEM((count, width, width), BF), pltpu.SemaphoreType.DMA((count,))],
        compiler_params=pltpu.CompilerParams(vmem_limit_bytes=48 * 2**20),
        cost_estimate=pl.CostEstimate(
            flops=2 * count * rows * width * width,
            bytes_accessed=2 * count * width * (width + rows),
            transcendentals=0,
        ),
        name="maps",
    )(x, *weights, *downs, *ups)
    return found[:count], found[count:]


def position_kernel(table_ref, gain_ref, query_w_hbm, key_w_hbm, query_a_ref, key_a_ref, query_b_ref, key_b_ref,
                    key_hot_ref, query_hot_ref, back_hot_ref,
                    key_rel_ref, query_rel_ref, back_rel_ref, low_ref, normed_ref, inverse_ref, query_u_ref, key_u_ref,
                    held, sems):
    copies = load_all([(query_w_hbm, held.at[0]), (key_w_hbm, held.at[1])], sems)
    values = table_ref[...]
    centered = values - jnp.mean(values, axis=1, keepdims=True)
    inverse = lax.rsqrt(jnp.mean(centered * centered, axis=1, keepdims=True) + EPSILON)
    normed = centered * inverse
    normed_ref[...] = normed
    inverse_ref[...] = inverse
    low = (normed * gain_ref[...]).astype(BF)
    low_ref[...] = low
    query_u = mm(low, query_a_ref[...], NT).astype(BF)
    key_u = mm(low, key_a_ref[...], NT).astype(BF)
    query_u_ref[...] = query_u
    key_u_ref[...] = key_u
    copies[0].wait()
    query = (mm(low, held[0]) + ADAPTER_SCALING * mm(query_u, query_b_ref[...])).astype(BF)
    query_rel_ref[...] = mm(query_hot_ref[...], query).astype(BF)
    back_rel_ref[...] = mm(back_hot_ref[...], query).astype(BF)
    copies[1].wait()
    key = (mm(low, held[1]) + ADAPTER_SCALING * mm(key_u, key_b_ref[...])).astype(BF)
    key_rel_ref[...] = mm(key_hot_ref[...], key).astype(BF)


def positions(table, gain, weights, downs, ups, hots):
    rows, width = table.shape
    rank = ups[0].shape[0]
    spans = hots[0].shape[0]
    vm = pl.BlockSpec(memory_space=pltpu.VMEM)
    relative = jax.ShapeDtypeStruct((spans, width), BF)
    inner = jax.ShapeDtypeStruct((rows, rank), BF)
    return pl.pallas_call(
        position_kernel,
        in_specs=[vm] * 2 + [pl.BlockSpec(memory_space=pl.ANY)] * 2 + [vm] * 7,
        out_specs=[vm] * 8,
        out_shape=[relative] * 3
        + [jax.ShapeDtypeStruct((rows, width), BF), jax.ShapeDtypeStruct((rows, width), F32),
           jax.ShapeDtypeStruct((rows, 1), F32), inner, inner],
        scratch_shapes=[pltpu.VMEM((2, width, width), BF), pltpu.SemaphoreType.DMA((2,))],
        compiler_params=pltpu.CompilerParams(vmem_limit_bytes=48 * 2**20),
        cost_estimate=pl.CostEstimate(
            flops=10 * rows * width * width, bytes_accessed=20 * rows * width, transcendentals=rows
        ),
        name="positions",
    )(table, gain.reshape(1, width), *weights, *downs, *ups, *hots)


def halo_kernel(key_g_ref, value_g_ref, key_w_ref, value_w_ref, key_a_ref, value_a_ref, key_b_ref, value_b_ref,
                grad_ref, key_u_ref, value_u_ref):
    key_u = (ADAPTER_SCALING * mm(key_g_ref[...], key_b_ref[...], NT)).astype(BF)
    value_u = (ADAPTER_SCALING * mm(value_g_ref[...], value_b_ref[...], NT)).astype(BF)
    key_u_ref[...] = key_u
    value_u_ref[...] = value_u
    grad_ref[...] = (
        mm(key_g_ref[...], key_w_ref[...], NT)
        + mm(value_g_ref[...], value_w_ref[...], NT)
        + mm(key_u, key_a_ref[...])
        + mm(value_u, value_a_ref[...])
    ).astype(BF)


def halo_gradients(key_g, value_g, weights, downs, ups):
    rows, width = key_g.shape
    rank = ups[0].shape[0]
    vm = pl.BlockSpec(memory_space=pltpu.VMEM)
    inner = jax.ShapeDtypeStruct((rows, rank), BF)
    return pl.pallas_call(
        halo_kernel,
        in_specs=[vm] * 8,
        out_specs=[vm] * 3,
        out_shape=[jax.ShapeDtypeStruct((rows, width), BF), inner, inner],
        compiler_params=pltpu.CompilerParams(vmem_limit_bytes=48 * 2**20),
        cost_estimate=pl.CostEstimate(
            flops=4 * rows * width * width, bytes_accessed=6 * rows * width + 4 * width * width, transcendentals=0
        ),
        name="halo_gradients",
    )(key_g, value_g, *weights, *downs, *ups)


def tail_kernel(shape, query_g_ref, key_g_ref, value_g_ref, key_halo_ref, value_halo_ref, key_hu_ref, value_hu_ref,
                x_ref, x_halo_ref, query_u_ref, key_u_ref, value_u_ref, key_uh_ref, value_uh_ref,
                key_rel_g_ref, query_rel_g_ref, key_hot_ref, back_hot_ref, low_ref, query_pu_ref, key_pu_ref,
                query_a_ref, key_a_ref, value_a_ref, query_b_ref, key_b_ref, value_b_ref,
                out_a_ref, out_b_ref, ff_ref, grad_one_ref, query_w_hbm, key_w_hbm, value_w_hbm,
                grad_ref, table_ref, late_ref, held, sems):
    groups, blocks, cores, rank = shape
    copies = load_all(
        [(query_w_hbm, held.at[0]), (key_w_hbm, held.at[1]), (value_w_hbm, held.at[2])], sems
    )
    position_q = mm(back_hot_ref[...], query_rel_g_ref[...], NT).astype(BF)
    position_k = mm(key_hot_ref[...], key_rel_g_ref[...], NT).astype(BF)
    low = low_ref[...]
    query_pg = (ADAPTER_SCALING * mm(position_q, query_b_ref[...], NT)).astype(BF)
    key_pg = (ADAPTER_SCALING * mm(position_k, key_b_ref[...], NT)).astype(BF)
    table = mm(query_pg, query_a_ref[...]) + mm(key_pg, key_a_ref[...])
    copies[0].wait()
    table += mm(position_q, held[0], NT)
    copies[1].wait()
    table = (table + mm(position_k, held[1], NT)).astype(BF)
    for group in range(groups):
        for block in range(blocks):
            for core in range(cores):
                start = ((group * blocks + block) * cores + core) * rank
                table_ref[core, block * groups + group] = table[start : start + rank]
    x = x_ref[...]
    x_halo = x_halo_ref[...]
    query_gu = (ADAPTER_SCALING * mm(query_g_ref[...], query_b_ref[...], NT)).astype(BF)
    key_gu = (ADAPTER_SCALING * mm(key_g_ref[...], key_b_ref[...], NT)).astype(BF)
    value_gu = (ADAPTER_SCALING * mm(value_g_ref[...], value_b_ref[...], NT)).astype(BF)
    pieces = [
        gather_rows(query_gu, x) + gather_rows(query_pg, low),
        gather_rows(key_gu, x) + gather_rows(key_hu_ref[...], x_halo) + gather_rows(key_pg, low),
        gather_rows(value_gu, x) + gather_rows(value_hu_ref[...], x_halo),
        out_a_ref[...],
        ADAPTER_SCALING
        * (gather_rows(query_u_ref[...], query_g_ref[...]) + gather_rows(query_pu_ref[...], position_q)),
        ADAPTER_SCALING
        * (
            gather_rows(key_u_ref[...], key_g_ref[...])
            + gather_rows(key_uh_ref[...], key_halo_ref[...])
            + gather_rows(key_pu_ref[...], position_k)
        ),
        ADAPTER_SCALING
        * (
            gather_rows(value_u_ref[...], value_g_ref[...])
            + gather_rows(value_uh_ref[...], value_halo_ref[...])
        ),
        out_b_ref[...],
    ]
    peers = late_ref.shape[0]
    part = len(pieces) * x.shape[1] // peers
    per = x.shape[1] // part
    rest = ff_ref.shape[1] // peers
    for peer in range(peers):
        late_ref[peer, :, part:] = ff_ref[:, peer * rest : (peer + 1) * rest].astype(BF)
    for index, piece in enumerate(pieces):
        for half in range(per):
            late_ref[index * per + half, :, :part] = piece[:, half * part : (half + 1) * part].astype(BF)
    copies[2].wait()
    grad_ref[...] = (
        grad_one_ref[...]
        + mm(query_g_ref[...], held[0], NT)
        + mm(key_g_ref[...], held[1], NT)
        + mm(value_g_ref[...], held[2], NT)
        + mm(query_gu, query_a_ref[...])
        + mm(key_gu, key_a_ref[...])
        + mm(value_gu, value_a_ref[...])
    )


def tail_gradients(shape, arrays, weights):
    groups, blocks, cores, rank = shape
    rows, width = arrays[0].shape
    vm = pl.BlockSpec(memory_space=pltpu.VMEM)
    peers = groups * blocks
    share = (8 * width + arrays[-2].shape[1]) // peers
    return pl.pallas_call(
        partial(tail_kernel, shape),
        in_specs=[vm] * len(arrays) + [pl.BlockSpec(memory_space=pl.ANY)] * 3,
        out_specs=[vm] * 3,
        out_shape=[
            jax.ShapeDtypeStruct((rows, width), F32),
            jax.ShapeDtypeStruct((cores, peers, rank, width), BF),
            jax.ShapeDtypeStruct((peers, rank, share), BF),
        ],
        scratch_shapes=[pltpu.VMEM((3, width, width), BF), pltpu.SemaphoreType.DMA((3,))],
        compiler_params=pltpu.CompilerParams(vmem_limit_bytes=58 * 2**20),
        cost_estimate=pl.CostEstimate(
            flops=16 * rows * width * width, bytes_accessed=60 * rows * width, transcendentals=0
        ),
        name="tail_gradients",
    )(*arrays, *weights)


def middle_kernel(seqs, context_ref, tokens_ref, cotangent_ref, out_w_hbm, up_w_hbm, down_w_hbm,
                  out_a_ref, out_b_ref, up_a_ref, up_b_ref, down_a_ref, down_b_ref, gain_one_ref, gain_two_ref,
                  layer_ref, grad_one_ref, grad_context_ref, out_ga_ref, out_gb_ref, ff_ref,
                  out_w, up_w, down_w, hidden_ref, low_ref, work_ref, act_ref, slope_ref, sems):
    rows, width = tokens_ref.shape
    ff = up_w.shape[1]
    share = rows // seqs
    chunk = 512
    copies = []
    for index, (source, target) in enumerate(((out_w_hbm, out_w), (up_w_hbm, up_w), (down_w_hbm, down_w))):
        copy = pltpu.make_async_copy(source, target, sems.at[index])
        copy.start()
        copies.append(copy)

    def parts(step):
        found = [step(s, slice(s * share, (s + 1) * share)) for s in range(seqs)]
        return found[0] if seqs == 1 else jnp.concatenate(found, axis=0)

    def inner(values, factor_ref, scale=1.0):
        return parts(lambda s, at: (scale * mm(values[at], factor_ref[s], NT)).astype(BF))

    def widened(inner_values, factor_ref, columns=slice(None)):
        return parts(lambda s, at: mm(inner_values[at], factor_ref[s, :, columns]))

    def factor_grad(left, right, s):
        at = slice(s * share, (s + 1) * share)
        return lax.dot_general(left[at], right[at], (((0,), (0,)), ((), ())), preferred_element_type=F32)

    def stats(values):
        centered = values - jnp.mean(values, axis=1, keepdims=True)
        inverse = lax.rsqrt(jnp.mean(centered * centered, axis=1, keepdims=True) + EPSILON)
        return centered * inverse, inverse

    def back(normed, inverse, gain, upstream):
        scaled = upstream * gain
        return inverse * (
            scaled
            - jnp.mean(scaled, axis=1, keepdims=True)
            - normed * jnp.mean(scaled * normed, axis=1, keepdims=True)
        )

    context = context_ref[...]
    inner_out = inner(context, out_a_ref)
    copies[0].wait()
    attended = mm(context, out_w[...]) + ADAPTER_SCALING * widened(inner_out, out_b_ref)
    normed_one, inverse_one = stats(tokens_ref[...] + attended)
    grad_one_ref[...] = normed_one
    hidden = normed_one * gain_one_ref[...]
    hidden_ref[...] = hidden
    low_ref[...] = hidden.astype(BF)
    low = low_ref[...]
    inner_up = inner(low, up_a_ref)
    copies[1].wait()
    for start in range(0, ff, chunk):
        columns = slice(start, start + chunk)
        pre = mm(low, up_w[:, columns]) + ADAPTER_SCALING * widened(inner_up, up_b_ref, columns)
        below = 0.5 + 0.5 * lax.erf(pre * math.sqrt(0.5))
        act_ref[:, columns] = (pre * below).astype(BF)
        density = jnp.exp(pre * pre * -0.5) * (1.0 / math.sqrt(2.0 * math.pi))
        slope_ref[:, columns] = (below + pre * density).astype(BF)
    act = act_ref[...]
    inner_down = inner(act, down_a_ref)
    copies[2].wait()
    branch = mm(act, down_w[...]) + ADAPTER_SCALING * widened(inner_down, down_b_ref)
    normed_two, inverse_two = stats(hidden_ref[...] + branch)
    layer_ref[...] = normed_two * gain_two_ref[...]
    work_ref[...] = back(normed_two, inverse_two, gain_two_ref[...], cotangent_ref[...])
    grad_low = work_ref[...].astype(BF)
    grad_inner = inner(grad_low, down_b_ref, ADAPTER_SCALING)
    for s in range(seqs):
        ff_ref[s, :, width + 2 * ff:] = ADAPTER_SCALING * factor_grad(inner_down, grad_low, s)
        ff_ref[s, :, width + ff:width + 2 * ff] = factor_grad(grad_inner, act, s)
    for start in range(0, ff, chunk):
        columns = slice(start, start + chunk)
        grad_act = mm(grad_low, down_w[columns, :], NT) + widened(grad_inner, down_a_ref, columns)
        slope_ref[:, columns] = (grad_act.astype(BF).astype(F32) * slope_ref[:, columns].astype(F32)).astype(BF)
    grad_pre = slope_ref[...]
    grad_inner = inner(grad_pre, up_b_ref, ADAPTER_SCALING)
    for s in range(seqs):
        ff_ref[s, :, width:width + ff] = ADAPTER_SCALING * factor_grad(inner_up, grad_pre, s)
        ff_ref[s, :, :width] = factor_grad(grad_inner, low, s)
    grad_hidden = mm(grad_pre, up_w[...], NT) + widened(grad_inner, up_a_ref)
    grad_one = back(grad_one_ref[...], inverse_one, gain_one_ref[...], grad_hidden + work_ref[...])
    grad_one_ref[...] = grad_one
    grad_low = grad_one.astype(BF)
    grad_inner = inner(grad_low, out_b_ref, ADAPTER_SCALING)
    for s in range(seqs):
        out_gb_ref[s] = ADAPTER_SCALING * factor_grad(inner_out, grad_low, s)
        out_ga_ref[s] = factor_grad(grad_inner, context, s)
    grad_context_ref[...] = (mm(grad_low, out_w[...], NT) + widened(grad_inner, out_a_ref)).astype(BF)


def middle(context, tokens, cotangent, out_weight, up_weight, down_weight, factors, gain_one, gain_two):
    seqs, share, width = tokens.shape
    rows = seqs * share
    ff = up_weight.shape[1]
    rank = factors[0].shape[1]
    vm = pl.BlockSpec(memory_space=pltpu.VMEM)
    hbm = pl.BlockSpec(memory_space=pl.ANY)
    wide = jax.ShapeDtypeStruct((rows, width), F32)
    factor = jax.ShapeDtypeStruct((seqs, rank, width), F32)
    found = pl.pallas_call(
        partial(middle_kernel, seqs),
        in_specs=[vm] * 3 + [hbm] * 3 + [vm] * 8,
        out_specs=[vm] * 6,
        out_shape=[wide, wide, jax.ShapeDtypeStruct((rows, width), BF), factor, factor,
                   jax.ShapeDtypeStruct((seqs, rank, 2 * width + 2 * ff), F32)],
        scratch_shapes=[
            pltpu.VMEM(out_weight.shape, BF), pltpu.VMEM(up_weight.shape, BF), pltpu.VMEM(down_weight.shape, BF),
            pltpu.VMEM((rows, width), F32), pltpu.VMEM((rows, width), BF), pltpu.VMEM((rows, width), F32),
            pltpu.VMEM((rows, ff), BF), pltpu.VMEM((rows, ff), BF), pltpu.SemaphoreType.DMA((3,)),
        ],
        compiler_params=pltpu.CompilerParams(vmem_limit_bytes=60 * 2**20),
        cost_estimate=pl.CostEstimate(flops=36 * rows * width * width, bytes_accessed=2 * 12 * width * width, transcendentals=rows * ff),
        name="middle",
    )(context.reshape(rows, width), tokens.reshape(rows, width), cotangent.reshape(rows, width),
      out_weight, up_weight, down_weight, *factors, gain_one.reshape(1, width), gain_two.reshape(1, width))
    return [array.reshape(seqs, share, width) for array in found[:3]] + list(found[3:])


def shifted(value, axes, steps):
    count = math.prod(lax.axis_size(axis) for axis in axes)
    initial, last = (max(0, -steps), min(count, count - steps))
    return lax.ppermute(value, axes, [(source, source + steps) for source in range(initial, last)])


def bucket_of(offset, buckets, distance_cap):
    middle = buckets // 2
    sign_of = np.sign(offset)
    magnitude = np.where((offset < middle) & (offset > -middle), middle - 1, np.abs(offset))
    log_place = (
        np.ceil(np.log(magnitude / middle) / np.log((distance_cap - 1) / middle) * (middle - 1))
        + middle
    )
    return np.where(np.abs(offset) <= middle, offset, log_place * sign_of).astype(np.int32)


def offset_tables():
    place = np.arange(2 * HALF)

    def hot(distance, sign):
        clipped = np.clip(distance, 1 - HALF, HALF - 1)
        bucket = np.clip(BUCK + sign * bucket_of(clipped, BUCK, SPAN), 0, 2 * BUCK - 1)
        return np.eye(2 * BUCK, dtype=np.float32)[bucket]

    return hot(HALF - place, 1), hot(place - HALF, -1), hot(HALF - 1 - place, -1)


def segment_ids(lengths, positions):
    bounds = jnp.cumsum(lengths, axis=-1, dtype=jnp.int32)
    return jnp.sum(
        (bounds[..., None, :] <= positions[:, None]).astype(jnp.int32), axis=-1, dtype=jnp.int32
    )


def product(pattern, left_side, right_side):
    return jnp.einsum(pattern, left_side, right_side, preferred_element_type=F32)


def norm_stats(values):
    centered = values - jnp.mean(values, axis=-1, keepdims=True)
    inverse = lax.rsqrt(jnp.mean(centered * centered, axis=-1, keepdims=True) + EPSILON)
    return (centered * inverse, inverse)


def norm_back(normed, inverse, scale_gain, upstream):
    scaled = upstream * scale_gain
    return inverse * (
        scaled
        - jnp.mean(scaled, axis=-1, keepdims=True)
        - normed * jnp.mean(scaled * normed, axis=-1, keepdims=True)
    )


def adapter_forward(rows_in, weight, down, up):
    inner = product("sti,sir->str", rows_in, down).astype(BF)
    mapped = product("sti,io->sto", rows_in, weight) + ADAPTER_SCALING * product(
        "str,sro->sto", inner, up
    )
    return (mapped, inner)


def adapter_back(rows_in, inner, weight, down, up, gradient):
    grad_up = ADAPTER_SCALING * product("str,sto->sro", inner, gradient)
    grad_inner = (ADAPTER_SCALING * product("sto,sro->str", gradient, up)).astype(BF)
    grad_down = product("sti,str->sir", rows_in, grad_inner)
    grad_in = product("sto,io->sti", gradient, weight) + product("str,sir->sti", grad_inner, down)
    return (grad_in, grad_down, grad_up)


def body(
    tokens,
    cotangent,
    doc_lengths,
    adapter_ids,
    query_weight,
    key_weight,
    value_weight,
    output_weight,
    up_weight,
    down_weight,
    attention_gain,
    feedforward_gain,
    position_gain,
    position_table,
    attention_down,
    attention_up,
    expand_down,
    expand_up,
    reduce_down,
    reduce_up,
):
    seqs, row_count, width = tokens.shape
    head_groups = lax.axis_size("head")
    head_index = lax.axis_index("head")
    seq_index = lax.axis_index("seq")
    by_rows = seqs == 1 and row_count >= HALF and row_count % (2 * TILE) == 0

    def chosen(stack, axis):
        return jnp.take(stack, adapter_ids, axis=axis).astype(BF)

    att_down = [chosen(attention_down[member], 0) for member in range(4)]
    att_up = [chosen(attention_up[member], 0) for member in range(4)]
    exp_down = chosen(expand_down, 0)
    exp_up = chosen(expand_up, 0)
    red_down = chosen(reduce_down, 0)
    red_up = chosen(reduce_up, 0)

    def turned(array):
        return jnp.swapaxes(array, -1, -2)

    token_low = tokens.astype(BF)
    frozen = (query_weight, key_weight, value_weight)

    def columns(matrix):
        if by_rows:
            return matrix
        local = width // head_groups
        return lax.dynamic_slice_in_dim(matrix, head_index * local, local, matrix.ndim - 1)

    if by_rows:
        block_axes = ("seq", "head")
        block_index = seq_index * head_groups + head_index
        query_count = row_count
    else:
        block_axes = ("seq",)
        block_index = seq_index
        query_count = row_count * head_groups
    blocks = math.prod(lax.axis_size(axis) for axis in block_axes)

    def halo(array):
        before = shifted(array[:, query_count - HALF :], block_axes, 1)
        after = shifted(array[:, :HALF], block_axes, -1)
        return jnp.concatenate([before, after], axis=1)

    downs = [turned(factor) for factor in att_down]
    hots = [jnp.asarray(hot, BF) for hot in offset_tables()]
    if by_rows:
        rows_halo = halo(token_low)
        (query, key, value), inners = maps(
            token_low[0], frozen, [down[0] for down in downs[:3]], [up[0] for up in att_up[:3]]
        )
        key_rel, query_rel, query_back, table_low, table_normed, table_inverse, *position_inners = positions(
            position_table,
            position_gain,
            frozen[:2],
            [down[0] for down in downs[:2]],
            [up[0] for up in att_up[:2]],
            hots,
        )
        (key_halo, value_halo), inners_halo = maps(
            rows_halo[0], frozen[1:], [down[0] for down in downs[1:3]], [up[0] for up in att_up[1:3]]
        )
        queries, keys, keys_halo, values, values_halo, key_rel, query_rel, query_back = (
            array[None]
            for array in (query, key, key_halo, value, value_halo, key_rel, query_rel, query_back)
        )
    else:
        projected = []
        inners = []
        for member in range(3):
            mapped, inner = adapter_forward(
                token_low, frozen[member], att_down[member], att_up[member]
            )
            projected.append(mapped.astype(BF))
            inners.append(inner)
        queries, keys, values = lax.all_to_all(
            jnp.stack(projected), "head", split_axis=3, concat_axis=2, tiled=True
        )
        keys_halo, values_halo = halo(keys), halo(values)
        table_normed, table_inverse = norm_stats(position_table)
        table_low = (table_normed * position_gain).astype(BF)
        position_inners = []
        tables = []
        for member in range(2):
            inner = product("pi,sir->spr", table_low, att_down[member]).astype(BF)
            mapped = product("pi,io->po", table_low, columns(frozen[member]))[
                None
            ] + ADAPTER_SCALING * product("spr,sro->spo", inner, columns(att_up[member]))
            position_inners.append(inner)
            tables.append(mapped.astype(BF))
        key_rel = product("cp,spo->sco", hots[0], tables[1]).astype(BF)
        query_rel = product("cp,spo->sco", hots[1], tables[0]).astype(BF)
        query_back = product("cp,spo->sco", hots[2], tables[0]).astype(BF)

    key_places = block_index * query_count - HALF + jnp.arange(query_count + 2 * HALF, dtype=jnp.int32)
    key_segments = segment_ids(doc_lengths, key_places)
    inside = (key_places >= 0) & (key_places < query_count * blocks)
    key_segments = jnp.where(inside[None, :], key_segments, DOCS)
    query_segments = key_segments[:, HALF : HALF + query_count]
    slot = jnp.arange(TILE, dtype=jnp.int32) % HEAD_DIM
    query_seg = (slot == query_segments[..., None]).astype(BF)
    open_slot = (slot == key_segments[..., None]) & (key_segments[..., None] < DOCS)
    key_bias = jnp.where(open_slot | (slot > DOCS), 0.0, NEGATIVE).astype(BF)

    context, probs, context_wide, inverse_total = attention_forward(
        queries, keys, keys_halo, values, values_halo, key_rel, query_rel, query_seg, key_bias
    )
    if by_rows:
        context_rows = context
    else:
        context_rows = lax.all_to_all(context, "head", split_axis=1, concat_axis=2, tiled=True)

    layer_output, grad_one, grad_context, grad_out_down, grad_out_up, grad_ff = middle(
        context_rows,
        tokens,
        cotangent,
        output_weight,
        up_weight,
        down_weight,
        (downs[3], att_up[3], turned(exp_down), exp_up, turned(red_down), red_up),
        attention_gain,
        feedforward_gain,
    )
    if not by_rows:
        grad_context = lax.all_to_all(grad_context, "head", split_axis=2, concat_axis=1, tiled=True)

    group = ADAPTERS // head_groups
    ids = lax.all_gather(adapter_ids, "batch", axis=0, tiled=True)
    slots = head_index * group + jnp.arange(group, dtype=jnp.int32)
    select = (ids[:, None] == slots[None, :]).astype(F32)

    def spread(array):
        chosen_by = select.reshape(select.shape + (1,) * (array.ndim - 1))
        return jnp.sum(chosen_by * array[:, None], axis=0)

    def unflat(array, widths):
        return jnp.split(array, np.cumsum(widths)[:-1].tolist(), axis=-1)

    ff_width = up_weight.shape[1]
    rank = exp_up.shape[1]
    peers = lax.axis_size("seq") * head_groups
    cores = lax.axis_size("batch")
    table_rows = position_table.shape[0]
    direct = by_rows and cores == 2 and table_rows == peers * cores * rank
    grad_q, grad_k, grad_k_halo, grad_v, grad_v_halo, grad_key_rel, grad_query_rel = attention_backward(
        queries,
        keys,
        keys_halo,
        values,
        values_halo,
        key_rel,
        query_back,
        probs,
        grad_context,
        context_wide,
        inverse_total,
    )

    def joined(total, from_above, from_below):
        if query_count == HALF:
            return total + from_above + from_below
        total = total.at[:, query_count - HALF :].add(from_above)
        return total.at[:, :HALF].add(from_below)

    def fold(total, halo_part):
        from_above = shifted(halo_part[:, :HALF], block_axes, -1).astype(F32)
        from_below = shifted(halo_part[:, HALF:], block_axes, 1).astype(F32)
        return joined(total.astype(F32), from_above, from_below)

    if direct:
        grad_halo, key_hu, value_hu = halo_gradients(
            grad_k_halo[0],
            grad_v_halo[0],
            frozen[1:],
            [down[0] for down in downs[1:3]],
            [up[0] for up in att_up[1:3]],
        )
        grad_tokens, table_parts, late_parts = tail_gradients(
            (head_groups, peers // head_groups, cores, rank),
            (
                grad_q[0], grad_k[0], grad_v[0], grad_k_halo[0], grad_v_halo[0], key_hu, value_hu,
                token_low[0], rows_halo[0], inners[0], inners[1], inners[2], inners_halo[0], inners_halo[1],
                grad_key_rel[0], grad_query_rel[0], hots[0].T, hots[2].T, table_low, *position_inners,
                downs[0][0], downs[1][0], downs[2][0], att_up[0][0], att_up[1][0], att_up[2][0],
                grad_out_down[0], grad_out_up[0], grad_ff[0], grad_one[0],
            ),
            frozen,
        )
        from_sides, table_total, late = reduce_late(
            grad_halo.reshape(2, HALF, width), table_parts, late_parts
        )
        input_grad = joined(
            grad_tokens[None],
            jnp.where(block_index < blocks - 1, from_sides[1].astype(F32), 0.0),
            jnp.where(block_index > 0, from_sides[0].astype(F32), 0.0),
        )
        table_total = table_total.reshape(table_rows // head_groups, width).astype(F32)
        late = jnp.transpose(late, (0, 2, 1, 3)).astype(F32)
        share = 8 * width // peers
        early = late[..., share:].reshape(cores, rank, -1)
        late = late[..., :share].reshape(cores, rank, -1)
    else:
        down_grads = []
        up_grads = []
        if by_rows:
            input_grad = grad_one
            grad_halo = 0.0
            for member, pieces in enumerate(
                (
                    ((token_low, inners[0][None], grad_q),),
                    ((token_low, inners[1][None], grad_k), (rows_halo, inners_halo[0][None], grad_k_halo)),
                    ((token_low, inners[2][None], grad_v), (rows_halo, inners_halo[1][None], grad_v_halo)),
                )
            ):
                found = [
                    adapter_back(rows, inner, frozen[member], att_down[member], att_up[member], gradient)
                    for rows, inner, gradient in pieces
                ]
                input_grad = input_grad + found[0][0]
                if member > 0:
                    grad_halo = grad_halo + found[1][0]
                down_grads.append(sum(turned(one[1]) for one in found))
                up_grads.append(sum(one[2] for one in found))
            input_grad = fold(input_grad, grad_halo.astype(BF))
            position_inners = [inner[None] for inner in position_inners]
        else:
            grad_qkv = jnp.stack(
                [grad_q, fold(grad_k, grad_k_halo).astype(BF), fold(grad_v, grad_v_halo).astype(BF)]
            )
            grad_qkv = lax.all_to_all(grad_qkv, "head", split_axis=2, concat_axis=3, tiled=True)
            input_grad = grad_one
            for member in range(3):
                grad_in, grad_dn, grad_upper = adapter_back(
                    token_low,
                    inners[member],
                    frozen[member],
                    att_down[member],
                    att_up[member],
                    grad_qkv[member],
                )
                input_grad = input_grad + grad_in
                down_grads.append(turned(grad_dn))
                up_grads.append(grad_upper)
        down_grads.append(grad_out_down)
        up_grads.append(grad_out_up)
        position_grads = (
            product("cb,soc->sbo", hots[2], grad_query_rel),
            product("cb,soc->sbo", hots[0], grad_key_rel),
        )
        grad_table_low = jnp.zeros(position_table.shape, F32)
        for member in range(2):
            gradient = position_grads[member].astype(BF)
            up = columns(att_up[member])
            grad_columns = ADAPTER_SCALING * product(
                "spr,spo->sro", position_inners[member], gradient
            )
            grad_inner = (ADAPTER_SCALING * product("spo,sro->spr", gradient, up)).astype(BF)
            grad_table_low = (
                grad_table_low
                + product("spo,io->pi", gradient, columns(frozen[member]))
                + product("spr,sir->pi", grad_inner, att_down[member])
            )
            down_grads[member] = down_grads[member] + product("spr,pi->sri", grad_inner, table_low)
            if not by_rows:
                grad_columns = lax.dynamic_update_slice_in_dim(
                    jnp.zeros_like(up_grads[member]),
                    grad_columns,
                    head_index * (width // head_groups),
                    2,
                )
            up_grads[member] = up_grads[member] + grad_columns
        late = jnp.concatenate(down_grads + up_grads, axis=-1)
        late = lax.all_gather(lax.psum(late, ("seq", "head")), "batch", axis=0, tiled=True)
        early = lax.all_gather(lax.psum(grad_ff, ("seq", "head")), "batch", axis=0, tiled=True)
        table_total = lax.psum(grad_table_low, ("seq", "batch"))
        table_total = lax.psum_scatter(table_total, "head", scatter_dimension=0, tiled=True)
    own_rows = table_rows // head_groups

    def head_rows(array):
        return lax.dynamic_slice_in_dim(array, head_index * own_rows, own_rows, 0)

    table_grad = norm_back(
        head_rows(table_normed), head_rows(table_inverse), position_gain, table_total
    )
    early = [spread(part) for part in unflat(early, [width, ff_width, ff_width, width])]
    late = [spread(part) for part in unflat(late, [width] * 8)]
    return (
        layer_output,
        input_grad,
        table_grad,
        jnp.stack([turned(part) for part in late[:4]]),
        jnp.stack(late[4:]),
        turned(early[0]),
        early[1],
        turned(early[2]),
        early[3],
    )


def solution(mesh):
    rows = P("batch", ("seq", "head"), None)
    return jax.shard_map(
        body,
        mesh=mesh,
        in_specs=(rows, rows, P("batch", None), P("batch")) + (P(),) * 16,
        out_specs=(
            rows,
            rows,
            P("head", None),
            P(None, "head", None, None),
            P(None, "head", None, None),
            P("head", None, None),
            P("head", None, None),
            P("head", None, None),
            P("head", None, None),
        ),
        check_vma=False,
    )
```

```python
from functools import partial
import math
from types import SimpleNamespace

import jax
import jax.numpy as jnp
import numpy as np
from jax import lax
from jax.experimental import pallas as pl
from jax.experimental.pallas import tpu as pltpu
from jax.sharding import PartitionSpec as P

HEADS = 16
HEAD_DIM = 64
BUCK = 256
SPAN = 512
ADAPTERS = 8
HALF = 512
DOCS = 8

EPSILON = 1e-07
ADAPTER_SCALING = 2.0
NEGATIVE = -1e30
PRECISE = lax.Precision.HIGHEST
TILE = 128
BF = jnp.bfloat16
F32 = jnp.float32
MESH = pl.DeviceIdType.MESH
VMEM = 63 * 2**20
NN = (((1,), (0,)), ((), ()))
NT = (((1,), (1,)), ((), ()))


def mm(a, b, dims=NN):
    return lax.dot_general(a, b, dims, preferred_element_type=F32)

def lanes(shape=(TILE, TILE)):
    return lax.broadcasted_iota(jnp.int32, shape, 1)

def rows(shape=(TILE, TILE)):
    return lax.broadcasted_iota(jnp.int32, shape, 0)

def skew(tile):
    return pltpu.roll(tile, 0, 1, stride=1, stride_axis=0)

def flip_matrix():
    return jnp.where(lanes() + rows() == TILE - 1, 1.0, 0.0).astype(BF)


class Loaded:
    def __init__(self, source, target, sem):
        self.target = target
        self.copy = pltpu.make_async_copy(source, target, sem)
        self.copy.start()

    def __call__(self):
        if self.copy is not None:
            self.copy.wait()
            self.copy = None
        return self.target[...]


def with_halo(own_ref, halo_ref):
    return jnp.concatenate([halo_ref[0, :HALF], own_ref[0], halo_ref[0, HALF:]], axis=0)


class Stored:
    def __init__(self, target, buffer, sem):
        self.buffer = buffer
        self.copy = pltpu.make_async_copy(buffer, target, sem)

    def put(self, value):
        self.buffer[...] = value
        self.copy.start()

    def wait(self):
        self.copy.wait()


def prepare_kernel(seqs, ids_ref, lengths_ref, base_ref, *refs):
    stacks = [stack.at[member] for stack in refs[:2] for member in range(4)] + list(refs[2:6])
    count = len(stacks)
    refs = refs[6:]
    outs = refs[: count + 2]
    buffers = refs[count + 2 : 2 * count + 2]
    made = refs[2 * count + 2 : 3 * count + 4]
    sems, out_sems = refs[3 * count + 4 :]
    outs = [Stored(target, buffer, out_sems.at[i]) for i, (target, buffer) in enumerate(zip(outs, made))]
    query_seg_ref, key_bias_ref = made[count:]
    copies = []
    for s in range(seqs):
        for index, (stack, buffer) in enumerate(zip(stacks, buffers)):
            copy = pltpu.make_async_copy(stack.at[ids_ref[s]], buffer.at[s], sems.at[s, index])
            copy.start()
            copies.append(copy)
    rows_k = key_bias_ref.shape[1]
    rows_q = query_seg_ref.shape[1]
    place = base_ref[0] + rows((rows_k, TILE))
    slot = lanes((rows_k, TILE)) % HEAD_DIM
    inside = (place >= 0) & (place < base_ref[1])
    for s in range(seqs):
        segment = jnp.zeros((rows_k, TILE), jnp.int32)
        bound = jnp.int32(0)
        for document in range(DOCS):
            bound = bound + lengths_ref[s, document]
            segment += jnp.where(place >= bound, 1, 0)
        segment = jnp.where(inside, segment, DOCS)
        same = slot == segment
        query_seg_ref[s] = jnp.where(same, 1.0, 0.0)[HALF : HALF + rows_q].astype(BF)
        open_slot = (same & (segment < DOCS)) | (slot > DOCS)
        key_bias_ref[s] = jnp.where(open_slot, 0.0, NEGATIVE).astype(BF)
    for out in outs[count:]:
        out.copy.start()
    for copy in copies:
        copy.wait()
    for buffer, out in zip(buffers, outs):
        out.put(buffer[...].astype(BF))
    for out in outs:
        out.wait()


def prepare(adapter_ids, lengths, base, stacks, query_count):
    seqs = adapter_ids.shape[0]
    hbm = pl.BlockSpec(memory_space=pltpu.HBM)
    sm = pl.BlockSpec(memory_space=pltpu.SMEM)
    shapes = [(seqs,) + stack.shape[2:] for stack in stacks[:2] for _ in range(4)]
    shapes += [(seqs,) + stack.shape[1:] for stack in stacks[2:]]
    count = len(shapes)
    columns = [(seqs, query_count, TILE), (seqs, query_count + 2 * HALF, TILE)]
    found = pl.pallas_call(
        partial(prepare_kernel, seqs),
        in_specs=[sm] * 3 + [hbm] * len(stacks),
        out_specs=[hbm] * (count + 2),
        out_shape=[jax.ShapeDtypeStruct(shape, BF) for shape in shapes + columns],
        scratch_shapes=[pltpu.VMEM(shape, F32) for shape in shapes]
        + [pltpu.VMEM(shape, BF) for shape in shapes + columns]
        + [pltpu.SemaphoreType.DMA((seqs, count)), pltpu.SemaphoreType.DMA((count + 2,))],
        compiler_params=pltpu.CompilerParams(vmem_limit_bytes=VMEM),
        cost_estimate=pl.CostEstimate(flops=10**6, bytes_accessed=6 * 10**6, transcendentals=0),
        name="prepare",
    )(adapter_ids, lengths, base, *stacks)
    return found[:count], found[count], found[count + 1]


def adapted(x, weight, inner, up):
    return (mm(x, weight) + ADAPTER_SCALING * mm(inner, up)).astype(BF)


def begin_kernel(x_ref, table_ref, gain_ref, query_a, key_a, value_a, query_b, key_b, value_b,
                 query_w, key_w, value_w, query_hot, back_hot, key_hot,
                 query_out, key_out, value_out, query_rel_out, back_rel_out, key_rel_out, low_out,
                 query_u, key_u, value_u, query_pu, key_pu, *scratch):
    loaded = scratch[:6]
    stored = scratch[6:13]
    load_sems, store_sems = scratch[13:]
    query_w, key_w, value_w, query_hot, back_hot, key_hot = (
        Loaded(source, target, load_sems.at[index])
        for index, (source, target) in enumerate(zip((query_w, key_w, value_w, query_hot, back_hot, key_hot), loaded))
    )
    outs = [
        Stored(target, buffer, store_sems.at[index])
        for index, (target, buffer) in enumerate(
            zip((query_out, key_out, value_out, query_rel_out, back_rel_out, key_rel_out, low_out), stored)
        )
    ]
    x = x_ref[...]
    query_u[...] = mm(x, query_a[...], NT).astype(BF)
    key_u[...] = mm(x, key_a[...], NT).astype(BF)
    value_u[...] = mm(x, value_a[...], NT).astype(BF)
    values = table_ref[...]
    centered = values - jnp.mean(values, axis=1, keepdims=True)
    inverse = lax.rsqrt(jnp.mean(centered * centered, axis=1, keepdims=True) + EPSILON)
    low = (centered * inverse * gain_ref[...]).astype(BF)
    outs[6].put(low)
    query_pu[...] = mm(low, query_a[...], NT).astype(BF)
    key_pu[...] = mm(low, key_a[...], NT).astype(BF)
    outs[0].put(adapted(x, query_w(), query_u[...], query_b[...]))
    position_q = adapted(low, query_w(), query_pu[...], query_b[...])
    outs[1].put(adapted(x, key_w(), key_u[...], key_b[...]))
    position_k = adapted(low, key_w(), key_pu[...], key_b[...])
    outs[2].put(adapted(x, value_w(), value_u[...], value_b[...]))
    outs[3].put(mm(query_hot(), position_q).astype(BF))
    outs[4].put(mm(back_hot(), position_q).astype(BF))
    outs[5].put(mm(key_hot(), position_k).astype(BF))
    for out in outs:
        out.wait()


def begin(x, table, gain, weights, downs, ups, hots):
    rows_x, width = x.shape
    rank = ups[0].shape[0]
    places = table.shape[0]
    spans = hots[0].shape[0]
    vm = pl.BlockSpec(memory_space=pltpu.VMEM)
    hbm = pl.BlockSpec(memory_space=pltpu.HBM)
    large = [(rows_x, width)] * 3 + [(spans, width)] * 3 + [(places, width)]
    inner = jax.ShapeDtypeStruct((rows_x, rank), BF)
    position_inner = jax.ShapeDtypeStruct((places, rank), BF)
    sources = (*weights, hots[1], hots[2], hots[0])
    found = pl.pallas_call(
        begin_kernel,
        in_specs=[vm] * 9 + [hbm] * 6,
        out_specs=[hbm] * 7 + [vm] * 5,
        out_shape=[jax.ShapeDtypeStruct(shape, BF) for shape in large] + [inner] * 3 + [position_inner] * 2,
        scratch_shapes=[pltpu.VMEM(source.shape, BF) for source in sources]
        + [pltpu.VMEM(shape, BF) for shape in large]
        + [pltpu.SemaphoreType.DMA((6,)), pltpu.SemaphoreType.DMA((7,))],
        compiler_params=pltpu.CompilerParams(vmem_limit_bytes=VMEM),
        cost_estimate=pl.CostEstimate(
            flops=6 * rows_x * width * width + 10 * places * width * width,
            bytes_accessed=24 * places * width + 6 * width * width,
            transcendentals=0,
        ),
        name="begin",
    )(x, table, gain.reshape(1, width), *downs, *ups, *sources)
    return found[:3], found[3:6], found[6], found[7:10], found[10:]


def halo_kernel(before_hbm, after_hbm, key_w, value_w, key_a, value_a, key_b, value_b, key_out, value_out,
                key_u, value_u, before_x, after_x, held_k, held_v, made, load_sems, store_sems):
    before, after, key_w, value_w = (
        Loaded(source, target, load_sems.at[index])
        for index, (source, target) in enumerate(
            ((before_hbm, before_x), (after_hbm, after_x), (key_w, held_k), (value_w, held_v))
        )
    )
    outs = []
    for side, x in ((0, before), (1, after)):
        at = slice(side * HALF, (side + 1) * HALF)
        key_u[at] = mm(x(), key_a[...], NT).astype(BF)
        value_u[at] = mm(x(), value_a[...], NT).astype(BF)
    for member, (weight, inner, up, target) in enumerate(
        ((key_w, key_u, key_b, key_out), (value_w, value_u, value_b, value_out))
    ):
        for side, x in ((0, before), (1, after)):
            at = slice(side * HALF, (side + 1) * HALF)
            out = Stored(target.at[pl.ds(side * HALF, HALF)], made.at[member, side], store_sems.at[member, side])
            out.put(adapted(x(), weight(), inner[at], up[...]))
            outs.append(out)
    for out in outs:
        out.wait()


def halo_maps(before, after, weights, downs, ups):
    half, width = before.shape
    rank = ups[0].shape[0]
    vm = pl.BlockSpec(memory_space=pltpu.VMEM)
    hbm = pl.BlockSpec(memory_space=pltpu.HBM)
    both = jax.ShapeDtypeStruct((2 * half, width), BF)
    inner = jax.ShapeDtypeStruct((2 * half, rank), BF)
    found = pl.pallas_call(
        halo_kernel,
        in_specs=[hbm] * 4 + [vm] * 4,
        out_specs=[hbm] * 2 + [vm] * 2,
        out_shape=[both, both, inner, inner],
        scratch_shapes=[pltpu.VMEM((half, width), BF)] * 2
        + [pltpu.VMEM((width, width), BF)] * 2
        + [pltpu.VMEM((2, 2, half, width), BF), pltpu.SemaphoreType.DMA((4,)), pltpu.SemaphoreType.DMA((2, 2))],
        compiler_params=pltpu.CompilerParams(vmem_limit_bytes=VMEM),
        cost_estimate=pl.CostEstimate(
            flops=8 * half * width * width, bytes_accessed=12 * half * width + 4 * width * width, transcendentals=0
        ),
        name="halo_maps",
    )(before, after, *weights, *downs, *ups)
    return found[:2], found[2:]


def relative_kernel(q_ref, k_ref, pk_ref, pq_ref, qs_ref, ks_ref):
    tiles = HALF // TILE
    span = 2 * tiles
    below = lanes() + rows() < TILE
    column = lanes((HALF, TILE)) < HEAD_DIM
    for h in range(2):
        own = column if h == 0 else ~column
        km = jnp.where(own, k_ref[0], jnp.zeros_like(k_ref[0]))
        qm = jnp.where(own, q_ref[0], jnp.zeros_like(q_ref[0]))
        for d in range(1, span):
            pairs = [(t, d + t - tiles) for t in range(tiles) if 0 <= d + t - tiles < tiles]
            first, last = pairs[0][1], pairs[-1][1]
            key_rel = mm(
                km[first * TILE : (last + 1) * TILE], pq_ref[0, (span - 1 - d) * TILE : (span + 1 - d) * TILE, :], NT
            ).astype(BF)
            for t, j in pairs:
                part = key_rel[(j - first) * TILE : (j - first + 1) * TILE]
                ks_ref[0, h, t, j * TILE : (j + 1) * TILE, :] = skew(
                    jnp.where(below, part[:, TILE:], part[:, :TILE])
                )
        query_rel = mm(qm, pk_ref[0], NT).astype(BF)
        for t in range(tiles):
            part = query_rel[t * TILE : (t + 1) * TILE]
            for d in range(span + 1):
                here = part[:, min(d, span - 1) * TILE : (min(d, span - 1) + 1) * TILE]
                if 0 < d < span:
                    here = jnp.where(below, here, part[:, (d - 1) * TILE : d * TILE])
                qs_ref[0, h, t, :, d * TILE : (d + 1) * TILE] = skew(here)


def relative_scores(q, k, pk, pq):
    n, rq, width = q.shape
    pairs = width // TILE
    off = 2 * HALF
    tiles = rq // TILE
    return pl.pallas_call(
        relative_kernel,
        grid=(n, pairs),
        in_specs=[column_spec(rq), column_spec(rq), column_spec(off), column_spec(off)],
        out_specs=[head_spec(tiles, TILE, off + TILE), head_spec(tiles, HALF, TILE)],
        out_shape=[jax.ShapeDtypeStruct((n, 2 * pairs, tiles, TILE, off + TILE), BF),
                   jax.ShapeDtypeStruct((n, 2 * pairs, tiles, HALF, TILE), BF)],
        compiler_params=pltpu.CompilerParams(dimension_semantics=("arbitrary", "arbitrary"), vmem_limit_bytes=VMEM),
        cost_estimate=pl.CostEstimate(
            flops=16 * n * rq * off * width, bytes_accessed=60 * 10**6, transcendentals=0
        ),
        name="relative_scores",
    )(q, k, pk, pq)


def column_spec(r):
    return pl.BlockSpec((1, r, TILE), lambda s, p: (s, 0, p))


def head_spec(*shape):
    return pl.BlockSpec((1, 2) + shape, lambda s, p: (s, p) + (0,) * len(shape))


def forward_kernel(q_ref, k_ref, kh_ref, v_ref, vh_ref, pq_ref, qhot_ref, kbias_ref, qs_ref, ko_ref,
                   ctx_ref, p_ref, ctxf_ref, inv_ref, kz_ref, vz_ref, ks_ref, s_ref):
    tiles = HALF // TILE
    span = 2 * tiles
    width = (span + 1) * TILE
    flip = flip_matrix()
    factor = math.log2(math.e) / math.sqrt(3 * HEAD_DIM)
    k = with_halo(k_ref, kh_ref)
    v = with_halo(v_ref, vh_ref)
    kb = kbias_ref[0]
    kcol = lanes(k.shape) < HEAD_DIM
    hcol = lanes(kh_ref.shape[1:]) < HEAD_DIM
    below = lanes() + rows() < TILE
    place = lanes() + rows()
    tcol = lanes() < HEAD_DIM
    for h in range(2):
        own = kcol if h == 0 else ~kcol
        kz_ref[h] = jnp.where(own, k, kb)
        vz_ref[h] = jnp.where(own, v, jnp.ones_like(v))
        km = jnp.where(hcol if h == 0 else ~hcol, kh_ref[0], jnp.zeros_like(kh_ref[0]))
        for t in range(tiles):
            ks_ref[h, t, (tiles - t) * TILE : (2 * tiles - t) * TILE, :] = ko_ref[0, h, t]
        for d in range(span + 1):
            pairs = [(t, d + t if d + t < tiles else d + t - tiles) for t in range(tiles) if not tiles <= d + t < 2 * tiles]
            if not pairs:
                continue
            low = max(span - 1 - d, 0) * TILE
            high = min(span + 1 - d, span) * TILE
            first, last = pairs[0][1], pairs[-1][1]
            key_rel = mm(km[first * TILE : (last + 1) * TILE], pq_ref[0, low:high, :], NT).astype(BF)
            for t, j in pairs:
                part = key_rel[(j - first) * TILE : (j - first + 1) * TILE]
                if 0 < d < span:
                    part = jnp.where(below, part[:, TILE:], part[:, :TILE])
                ks_ref[h, t, d * TILE : (d + 1) * TILE, :] = skew(part)

    for t in range(tiles):
        at = slice(t * TILE, (t + 1) * TILE)
        window = slice(t * TILE, t * TILE + width)
        q = q_ref[0, at, :]
        hot = qhot_ref[0, at, :]
        outs = []
        for h in range(2):
            own = tcol if h == 0 else ~tcol
            q_side = mm(flip, jnp.where(own, q, hot)).astype(BF)
            left = jnp.concatenate([q_side, flip], axis=1)
            right = jnp.concatenate([kz_ref[h, window, :], ks_ref[h, t]], axis=1)
            s_ref[h] = mm(left, right, NT) + mm(flip, qs_ref[0, h, t])
        for h in range(2):
            own = tcol if h == 0 else ~tcol
            first = s_ref[h, :, :TILE]
            s_ref[h, :, :TILE] = jnp.where(place > TILE - 1, first, NEGATIVE)
            last = s_ref[h, :, span * TILE :]
            s_ref[h, :, span * TILE :] = jnp.where(place < TILE - 1, last, NEGATIVE)
            middle = s_ref[h, :, tiles * TILE : (tiles + 1) * TILE]
            s_ref[h, :, tiles * TILE : (tiles + 1) * TILE] = jnp.where(
                (place == TILE - 1) & (middle < 0.1 * NEGATIVE), 0.0, middle
            )
            top = s_ref[h, :, :TILE]
            for d in range(1, span + 1):
                top = jnp.maximum(top, s_ref[h, :, d * TILE : (d + 1) * TILE])
            peak = jnp.max(top, axis=1, keepdims=True)
            prob = jnp.exp2((s_ref[h] - peak) * factor).astype(BF)
            a = t % 2
            row_at = slice(a * TILE, (a + 1) * TILE)
            p_ref[0, h, t // 2, row_at, a * TILE : a * TILE + width] = prob
            p_ref[0, h, t // 2, row_at, (1 - a) * width : (1 - a) * width + TILE] = jnp.zeros((TILE, TILE), BF)
            total = mm(prob, vz_ref[h, window, :])
            inv = 1.0 / jnp.where(own, pltpu.roll(total, HEAD_DIM, 1), total)
            inv_ref[0, h, at, :] = inv
            outs.append(total * inv)
        ctx = jnp.where(tcol, outs[0], outs[1])
        ctxf_ref[0, at, :] = ctx
        ctx_ref[0, at, :] = mm(flip, ctx.astype(BF)).astype(BF)


def attention_forward(q, k, k_halo, v, v_halo, pq, qhot, kbias, query_scores, key_scores):
    n, rq, width = q.shape
    off = 2 * HALF
    rk = rq + off
    pairs = width // TILE
    tiles = rq // TILE

    def whole(r):
        return pl.BlockSpec((1, r, TILE), lambda s, p: (s, 0, 0))

    return pl.pallas_call(
        forward_kernel,
        grid=(n, pairs),
        in_specs=[column_spec(rq), column_spec(rq), column_spec(off), column_spec(rq), column_spec(off),
                  column_spec(off), whole(rq), whole(rk), head_spec(tiles, TILE, off + TILE), head_spec(tiles, HALF, TILE)],
        out_specs=[column_spec(rq), head_spec(tiles // 2, 2 * TILE, off + 2 * TILE), column_spec(rq), head_spec(rq, TILE)],
        out_shape=[jax.ShapeDtypeStruct((n, rq, width), BF),
                   jax.ShapeDtypeStruct((n, 2 * pairs, tiles // 2, 2 * TILE, off + 2 * TILE), BF),
                   jax.ShapeDtypeStruct((n, rq, width), F32),
                   jax.ShapeDtypeStruct((n, 2 * pairs, rq, TILE), F32)],
        scratch_shapes=[pltpu.VMEM((2, rk, TILE), BF), pltpu.VMEM((2, rk, TILE), BF),
                        pltpu.VMEM((2, tiles, off + TILE, TILE), BF),
                        pltpu.VMEM((2, TILE, off + TILE), F32)],
        compiler_params=pltpu.CompilerParams(dimension_semantics=("arbitrary", "arbitrary"), vmem_limit_bytes=VMEM),
        cost_estimate=pl.CostEstimate(
            flops=32 * n * rq * off * width, bytes_accessed=60 * 10**6, transcendentals=0
        ),
        name="attention_forward",
    )(q, k, k_halo, v, v_halo, pq, qhot, kbias, query_scores, key_scores)


def spread_kernel(group, ids_ref, slot_ref, late_ref, table_ref, places_ref, gain_ref,
                  table_out, down_out, up_out, expand_down, expand_up, reduce_down, reduce_up):
    cores, peers, rank, share = late_ref.shape
    width = table_ref.shape[3]
    ff = expand_up.shape[2]
    part = 8 * width // peers
    rest = share - part
    weights = [
        [jnp.where(ids_ref[s] == slot_ref[0] + a, 1.0, 0.0) for a in range(group)] for s in range(cores)
    ]

    def fill(out, a, pieces):
        for column, piece in pieces:
            value = sum(weights[s][a] * late_ref[s, piece[0], :, piece[1]].astype(F32) for s in range(cores))
            out[:, column] = value

    per = width // part
    starts = ((expand_down, 0, width), (expand_up, width, ff), (reduce_down, width + ff, ff), (reduce_up, width + 2 * ff, width))
    for a in range(group):
        for member in range(8):
            out = (down_out if member < 4 else up_out).at[member % 4, a]
            fill(out, a, [
                (slice(half * part, (half + 1) * part), (member * per + half, slice(0, part))) for half in range(per)
            ])
        for out, start, count in starts:
            pieces = []
            at = start
            while at < start + count:
                peer, offset = at // rest, at % rest
                length = min(rest - offset, start + count - at)
                pieces.append((slice(at - start, at - start + length), (peer, slice(part + offset, part + offset + length))))
                at += length
            fill(out.at[a], a, pieces)
    values = places_ref[...]
    centered = values - jnp.mean(values, axis=1, keepdims=True)
    inverse = lax.rsqrt(jnp.mean(centered * centered, axis=1, keepdims=True) + EPSILON)
    normed = centered * inverse
    upstream = table_ref[...].reshape(values.shape).astype(F32) * gain_ref[...]
    table_out[...] = inverse * (
        upstream
        - jnp.mean(upstream, axis=1, keepdims=True)
        - normed * jnp.mean(upstream * normed, axis=1, keepdims=True)
    )


def spread_all(ids, slot, late, table, places, gain, ff):
    rank = late.shape[2]
    width = table.shape[3]
    group = slot.shape[0]
    vm = pl.BlockSpec(memory_space=pltpu.VMEM)
    sm = pl.BlockSpec(memory_space=pltpu.SMEM)

    def out(*shape):
        return jax.ShapeDtypeStruct(shape, F32)

    return pl.pallas_call(
        partial(spread_kernel, group),
        in_specs=[sm, sm] + [vm] * 4,
        out_specs=[vm] * 7,
        out_shape=[out(*places.shape), out(4, group, rank, width), out(4, group, rank, width), out(group, rank, width),
                   out(group, rank, ff), out(group, rank, ff), out(group, rank, width)],
        compiler_params=pltpu.CompilerParams(vmem_limit_bytes=VMEM),
        name="spread_all",
    )(ids, slot, late, table, places, gain.reshape(1, width))


def backward_kernel(q_ref, k_ref, kh_ref, v_ref, vh_ref, pk_ref, pq_ref, p_ref, g_ref, ctxf_ref, inv_ref,
                    dq_ref, dk_ref, dkh_ref, dv_ref, dvh_ref, dpk_ref, dpq_ref,
                    kx_ref, vx_ref, qr_ref, gr_ref, e_ref, gc_ref, gk_ref, dvt_ref):
    rows_q = q_ref.shape[1]
    rows_k = kx_ref.shape[0]
    kx_ref[...] = with_halo(k_ref, kh_ref)
    vx_ref[...] = with_halo(v_ref, vh_ref)
    tiles = rows_q // TILE
    key_tiles = rows_k // TILE
    span = 2 * HALF // TILE
    wide = (span + 2) * TILE
    flip = flip_matrix()
    scale = 1.0 / math.sqrt(3 * HEAD_DIM)
    tcol = lanes() < HEAD_DIM
    qcol = lanes((rows_q, TILE)) < HEAD_DIM
    over = lanes() > rows()
    under = lanes() >= rows()

    @pl.when((pl.program_id(0) == 0) & (pl.program_id(1) == 0))
    def _():
        gk_ref[...] = jnp.zeros_like(gk_ref)

    for t in range(tiles):
        at = slice(t * TILE, (t + 1) * TILE)
        qr_ref[at] = mm(flip, q_ref[0, at]).astype(BF)
        gr_ref[at] = mm(flip, g_ref[0, at]).astype(BF)
    q_rev = qr_ref[...]
    g_rev = gr_ref[...]
    q_turned = q_rev.T
    k_turned = kx_ref[...].T
    product = g_rev.astype(F32) * ctxf_ref[0]
    dvt_ref[...] = jnp.zeros_like(dvt_ref)
    dq_parts = []
    dk_parts = []
    for h in range(2):
        own = qcol if h == 0 else ~qcol
        part = slice(h * HEAD_DIM, (h + 1) * HEAD_DIM)
        g_masked = jnp.where(own, g_rev, jnp.zeros_like(g_rev))
        inv = inv_ref[0, h]
        delta = jnp.sum(jnp.where(own, product, 0.0), axis=1, keepdims=True) * inv
        g_turned = (g_rev.astype(F32) * inv).astype(BF).T[part]
        dq_main = []
        for u in range(tiles // 2):
            at = slice(u * 2 * TILE, (u + 1) * 2 * TILE)
            window = slice(u * 2 * TILE, u * 2 * TILE + wide)
            prob = p_ref[0, h, u]
            g_probs = mm(g_masked[at], vx_ref[window], NT)
            inv_u = jnp.concatenate([inv[at]] * (span + 2), axis=1)
            delta_u = jnp.concatenate([delta[at]] * (span + 2), axis=1)
            e = (prob.astype(F32) * (g_probs * inv_u - delta_u)).astype(BF)
            e_ref[h, u] = e
            dvt_ref[part, window] += mm(g_turned[:, at], prob)
            dq_main.append(mm(e, kx_ref[window]))
            for a in range(2):
                for t in range(span):
                    def turned(d):
                        return pltpu.roll(e_ref[h, u, a * TILE:(a + 1) * TILE, (a + d) * TILE:(a + d + 1) * TILE], 1, 1, stride=1, stride_axis=0)
                    here = turned(t) if t == 0 else after
                    after = turned(t + 1)
                    gc_ref[h, (2 * u + a) * TILE:(2 * u + a + 1) * TILE, t * TILE:(t + 1) * TILE] = jnp.where(over, after, here)
        dq_parts.append(jnp.concatenate(dq_main, axis=0) + mm(gc_ref[h], pk_ref[0]))
        dpk_ref[0, part, :] = (mm(q_turned[part], gc_ref[h]) * scale).astype(BF)
        dk_tiles = []
        for kt in range(key_tiles):
            dlow = max(0, kt - tiles + 1)
            dhigh = min(span, kt)
            flat = []
            spun = {}
            for d in range(dlow, dhigh + 1):
                qt = kt - d
                a = qt % 2
                et = e_ref[h, qt // 2, a * TILE:(a + 1) * TILE, (a + d) * TILE:(a + d + 1) * TILE].T
                flat.append((qt, et))
                spun[d] = skew(et)
            tlow = max(dlow - 1, 0)
            thigh = min(dhigh, span - 1)
            for t in range(tlow, thigh + 1):
                zero = jnp.zeros((TILE, TILE), BF)
                gk_ref[h, kt * TILE:(kt + 1) * TILE, t * TILE:(t + 1) * TILE] = jnp.where(under, spun.get(t + 1, zero), spun.get(t, zero))
            flat = flat[::-1]
            left = jnp.concatenate([et for _, et in flat] + [gk_ref[h, kt * TILE:(kt + 1) * TILE, tlow * TILE:(thigh + 1) * TILE]], axis=1)
            right = jnp.concatenate([q_rev[flat[0][0] * TILE:(flat[-1][0] + 1) * TILE], pq_ref[0, tlow * TILE:(thigh + 1) * TILE]], axis=0)
            dk_tiles.append(mm(left, right))
        dk_parts.append(jnp.concatenate(dk_tiles, axis=0))
        dpq_ref[0, part, :] = (mm(k_turned[part], gk_ref[h]) * scale).astype(BF)
    dq = (jnp.where(qcol, dq_parts[0], dq_parts[1]) * scale).astype(BF)
    for t in range(tiles):
        at = slice(t * TILE, (t + 1) * TILE)
        dq_ref[0, at] = mm(flip, dq[at]).astype(BF)
    kcol = lanes((rows_k, TILE)) < HEAD_DIM
    dk = (jnp.where(kcol, dk_parts[0], dk_parts[1]) * scale).astype(BF)
    dv = dvt_ref[...].astype(BF).T
    for whole, own_ref, halo_ref in ((dk, dk_ref, dkh_ref), (dv, dv_ref, dvh_ref)):
        halo_ref[0, :HALF] = whole[:HALF]
        own_ref[0] = whole[HALF : HALF + rows_q]
        halo_ref[0, HALF:] = whole[HALF + rows_q :]


def attention_backward(q, k, k_halo, v, v_halo, pk, pq, probs, g, ctxf, inv):
    n, rq, width = q.shape
    off = 2 * HALF
    rk = rq + off
    pairs = width // TILE
    wide = off + 2 * TILE
    def col(r):
        return pl.BlockSpec((1, r, TILE), lambda s, p: (s, 0, p))
    def row(r):
        return pl.BlockSpec((1, TILE, r), lambda s, p: (s, p, 0))
    return pl.pallas_call(
        backward_kernel,
        grid=(n, pairs),
        in_specs=[col(rq), col(rq), col(off), col(rq), col(off), col(off), col(off),
                  pl.BlockSpec((1, 2, rq // (2 * TILE), 2 * TILE, wide), lambda s, p: (s, p, 0, 0, 0)),
                  col(rq), col(rq),
                  pl.BlockSpec((1, 2, rq, TILE), lambda s, p: (s, p, 0, 0))],
        out_specs=[col(rq), col(rq), col(off), col(rq), col(off), row(off), row(off)],
        out_shape=[jax.ShapeDtypeStruct((n, rq, width), BF),
                   jax.ShapeDtypeStruct((n, rq, width), BF),
                   jax.ShapeDtypeStruct((n, off, width), BF),
                   jax.ShapeDtypeStruct((n, rq, width), BF),
                   jax.ShapeDtypeStruct((n, off, width), BF),
                   jax.ShapeDtypeStruct((n, width, off), BF),
                   jax.ShapeDtypeStruct((n, width, off), BF)],
        scratch_shapes=[pltpu.VMEM((rk, TILE), BF), pltpu.VMEM((rk, TILE), BF), pltpu.VMEM((rq, TILE), BF), pltpu.VMEM((rq, TILE), BF),
                        pltpu.VMEM((2, rq // (2 * TILE), 2 * TILE, wide), BF),
                        pltpu.VMEM((2, rq, off), BF),
                        pltpu.VMEM((2, rk, off), BF),
                        pltpu.VMEM((TILE, rk), F32)],
        compiler_params=pltpu.CompilerParams(dimension_semantics=("arbitrary", "arbitrary"), vmem_limit_bytes=VMEM),
        name="attention_backward",
    )(q, k, k_halo, v, v_halo, pk, pq, probs, g, ctxf, inv)

def gather_rows(left, right):
    return lax.dot_general(left, right, (((0,), (0,)), ((), ())), preferred_element_type=F32)


def finish_kernel(shape, names, *refs):
    groups, blocks, cores, rank = shape
    r = SimpleNamespace(**dict(zip(names, refs)))
    seq, head, core = lax.axis_index("seq"), lax.axis_index("head"), lax.axis_index("batch")
    peers = blocks * groups
    me = seq * groups + head
    partner = (seq, head, 1 - core)
    width = r.table_out.shape[3]

    held = SimpleNamespace()
    for index, name in enumerate(names[:LOADS]):
        setattr(held, name, Loaded(refs[index], refs[len(refs) - LOADS + index], r.load_sems.at[index]))

    def place(p):
        return (p // groups, p % groups, core)

    def remote(src, dst, send, recv, device):
        return pltpu.make_async_remote_copy(
            src_ref=src, dst_ref=dst, send_sem=send, recv_sem=recv, device_id=device, device_id_type=MESH
        )

    def each(count, step):
        lax.fori_loop(1, count, lambda k, c: (step(k), c)[1], 0)

    barrier = pltpu.get_barrier_semaphore()
    pl.semaphore_signal(barrier, inc=1, device_id=partner, device_id_type=MESH)
    each(peers, lambda k: pl.semaphore_signal(barrier, inc=1, device_id=place((me + k) % peers), device_id_type=MESH))

    def inner_grad(gradient, up):
        return (ADAPTER_SCALING * mm(gradient, up[...], NT)).astype(BF)

    halo_buf, halo_recv, halo_sems = r.halo_buf, r.halo_recv, r.halo_sems
    half = HALF // 2

    def halves(array):
        return array.astype(BF).reshape(2, half, width)

    def crossing(side, piece):
        there = place(jnp.maximum(me - 1, 0) if side == 0 else jnp.minimum(me + 1, peers - 1))
        return remote(
            halo_buf.at[side, piece], halo_recv.at[1 - side, piece],
            halo_sems.at[4 * side + 2 * piece], halo_sems.at[4 * side + 2 * piece + 1], there,
        )

    def start_crossing(side, piece):
        @pl.when(me > 0 if side == 0 else me < peers - 1)
        def _():
            crossing(side, piece).start()
    key_halo, value_halo = held.key_halo(), held.value_halo()
    key_hu, value_hu = inner_grad(key_halo, r.key_b), inner_grad(value_halo, r.value_b)
    key_w, value_w = held.key_w(), held.value_w()
    for side in range(2):
        at = slice(side * HALF, (side + 1) * HALF)
        halo_buf[side] = halves(
            mm(key_halo[at], key_w, NT)
            + mm(value_halo[at], value_w, NT)
            + mm(key_hu[at], r.key_a[...])
            + mm(value_hu[at], r.value_a[...])
        )
        if side == 0:
            pl.semaphore_wait(barrier, peers)

        start_crossing(side, 0)

    table_ref, stage_ref, recv_ref, sum_ref = r.table, r.stage, r.recv, r.sum
    core_ref, core_sems = r.core, r.core_sems
    position_q = mm(held.back_hot(), held.query_rel_g(), NT).astype(BF)
    position_k = mm(held.key_hot(), held.key_rel_g(), NT).astype(BF)
    query_pg, key_pg = inner_grad(position_q, r.query_b), inner_grad(position_k, r.key_b)
    query_w = held.query_w()
    table = (
        mm(position_q, query_w, NT)
        + mm(position_k, key_w, NT)
        + mm(query_pg, r.query_a[...])
        + mm(key_pg, r.key_a[...])
    ).astype(BF)
    for group in range(groups):
        for block in range(blocks):
            for side in range(cores):
                start = ((group * blocks + block) * cores + side) * rank
                table_ref[side, block * groups + group] = table[start : start + rank]
    swap = remote(table_ref.at[1 - core], core_ref, core_sems.at[0], core_sems.at[1], partner)
    swap.start()

    x, x_before, x_after, low = held.x(), held.x_before(), held.x_after(), held.low()
    query_g, key_g, value_g = held.query_g(), held.key_g(), held.value_g()
    query_gu, key_gu, value_gu = inner_grad(query_g, r.query_b), inner_grad(key_g, r.key_b), inner_grad(value_g, r.value_b)
    def of_halo(inner):
        return gather_rows(inner[:HALF], x_before) + gather_rows(inner[HALF:], x_after)

    pieces = [
        gather_rows(query_gu, x) + gather_rows(query_pg, low),
        gather_rows(key_gu, x) + of_halo(key_hu) + gather_rows(key_pg, low),
        gather_rows(value_gu, x) + of_halo(value_hu),
        r.out_ga[...],
        ADAPTER_SCALING * (gather_rows(r.query_u[...], query_g) + gather_rows(r.query_pu[...], position_q)),
        ADAPTER_SCALING
        * (
            gather_rows(r.key_u[...], key_g)
            + gather_rows(r.key_uh[...], key_halo)
            + gather_rows(r.key_pu[...], position_k)
        ),
        ADAPTER_SCALING * (gather_rows(r.value_u[...], value_g) + gather_rows(r.value_uh[...], value_halo)),
        r.out_gb[...],
    ]
    part = len(pieces) * width // peers
    per = width // part
    rest = r.ff.shape[1] // peers
    for index, piece in enumerate(pieces):
        for half in range(per):
            stage_ref[index * per + half, :, width : width + part] = piece[:, half * part : (half + 1) * part].astype(BF)
    for peer in range(peers):
        stage_ref[peer, :, width + part :] = r.ff[:, peer * rest : (peer + 1) * rest].astype(BF)

    send_sems, recv_sems = r.send_sems, r.recv_sems
    swap.wait()

    def to_peer(p):
        return remote(stage_ref.at[p], recv_ref.at[me], send_sems.at[p], recv_sems.at[me], place(p))

    def send(k):
        p = (me + k) % peers
        stage_ref[p, :, :width] = (table_ref[core, p].astype(F32) + core_ref[p].astype(F32)).astype(BF)
        to_peer(p).start()

    each(peers, send)
    start_crossing(0, 1)
    start_crossing(1, 1)
    sum_ref[:, :width] = table_ref[core, me].astype(F32) + core_ref[me].astype(F32)
    sum_ref[:, width:] = stage_ref[me, :, width:].astype(F32)

    grad_ref = r.grad_out
    grad_ref[...] = (
        held.grad_one()
        + mm(query_g, query_w, NT)
        + mm(key_g, key_w, NT)
        + mm(value_g, value_w, NT)
        + mm(query_gu, r.query_a[...])
        + mm(key_gu, r.key_a[...])
        + mm(value_gu, r.value_a[...])
    )

    def take(k):
        p = (me + peers - k) % peers
        remote(stage_ref.at[p], recv_ref.at[p], send_sems.at[p], recv_sems.at[p], place(p)).wait_recv()
        sum_ref[...] += recv_ref[p].astype(F32)

    each(peers, take)
    mine_t, mine_l, table_out, late_out = r.mine_t, r.mine_l, r.table_out, r.late_out
    mine_t[...] = sum_ref[:, :width].astype(BF)
    mine_l[...] = sum_ref[:, width:].astype(BF)
    late_out[core, me] = mine_l[...]
    table_out[seq, core] = mine_t[...]

    def give_l(p):
        return remote(mine_l, late_out.at[core, me], r.spread_l.at[p], r.arrive_l.at[me], place(p))

    def give_t(s):
        return remote(mine_t, table_out.at[seq, core], r.spread_t.at[s], r.arrive_t.at[seq], (s, head, core))

    each(peers, lambda k: give_l((me + k) % peers).start())
    each(blocks, lambda k: give_t((seq + k) % blocks).start())

    def on_l(p):
        return remote(late_out.at[core, p], late_out.at[core, p], r.pass_l.at[p], r.other_l.at[p], partner)

    def on_t(s):
        return remote(table_out.at[s, core], table_out.at[s, core], r.pass_t.at[s], r.other_t.at[s], partner)

    on_l(me).start()
    on_t(seq).start()

    def got_l(k):
        p = (me + peers - k) % peers
        remote(mine_l, late_out.at[core, p], r.spread_l.at[p], r.arrive_l.at[p], place(p)).wait_recv()
        on_l(p).start()

    def got_t(k):
        s = (seq + blocks - k) % blocks
        remote(mine_t, table_out.at[s, core], r.spread_t.at[s], r.arrive_t.at[s], (s, head, core)).wait_recv()
        on_t(s).start()

    each(peers, got_l)
    each(blocks, got_t)

    @pl.when(me > 0)
    def _():
        for piece in range(2):
            crossing(0, piece).wait_send()
            crossing(1, piece).wait_recv()
        grad_ref[...] += halo_recv[0].astype(F32).reshape(HALF, width)

    @pl.when(me < peers - 1)
    def _():
        for piece in range(2):
            crossing(1, piece).wait_send()
            crossing(0, piece).wait_recv()
        grad_ref[...] += halo_recv[1].astype(F32).reshape(HALF, width)

    def end_l(k):
        p = k - 1
        remote(late_out.at[1 - core, p], late_out.at[1 - core, p], r.pass_l.at[p], r.other_l.at[p], partner).wait_recv()
        on_l(p).wait_send()

    def end_t(k):
        s = k - 1
        remote(table_out.at[s, 1 - core], table_out.at[s, 1 - core], r.pass_t.at[s], r.other_t.at[s], partner).wait_recv()
        on_t(s).wait_send()

    each(peers + 1, end_l)
    each(blocks + 1, end_t)

    def sent(k):
        p = (me + k) % peers
        to_peer(p).wait_send()
        give_l(p).wait_send()

    each(peers, sent)
    each(blocks, lambda k: give_t((seq + k) % blocks).wait_send())


LOADS = 17


def finish(shape, **arrays):
    groups, blocks, cores, rank = shape
    peers = groups * blocks
    rows, width = arrays[list(arrays)[LOADS - 1]].shape
    share = (8 * width + arrays[list(arrays)[-1]].shape[1]) // peers
    vm = pl.BlockSpec(memory_space=pltpu.VMEM)
    hbm = pl.BlockSpec(memory_space=pltpu.HBM)
    dma = pltpu.SemaphoreType.DMA
    outputs = dict(
        grad_out=jax.ShapeDtypeStruct((rows, width), F32),
        table_out=jax.ShapeDtypeStruct((blocks, cores, rank, width), BF),
        late_out=jax.ShapeDtypeStruct((cores, peers, rank, share), BF),
    )
    scratch = dict(
        load_sems=dma((LOADS,)),
        halo_buf=pltpu.VMEM((2, 2, HALF // 2, width), BF),
        halo_recv=pltpu.VMEM((2, 2, HALF // 2, width), BF),
        halo_sems=dma((8,)),
        table=pltpu.VMEM((cores, peers, rank, width), BF),
        core=pltpu.VMEM((peers, rank, width), BF),
        stage=pltpu.VMEM((peers, rank, width + share), BF),
        recv=pltpu.VMEM((peers, rank, width + share), BF),
        sum=pltpu.VMEM((rank, width + share), F32),
        mine_t=pltpu.VMEM((rank, width), BF),
        mine_l=pltpu.VMEM((rank, share), BF),
        core_sems=dma((2,)),
        send_sems=dma((peers,)),
        recv_sems=dma((peers,)),
        spread_l=dma((peers,)),
        arrive_l=dma((peers,)),
        pass_l=dma((peers,)),
        other_l=dma((peers,)),
        spread_t=dma((blocks,)),
        arrive_t=dma((blocks,)),
        pass_t=dma((blocks,)),
        other_t=dma((blocks,)),
    )
    names = (*arrays, *outputs, *scratch)
    kept = [pltpu.VMEM(array.shape, array.dtype) for array in list(arrays.values())[:LOADS]]
    return pl.pallas_call(
        partial(finish_kernel, shape, names),
        in_specs=[hbm] * LOADS + [vm] * (len(arrays) - LOADS),
        out_specs=[vm] * 3,
        out_shape=list(outputs.values()),
        scratch_shapes=list(scratch.values()) + kept,
        compiler_params=pltpu.CompilerParams(
            collective_id=0, has_side_effects=True, vmem_limit_bytes=VMEM
        ),
        name="finish",
    )(*arrays.values())


def middle_kernel(seqs, context_ref, tokens_ref, cotangent_ref, out_w_hbm, up_w_hbm, down_w_hbm,
                  out_a_ref, out_b_ref, up_a_ref, up_b_ref, down_a_ref, down_b_ref, gain_one_ref, gain_two_ref,
                  layer_ref, grad_one_ref, grad_context_ref, out_ga_ref, out_gb_ref, ff_ref,
                  out_w, up_w, down_w, hidden_ref, low_ref, work_ref, act_ref, slope_ref, sems):
    rows, width = tokens_ref.shape
    ff = up_w.shape[1]
    share = rows // seqs
    chunk = 512
    copies = []
    for index, (source, target) in enumerate(((out_w_hbm, out_w), (up_w_hbm, up_w), (down_w_hbm, down_w))):
        copy = pltpu.make_async_copy(source, target, sems.at[index])
        copy.start()
        copies.append(copy)

    def parts(step):
        found = [step(s, slice(s * share, (s + 1) * share)) for s in range(seqs)]
        return found[0] if seqs == 1 else jnp.concatenate(found, axis=0)

    def inner(values, factor_ref, scale=1.0):
        return parts(lambda s, at: (scale * mm(values[at], factor_ref[s], NT)).astype(BF))

    def widened(inner_values, factor_ref, columns=slice(None)):
        return parts(lambda s, at: mm(inner_values[at], factor_ref[s, :, columns]))

    def factor_grad(left, right, s):
        at = slice(s * share, (s + 1) * share)
        return lax.dot_general(left[at], right[at], (((0,), (0,)), ((), ())), preferred_element_type=F32)

    def stats(values):
        centered = values - jnp.mean(values, axis=1, keepdims=True)
        inverse = lax.rsqrt(jnp.mean(centered * centered, axis=1, keepdims=True) + EPSILON)
        return centered * inverse, inverse

    def back(normed, inverse, gain, upstream):
        scaled = upstream * gain
        return inverse * (
            scaled
            - jnp.mean(scaled, axis=1, keepdims=True)
            - normed * jnp.mean(scaled * normed, axis=1, keepdims=True)
        )

    context = context_ref[...]
    inner_out = inner(context, out_a_ref)
    copies[0].wait()
    attended = mm(context, out_w[...]) + ADAPTER_SCALING * widened(inner_out, out_b_ref)
    normed_one, inverse_one = stats(tokens_ref[...] + attended)
    grad_one_ref[...] = normed_one
    hidden = normed_one * gain_one_ref[...]
    hidden_ref[...] = hidden
    low_ref[...] = hidden.astype(BF)
    low = low_ref[...]
    inner_up = inner(low, up_a_ref)
    copies[1].wait()
    for start in range(0, ff, chunk):
        columns = slice(start, start + chunk)
        pre = mm(low, up_w[:, columns]) + ADAPTER_SCALING * widened(inner_up, up_b_ref, columns)
        below = 0.5 + 0.5 * lax.erf(pre * math.sqrt(0.5))
        act_ref[:, columns] = (pre * below).astype(BF)
        density = jnp.exp(pre * pre * -0.5) * (1.0 / math.sqrt(2.0 * math.pi))
        slope_ref[:, columns] = (below + pre * density).astype(BF)
    act = act_ref[...]
    inner_down = inner(act, down_a_ref)
    copies[2].wait()
    branch = mm(act, down_w[...]) + ADAPTER_SCALING * widened(inner_down, down_b_ref)
    normed_two, inverse_two = stats(hidden_ref[...] + branch)
    layer_ref[...] = normed_two * gain_two_ref[...]
    work_ref[...] = back(normed_two, inverse_two, gain_two_ref[...], cotangent_ref[...])
    grad_low = work_ref[...].astype(BF)
    grad_inner = inner(grad_low, down_b_ref, ADAPTER_SCALING)
    for s in range(seqs):
        ff_ref[s, :, width + 2 * ff:] = ADAPTER_SCALING * factor_grad(inner_down, grad_low, s)
        ff_ref[s, :, width + ff:width + 2 * ff] = factor_grad(grad_inner, act, s)
    for start in range(0, ff, chunk):
        columns = slice(start, start + chunk)
        grad_act = mm(grad_low, down_w[columns, :], NT) + widened(grad_inner, down_a_ref, columns)
        slope_ref[:, columns] = (grad_act.astype(BF).astype(F32) * slope_ref[:, columns].astype(F32)).astype(BF)
    grad_pre = slope_ref[...]
    grad_inner = inner(grad_pre, up_b_ref, ADAPTER_SCALING)
    for s in range(seqs):
        ff_ref[s, :, width:width + ff] = ADAPTER_SCALING * factor_grad(inner_up, grad_pre, s)
        ff_ref[s, :, :width] = factor_grad(grad_inner, low, s)
    grad_hidden = mm(grad_pre, up_w[...], NT) + widened(grad_inner, up_a_ref)
    grad_one = back(grad_one_ref[...], inverse_one, gain_one_ref[...], grad_hidden + work_ref[...])
    grad_one_ref[...] = grad_one
    grad_low = grad_one.astype(BF)
    grad_inner = inner(grad_low, out_b_ref, ADAPTER_SCALING)
    for s in range(seqs):
        out_gb_ref[s] = ADAPTER_SCALING * factor_grad(inner_out, grad_low, s)
        out_ga_ref[s] = factor_grad(grad_inner, context, s)
    grad_context_ref[...] = (mm(grad_low, out_w[...], NT) + widened(grad_inner, out_a_ref)).astype(BF)


def middle(context, tokens, cotangent, out_weight, up_weight, down_weight, factors, gain_one, gain_two):
    seqs, share, width = tokens.shape
    rows = seqs * share
    ff = up_weight.shape[1]
    rank = factors[0].shape[1]
    vm = pl.BlockSpec(memory_space=pltpu.VMEM)
    hbm = pl.BlockSpec(memory_space=pltpu.HBM)
    wide = jax.ShapeDtypeStruct((rows, width), F32)
    factor = jax.ShapeDtypeStruct((seqs, rank, width), F32)
    found = pl.pallas_call(
        partial(middle_kernel, seqs),
        in_specs=[vm] * 3 + [hbm] * 3 + [vm] * 8,
        out_specs=[vm] * 6,
        out_shape=[wide, wide, jax.ShapeDtypeStruct((rows, width), BF), factor, factor,
                   jax.ShapeDtypeStruct((seqs, rank, 2 * width + 2 * ff), F32)],
        scratch_shapes=[
            pltpu.VMEM(out_weight.shape, BF), pltpu.VMEM(up_weight.shape, BF), pltpu.VMEM(down_weight.shape, BF),
            pltpu.VMEM((rows, width), F32), pltpu.VMEM((rows, width), BF), pltpu.VMEM((rows, width), F32),
            pltpu.VMEM((rows, ff), BF), pltpu.VMEM((rows, ff), BF), pltpu.SemaphoreType.DMA((3,)),
        ],
        compiler_params=pltpu.CompilerParams(vmem_limit_bytes=VMEM),
        cost_estimate=pl.CostEstimate(flops=36 * rows * width * width, bytes_accessed=2 * 12 * width * width, transcendentals=rows * ff),
        name="middle",
    )(context.reshape(rows, width), tokens.reshape(rows, width), cotangent.reshape(rows, width),
      out_weight, up_weight, down_weight, *factors, gain_one.reshape(1, width), gain_two.reshape(1, width))
    return [array.reshape(seqs, share, width) for array in found[:3]] + list(found[3:])


def shifted(value, axes, steps):
    count = math.prod(lax.axis_size(axis) for axis in axes)
    initial, last = (max(0, -steps), min(count, count - steps))
    return lax.ppermute(value, axes, [(source, source + steps) for source in range(initial, last)])


def bucket_of(offset, buckets, distance_cap):
    middle = buckets // 2
    sign_of = np.sign(offset)
    magnitude = np.where((offset < middle) & (offset > -middle), middle - 1, np.abs(offset))
    log_place = (
        np.ceil(np.log(magnitude / middle) / np.log((distance_cap - 1) / middle) * (middle - 1))
        + middle
    )
    return np.where(np.abs(offset) <= middle, offset, log_place * sign_of).astype(np.int32)


def offset_tables():
    place = np.arange(2 * HALF)

    def hot(distance, sign):
        clipped = np.clip(distance, 1 - HALF, HALF - 1)
        bucket = np.clip(BUCK + sign * bucket_of(clipped, BUCK, SPAN), 0, 2 * BUCK - 1)
        return np.eye(2 * BUCK, dtype=np.float32)[bucket]

    return hot(HALF - place, 1), hot(place - HALF, -1), hot(HALF - 1 - place, -1)


def segment_ids(lengths, positions):
    bounds = jnp.cumsum(lengths, axis=-1, dtype=jnp.int32)
    return jnp.sum(
        (bounds[..., None, :] <= positions[:, None]).astype(jnp.int32), axis=-1, dtype=jnp.int32
    )


def product(pattern, left_side, right_side):
    return jnp.einsum(pattern, left_side, right_side, preferred_element_type=F32)


def norm_stats(values):
    centered = values - jnp.mean(values, axis=-1, keepdims=True)
    inverse = lax.rsqrt(jnp.mean(centered * centered, axis=-1, keepdims=True) + EPSILON)
    return (centered * inverse, inverse)


def norm_back(normed, inverse, scale_gain, upstream):
    scaled = upstream * scale_gain
    return inverse * (
        scaled
        - jnp.mean(scaled, axis=-1, keepdims=True)
        - normed * jnp.mean(scaled * normed, axis=-1, keepdims=True)
    )


def adapter_forward(rows_in, weight, down, up):
    inner = product("sti,sir->str", rows_in, down).astype(BF)
    mapped = product("sti,io->sto", rows_in, weight) + ADAPTER_SCALING * product(
        "str,sro->sto", inner, up
    )
    return (mapped, inner)


def adapter_back(rows_in, inner, weight, down, up, gradient):
    grad_up = ADAPTER_SCALING * product("str,sto->sro", inner, gradient)
    grad_inner = (ADAPTER_SCALING * product("sto,sro->str", gradient, up)).astype(BF)
    grad_down = product("sti,str->sir", rows_in, grad_inner)
    grad_in = product("sto,io->sti", gradient, weight) + product("str,sir->sti", grad_inner, down)
    return (grad_in, grad_down, grad_up)


def body(
    tokens,
    cotangent,
    doc_lengths,
    adapter_ids,
    query_weight,
    key_weight,
    value_weight,
    output_weight,
    up_weight,
    down_weight,
    attention_gain,
    feedforward_gain,
    position_gain,
    position_table,
    attention_down,
    attention_up,
    expand_down,
    expand_up,
    reduce_down,
    reduce_up,
):
    seqs, row_count, width = tokens.shape
    head_groups = lax.axis_size("head")
    head_index = lax.axis_index("head")
    seq_index = lax.axis_index("seq")
    by_rows = seqs == 1 and row_count == HALF

    def turned(array):
        return jnp.swapaxes(array, -1, -2)

    token_low = tokens.astype(BF)
    frozen = (query_weight, key_weight, value_weight)

    def columns(matrix):
        if by_rows:
            return matrix
        local = width // head_groups
        return lax.dynamic_slice_in_dim(matrix, head_index * local, local, matrix.ndim - 1)

    if by_rows:
        block_axes = ("seq", "head")
        block_index = seq_index * head_groups + head_index
        query_count = row_count
    else:
        block_axes = ("seq",)
        block_index = seq_index
        query_count = row_count * head_groups
    blocks = math.prod(lax.axis_size(axis) for axis in block_axes)

    first_place = block_index * query_count - HALF
    factors, query_seg, key_bias = prepare(
        adapter_ids,
        doc_lengths,
        jnp.stack([first_place, query_count * blocks]).astype(jnp.int32),
        [turned(attention_down), attention_up, turned(expand_down), expand_up, turned(reduce_down), reduce_up],
        query_count,
    )
    downs, att_up = factors[:4], factors[4:8]
    att_down = [turned(factor) for factor in downs]

    def halo(array):
        before = shifted(array[:, query_count - HALF :], block_axes, 1)
        after = shifted(array[:, :HALF], block_axes, -1)
        return before, after

    hots = [jnp.asarray(hot, BF) for hot in offset_tables()]
    if by_rows:
        before, after = halo(token_low)
        (query, key, value), (query_rel, query_back, key_rel), table_low, inners, position_inners = begin(
            token_low[0],
            position_table,
            position_gain,
            frozen,
            [down[0] for down in downs[:3]],
            [up[0] for up in att_up[:3]],
            hots,
        )
        (key_halo, value_halo), inners_halo = halo_maps(
            before[0], after[0], frozen[1:], [down[0] for down in downs[1:3]], [up[0] for up in att_up[1:3]]
        )
        queries, keys, keys_halo, values, values_halo, key_rel, query_rel, query_back = (
            array[None]
            for array in (query, key, key_halo, value, value_halo, key_rel, query_rel, query_back)
        )
    else:
        projected = []
        inners = []
        for member in range(3):
            mapped, inner = adapter_forward(
                token_low, frozen[member], att_down[member], att_up[member]
            )
            projected.append(mapped.astype(BF))
            inners.append(inner)
        queries, keys, values = lax.all_to_all(
            jnp.stack(projected), "head", split_axis=3, concat_axis=2, tiled=True
        )
        keys_halo, values_halo = (jnp.concatenate(halo(array), axis=1) for array in (keys, values))
        table_low = (norm_stats(position_table)[0] * position_gain).astype(BF)
        position_inners = []
        tables = []
        for member in range(2):
            inner = product("pi,sir->spr", table_low, att_down[member]).astype(BF)
            mapped = product("pi,io->po", table_low, columns(frozen[member]))[
                None
            ] + ADAPTER_SCALING * product("spr,sro->spo", inner, columns(att_up[member]))
            position_inners.append(inner)
            tables.append(mapped.astype(BF))
        key_rel = product("cp,spo->sco", hots[0], tables[1]).astype(BF)
        query_rel = product("cp,spo->sco", hots[1], tables[0]).astype(BF)
        query_back = product("cp,spo->sco", hots[2], tables[0]).astype(BF)

    query_scores, key_scores = relative_scores(queries, keys, key_rel, query_rel)
    context, probs, context_wide, inverse_total = attention_forward(
        queries, keys, keys_halo, values, values_halo, query_rel, query_seg, key_bias, query_scores, key_scores
    )
    if by_rows:
        context_rows = context
    else:
        context_rows = lax.all_to_all(context, "head", split_axis=1, concat_axis=2, tiled=True)

    layer_output, grad_one, grad_context, grad_out_down, grad_out_up, grad_ff = middle(
        context_rows,
        tokens,
        cotangent,
        output_weight,
        up_weight,
        down_weight,
        (downs[3], att_up[3], *factors[8:]),
        attention_gain,
        feedforward_gain,
    )
    if not by_rows:
        grad_context = lax.all_to_all(grad_context, "head", split_axis=2, concat_axis=1, tiled=True)

    group = ADAPTERS // head_groups
    ids = lax.all_gather(adapter_ids, "batch", axis=0, tiled=True)
    slots = head_index * group + jnp.arange(group, dtype=jnp.int32)
    select = (ids[:, None] == slots[None, :]).astype(F32)

    def spread(array):
        chosen_by = select.reshape(select.shape + (1,) * (array.ndim - 1))
        return jnp.sum(chosen_by * array[:, None], axis=0)

    def unflat(array, widths):
        return jnp.split(array, np.cumsum(widths)[:-1].tolist(), axis=-1)

    ff_width = up_weight.shape[1]
    rank = attention_up.shape[2]
    peers = lax.axis_size("seq") * head_groups
    cores = lax.axis_size("batch")
    table_rows = position_table.shape[0]
    direct = by_rows and cores == 2 and table_rows == peers * cores * rank
    grad_q, grad_k, grad_k_halo, grad_v, grad_v_halo, grad_key_rel, grad_query_rel = attention_backward(
        queries,
        keys,
        keys_halo,
        values,
        values_halo,
        key_rel,
        query_back,
        probs,
        grad_context,
        context_wide,
        inverse_total,
    )

    def joined(total, from_above, from_below):
        if query_count == HALF:
            return total + from_above + from_below
        total = total.at[:, query_count - HALF :].add(from_above)
        return total.at[:, :HALF].add(from_below)

    def fold(total, halo_part):
        from_above = shifted(halo_part[:, :HALF], block_axes, -1).astype(F32)
        from_below = shifted(halo_part[:, HALF:], block_axes, 1).astype(F32)
        return joined(total.astype(F32), from_above, from_below)

    if direct:
        grad_tokens, table_total, late = finish(
            (head_groups, peers // head_groups, cores, rank),
            key_halo=grad_k_halo[0],
            value_halo=grad_v_halo[0],
            key_w=key_weight,
            value_w=value_weight,
            back_hot=hots[2].T,
            query_rel_g=grad_query_rel[0],
            key_hot=hots[0].T,
            key_rel_g=grad_key_rel[0],
            query_w=query_weight,
            x=token_low[0],
            x_before=before[0],
            x_after=after[0],
            low=table_low,
            query_g=grad_q[0],
            key_g=grad_k[0],
            value_g=grad_v[0],
            grad_one=grad_one[0],
            query_a=downs[0][0],
            key_a=downs[1][0],
            value_a=downs[2][0],
            query_b=att_up[0][0],
            key_b=att_up[1][0],
            value_b=att_up[2][0],
            query_u=inners[0],
            key_u=inners[1],
            value_u=inners[2],
            key_uh=inners_halo[0],
            value_uh=inners_halo[1],
            query_pu=position_inners[0],
            key_pu=position_inners[1],
            out_ga=grad_out_down[0],
            out_gb=grad_out_up[0],
            ff=grad_ff[0],
        )
        input_grad = grad_tokens[None]
        places = lax.dynamic_slice_in_dim(
            position_table, head_index * (table_rows // head_groups), table_rows // head_groups, 0
        )
        table_grad, down_grad, up_grad, *ff_grads = spread_all(
            ids, slots, late, table_total, places, position_gain, ff_width
        )
        return (
            layer_output,
            input_grad,
            table_grad,
            turned(down_grad),
            up_grad,
            turned(ff_grads[0]),
            ff_grads[1],
            turned(ff_grads[2]),
            ff_grads[3],
        )
    else:
        down_grads = []
        up_grads = []
        if by_rows:
            input_grad = grad_one
            grad_halo = 0.0
            rows_halo = jnp.concatenate([before, after], axis=1)
            for member, pieces in enumerate(
                (
                    ((token_low, inners[0][None], grad_q),),
                    ((token_low, inners[1][None], grad_k), (rows_halo, inners_halo[0][None], grad_k_halo)),
                    ((token_low, inners[2][None], grad_v), (rows_halo, inners_halo[1][None], grad_v_halo)),
                )
            ):
                found = [
                    adapter_back(rows, inner, frozen[member], att_down[member], att_up[member], gradient)
                    for rows, inner, gradient in pieces
                ]
                input_grad = input_grad + found[0][0]
                if member > 0:
                    grad_halo = grad_halo + found[1][0]
                down_grads.append(sum(turned(one[1]) for one in found))
                up_grads.append(sum(one[2] for one in found))
            input_grad = fold(input_grad, grad_halo.astype(BF))
            position_inners = [inner[None] for inner in position_inners]
        else:
            grad_qkv = jnp.stack(
                [grad_q, fold(grad_k, grad_k_halo).astype(BF), fold(grad_v, grad_v_halo).astype(BF)]
            )
            grad_qkv = lax.all_to_all(grad_qkv, "head", split_axis=2, concat_axis=3, tiled=True)
            input_grad = grad_one
            for member in range(3):
                grad_in, grad_dn, grad_upper = adapter_back(
                    token_low,
                    inners[member],
                    frozen[member],
                    att_down[member],
                    att_up[member],
                    grad_qkv[member],
                )
                input_grad = input_grad + grad_in
                down_grads.append(turned(grad_dn))
                up_grads.append(grad_upper)
        down_grads.append(grad_out_down)
        up_grads.append(grad_out_up)
        position_grads = (
            product("cb,soc->sbo", hots[2], grad_query_rel),
            product("cb,soc->sbo", hots[0], grad_key_rel),
        )
        grad_table_low = jnp.zeros(position_table.shape, F32)
        for member in range(2):
            gradient = position_grads[member].astype(BF)
            up = columns(att_up[member])
            grad_columns = ADAPTER_SCALING * product(
                "spr,spo->sro", position_inners[member], gradient
            )
            grad_inner = (ADAPTER_SCALING * product("spo,sro->spr", gradient, up)).astype(BF)
            grad_table_low = (
                grad_table_low
                + product("spo,io->pi", gradient, columns(frozen[member]))
                + product("spr,sir->pi", grad_inner, att_down[member])
            )
            down_grads[member] = down_grads[member] + product("spr,pi->sri", grad_inner, table_low)
            if not by_rows:
                grad_columns = lax.dynamic_update_slice_in_dim(
                    jnp.zeros_like(up_grads[member]),
                    grad_columns,
                    head_index * (width // head_groups),
                    2,
                )
            up_grads[member] = up_grads[member] + grad_columns
        late = jnp.concatenate(down_grads + up_grads, axis=-1)
        late = lax.all_gather(lax.psum(late, ("seq", "head")), "batch", axis=0, tiled=True)
        early = lax.all_gather(lax.psum(grad_ff, ("seq", "head")), "batch", axis=0, tiled=True)
        table_total = lax.psum(grad_table_low, ("seq", "batch"))
        table_total = lax.psum_scatter(table_total, "head", scatter_dimension=0, tiled=True)
    own_rows = table_rows // head_groups

    def head_rows(array):
        return lax.dynamic_slice_in_dim(array, head_index * own_rows, own_rows, 0)

    table_normed, table_inverse = norm_stats(head_rows(position_table))
    table_grad = norm_back(table_normed, table_inverse, position_gain, table_total)
    early = [spread(part) for part in unflat(early, [width, ff_width, ff_width, width])]
    late = [spread(part) for part in unflat(late, [width] * 8)]
    return (
        layer_output,
        input_grad,
        table_grad,
        jnp.stack([turned(part) for part in late[:4]]),
        jnp.stack(late[4:]),
        turned(early[0]),
        early[1],
        turned(early[2]),
        early[3],
    )


def solution(mesh):
    rows = P("batch", ("seq", "head"), None)
    return jax.shard_map(
        body,
        mesh=mesh,
        in_specs=(rows, rows, P("batch", None), P("batch")) + (P(),) * 16,
        out_specs=(
            rows,
            rows,
            P("head", None),
            P(None, "head", None, None),
            P(None, "head", None, None),
            P("head", None, None),
            P("head", None, None),
            P("head", None, None),
            P("head", None, None),
        ),
        check_vma=False,
    )
```

```python
from functools import partial
import math
from types import SimpleNamespace

import jax
import jax.numpy as jnp
import numpy as np
from jax import lax
from jax.experimental import pallas as pl
from jax.experimental.pallas import tpu as pltpu
from jax.sharding import PartitionSpec as P

HEADS = 16
HEAD_DIM = 64
BUCK = 256
SPAN = 512
ADAPTERS = 8
HALF = 512
DOCS = 8

EPSILON = 1e-07
ADAPTER_SCALING = 2.0
NEGATIVE = -1e30
PRECISE = lax.Precision.HIGHEST
TILE = 128
BF = jnp.bfloat16
F32 = jnp.float32
MESH = pl.DeviceIdType.MESH
VMEM = 63 * 2**20
NN = (((1,), (0,)), ((), ()))
NT = (((1,), (1,)), ((), ()))


def mm(a, b, dims=NN):
    return lax.dot_general(a, b, dims, preferred_element_type=F32)

def lanes(shape=(TILE, TILE)):
    return lax.broadcasted_iota(jnp.int32, shape, 1)

def rows(shape=(TILE, TILE)):
    return lax.broadcasted_iota(jnp.int32, shape, 0)

def skew(tile):
    return pltpu.roll(tile, 0, 1, stride=1, stride_axis=0)

def flip_matrix():
    return jnp.where(lanes() + rows() == TILE - 1, 1.0, 0.0).astype(BF)


class Loaded:
    def __init__(self, source, target, sem):
        self.target = target
        self.copy = pltpu.make_async_copy(source, target, sem)
        self.copy.start()

    def __call__(self):
        if self.copy is not None:
            self.copy.wait()
            self.copy = None
        return self.target[...]


def with_halo(own_ref, halo_ref):
    return jnp.concatenate([halo_ref[0, :HALF], own_ref[0], halo_ref[0, HALF:]], axis=0)


class Stored:
    def __init__(self, target, buffer, sem):
        self.buffer = buffer
        self.copy = pltpu.make_async_copy(buffer, target, sem)

    def put(self, value):
        self.buffer[...] = value
        self.copy.start()

    def wait(self):
        self.copy.wait()


def prepare_kernel(seqs, ids_ref, lengths_ref, base_ref, *refs):
    stacks = [stack.at[member] for stack in refs[:2] for member in range(4)] + list(refs[2:6])
    count = len(stacks)
    refs = refs[6:]
    outs = refs[: count + 2]
    buffers = refs[count + 2 : 2 * count + 2]
    made = refs[2 * count + 2 : 3 * count + 4]
    sems, out_sems = refs[3 * count + 4 :]
    outs = [Stored(target, buffer, out_sems.at[i]) for i, (target, buffer) in enumerate(zip(outs, made))]
    query_seg_ref, key_bias_ref = made[count:]
    copies = []
    for s in range(seqs):
        for index, (stack, buffer) in enumerate(zip(stacks, buffers)):
            copy = pltpu.make_async_copy(stack.at[ids_ref[s]], buffer.at[s], sems.at[s, index])
            copy.start()
            copies.append(copy)
    rows_k = key_bias_ref.shape[1]
    rows_q = query_seg_ref.shape[1]
    place = base_ref[0] + rows((rows_k, TILE))
    slot = lanes((rows_k, TILE)) % HEAD_DIM
    inside = (place >= 0) & (place < base_ref[1])
    for s in range(seqs):
        segment = jnp.zeros((rows_k, TILE), jnp.int32)
        bound = jnp.int32(0)
        for document in range(DOCS):
            bound = bound + lengths_ref[s, document]
            segment += jnp.where(place >= bound, 1, 0)
        segment = jnp.where(inside, segment, DOCS)
        same = slot == segment
        query_seg_ref[s] = jnp.where(same, 1.0, 0.0)[HALF : HALF + rows_q].astype(BF)
        open_slot = (same & (segment < DOCS)) | (slot > DOCS)
        key_bias_ref[s] = jnp.where(open_slot, 0.0, NEGATIVE).astype(BF)
    for out in outs[count:]:
        out.copy.start()
    for copy in copies:
        copy.wait()
    for buffer, out in zip(buffers, outs):
        out.put(buffer[...].astype(BF))
    for out in outs:
        out.wait()


def prepare(adapter_ids, lengths, base, stacks, query_count):
    seqs = adapter_ids.shape[0]
    hbm = pl.BlockSpec(memory_space=pltpu.HBM)
    sm = pl.BlockSpec(memory_space=pltpu.SMEM)
    shapes = [(seqs,) + stack.shape[2:] for stack in stacks[:2] for _ in range(4)]
    shapes += [(seqs,) + stack.shape[1:] for stack in stacks[2:]]
    count = len(shapes)
    columns = [(seqs, query_count, TILE), (seqs, query_count + 2 * HALF, TILE)]
    found = pl.pallas_call(
        partial(prepare_kernel, seqs),
        in_specs=[sm] * 3 + [hbm] * len(stacks),
        out_specs=[hbm] * (count + 2),
        out_shape=[jax.ShapeDtypeStruct(shape, BF) for shape in shapes + columns],
        scratch_shapes=[pltpu.VMEM(shape, F32) for shape in shapes]
        + [pltpu.VMEM(shape, BF) for shape in shapes + columns]
        + [pltpu.SemaphoreType.DMA((seqs, count)), pltpu.SemaphoreType.DMA((count + 2,))],
        compiler_params=pltpu.CompilerParams(vmem_limit_bytes=VMEM),
        cost_estimate=pl.CostEstimate(flops=10**6, bytes_accessed=6 * 10**6, transcendentals=0),
        name="prepare",
    )(adapter_ids, lengths, base, *stacks)
    return found[:count], found[count], found[count + 1]


def adapted(x, weight, inner, up):
    return (mm(x, weight) + ADAPTER_SCALING * mm(inner, up)).astype(BF)


def begin_kernel(x_ref, table_ref, gain_ref, query_a, key_a, value_a, query_b, key_b, value_b,
                 query_w, key_w, value_w, query_hot, back_hot, key_hot,
                 query_out, key_out, value_out, query_rel_out, back_rel_out, key_rel_out, low_out,
                 query_u, key_u, value_u, query_pu, key_pu, *scratch):
    loaded = scratch[:6]
    stored = scratch[6:13]
    load_sems, store_sems = scratch[13:]
    query_w, key_w, value_w, query_hot, back_hot, key_hot = (
        Loaded(source, target, load_sems.at[index])
        for index, (source, target) in enumerate(zip((query_w, key_w, value_w, query_hot, back_hot, key_hot), loaded))
    )
    outs = [
        Stored(target, buffer, store_sems.at[index])
        for index, (target, buffer) in enumerate(
            zip((query_out, key_out, value_out, query_rel_out, back_rel_out, key_rel_out, low_out), stored)
        )
    ]
    x = x_ref[...]
    query_u[...] = mm(x, query_a[...], NT).astype(BF)
    key_u[...] = mm(x, key_a[...], NT).astype(BF)
    value_u[...] = mm(x, value_a[...], NT).astype(BF)
    values = table_ref[...]
    centered = values - jnp.mean(values, axis=1, keepdims=True)
    inverse = lax.rsqrt(jnp.mean(centered * centered, axis=1, keepdims=True) + EPSILON)
    low = (centered * inverse * gain_ref[...]).astype(BF)
    outs[6].put(low)
    query_pu[...] = mm(low, query_a[...], NT).astype(BF)
    key_pu[...] = mm(low, key_a[...], NT).astype(BF)
    outs[0].put(adapted(x, query_w(), query_u[...], query_b[...]))
    position_q = adapted(low, query_w(), query_pu[...], query_b[...])
    outs[1].put(adapted(x, key_w(), key_u[...], key_b[...]))
    position_k = adapted(low, key_w(), key_pu[...], key_b[...])
    outs[2].put(adapted(x, value_w(), value_u[...], value_b[...]))
    outs[3].put(mm(query_hot(), position_q).astype(BF))
    outs[4].put(mm(back_hot(), position_q).astype(BF))
    outs[5].put(mm(key_hot(), position_k).astype(BF))
    for out in outs:
        out.wait()


def begin(x, table, gain, weights, downs, ups, hots):
    rows_x, width = x.shape
    rank = ups[0].shape[0]
    places = table.shape[0]
    spans = hots[0].shape[0]
    vm = pl.BlockSpec(memory_space=pltpu.VMEM)
    hbm = pl.BlockSpec(memory_space=pltpu.HBM)
    large = [(rows_x, width)] * 3 + [(spans, width)] * 3 + [(places, width)]
    inner = jax.ShapeDtypeStruct((rows_x, rank), BF)
    position_inner = jax.ShapeDtypeStruct((places, rank), BF)
    sources = (*weights, hots[1], hots[2], hots[0])
    found = pl.pallas_call(
        begin_kernel,
        in_specs=[vm] * 9 + [hbm] * 6,
        out_specs=[hbm] * 7 + [vm] * 5,
        out_shape=[jax.ShapeDtypeStruct(shape, BF) for shape in large] + [inner] * 3 + [position_inner] * 2,
        scratch_shapes=[pltpu.VMEM(source.shape, BF) for source in sources]
        + [pltpu.VMEM(shape, BF) for shape in large]
        + [pltpu.SemaphoreType.DMA((6,)), pltpu.SemaphoreType.DMA((7,))],
        compiler_params=pltpu.CompilerParams(vmem_limit_bytes=VMEM),
        cost_estimate=pl.CostEstimate(
            flops=6 * rows_x * width * width + 10 * places * width * width,
            bytes_accessed=24 * places * width + 6 * width * width,
            transcendentals=0,
        ),
        name="begin",
    )(x, table, gain.reshape(1, width), *downs, *ups, *sources)
    return found[:3], found[3:6], found[6], found[7:10], found[10:]


def relative_kernel(q_ref, k_ref, pk_ref, pq_ref, qs_ref, ks_ref):
    tiles = HALF // TILE
    span = 2 * tiles
    below = lanes() + rows() < TILE
    column = lanes((HALF, TILE)) < HEAD_DIM
    for h in range(2):
        own = column if h == 0 else ~column
        km = jnp.where(own, k_ref[0], jnp.zeros_like(k_ref[0]))
        qm = jnp.where(own, q_ref[0], jnp.zeros_like(q_ref[0]))
        for d in range(1, span):
            pairs = [(t, d + t - tiles) for t in range(tiles) if 0 <= d + t - tiles < tiles]
            first, last = pairs[0][1], pairs[-1][1]
            key_rel = mm(
                km[first * TILE : (last + 1) * TILE], pq_ref[0, (span - 1 - d) * TILE : (span + 1 - d) * TILE, :], NT
            ).astype(BF)
            for t, j in pairs:
                part = key_rel[(j - first) * TILE : (j - first + 1) * TILE]
                ks_ref[0, h, t, :, j * TILE : (j + 1) * TILE] = skew(
                    jnp.where(below, part[:, TILE:], part[:, :TILE])
                ).T
        query_rel = mm(qm, pk_ref[0], NT).astype(BF)
        for t in range(tiles):
            part = query_rel[t * TILE : (t + 1) * TILE]
            for d in range(span + 1):
                here = part[:, min(d, span - 1) * TILE : (min(d, span - 1) + 1) * TILE]
                if 0 < d < span:
                    here = jnp.where(below, here, part[:, (d - 1) * TILE : d * TILE])
                qs_ref[0, h, t, :, d * TILE : (d + 1) * TILE] = skew(here)


def relative_scores(q, k, pk, pq):
    n, rq, width = q.shape
    pairs = width // TILE
    off = 2 * HALF
    tiles = rq // TILE
    return pl.pallas_call(
        relative_kernel,
        grid=(n, pairs),
        in_specs=[column_spec(rq), column_spec(rq), column_spec(off), column_spec(off)],
        out_specs=[head_spec(tiles, TILE, off + TILE), head_spec(tiles, TILE, HALF)],
        out_shape=[jax.ShapeDtypeStruct((n, 2 * pairs, tiles, TILE, off + TILE), BF),
                   jax.ShapeDtypeStruct((n, 2 * pairs, tiles, TILE, HALF), BF)],
        compiler_params=pltpu.CompilerParams(dimension_semantics=("arbitrary", "arbitrary"), vmem_limit_bytes=VMEM),
        cost_estimate=pl.CostEstimate(
            flops=16 * n * rq * off * width, bytes_accessed=60 * 10**6, transcendentals=0
        ),
        name="relative_scores",
    )(q, k, pk, pq)


def column_spec(r):
    return pl.BlockSpec((1, r, TILE), lambda s, p: (s, 0, p))


def head_spec(*shape):
    return pl.BlockSpec((1, 2) + shape, lambda s, p: (s, p) + (0,) * len(shape))


def forward_kernel(mapped, q_ref, k_ref, v_ref, pq_ref, qhot_ref, kbias_ref, qs_ref, ko_ref, *refs):
    if mapped:
        kh_ref, vh_ref, ctx_ref, p_ref, ctxf_ref, inv_ref, kz_ref, vz_ref, ks_ref, s_ref = refs
    else:
        before, after, key_w, value_w, key_a, value_a, key_b, value_b = refs[:8]
        ctx_ref, p_ref, ctxf_ref, inv_ref, kh_ref, vh_ref, key_u, value_u, kz_ref, vz_ref, ks_ref, s_ref = refs[8:]

        @pl.when(pl.program_id(1) == 0)
        def _():
            for side, x in ((0, before), (1, after)):
                at = slice(side * HALF, (side + 1) * HALF)
                key_u[at] = mm(x[...], key_a[...], NT).astype(BF)
                value_u[at] = mm(x[...], value_a[...], NT).astype(BF)

        weights = jnp.concatenate([key_w[...], value_w[...]], axis=1)
        nothing = jnp.zeros_like(key_b[...])
        ups = jnp.concatenate(
            [jnp.concatenate([key_b[...], nothing], axis=1), jnp.concatenate([nothing, value_b[...]], axis=1)], axis=0
        )
        for side, x in ((0, before), (1, after)):
            at = slice(side * HALF, (side + 1) * HALF)
            inner = jnp.concatenate([key_u[at], value_u[at]], axis=1)
            both = adapted(x[...], weights, inner, ups)
            kh_ref[0, at] = both[:, :TILE]
            vh_ref[0, at] = both[:, TILE:]
    tiles = HALF // TILE
    span = 2 * tiles
    width = (span + 1) * TILE
    flip = flip_matrix()
    factor = math.log2(math.e) / math.sqrt(3 * HEAD_DIM)
    k = with_halo(k_ref, kh_ref)
    v = with_halo(v_ref, vh_ref)
    kb = kbias_ref[0]
    kcol = lanes(k.shape) < HEAD_DIM
    hcol = lanes(kh_ref.shape[1:]) < HEAD_DIM
    below = lanes() + rows() < TILE
    place = lanes() + rows()
    tcol = lanes() < HEAD_DIM
    for h in range(2):
        own = kcol if h == 0 else ~kcol
        kz_ref[h] = jnp.where(own, k, kb)
        vz_ref[h] = jnp.where(own, v, jnp.ones_like(v))
        km = jnp.where(hcol if h == 0 else ~hcol, kh_ref[0], jnp.zeros_like(kh_ref[0]))
        for d in range(span + 1):
            pairs = [(t, d + t if d + t < tiles else d + t - tiles) for t in range(tiles) if not tiles <= d + t < 2 * tiles]
            if not pairs:
                continue
            low = max(span - 1 - d, 0) * TILE
            high = min(span + 1 - d, span) * TILE
            first, last = pairs[0][1], pairs[-1][1]
            key_rel = mm(km[first * TILE : (last + 1) * TILE], pq_ref[0, low:high, :], NT).astype(BF)
            for t, j in pairs:
                part = key_rel[(j - first) * TILE : (j - first + 1) * TILE]
                if 0 < d < span:
                    part = jnp.where(below, part[:, TILE:], part[:, :TILE])
                w = d if d < tiles else d - tiles
                ks_ref[h, t, :, w * TILE : (w + 1) * TILE] = skew(part).T

    flips = jnp.concatenate([flip, flip], axis=1)

    def scores(t):
        at = slice(t * TILE, (t + 1) * TILE)
        window = slice(t * TILE, t * TILE + width)
        q = q_ref[0, at, :]
        hot = qhot_ref[0, at, :]
        edge = (tiles - t) * TILE
        for h in range(2):
            q_side = mm(flip, jnp.where(tcol if h == 0 else ~tcol, q, hot)).astype(BF)
            key_side = jnp.concatenate([ks_ref[h, t, :, :edge], ko_ref[0, h, t], ks_ref[h, t, :, edge:]], axis=1)
            relative = jnp.concatenate([qs_ref[0, h, t], key_side], axis=0)
            s_ref[2 * (t % 2) + h] = mm(q_side, kz_ref[h, window, :], NT) + mm(flips, relative)

    scores(0)
    for t in range(tiles):
        if t + 1 < tiles:
            scores(t + 1)
        at = slice(t * TILE, (t + 1) * TILE)
        window = slice(t * TILE, t * TILE + width)
        outs = []
        for h in range(2):
            own = tcol if h == 0 else ~tcol
            first = s_ref[2 * (t % 2) + h, :, :TILE]
            s_ref[2 * (t % 2) + h, :, :TILE] = jnp.where(place > TILE - 1, first, NEGATIVE)
            last = s_ref[2 * (t % 2) + h, :, span * TILE :]
            s_ref[2 * (t % 2) + h, :, span * TILE :] = jnp.where(place < TILE - 1, last, NEGATIVE)
            middle = s_ref[2 * (t % 2) + h, :, tiles * TILE : (tiles + 1) * TILE]
            s_ref[2 * (t % 2) + h, :, tiles * TILE : (tiles + 1) * TILE] = jnp.where(
                (place == TILE - 1) & (middle < 0.1 * NEGATIVE), 0.0, middle
            )
            top = s_ref[2 * (t % 2) + h, :, :TILE]
            for d in range(1, span + 1):
                top = jnp.maximum(top, s_ref[2 * (t % 2) + h, :, d * TILE : (d + 1) * TILE])
            peak = jnp.max(top, axis=1, keepdims=True)
            prob = jnp.exp2((s_ref[2 * (t % 2) + h] - peak) * factor).astype(BF)
            a = t % 2
            row_at = slice(a * TILE, (a + 1) * TILE)
            p_ref[0, h, t // 2, row_at, a * TILE : a * TILE + width] = prob
            p_ref[0, h, t // 2, row_at, (1 - a) * width : (1 - a) * width + TILE] = jnp.zeros((TILE, TILE), BF)
            total = mm(prob, vz_ref[h, window, :])
            inv = 1.0 / jnp.where(own, pltpu.roll(total, HEAD_DIM, 1), total)
            inv_ref[0, h, at, :] = inv
            outs.append(total * inv)
        ctx = jnp.where(tcol, outs[0], outs[1])
        ctxf_ref[0, at, :] = ctx
        ctx_ref[0, at, :] = mm(flip, ctx.astype(BF)).astype(BF)


def attention_forward(q, k, v, pq, qhot, kbias, query_scores, key_scores, halo):
    n, rq, width = q.shape
    off = 2 * HALF
    rk = rq + off
    pairs = width // TILE
    tiles = rq // TILE

    def whole(r):
        return pl.BlockSpec((1, r, TILE), lambda s, p: (s, 0, 0))

    mapped = len(halo) == 2
    in_specs = [column_spec(rq), column_spec(rq), column_spec(rq), column_spec(off), whole(rq), whole(rk),
                head_spec(tiles, TILE, off + TILE), head_spec(tiles, TILE, HALF)]
    out_specs = [column_spec(rq), head_spec(tiles // 2, 2 * TILE, off + 2 * TILE), column_spec(rq), head_spec(rq, TILE)]
    out_shape = [jax.ShapeDtypeStruct((n, rq, width), BF),
                 jax.ShapeDtypeStruct((n, 2 * pairs, tiles // 2, 2 * TILE, off + 2 * TILE), BF),
                 jax.ShapeDtypeStruct((n, rq, width), F32),
                 jax.ShapeDtypeStruct((n, 2 * pairs, rq, TILE), F32)]
    if mapped:
        in_specs += [column_spec(off)] * 2
    else:
        rank = halo[4].shape[0]

        def once(*shape):
            return pl.BlockSpec(shape, lambda s, p: (0,) * len(shape))

        def columns(r):
            return pl.BlockSpec((r, TILE), lambda s, p: (0, p))

        in_specs += [once(HALF, width)] * 2 + [columns(width)] * 2 + [once(rank, width)] * 2 + [columns(rank)] * 2
        out_specs += [column_spec(off)] * 2 + [once(off, rank)] * 2
        out_shape += [jax.ShapeDtypeStruct((n, off, width), BF)] * 2 + [jax.ShapeDtypeStruct((off, rank), BF)] * 2
    return pl.pallas_call(
        partial(forward_kernel, mapped),
        grid=(n, pairs),
        in_specs=in_specs,
        out_specs=out_specs,
        out_shape=out_shape,
        scratch_shapes=[pltpu.VMEM((2, rk, TILE), BF), pltpu.VMEM((2, rk, TILE), BF),
                        pltpu.VMEM((2, tiles, TILE, HALF + TILE), BF),
                        pltpu.VMEM((4, TILE, off + TILE), F32)],
        compiler_params=pltpu.CompilerParams(dimension_semantics=("arbitrary", "arbitrary"), vmem_limit_bytes=VMEM),
        cost_estimate=pl.CostEstimate(
            flops=32 * n * rq * off * width, bytes_accessed=60 * 10**6, transcendentals=0
        ),
        name="attention_forward",
    )(q, k, v, pq, qhot, kbias, query_scores, key_scores, *halo)


def spread_kernel(group, head_ref, ids_ref, late_ref, table_ref, places_hbm, gain_ref,
                  table_out, down_out, up_out, expand_down, expand_up, reduce_down, reduce_up, places_ref, sem):
    cores, peers, rank, share = late_ref.shape
    width = table_ref.shape[3]
    ff = expand_up.shape[2]
    part = 8 * width // peers
    rest = share - part
    count = places_ref.shape[0]
    fetch = pltpu.make_async_copy(places_hbm.at[pl.ds(pl.multiple_of(head_ref[0] * count, count), count)], places_ref, sem)
    fetch.start()
    first = head_ref[0] * group
    weights = [
        [jnp.where(ids_ref[s, :1, :1] == (first + a).astype(F32), 1.0, 0.0) for a in range(group)] for s in range(cores)
    ]

    def fill(out, a, pieces):
        for column, piece in pieces:
            value = sum(weights[s][a] * late_ref[s, piece[0], :, piece[1]].astype(F32) for s in range(cores))
            out[:, column] = value

    per = width // part
    starts = ((expand_down, 0, width), (expand_up, width, ff), (reduce_down, width + ff, ff), (reduce_up, width + 2 * ff, width))
    for a in range(group):
        for member in range(8):
            out = (down_out if member < 4 else up_out).at[member % 4, a]
            fill(out, a, [
                (slice(half * part, (half + 1) * part), (member * per + half, slice(0, part))) for half in range(per)
            ])
        for out, start, count in starts:
            pieces = []
            at = start
            while at < start + count:
                peer, offset = at // rest, at % rest
                length = min(rest - offset, start + count - at)
                pieces.append((slice(at - start, at - start + length), (peer, slice(part + offset, part + offset + length))))
                at += length
            fill(out.at[a], a, pieces)
    fetch.wait()
    values = places_ref[...]
    centered = values - jnp.mean(values, axis=1, keepdims=True)
    inverse = lax.rsqrt(jnp.mean(centered * centered, axis=1, keepdims=True) + EPSILON)
    normed = centered * inverse
    upstream = table_ref[...].reshape(values.shape).astype(F32) * gain_ref[...]
    table_out[...] = inverse * (
        upstream
        - jnp.mean(upstream, axis=1, keepdims=True)
        - normed * jnp.mean(upstream * normed, axis=1, keepdims=True)
    )


def spread_all(group, head, ids, late, table, places, gain, ff):
    rank = late.shape[2]
    width = table.shape[3]
    own = (places.shape[0] * group // ADAPTERS, width)
    vm = pl.BlockSpec(memory_space=pltpu.VMEM)
    sm = pl.BlockSpec(memory_space=pltpu.SMEM)

    def out(*shape):
        return jax.ShapeDtypeStruct(shape, F32)

    return pl.pallas_call(
        partial(spread_kernel, group),
        in_specs=[sm, vm, vm, vm, pl.BlockSpec(memory_space=pltpu.HBM), vm],
        out_specs=[vm] * 7,
        out_shape=[out(*own), out(4, group, rank, width), out(4, group, rank, width), out(group, rank, width),
                   out(group, rank, ff), out(group, rank, ff), out(group, rank, width)],
        scratch_shapes=[pltpu.VMEM(own, F32), pltpu.SemaphoreType.DMA],
        compiler_params=pltpu.CompilerParams(vmem_limit_bytes=VMEM),
        name="spread_all",
    )(head, ids, late, table, places, gain.reshape(1, width))


def backward_kernel(q_ref, k_ref, kh_ref, v_ref, vh_ref, pk_ref, pq_ref, p_ref, g_ref, ctxf_ref, inv_ref,
                    dq_ref, dk_ref, dkh_ref, dv_ref, dvh_ref, dpk_ref, dpq_ref,
                    kx_ref, vx_ref, qr_ref, gr_ref, e_ref, gc_ref, gk_ref, dvt_ref, dkt_ref):
    rows_q = q_ref.shape[1]
    rows_k = kx_ref.shape[0]
    kx_ref[...] = with_halo(k_ref, kh_ref)
    vx_ref[...] = with_halo(v_ref, vh_ref)
    tiles = rows_q // TILE
    key_tiles = rows_k // TILE
    span = 2 * HALF // TILE
    wide = (span + 2) * TILE
    flip = flip_matrix()
    scale = 1.0 / math.sqrt(3 * HEAD_DIM)
    tcol = lanes() < HEAD_DIM
    qcol = lanes((rows_q, TILE)) < HEAD_DIM
    over = lanes() > rows()
    under = lanes() >= rows()

    @pl.when((pl.program_id(0) == 0) & (pl.program_id(1) == 0))
    def _():
        gk_ref[...] = jnp.zeros_like(gk_ref)

    for t in range(tiles):
        at = slice(t * TILE, (t + 1) * TILE)
        qr_ref[at] = mm(flip, q_ref[0, at]).astype(BF)
        gr_ref[at] = mm(flip, g_ref[0, at]).astype(BF)
    q_rev = qr_ref[...]
    g_rev = gr_ref[...]
    q_turned = q_rev.T
    k_turned = kx_ref[...].T
    product = g_rev.astype(F32) * ctxf_ref[0]
    dvt_ref[...] = jnp.zeros_like(dvt_ref)
    dkt_ref[...] = jnp.zeros_like(dkt_ref)
    zero = jnp.zeros((TILE, TILE), BF)
    dq_main = [[], []]
    dq_parts = [None, None]
    dk_tiles = [[], []]

    def of_head(h):
        own = qcol if h == 0 else ~qcol
        inv = inv_ref[0, h]
        delta = jnp.sum(jnp.where(own, product, 0.0), axis=1, keepdims=True) * inv
        g_turned = (g_rev.astype(F32) * inv).astype(BF).T[h * HEAD_DIM : (h + 1) * HEAD_DIM]
        return jnp.where(own, g_rev, jnp.zeros_like(g_rev)), inv, delta, g_turned

    heads = [of_head(h) for h in range(2)]

    def errors(h, u):
        g_masked, inv, delta, g_turned = heads[h]
        part = slice(h * HEAD_DIM, (h + 1) * HEAD_DIM)
        at = slice(u * 2 * TILE, (u + 1) * 2 * TILE)
        window = slice(u * 2 * TILE, u * 2 * TILE + wide)
        prob = p_ref[0, h, u]
        g_probs = mm(g_masked[at], vx_ref[window], NT)
        inv_u = jnp.concatenate([inv[at]] * (span + 2), axis=1)
        delta_u = jnp.concatenate([delta[at]] * (span + 2), axis=1)
        e = (prob.astype(F32) * (g_probs * inv_u - delta_u)).astype(BF)
        e_ref[h, u] = e
        dvt_ref[part, window] += mm(g_turned[:, at], prob)
        dkt_ref[part, window] += mm(q_turned[part, at], e)
        dq_main[h].append(mm(e, kx_ref[window]))

    def error(h, t, d):
        a = t % 2
        return e_ref[h, t // 2, a * TILE : (a + 1) * TILE, (a + d) * TILE : (a + d + 1) * TILE]

    def distances(h, t):
        here = None
        for d in range(span + 1):
            block = pltpu.roll(error(h, t, d), 1, 1, stride=1, stride_axis=0)
            if d > 0:
                gc_ref[h, t * TILE : (t + 1) * TILE, (d - 1) * TILE : d * TILE] = jnp.where(over, block, here)
            here = block

    def end_queries(h):
        part = slice(h * HEAD_DIM, (h + 1) * HEAD_DIM)
        dq_parts[h] = jnp.concatenate(dq_main[h], axis=0) + mm(gc_ref[h], pk_ref[0])
        dpk_ref[0, part, :] = (mm(q_turned[part], gc_ref[h]) * scale).astype(BF)

    def keys(h, j):
        spun = {j - t: skew(error(h, t, j - t).T) for t in range(tiles) if 0 <= j - t <= span}
        low = max(min(spun) - 1, 0)
        high = min(max(spun), span - 1)
        at = slice(j * TILE, (j + 1) * TILE)
        for c in range(low, high + 1):
            gk_ref[h, at, c * TILE : (c + 1) * TILE] = jnp.where(under, spun.get(c + 1, zero), spun.get(c, zero))
        cols = slice(low * TILE, (high + 1) * TILE)
        dk_tiles[h].append(mm(gk_ref[h, at, cols], pq_ref[0, cols]))

    def end_keys(h):
        part = slice(h * HEAD_DIM, (h + 1) * HEAD_DIM)
        for c in range(0, span, 2):
            near = slice(c * TILE, (c + tiles + 2) * TILE)
            cols = slice(c * TILE, (c + 2) * TILE)
            dpq_ref[0, part, cols] = (mm(k_turned[part, near], gk_ref[h, near, cols]) * scale).astype(BF)

    for h in range(2):
        for u in range(tiles // 2):
            errors(h, u)
            distances(h, 2 * u)
            distances(h, 2 * u + 1)
        end_queries(h)
        for j in range(key_tiles):
            keys(h, j)
        end_keys(h)
    dk_parts = [jnp.concatenate(found, axis=0) for found in dk_tiles]
    dq = (jnp.where(qcol, dq_parts[0], dq_parts[1]) * scale).astype(BF)
    for t in range(tiles):
        at = slice(t * TILE, (t + 1) * TILE)
        dq_ref[0, at] = mm(flip, dq[at]).astype(BF)
    kcol = lanes((rows_k, TILE)) < HEAD_DIM
    dk = ((dkt_ref[...].T + jnp.where(kcol, dk_parts[0], dk_parts[1])) * scale).astype(BF)
    dv = dvt_ref[...].astype(BF).T
    for whole, own_ref, halo_ref in ((dk, dk_ref, dkh_ref), (dv, dv_ref, dvh_ref)):
        halo_ref[0, :HALF] = whole[:HALF]
        own_ref[0] = whole[HALF : HALF + rows_q]
        halo_ref[0, HALF:] = whole[HALF + rows_q :]


def attention_backward(q, k, k_halo, v, v_halo, pk, pq, probs, g, ctxf, inv):
    n, rq, width = q.shape
    off = 2 * HALF
    rk = rq + off
    pairs = width // TILE
    wide = off + 2 * TILE
    def col(r):
        return pl.BlockSpec((1, r, TILE), lambda s, p: (s, 0, p))
    def row(r):
        return pl.BlockSpec((1, TILE, r), lambda s, p: (s, p, 0))
    return pl.pallas_call(
        backward_kernel,
        grid=(n, pairs),
        in_specs=[col(rq), col(rq), col(off), col(rq), col(off), col(off), col(off),
                  pl.BlockSpec((1, 2, rq // (2 * TILE), 2 * TILE, wide), lambda s, p: (s, p, 0, 0, 0)),
                  col(rq), col(rq),
                  pl.BlockSpec((1, 2, rq, TILE), lambda s, p: (s, p, 0, 0))],
        out_specs=[col(rq), col(rq), col(off), col(rq), col(off), row(off), row(off)],
        out_shape=[jax.ShapeDtypeStruct((n, rq, width), BF),
                   jax.ShapeDtypeStruct((n, rq, width), BF),
                   jax.ShapeDtypeStruct((n, off, width), BF),
                   jax.ShapeDtypeStruct((n, rq, width), BF),
                   jax.ShapeDtypeStruct((n, off, width), BF),
                   jax.ShapeDtypeStruct((n, width, off), BF),
                   jax.ShapeDtypeStruct((n, width, off), BF)],
        scratch_shapes=[pltpu.VMEM((rk, TILE), BF), pltpu.VMEM((rk, TILE), BF), pltpu.VMEM((rq, TILE), BF), pltpu.VMEM((rq, TILE), BF),
                        pltpu.VMEM((2, rq // (2 * TILE), 2 * TILE, wide), BF),
                        pltpu.VMEM((2, rq, off), BF),
                        pltpu.VMEM((2, rk, off), BF),
                        pltpu.VMEM((TILE, rk), F32), pltpu.VMEM((TILE, rk), F32)],
        compiler_params=pltpu.CompilerParams(dimension_semantics=("arbitrary", "arbitrary"), vmem_limit_bytes=VMEM),
        name="attention_backward",
    )(q, k, k_halo, v, v_halo, pk, pq, probs, g, ctxf, inv)

def gather_rows(left, right):
    return lax.dot_general(left, right, (((0,), (0,)), ((), ())), preferred_element_type=F32)


def finish_kernel(shape, names, *refs):
    groups, blocks, cores, rank = shape
    r = SimpleNamespace(**dict(zip(names, refs)))
    seq, head, core = lax.axis_index("seq"), lax.axis_index("head"), lax.axis_index("batch")
    peers = blocks * groups
    me = seq * groups + head
    partner = (seq, head, 1 - core)
    width = r.table_out.shape[3]

    held = SimpleNamespace()
    for index, name in enumerate(names[:LOADS]):
        setattr(held, name, Loaded(refs[index], refs[len(refs) - LOADS + index], r.load_sems.at[index]))

    def place(p):
        return (p // groups, p % groups, core)

    def remote(src, dst, send, recv, device):
        return pltpu.make_async_remote_copy(
            src_ref=src, dst_ref=dst, send_sem=send, recv_sem=recv, device_id=device, device_id_type=MESH
        )

    def each(count, step):
        lax.fori_loop(1, count, lambda k, c: (step(k), c)[1], 0)

    barrier = pltpu.get_barrier_semaphore()
    pl.semaphore_signal(barrier, inc=1, device_id=partner, device_id_type=MESH)
    each(peers, lambda k: pl.semaphore_signal(barrier, inc=1, device_id=place((me + k) % peers), device_id_type=MESH))

    def inner_grad(gradient, up):
        return (ADAPTER_SCALING * mm(gradient, up[...], NT)).astype(BF)

    halo_buf, halo_recv, halo_sems = r.halo_buf, r.halo_recv, r.halo_sems
    half = HALF // 2

    def halves(array):
        return array.astype(BF).reshape(2, half, width)

    def crossing(side, piece):
        there = place(jnp.maximum(me - 1, 0) if side == 0 else jnp.minimum(me + 1, peers - 1))
        return remote(
            halo_buf.at[side, piece], halo_recv.at[1 - side, piece],
            halo_sems.at[4 * side + 2 * piece], halo_sems.at[4 * side + 2 * piece + 1], there,
        )

    def start_crossing(side, piece):
        @pl.when(me > 0 if side == 0 else me < peers - 1)
        def _():
            crossing(side, piece).start()
    key_halo, value_halo = held.key_halo(), held.value_halo()
    key_hu, value_hu = inner_grad(key_halo, r.key_b), inner_grad(value_halo, r.value_b)
    key_w, value_w = held.key_w(), held.value_w()
    for side in range(2):
        at = slice(side * HALF, (side + 1) * HALF)
        halo_buf[side] = halves(
            mm(key_halo[at], key_w, NT)
            + mm(value_halo[at], value_w, NT)
            + mm(key_hu[at], r.key_a[...])
            + mm(value_hu[at], r.value_a[...])
        )
        if side == 0:
            pl.semaphore_wait(barrier, peers)

        start_crossing(side, 0)

    table_ref, stage_ref, recv_ref, sum_ref = r.table, r.stage, r.recv, r.sum
    core_ref, core_sems = r.core, r.core_sems
    position_q = mm(held.back_hot(), held.query_rel_g(), NT).astype(BF)
    position_k = mm(held.key_hot(), held.key_rel_g(), NT).astype(BF)
    query_pg, key_pg = inner_grad(position_q, r.query_b), inner_grad(position_k, r.key_b)
    query_w = held.query_w()
    table = (
        mm(position_q, query_w, NT)
        + mm(position_k, key_w, NT)
        + mm(query_pg, r.query_a[...])
        + mm(key_pg, r.key_a[...])
    ).astype(BF)
    for group in range(groups):
        for block in range(blocks):
            for side in range(cores):
                start = ((group * blocks + block) * cores + side) * rank
                table_ref[side, block * groups + group] = table[start : start + rank]
    swap = remote(table_ref.at[1 - core], core_ref, core_sems.at[0], core_sems.at[1], partner)
    swap.start()
    r.ids_out[core] = r.own_id[...]
    tell = remote(r.own_id, r.ids_out.at[core], core_sems.at[2], core_sems.at[3], partner)
    tell.start()

    x, x_before, x_after, low = held.x(), held.x_before(), held.x_after(), held.low()
    query_g, key_g, value_g = held.query_g(), held.key_g(), held.value_g()
    query_gu, key_gu, value_gu = inner_grad(query_g, r.query_b), inner_grad(key_g, r.key_b), inner_grad(value_g, r.value_b)
    def of_halo(inner):
        return gather_rows(inner[:HALF], x_before) + gather_rows(inner[HALF:], x_after)

    pieces = [
        gather_rows(query_gu, x) + gather_rows(query_pg, low),
        gather_rows(key_gu, x) + of_halo(key_hu) + gather_rows(key_pg, low),
        gather_rows(value_gu, x) + of_halo(value_hu),
        r.out_ga[...],
        ADAPTER_SCALING * (gather_rows(r.query_u[...], query_g) + gather_rows(r.query_pu[...], position_q)),
        ADAPTER_SCALING
        * (
            gather_rows(r.key_u[...], key_g)
            + gather_rows(r.key_uh[...], key_halo)
            + gather_rows(r.key_pu[...], position_k)
        ),
        ADAPTER_SCALING * (gather_rows(r.value_u[...], value_g) + gather_rows(r.value_uh[...], value_halo)),
        r.out_gb[...],
    ]
    part = len(pieces) * width // peers
    per = width // part
    rest = r.ff.shape[1] // peers
    for index, piece in enumerate(pieces):
        for half in range(per):
            stage_ref[index * per + half, :, width : width + part] = piece[:, half * part : (half + 1) * part].astype(BF)
    for peer in range(peers):
        stage_ref[peer, :, width + part :] = r.ff[:, peer * rest : (peer + 1) * rest].astype(BF)

    send_sems, recv_sems = r.send_sems, r.recv_sems
    swap.wait()

    def to_peer(p):
        return remote(stage_ref.at[p], recv_ref.at[me], send_sems.at[p], recv_sems.at[me], place(p))

    def send(k):
        p = (me + k) % peers
        stage_ref[p, :, :width] = (table_ref[core, p].astype(F32) + core_ref[p].astype(F32)).astype(BF)
        to_peer(p).start()

    each(peers, send)
    start_crossing(0, 1)
    start_crossing(1, 1)
    sum_ref[:, :width] = table_ref[core, me].astype(F32) + core_ref[me].astype(F32)
    sum_ref[:, width:] = stage_ref[me, :, width:].astype(F32)

    grad_ref = r.grad_out
    grad_ref[...] = (
        held.grad_one()
        + mm(query_g, query_w, NT)
        + mm(key_g, key_w, NT)
        + mm(value_g, value_w, NT)
        + mm(query_gu, r.query_a[...])
        + mm(key_gu, r.key_a[...])
        + mm(value_gu, r.value_a[...])
    )

    def take(k):
        p = (me + peers - k) % peers
        remote(stage_ref.at[p], recv_ref.at[p], send_sems.at[p], recv_sems.at[p], place(p)).wait_recv()
        sum_ref[...] += recv_ref[p].astype(F32)

    each(peers, take)
    mine_t, mine_l, table_out, late_out = r.mine_t, r.mine_l, r.table_out, r.late_out
    mine_t[...] = sum_ref[:, :width].astype(BF)
    mine_l[...] = sum_ref[:, width:].astype(BF)
    late_out[core, me] = mine_l[...]
    table_out[seq, core] = mine_t[...]

    def give_l(p):
        return remote(mine_l, late_out.at[core, me], r.spread_l.at[p], r.arrive_l.at[me], place(p))

    def give_t(s):
        return remote(mine_t, table_out.at[seq, core], r.spread_t.at[s], r.arrive_t.at[seq], (s, head, core))

    each(peers, lambda k: give_l((me + k) % peers).start())
    each(blocks, lambda k: give_t((seq + k) % blocks).start())

    def on_l(p):
        return remote(late_out.at[core, p], late_out.at[core, p], r.pass_l.at[p], r.other_l.at[p], partner)

    def on_t(s):
        return remote(table_out.at[s, core], table_out.at[s, core], r.pass_t.at[s], r.other_t.at[s], partner)

    on_l(me).start()
    on_t(seq).start()

    def got_l(k):
        p = (me + peers - k) % peers
        remote(mine_l, late_out.at[core, p], r.spread_l.at[p], r.arrive_l.at[p], place(p)).wait_recv()
        on_l(p).start()

    def got_t(k):
        s = (seq + blocks - k) % blocks
        remote(mine_t, table_out.at[s, core], r.spread_t.at[s], r.arrive_t.at[s], (s, head, core)).wait_recv()
        on_t(s).start()

    each(peers, got_l)
    each(blocks, got_t)

    @pl.when(me > 0)
    def _():
        for piece in range(2):
            crossing(0, piece).wait_send()
            crossing(1, piece).wait_recv()
        grad_ref[...] += halo_recv[0].astype(F32).reshape(HALF, width)

    @pl.when(me < peers - 1)
    def _():
        for piece in range(2):
            crossing(1, piece).wait_send()
            crossing(0, piece).wait_recv()
        grad_ref[...] += halo_recv[1].astype(F32).reshape(HALF, width)

    def end_l(k):
        p = k - 1
        remote(late_out.at[1 - core, p], late_out.at[1 - core, p], r.pass_l.at[p], r.other_l.at[p], partner).wait_recv()
        on_l(p).wait_send()

    def end_t(k):
        s = k - 1
        remote(table_out.at[s, 1 - core], table_out.at[s, 1 - core], r.pass_t.at[s], r.other_t.at[s], partner).wait_recv()
        on_t(s).wait_send()

    tell.wait()
    each(peers + 1, end_l)
    each(blocks + 1, end_t)

    def sent(k):
        p = (me + k) % peers
        to_peer(p).wait_send()
        give_l(p).wait_send()

    each(peers, sent)
    each(blocks, lambda k: give_t((seq + k) % blocks).wait_send())


LOADS = 17


def finish(shape, **arrays):
    groups, blocks, cores, rank = shape
    peers = groups * blocks
    rows, width = arrays[list(arrays)[LOADS - 1]].shape
    share = (8 * width + arrays[list(arrays)[-1]].shape[1]) // peers
    vm = pl.BlockSpec(memory_space=pltpu.VMEM)
    hbm = pl.BlockSpec(memory_space=pltpu.HBM)
    dma = pltpu.SemaphoreType.DMA
    outputs = dict(
        grad_out=jax.ShapeDtypeStruct((rows, width), F32),
        table_out=jax.ShapeDtypeStruct((blocks, cores, rank, width), BF),
        late_out=jax.ShapeDtypeStruct((cores, peers, rank, share), BF),
        ids_out=jax.ShapeDtypeStruct((cores, 8, TILE), F32),
    )
    scratch = dict(
        load_sems=dma((LOADS,)),
        halo_buf=pltpu.VMEM((2, 2, HALF // 2, width), BF),
        halo_recv=pltpu.VMEM((2, 2, HALF // 2, width), BF),
        halo_sems=dma((8,)),
        table=pltpu.VMEM((cores, peers, rank, width), BF),
        core=pltpu.VMEM((peers, rank, width), BF),
        stage=pltpu.VMEM((peers, rank, width + share), BF),
        recv=pltpu.VMEM((peers, rank, width + share), BF),
        sum=pltpu.VMEM((rank, width + share), F32),
        mine_t=pltpu.VMEM((rank, width), BF),
        mine_l=pltpu.VMEM((rank, share), BF),
        core_sems=dma((4,)),
        send_sems=dma((peers,)),
        recv_sems=dma((peers,)),
        spread_l=dma((peers,)),
        arrive_l=dma((peers,)),
        pass_l=dma((peers,)),
        other_l=dma((peers,)),
        spread_t=dma((blocks,)),
        arrive_t=dma((blocks,)),
        pass_t=dma((blocks,)),
        other_t=dma((blocks,)),
    )
    names = (*arrays, *outputs, *scratch)
    kept = [pltpu.VMEM(array.shape, array.dtype) for array in list(arrays.values())[:LOADS]]
    return pl.pallas_call(
        partial(finish_kernel, shape, names),
        in_specs=[hbm] * LOADS + [vm] * (len(arrays) - LOADS),
        out_specs=[vm] * len(outputs),
        out_shape=list(outputs.values()),
        scratch_shapes=list(scratch.values()) + kept,
        compiler_params=pltpu.CompilerParams(
            collective_id=0, has_side_effects=True, vmem_limit_bytes=VMEM
        ),
        name="finish",
    )(*arrays.values())


def middle_kernel(seqs, context_ref, tokens_ref, cotangent_ref, out_w_hbm, up_w_hbm, down_w_hbm,
                  out_a_ref, out_b_ref, up_a_ref, up_b_ref, down_a_ref, down_b_ref, gain_one_ref, gain_two_ref,
                  layer_ref, grad_one_ref, grad_context_ref, out_ga_ref, out_gb_ref, ff_ref,
                  out_w, up_w, down_w, hidden_ref, low_ref, work_ref, act_ref, slope_ref, sems):
    rows, width = tokens_ref.shape
    ff = up_w.shape[1]
    share = rows // seqs
    chunk = 512
    copies = []
    for index, (source, target) in enumerate(((out_w_hbm, out_w), (up_w_hbm, up_w), (down_w_hbm, down_w))):
        copy = pltpu.make_async_copy(source, target, sems.at[index])
        copy.start()
        copies.append(copy)

    def parts(step):
        found = [step(s, slice(s * share, (s + 1) * share)) for s in range(seqs)]
        return found[0] if seqs == 1 else jnp.concatenate(found, axis=0)

    def inner(values, factor_ref, scale=1.0):
        return parts(lambda s, at: (scale * mm(values[at], factor_ref[s], NT)).astype(BF))

    def widened(inner_values, factor_ref, columns=slice(None)):
        return parts(lambda s, at: mm(inner_values[at], factor_ref[s, :, columns]))

    def factor_grad(left, right, s):
        at = slice(s * share, (s + 1) * share)
        return lax.dot_general(left[at], right[at], (((0,), (0,)), ((), ())), preferred_element_type=F32)

    def stats(values):
        centered = values - jnp.mean(values, axis=1, keepdims=True)
        inverse = lax.rsqrt(jnp.mean(centered * centered, axis=1, keepdims=True) + EPSILON)
        return centered * inverse, inverse

    def back(normed, inverse, gain, upstream):
        scaled = upstream * gain
        return inverse * (
            scaled
            - jnp.mean(scaled, axis=1, keepdims=True)
            - normed * jnp.mean(scaled * normed, axis=1, keepdims=True)
        )

    context = context_ref[...]
    inner_out = inner(context, out_a_ref)
    copies[0].wait()
    attended = mm(context, out_w[...]) + ADAPTER_SCALING * widened(inner_out, out_b_ref)
    normed_one, inverse_one = stats(tokens_ref[...] + attended)
    grad_one_ref[...] = normed_one
    hidden = normed_one * gain_one_ref[...]
    hidden_ref[...] = hidden
    low_ref[...] = hidden.astype(BF)
    low = low_ref[...]
    inner_up = inner(low, up_a_ref)
    copies[1].wait()
    for start in range(0, ff, chunk):
        columns = slice(start, start + chunk)
        pre = mm(low, up_w[:, columns]) + ADAPTER_SCALING * widened(inner_up, up_b_ref, columns)
        below = 0.5 + 0.5 * lax.erf(pre * math.sqrt(0.5))
        act_ref[:, columns] = (pre * below).astype(BF)
        density = jnp.exp(pre * pre * -0.5) * (1.0 / math.sqrt(2.0 * math.pi))
        slope_ref[:, columns] = (below + pre * density).astype(BF)
    act = act_ref[...]
    inner_down = inner(act, down_a_ref)
    copies[2].wait()
    branch = mm(act, down_w[...]) + ADAPTER_SCALING * widened(inner_down, down_b_ref)
    normed_two, inverse_two = stats(hidden_ref[...] + branch)
    layer_ref[...] = normed_two * gain_two_ref[...]
    work_ref[...] = back(normed_two, inverse_two, gain_two_ref[...], cotangent_ref[...])
    grad_low = work_ref[...].astype(BF)
    grad_inner = inner(grad_low, down_b_ref, ADAPTER_SCALING)
    for s in range(seqs):
        ff_ref[s, :, width + 2 * ff:] = ADAPTER_SCALING * factor_grad(inner_down, grad_low, s)
        ff_ref[s, :, width + ff:width + 2 * ff] = factor_grad(grad_inner, act, s)
    for start in range(0, ff, chunk):
        columns = slice(start, start + chunk)
        grad_act = mm(grad_low, down_w[columns, :], NT) + widened(grad_inner, down_a_ref, columns)
        slope_ref[:, columns] = (grad_act.astype(BF).astype(F32) * slope_ref[:, columns].astype(F32)).astype(BF)
    grad_pre = slope_ref[...]
    grad_inner = inner(grad_pre, up_b_ref, ADAPTER_SCALING)
    for s in range(seqs):
        ff_ref[s, :, width:width + ff] = ADAPTER_SCALING * factor_grad(inner_up, grad_pre, s)
        ff_ref[s, :, :width] = factor_grad(grad_inner, low, s)
    grad_hidden = mm(grad_pre, up_w[...], NT) + widened(grad_inner, up_a_ref)
    grad_one = back(grad_one_ref[...], inverse_one, gain_one_ref[...], grad_hidden + work_ref[...])
    grad_one_ref[...] = grad_one
    grad_low = grad_one.astype(BF)
    grad_inner = inner(grad_low, out_b_ref, ADAPTER_SCALING)
    for s in range(seqs):
        out_gb_ref[s] = ADAPTER_SCALING * factor_grad(inner_out, grad_low, s)
        out_ga_ref[s] = factor_grad(grad_inner, context, s)
    grad_context_ref[...] = (mm(grad_low, out_w[...], NT) + widened(grad_inner, out_a_ref)).astype(BF)


def middle(context, tokens, cotangent, out_weight, up_weight, down_weight, factors, gain_one, gain_two):
    seqs, share, width = tokens.shape
    rows = seqs * share
    ff = up_weight.shape[1]
    rank = factors[0].shape[1]
    vm = pl.BlockSpec(memory_space=pltpu.VMEM)
    hbm = pl.BlockSpec(memory_space=pltpu.HBM)
    wide = jax.ShapeDtypeStruct((rows, width), F32)
    factor = jax.ShapeDtypeStruct((seqs, rank, width), F32)
    found = pl.pallas_call(
        partial(middle_kernel, seqs),
        in_specs=[vm] * 3 + [hbm] * 3 + [vm] * 8,
        out_specs=[vm] * 6,
        out_shape=[wide, wide, jax.ShapeDtypeStruct((rows, width), BF), factor, factor,
                   jax.ShapeDtypeStruct((seqs, rank, 2 * width + 2 * ff), F32)],
        scratch_shapes=[
            pltpu.VMEM(out_weight.shape, BF), pltpu.VMEM(up_weight.shape, BF), pltpu.VMEM(down_weight.shape, BF),
            pltpu.VMEM((rows, width), F32), pltpu.VMEM((rows, width), BF), pltpu.VMEM((rows, width), F32),
            pltpu.VMEM((rows, ff), BF), pltpu.VMEM((rows, ff), BF), pltpu.SemaphoreType.DMA((3,)),
        ],
        compiler_params=pltpu.CompilerParams(vmem_limit_bytes=VMEM),
        cost_estimate=pl.CostEstimate(flops=36 * rows * width * width, bytes_accessed=2 * 12 * width * width, transcendentals=rows * ff),
        name="middle",
    )(context.reshape(rows, width), tokens.reshape(rows, width), cotangent.reshape(rows, width),
      out_weight, up_weight, down_weight, *factors, gain_one.reshape(1, width), gain_two.reshape(1, width))
    return [array.reshape(seqs, share, width) for array in found[:3]] + list(found[3:])


def shifted(value, axes, steps):
    count = math.prod(lax.axis_size(axis) for axis in axes)
    initial, last = (max(0, -steps), min(count, count - steps))
    return lax.ppermute(value, axes, [(source, source + steps) for source in range(initial, last)])


def bucket_of(offset, buckets, distance_cap):
    middle = buckets // 2
    sign_of = np.sign(offset)
    magnitude = np.where((offset < middle) & (offset > -middle), middle - 1, np.abs(offset))
    log_place = (
        np.ceil(np.log(magnitude / middle) / np.log((distance_cap - 1) / middle) * (middle - 1))
        + middle
    )
    return np.where(np.abs(offset) <= middle, offset, log_place * sign_of).astype(np.int32)


def offset_tables():
    place = np.arange(2 * HALF)

    def hot(distance, sign):
        clipped = np.clip(distance, 1 - HALF, HALF - 1)
        bucket = np.clip(BUCK + sign * bucket_of(clipped, BUCK, SPAN), 0, 2 * BUCK - 1)
        return np.eye(2 * BUCK, dtype=np.float32)[bucket]

    return hot(HALF - place, 1), hot(place - HALF, -1), hot(HALF - 1 - place, -1)


def segment_ids(lengths, positions):
    bounds = jnp.cumsum(lengths, axis=-1, dtype=jnp.int32)
    return jnp.sum(
        (bounds[..., None, :] <= positions[:, None]).astype(jnp.int32), axis=-1, dtype=jnp.int32
    )


def product(pattern, left_side, right_side):
    return jnp.einsum(pattern, left_side, right_side, preferred_element_type=F32)


def norm_stats(values):
    centered = values - jnp.mean(values, axis=-1, keepdims=True)
    inverse = lax.rsqrt(jnp.mean(centered * centered, axis=-1, keepdims=True) + EPSILON)
    return (centered * inverse, inverse)


def norm_back(normed, inverse, scale_gain, upstream):
    scaled = upstream * scale_gain
    return inverse * (
        scaled
        - jnp.mean(scaled, axis=-1, keepdims=True)
        - normed * jnp.mean(scaled * normed, axis=-1, keepdims=True)
    )


def adapter_forward(rows_in, weight, down, up):
    inner = product("sti,sir->str", rows_in, down).astype(BF)
    mapped = product("sti,io->sto", rows_in, weight) + ADAPTER_SCALING * product(
        "str,sro->sto", inner, up
    )
    return (mapped, inner)


def adapter_back(rows_in, inner, weight, down, up, gradient):
    grad_up = ADAPTER_SCALING * product("str,sto->sro", inner, gradient)
    grad_inner = (ADAPTER_SCALING * product("sto,sro->str", gradient, up)).astype(BF)
    grad_down = product("sti,str->sir", rows_in, grad_inner)
    grad_in = product("sto,io->sti", gradient, weight) + product("str,sir->sti", grad_inner, down)
    return (grad_in, grad_down, grad_up)


def body(
    tokens,
    cotangent,
    doc_lengths,
    adapter_ids,
    query_weight,
    key_weight,
    value_weight,
    output_weight,
    up_weight,
    down_weight,
    attention_gain,
    feedforward_gain,
    position_gain,
    position_table,
    attention_down,
    attention_up,
    expand_down,
    expand_up,
    reduce_down,
    reduce_up,
):
    seqs, row_count, width = tokens.shape
    head_groups = lax.axis_size("head")
    head_index = lax.axis_index("head")
    seq_index = lax.axis_index("seq")
    by_rows = seqs == 1 and row_count == HALF

    def turned(array):
        return jnp.swapaxes(array, -1, -2)

    token_low = lax.optimization_barrier(tokens.astype(BF))
    frozen = (query_weight, key_weight, value_weight)

    def columns(matrix):
        if by_rows:
            return matrix
        local = width // head_groups
        return lax.dynamic_slice_in_dim(matrix, head_index * local, local, matrix.ndim - 1)

    if by_rows:
        block_axes = ("seq", "head")
        block_index = seq_index * head_groups + head_index
        query_count = row_count
    else:
        block_axes = ("seq",)
        block_index = seq_index
        query_count = row_count * head_groups
    blocks = math.prod(lax.axis_size(axis) for axis in block_axes)

    first_place = block_index * query_count - HALF
    factors, query_seg, key_bias = prepare(
        adapter_ids,
        doc_lengths,
        jnp.stack([first_place, query_count * blocks]).astype(jnp.int32),
        [turned(attention_down), attention_up, turned(expand_down), expand_up, turned(reduce_down), reduce_up],
        query_count,
    )
    downs, att_up = factors[:4], factors[4:8]
    att_down = [turned(factor) for factor in downs]

    def halo(array):
        before = shifted(array[:, query_count - HALF :], block_axes, 1)
        after = shifted(array[:, :HALF], block_axes, -1)
        return before, after

    hots = [jnp.asarray(hot, BF) for hot in offset_tables()]
    if by_rows:
        before, after = halo(token_low)
        (query, key, value), (query_rel, query_back, key_rel), table_low, inners, position_inners = begin(
            token_low[0],
            position_table,
            position_gain,
            frozen,
            [down[0] for down in downs[:3]],
            [up[0] for up in att_up[:3]],
            hots,
        )
        queries, keys, values, key_rel, query_rel, query_back = (
            array[None] for array in (query, key, value, key_rel, query_rel, query_back)
        )
    else:
        projected = []
        inners = []
        for member in range(3):
            mapped, inner = adapter_forward(
                token_low, frozen[member], att_down[member], att_up[member]
            )
            projected.append(mapped.astype(BF))
            inners.append(inner)
        queries, keys, values = lax.all_to_all(
            jnp.stack(projected), "head", split_axis=3, concat_axis=2, tiled=True
        )
        keys_halo, values_halo = (jnp.concatenate(halo(array), axis=1) for array in (keys, values))
        table_low = (norm_stats(position_table)[0] * position_gain).astype(BF)
        position_inners = []
        tables = []
        for member in range(2):
            inner = product("pi,sir->spr", table_low, att_down[member]).astype(BF)
            mapped = product("pi,io->po", table_low, columns(frozen[member]))[
                None
            ] + ADAPTER_SCALING * product("spr,sro->spo", inner, columns(att_up[member]))
            position_inners.append(inner)
            tables.append(mapped.astype(BF))
        key_rel = product("cp,spo->sco", hots[0], tables[1]).astype(BF)
        query_rel = product("cp,spo->sco", hots[1], tables[0]).astype(BF)
        query_back = product("cp,spo->sco", hots[2], tables[0]).astype(BF)

    query_scores, key_scores = relative_scores(queries, keys, key_rel, query_rel)
    if by_rows:
        sides = (before[0], after[0], *frozen[1:], downs[1][0], downs[2][0], att_up[1][0], att_up[2][0])
    else:
        sides = (keys_halo, values_halo)
    context, probs, context_wide, inverse_total, *made = attention_forward(
        queries, keys, values, query_rel, query_seg, key_bias, query_scores, key_scores, sides
    )
    if by_rows:
        keys_halo, values_halo, *inners_halo = made
    if by_rows:
        context_rows = context
    else:
        context_rows = lax.all_to_all(context, "head", split_axis=1, concat_axis=2, tiled=True)

    layer_output, grad_one, grad_context, grad_out_down, grad_out_up, grad_ff = middle(
        context_rows,
        tokens,
        cotangent,
        output_weight,
        up_weight,
        down_weight,
        (downs[3], att_up[3], *factors[8:]),
        attention_gain,
        feedforward_gain,
    )
    if not by_rows:
        grad_context = lax.all_to_all(grad_context, "head", split_axis=2, concat_axis=1, tiled=True)

    group = ADAPTERS // head_groups
    def spread(array):
        chosen_by = select.reshape(select.shape + (1,) * (array.ndim - 1))
        return jnp.sum(chosen_by * array[:, None], axis=0)

    def unflat(array, widths):
        return jnp.split(array, np.cumsum(widths)[:-1].tolist(), axis=-1)

    ff_width = up_weight.shape[1]
    rank = attention_up.shape[2]
    peers = lax.axis_size("seq") * head_groups
    cores = lax.axis_size("batch")
    table_rows = position_table.shape[0]
    direct = by_rows and cores == 2 and table_rows == peers * cores * rank
    grad_q, grad_k, grad_k_halo, grad_v, grad_v_halo, grad_key_rel, grad_query_rel = attention_backward(
        queries,
        keys,
        keys_halo,
        values,
        values_halo,
        key_rel,
        query_back,
        probs,
        grad_context,
        context_wide,
        inverse_total,
    )

    def joined(total, from_above, from_below):
        if query_count == HALF:
            return total + from_above + from_below
        total = total.at[:, query_count - HALF :].add(from_above)
        return total.at[:, :HALF].add(from_below)

    def fold(total, halo_part):
        from_above = shifted(halo_part[:, :HALF], block_axes, -1).astype(F32)
        from_below = shifted(halo_part[:, HALF:], block_axes, 1).astype(F32)
        return joined(total.astype(F32), from_above, from_below)

    if direct:
        grad_tokens, table_total, late, both_ids = finish(
            (head_groups, peers // head_groups, cores, rank),
            key_halo=grad_k_halo[0],
            value_halo=grad_v_halo[0],
            key_w=key_weight,
            value_w=value_weight,
            back_hot=hots[2].T,
            query_rel_g=grad_query_rel[0],
            key_hot=hots[0].T,
            key_rel_g=grad_key_rel[0],
            query_w=query_weight,
            x=token_low[0],
            x_before=before[0],
            x_after=after[0],
            low=table_low,
            query_g=grad_q[0],
            key_g=grad_k[0],
            value_g=grad_v[0],
            grad_one=grad_one[0],
            query_a=downs[0][0],
            key_a=downs[1][0],
            value_a=downs[2][0],
            query_b=att_up[0][0],
            key_b=att_up[1][0],
            value_b=att_up[2][0],
            query_u=inners[0],
            key_u=inners[1],
            value_u=inners[2],
            key_uh=inners_halo[0],
            value_uh=inners_halo[1],
            query_pu=position_inners[0],
            key_pu=position_inners[1],
            own_id=jnp.broadcast_to(adapter_ids.astype(F32)[:, None], (8, TILE)),
            out_ga=grad_out_down[0],
            out_gb=grad_out_up[0],
            ff=grad_ff[0],
        )
        input_grad = grad_tokens[None]
        table_grad, down_grad, up_grad, *ff_grads = spread_all(
            group,
            head_index.astype(jnp.int32).reshape(1),
            both_ids,
            late,
            table_total,
            position_table,
            position_gain,
            ff_width,
        )
        return (
            layer_output,
            input_grad,
            table_grad,
            turned(down_grad),
            up_grad,
            turned(ff_grads[0]),
            ff_grads[1],
            turned(ff_grads[2]),
            ff_grads[3],
        )
    else:
        ids = lax.all_gather(adapter_ids, "batch", axis=0, tiled=True)
        slots = head_index * group + jnp.arange(group, dtype=jnp.int32)
        select = (ids[:, None] == slots[None, :]).astype(F32)
        down_grads = []
        up_grads = []
        if by_rows:
            input_grad = grad_one
            grad_halo = 0.0
            rows_halo = jnp.concatenate([before, after], axis=1)
            for member, pieces in enumerate(
                (
                    ((token_low, inners[0][None], grad_q),),
                    ((token_low, inners[1][None], grad_k), (rows_halo, inners_halo[0][None], grad_k_halo)),
                    ((token_low, inners[2][None], grad_v), (rows_halo, inners_halo[1][None], grad_v_halo)),
                )
            ):
                found = [
                    adapter_back(rows, inner, frozen[member], att_down[member], att_up[member], gradient)
                    for rows, inner, gradient in pieces
                ]
                input_grad = input_grad + found[0][0]
                if member > 0:
                    grad_halo = grad_halo + found[1][0]
                down_grads.append(sum(turned(one[1]) for one in found))
                up_grads.append(sum(one[2] for one in found))
            input_grad = fold(input_grad, grad_halo.astype(BF))
            position_inners = [inner[None] for inner in position_inners]
        else:
            grad_qkv = jnp.stack(
                [grad_q, fold(grad_k, grad_k_halo).astype(BF), fold(grad_v, grad_v_halo).astype(BF)]
            )
            grad_qkv = lax.all_to_all(grad_qkv, "head", split_axis=2, concat_axis=3, tiled=True)
            input_grad = grad_one
            for member in range(3):
                grad_in, grad_dn, grad_upper = adapter_back(
                    token_low,
                    inners[member],
                    frozen[member],
                    att_down[member],
                    att_up[member],
                    grad_qkv[member],
                )
                input_grad = input_grad + grad_in
                down_grads.append(turned(grad_dn))
                up_grads.append(grad_upper)
        down_grads.append(grad_out_down)
        up_grads.append(grad_out_up)
        position_grads = (
            product("cb,soc->sbo", hots[2], grad_query_rel),
            product("cb,soc->sbo", hots[0], grad_key_rel),
        )
        grad_table_low = jnp.zeros(position_table.shape, F32)
        for member in range(2):
            gradient = position_grads[member].astype(BF)
            up = columns(att_up[member])
            grad_columns = ADAPTER_SCALING * product(
                "spr,spo->sro", position_inners[member], gradient
            )
            grad_inner = (ADAPTER_SCALING * product("spo,sro->spr", gradient, up)).astype(BF)
            grad_table_low = (
                grad_table_low
                + product("spo,io->pi", gradient, columns(frozen[member]))
                + product("spr,sir->pi", grad_inner, att_down[member])
            )
            down_grads[member] = down_grads[member] + product("spr,pi->sri", grad_inner, table_low)
            if not by_rows:
                grad_columns = lax.dynamic_update_slice_in_dim(
                    jnp.zeros_like(up_grads[member]),
                    grad_columns,
                    head_index * (width // head_groups),
                    2,
                )
            up_grads[member] = up_grads[member] + grad_columns
        late = jnp.concatenate(down_grads + up_grads, axis=-1)
        late = lax.all_gather(lax.psum(late, ("seq", "head")), "batch", axis=0, tiled=True)
        early = lax.all_gather(lax.psum(grad_ff, ("seq", "head")), "batch", axis=0, tiled=True)
        table_total = lax.psum(grad_table_low, ("seq", "batch"))
        table_total = lax.psum_scatter(table_total, "head", scatter_dimension=0, tiled=True)
    own_rows = table_rows // head_groups

    def head_rows(array):
        return lax.dynamic_slice_in_dim(array, head_index * own_rows, own_rows, 0)

    table_normed, table_inverse = norm_stats(head_rows(position_table))
    table_grad = norm_back(table_normed, table_inverse, position_gain, table_total)
    early = [spread(part) for part in unflat(early, [width, ff_width, ff_width, width])]
    late = [spread(part) for part in unflat(late, [width] * 8)]
    return (
        layer_output,
        input_grad,
        table_grad,
        jnp.stack([turned(part) for part in late[:4]]),
        jnp.stack(late[4:]),
        turned(early[0]),
        early[1],
        turned(early[2]),
        early[3],
    )


def solution(mesh):
    rows = P("batch", ("seq", "head"), None)
    return jax.shard_map(
        body,
        mesh=mesh,
        in_specs=(rows, rows, P("batch", None), P("batch")) + (P(),) * 16,
        out_specs=(
            rows,
            rows,
            P("head", None),
            P(None, "head", None, None),
            P(None, "head", None, None),
            P("head", None, None),
            P("head", None, None),
            P("head", None, None),
            P("head", None, None),
        ),
        check_vma=False,
    )
```

```python
from functools import partial
import math
from types import SimpleNamespace

import jax
import jax.numpy as jnp
import numpy as np
from jax import lax
from jax.experimental import pallas as pl
from jax.experimental.pallas import tpu as pltpu
from jax.sharding import PartitionSpec as P

HEADS = 16
HEAD_DIM = 64
BUCK = 256
SPAN = 512
ADAPTERS = 8
HALF = 512
DOCS = 8

EPSILON = 1e-07
ADAPTER_SCALING = 2.0
NEGATIVE = -1e30
PRECISE = lax.Precision.HIGHEST
TILE = 128
BF = jnp.bfloat16
F32 = jnp.float32
MESH = pl.DeviceIdType.MESH
VMEM = 63 * 2**20
NN = (((1,), (0,)), ((), ()))
NT = (((1,), (1,)), ((), ()))


def mm(a, b, dims=NN):
    return lax.dot_general(a, b, dims, preferred_element_type=F32)

def lanes(shape=(TILE, TILE)):
    return lax.broadcasted_iota(jnp.int32, shape, 1)

def rows(shape=(TILE, TILE)):
    return lax.broadcasted_iota(jnp.int32, shape, 0)

def skew(tile):
    return pltpu.roll(tile, 0, 1, stride=1, stride_axis=0)

def flip_matrix():
    return jnp.where(lanes() + rows() == TILE - 1, 1.0, 0.0).astype(BF)


class Loaded:
    def __init__(self, source, target, sem, start=True):
        self.target = target
        self.copy = pltpu.make_async_copy(source, target, sem)
        if start:
            self.copy.start()

    def __call__(self):
        if self.copy is not None:
            self.copy.wait()
            self.copy = None
        return self.target[...]


def with_halo(own_ref, halo_ref):
    return jnp.concatenate([halo_ref[0, :HALF], own_ref[0], halo_ref[0, HALF:]], axis=0)


class Stored:
    def __init__(self, target, buffer, sem):
        self.buffer = buffer
        self.copy = pltpu.make_async_copy(buffer, target, sem)

    def put(self, value):
        self.buffer[...] = value
        self.copy.start()

    def wait(self):
        self.copy.wait()


def prepare_kernel(seqs, ids_ref, lengths_ref, base_ref, *refs):
    stacks = [stack.at[member] for stack in refs[:2] for member in range(4)] + list(refs[2:6])
    count = len(stacks)
    refs = refs[6:]
    outs = refs[: count + 2]
    buffers = refs[count + 2 : 2 * count + 2]
    made = refs[2 * count + 2 : 3 * count + 4]
    sems, out_sems = refs[3 * count + 4 :]
    outs = [Stored(target, buffer, out_sems.at[i]) for i, (target, buffer) in enumerate(zip(outs, made))]
    query_seg_ref, key_bias_ref = made[count:]
    copies = []
    for s in range(seqs):
        for index, (stack, buffer) in enumerate(zip(stacks, buffers)):
            copy = pltpu.make_async_copy(stack.at[ids_ref[s]], buffer.at[s], sems.at[s, index])
            copy.start()
            copies.append(copy)
    rows_k = key_bias_ref.shape[1]
    rows_q = query_seg_ref.shape[1]
    place = base_ref[0] + rows((rows_k, TILE))
    slot = lanes((rows_k, TILE)) % HEAD_DIM
    inside = (place >= 0) & (place < base_ref[1])
    for s in range(seqs):
        segment = jnp.zeros((rows_k, TILE), jnp.int32)
        bound = jnp.int32(0)
        for document in range(DOCS):
            bound = bound + lengths_ref[s, document]
            segment += jnp.where(place >= bound, 1, 0)
        segment = jnp.where(inside, segment, DOCS)
        same = slot == segment
        query_seg_ref[s] = jnp.where(same, 1.0, 0.0)[HALF : HALF + rows_q].astype(BF)
        open_slot = (same & (segment < DOCS)) | (slot > DOCS)
        key_bias_ref[s] = jnp.where(open_slot, 0.0, NEGATIVE).astype(BF)
    for out in outs[count:]:
        out.copy.start()
    for copy in copies:
        copy.wait()
    for buffer, out in zip(buffers, outs):
        out.put(buffer[...].astype(BF))
    for out in outs:
        out.wait()


def prepare(adapter_ids, lengths, base, stacks, query_count):
    seqs = adapter_ids.shape[0]
    hbm = pl.BlockSpec(memory_space=pltpu.HBM)
    sm = pl.BlockSpec(memory_space=pltpu.SMEM)
    shapes = [(seqs,) + stack.shape[2:] for stack in stacks[:2] for _ in range(4)]
    shapes += [(seqs,) + stack.shape[1:] for stack in stacks[2:]]
    count = len(shapes)
    columns = [(seqs, query_count, TILE), (seqs, query_count + 2 * HALF, TILE)]
    found = pl.pallas_call(
        partial(prepare_kernel, seqs),
        in_specs=[sm] * 3 + [hbm] * len(stacks),
        out_specs=[hbm] * (count + 2),
        out_shape=[jax.ShapeDtypeStruct(shape, BF) for shape in shapes + columns],
        scratch_shapes=[pltpu.VMEM(shape, F32) for shape in shapes]
        + [pltpu.VMEM(shape, BF) for shape in shapes + columns]
        + [pltpu.SemaphoreType.DMA((seqs, count)), pltpu.SemaphoreType.DMA((count + 2,))],
        compiler_params=pltpu.CompilerParams(vmem_limit_bytes=VMEM),
        cost_estimate=pl.CostEstimate(flops=10**6, bytes_accessed=6 * 10**6, transcendentals=0),
        name="prepare",
    )(adapter_ids, lengths, base, *stacks)
    return found[:count], found[count], found[count + 1]


def adapted(x, weight, inner, up):
    return (mm(x, weight) + ADAPTER_SCALING * mm(inner, up)).astype(BF)


def begin_kernel(x_ref, table_ref, gain_ref, query_a, key_a, value_a, query_b, key_b, value_b,
                 query_w, key_w, value_w, query_hot, back_hot, key_hot,
                 query_out, key_out, value_out, query_rel_out, back_rel_out, key_rel_out, low_out,
                 query_u, key_u, value_u, query_pu, key_pu, *scratch):
    loaded = scratch[:6]
    stored = scratch[6:13]
    load_sems, store_sems = scratch[13:]
    query_w, key_w, value_w, query_hot, back_hot, key_hot = (
        Loaded(source, target, load_sems.at[index])
        for index, (source, target) in enumerate(zip((query_w, key_w, value_w, query_hot, back_hot, key_hot), loaded))
    )
    outs = [
        Stored(target, buffer, store_sems.at[index])
        for index, (target, buffer) in enumerate(
            zip((query_out, key_out, value_out, query_rel_out, back_rel_out, key_rel_out, low_out), stored)
        )
    ]
    x = x_ref[...]
    query_u[...] = mm(x, query_a[...], NT).astype(BF)
    key_u[...] = mm(x, key_a[...], NT).astype(BF)
    value_u[...] = mm(x, value_a[...], NT).astype(BF)
    values = table_ref[...]
    centered = values - jnp.mean(values, axis=1, keepdims=True)
    inverse = lax.rsqrt(jnp.mean(centered * centered, axis=1, keepdims=True) + EPSILON)
    low = (centered * inverse * gain_ref[...]).astype(BF)
    outs[6].put(low)
    query_pu[...] = mm(low, query_a[...], NT).astype(BF)
    key_pu[...] = mm(low, key_a[...], NT).astype(BF)
    outs[0].put(adapted(x, query_w(), query_u[...], query_b[...]))
    position_q = adapted(low, query_w(), query_pu[...], query_b[...])
    outs[1].put(adapted(x, key_w(), key_u[...], key_b[...]))
    position_k = adapted(low, key_w(), key_pu[...], key_b[...])
    outs[2].put(adapted(x, value_w(), value_u[...], value_b[...]))
    outs[3].put(mm(query_hot(), position_q).astype(BF))
    outs[4].put(mm(back_hot(), position_q).astype(BF))
    outs[5].put(mm(key_hot(), position_k).astype(BF))
    for out in outs:
        out.wait()


def begin(x, table, gain, weights, downs, ups, hots):
    rows_x, width = x.shape
    rank = ups[0].shape[0]
    places = table.shape[0]
    spans = hots[0].shape[0]
    vm = pl.BlockSpec(memory_space=pltpu.VMEM)
    hbm = pl.BlockSpec(memory_space=pltpu.HBM)
    large = [(rows_x, width)] * 3 + [(spans, width)] * 3 + [(places, width)]
    inner = jax.ShapeDtypeStruct((rows_x, rank), BF)
    position_inner = jax.ShapeDtypeStruct((places, rank), BF)
    sources = (*weights, hots[1], hots[2], hots[0])
    found = pl.pallas_call(
        begin_kernel,
        in_specs=[vm] * 9 + [hbm] * 6,
        out_specs=[hbm] * 7 + [vm] * 5,
        out_shape=[jax.ShapeDtypeStruct(shape, BF) for shape in large] + [inner] * 3 + [position_inner] * 2,
        scratch_shapes=[pltpu.VMEM(source.shape, BF) for source in sources]
        + [pltpu.VMEM(shape, BF) for shape in large]
        + [pltpu.SemaphoreType.DMA((6,)), pltpu.SemaphoreType.DMA((7,))],
        compiler_params=pltpu.CompilerParams(vmem_limit_bytes=VMEM),
        cost_estimate=pl.CostEstimate(
            flops=6 * rows_x * width * width + 10 * places * width * width,
            bytes_accessed=24 * places * width + 6 * width * width,
            transcendentals=0,
        ),
        name="begin",
    )(x, table, gain.reshape(1, width), *downs, *ups, *sources)
    return found[:3], found[3:6], found[6], found[7:10], found[10:]


def relative_kernel(q_ref, k_ref, pk_ref, pq_ref, qs_ref, ks_ref):
    tiles = HALF // TILE
    span = 2 * tiles
    below = lanes() + rows() < TILE
    column = lanes((HALF, TILE)) < HEAD_DIM
    for h in range(2):
        own = column if h == 0 else ~column
        km = jnp.where(own, k_ref[0], jnp.zeros_like(k_ref[0]))
        qm = jnp.where(own, q_ref[0], jnp.zeros_like(q_ref[0]))
        for d in range(1, span):
            pairs = [(t, d + t - tiles) for t in range(tiles) if 0 <= d + t - tiles < tiles]
            first, last = pairs[0][1], pairs[-1][1]
            key_rel = mm(
                km[first * TILE : (last + 1) * TILE], pq_ref[0, (span - 1 - d) * TILE : (span + 1 - d) * TILE, :], NT
            ).astype(BF)
            for t, j in pairs:
                part = key_rel[(j - first) * TILE : (j - first + 1) * TILE]
                ks_ref[0, h, t, :, j * TILE : (j + 1) * TILE] = skew(
                    jnp.where(below, part[:, TILE:], part[:, :TILE])
                ).T
        query_rel = mm(qm, pk_ref[0], NT).astype(BF)
        for t in range(tiles):
            part = query_rel[t * TILE : (t + 1) * TILE]
            for d in range(span + 1):
                here = part[:, min(d, span - 1) * TILE : (min(d, span - 1) + 1) * TILE]
                if 0 < d < span:
                    here = jnp.where(below, here, part[:, (d - 1) * TILE : d * TILE])
                qs_ref[0, h, t, :, d * TILE : (d + 1) * TILE] = skew(here)


def relative_scores(q, k, pk, pq):
    n, rq, width = q.shape
    pairs = width // TILE
    off = 2 * HALF
    tiles = rq // TILE
    return pl.pallas_call(
        relative_kernel,
        grid=(n, pairs),
        in_specs=[column_spec(rq), column_spec(rq), column_spec(off), column_spec(off)],
        out_specs=[head_spec(tiles, TILE, off + TILE), head_spec(tiles, TILE, HALF)],
        out_shape=[jax.ShapeDtypeStruct((n, 2 * pairs, tiles, TILE, off + TILE), BF),
                   jax.ShapeDtypeStruct((n, 2 * pairs, tiles, TILE, HALF), BF)],
        compiler_params=pltpu.CompilerParams(dimension_semantics=("arbitrary", "arbitrary"), vmem_limit_bytes=VMEM),
        cost_estimate=pl.CostEstimate(
            flops=16 * n * rq * off * width, bytes_accessed=60 * 10**6, transcendentals=0
        ),
        name="relative_scores",
    )(q, k, pk, pq)


def column_spec(r):
    return pl.BlockSpec((1, r, TILE), lambda s, p: (s, 0, p))


def head_spec(*shape):
    return pl.BlockSpec((1, 2) + shape, lambda s, p: (s, p) + (0,) * len(shape))


def forward_kernel(mapped, q_ref, k_ref, v_ref, pq_ref, qhot_ref, kbias_ref, qs_ref, ko_ref, *refs):
    if mapped:
        kh_ref, vh_ref, ctx_ref, p_ref, ctxf_ref, inv_ref, kz_ref, vz_ref, ks_ref, s_ref = refs
    else:
        before, after, key_w, value_w, key_a, value_a, key_b, value_b = refs[:8]
        ctx_ref, p_ref, ctxf_ref, inv_ref, kh_ref, vh_ref, key_u, value_u, kz_ref, vz_ref, ks_ref, s_ref = refs[8:]

        @pl.when(pl.program_id(1) == 0)
        def _():
            for side, x in ((0, before), (1, after)):
                at = slice(side * HALF, (side + 1) * HALF)
                key_u[at] = mm(x[...], key_a[...], NT).astype(BF)
                value_u[at] = mm(x[...], value_a[...], NT).astype(BF)

        weights = jnp.concatenate([key_w[...], value_w[...]], axis=1)
        nothing = jnp.zeros_like(key_b[...])
        ups = jnp.concatenate(
            [jnp.concatenate([key_b[...], nothing], axis=1), jnp.concatenate([nothing, value_b[...]], axis=1)], axis=0
        )
        for side, x in ((0, before), (1, after)):
            at = slice(side * HALF, (side + 1) * HALF)
            inner = jnp.concatenate([key_u[at], value_u[at]], axis=1)
            both = adapted(x[...], weights, inner, ups)
            kh_ref[0, at] = both[:, :TILE]
            vh_ref[0, at] = both[:, TILE:]
    tiles = HALF // TILE
    span = 2 * tiles
    width = (span + 1) * TILE
    flip = flip_matrix()
    factor = math.log2(math.e) / math.sqrt(3 * HEAD_DIM)
    k = with_halo(k_ref, kh_ref)
    v = with_halo(v_ref, vh_ref)
    kb = kbias_ref[0]
    kcol = lanes(k.shape) < HEAD_DIM
    hcol = lanes(kh_ref.shape[1:]) < HEAD_DIM
    below = lanes() + rows() < TILE
    place = lanes() + rows()
    tcol = lanes() < HEAD_DIM
    for h in range(2):
        own = kcol if h == 0 else ~kcol
        kz_ref[h] = jnp.where(own, k, kb)
        vz_ref[h] = jnp.where(own, v, jnp.ones_like(v))
        km = jnp.where(hcol if h == 0 else ~hcol, kh_ref[0], jnp.zeros_like(kh_ref[0]))
        for d in range(span + 1):
            pairs = [(t, d + t if d + t < tiles else d + t - tiles) for t in range(tiles) if not tiles <= d + t < 2 * tiles]
            if not pairs:
                continue
            low = max(span - 1 - d, 0) * TILE
            high = min(span + 1 - d, span) * TILE
            first, last = pairs[0][1], pairs[-1][1]
            key_rel = mm(km[first * TILE : (last + 1) * TILE], pq_ref[0, low:high, :], NT).astype(BF)
            for t, j in pairs:
                part = key_rel[(j - first) * TILE : (j - first + 1) * TILE]
                if 0 < d < span:
                    part = jnp.where(below, part[:, TILE:], part[:, :TILE])
                w = d if d < tiles else d - tiles
                ks_ref[h, t, :, w * TILE : (w + 1) * TILE] = skew(part).T

    flips = jnp.concatenate([flip, flip], axis=1)

    def scores(t):
        at = slice(t * TILE, (t + 1) * TILE)
        window = slice(t * TILE, t * TILE + width)
        q = q_ref[0, at, :]
        hot = qhot_ref[0, at, :]
        edge = (tiles - t) * TILE
        for h in range(2):
            q_side = mm(flip, jnp.where(tcol if h == 0 else ~tcol, q, hot)).astype(BF)
            key_side = jnp.concatenate([ks_ref[h, t, :, :edge], ko_ref[0, h, t], ks_ref[h, t, :, edge:]], axis=1)
            relative = jnp.concatenate([qs_ref[0, h, t], key_side], axis=0)
            s_ref[2 * (t % 2) + h] = mm(q_side, kz_ref[h, window, :], NT) + mm(flips, relative)

    scores(0)
    for t in range(tiles):
        if t + 1 < tiles:
            scores(t + 1)
        at = slice(t * TILE, (t + 1) * TILE)
        window = slice(t * TILE, t * TILE + width)
        outs = []
        for h in range(2):
            own = tcol if h == 0 else ~tcol
            first = s_ref[2 * (t % 2) + h, :, :TILE]
            s_ref[2 * (t % 2) + h, :, :TILE] = jnp.where(place > TILE - 1, first, NEGATIVE)
            last = s_ref[2 * (t % 2) + h, :, span * TILE :]
            s_ref[2 * (t % 2) + h, :, span * TILE :] = jnp.where(place < TILE - 1, last, NEGATIVE)
            middle = s_ref[2 * (t % 2) + h, :, tiles * TILE : (tiles + 1) * TILE]
            s_ref[2 * (t % 2) + h, :, tiles * TILE : (tiles + 1) * TILE] = jnp.where(
                (place == TILE - 1) & (middle < 0.1 * NEGATIVE), 0.0, middle
            )
            top = s_ref[2 * (t % 2) + h, :, :TILE]
            for d in range(1, span + 1):
                top = jnp.maximum(top, s_ref[2 * (t % 2) + h, :, d * TILE : (d + 1) * TILE])
            peak = jnp.max(top, axis=1, keepdims=True)
            prob = jnp.exp2((s_ref[2 * (t % 2) + h] - peak) * factor).astype(BF)
            a = t % 2
            row_at = slice(a * TILE, (a + 1) * TILE)
            p_ref[0, h, t // 2, row_at, a * TILE : a * TILE + width] = prob
            p_ref[0, h, t // 2, row_at, (1 - a) * width : (1 - a) * width + TILE] = jnp.zeros((TILE, TILE), BF)
            total = mm(prob, vz_ref[h, window, :])
            inv = 1.0 / jnp.where(own, pltpu.roll(total, HEAD_DIM, 1), total)
            inv_ref[0, h, at, :] = inv
            outs.append(total * inv)
        ctx = jnp.where(tcol, outs[0], outs[1])
        ctxf_ref[0, at, :] = ctx
        ctx_ref[0, at, :] = mm(flip, ctx.astype(BF)).astype(BF)


def attention_forward(q, k, v, pq, qhot, kbias, query_scores, key_scores, halo):
    n, rq, width = q.shape
    off = 2 * HALF
    rk = rq + off
    pairs = width // TILE
    tiles = rq // TILE

    def whole(r):
        return pl.BlockSpec((1, r, TILE), lambda s, p: (s, 0, 0))

    mapped = len(halo) == 2
    in_specs = [column_spec(rq), column_spec(rq), column_spec(rq), column_spec(off), whole(rq), whole(rk),
                head_spec(tiles, TILE, off + TILE), head_spec(tiles, TILE, HALF)]
    out_specs = [column_spec(rq), head_spec(tiles // 2, 2 * TILE, off + 2 * TILE), column_spec(rq), head_spec(rq, TILE)]
    out_shape = [jax.ShapeDtypeStruct((n, rq, width), BF),
                 jax.ShapeDtypeStruct((n, 2 * pairs, tiles // 2, 2 * TILE, off + 2 * TILE), BF),
                 jax.ShapeDtypeStruct((n, rq, width), F32),
                 jax.ShapeDtypeStruct((n, 2 * pairs, rq, TILE), F32)]
    if mapped:
        in_specs += [column_spec(off)] * 2
    else:
        rank = halo[4].shape[0]

        def once(*shape):
            return pl.BlockSpec(shape, lambda s, p: (0,) * len(shape))

        def columns(r):
            return pl.BlockSpec((r, TILE), lambda s, p: (0, p))

        in_specs += [once(HALF, width)] * 2 + [columns(width)] * 2 + [once(rank, width)] * 2 + [columns(rank)] * 2
        out_specs += [column_spec(off)] * 2 + [once(off, rank)] * 2
        out_shape += [jax.ShapeDtypeStruct((n, off, width), BF)] * 2 + [jax.ShapeDtypeStruct((off, rank), BF)] * 2
    return pl.pallas_call(
        partial(forward_kernel, mapped),
        grid=(n, pairs),
        in_specs=in_specs,
        out_specs=out_specs,
        out_shape=out_shape,
        scratch_shapes=[pltpu.VMEM((2, rk, TILE), BF), pltpu.VMEM((2, rk, TILE), BF),
                        pltpu.VMEM((2, tiles, TILE, HALF + TILE), BF),
                        pltpu.VMEM((4, TILE, off + TILE), F32)],
        compiler_params=pltpu.CompilerParams(dimension_semantics=("arbitrary", "arbitrary"), vmem_limit_bytes=VMEM),
        cost_estimate=pl.CostEstimate(
            flops=32 * n * rq * off * width, bytes_accessed=60 * 10**6, transcendentals=0
        ),
        name="attention_forward",
    )(q, k, v, pq, qhot, kbias, query_scores, key_scores, *halo)


def spread_kernel(group, head_ref, ids_ref, late_ref, ff_ref, table_ref, places_hbm, grad_hbm, gain_ref,
                  table_out, down_out, up_out, expand_down, expand_up, reduce_down, reduce_up, grad_out, places_ref, grad_ref, sems):
    cores, peers, rank, part = late_ref.shape
    grad_in = Loaded(grad_hbm, grad_ref, sems.at[1])
    grad_done = Stored(grad_out, grad_ref, sems.at[2])
    width = table_ref.shape[3]
    ff = expand_up.shape[2]
    rest = ff_ref.shape[3]
    count = places_ref.shape[0]
    fetch = pltpu.make_async_copy(places_hbm.at[pl.ds(pl.multiple_of(head_ref[0] * count, count), count)], places_ref, sems.at[0])
    fetch.start()
    first = head_ref[0] * group
    weights = [
        [jnp.where(ids_ref[s, :1, :1] == (first + a).astype(F32), 1.0, 0.0) for a in range(group)] for s in range(cores)
    ]

    def fill(out, a, source, pieces):
        for column, piece in pieces:
            value = sum(weights[s][a] * source[s, piece[0], :, piece[1]].astype(F32) for s in range(cores))
            out[:, column] = value

    per = width // part
    starts = ((expand_down, 0, width), (expand_up, width, ff), (reduce_down, width + ff, ff), (reduce_up, width + 2 * ff, width))
    for a in range(group):
        for member in range(8):
            out = (down_out if member < 4 else up_out).at[member % 4, a]
            fill(out, a, late_ref, [
                (slice(half * part, (half + 1) * part), (member * per + half, slice(0, part))) for half in range(per)
            ])
        for out, start, count in starts:
            pieces = []
            at = start
            while at < start + count:
                peer, offset = at // rest, at % rest
                length = min(rest - offset, start + count - at)
                pieces.append((slice(at - start, at - start + length), (peer, slice(offset, offset + length))))
                at += length
            fill(out.at[a], a, ff_ref, pieces)
    grad_in()
    grad_done.copy.start()
    fetch.wait()
    values = places_ref[...]
    centered = values - jnp.mean(values, axis=1, keepdims=True)
    inverse = lax.rsqrt(jnp.mean(centered * centered, axis=1, keepdims=True) + EPSILON)
    normed = centered * inverse
    upstream = table_ref[...].reshape(values.shape).astype(F32) * gain_ref[...]
    table_out[...] = inverse * (
        upstream
        - jnp.mean(upstream, axis=1, keepdims=True)
        - normed * jnp.mean(upstream * normed, axis=1, keepdims=True)
    )
    grad_done.wait()


def spread_all(group, head, ids, late, ff_late, table, places, grad, gain, ff):
    rank = late.shape[2]
    width = table.shape[3]
    own = (places.shape[0] * group // ADAPTERS, width)
    vm = pl.BlockSpec(memory_space=pltpu.VMEM)
    sm = pl.BlockSpec(memory_space=pltpu.SMEM)
    hbm = pl.BlockSpec(memory_space=pltpu.HBM)

    def out(*shape):
        return jax.ShapeDtypeStruct(shape, F32)

    return pl.pallas_call(
        partial(spread_kernel, group),
        in_specs=[sm, vm, vm, vm, vm, hbm, hbm, vm],
        out_specs=[vm] * 7 + [hbm],
        out_shape=[out(*own), out(4, group, rank, width), out(4, group, rank, width), out(group, rank, width),
                   out(group, rank, ff), out(group, rank, ff), out(group, rank, width), out(*grad.shape)],
        scratch_shapes=[pltpu.VMEM(own, F32), pltpu.VMEM(grad.shape, F32), pltpu.SemaphoreType.DMA((3,))],
        compiler_params=pltpu.CompilerParams(vmem_limit_bytes=VMEM),
        name="spread_all",
    )(head, ids, late, ff_late, table, places, grad, gain.reshape(1, width))


def backward_kernel(handed, q_ref, k_ref, kh_ref, v_ref, vh_ref, pk_ref, pq_ref, p_ref, g_ref, ctxf_ref, inv_ref, *refs):
    if handed:
        layer_ref, layer_out, *refs = refs
        layer_out[...] = layer_ref[...]
    dq_ref, dk_ref, dkh_ref, dv_ref, dvh_ref, dpk_ref, dpq_ref, kx_ref, vx_ref = refs[:9]
    qr_ref, gr_ref, e_ref, gc_ref, gk_ref, dvt_ref, dkt_ref = refs[9:]
    rows_q = q_ref.shape[1]
    rows_k = kx_ref.shape[0]
    kx_ref[...] = with_halo(k_ref, kh_ref)
    vx_ref[...] = with_halo(v_ref, vh_ref)
    tiles = rows_q // TILE
    key_tiles = rows_k // TILE
    span = 2 * HALF // TILE
    wide = (span + 2) * TILE
    flip = flip_matrix()
    scale = 1.0 / math.sqrt(3 * HEAD_DIM)
    tcol = lanes() < HEAD_DIM
    qcol = lanes((rows_q, TILE)) < HEAD_DIM
    over = lanes() > rows()
    under = lanes() >= rows()

    @pl.when((pl.program_id(0) == 0) & (pl.program_id(1) == 0))
    def _():
        gk_ref[...] = jnp.zeros_like(gk_ref)

    for t in range(tiles):
        at = slice(t * TILE, (t + 1) * TILE)
        qr_ref[at] = mm(flip, q_ref[0, at]).astype(BF)
        gr_ref[at] = mm(flip, g_ref[0, at]).astype(BF)
    q_rev = qr_ref[...]
    g_rev = gr_ref[...]
    q_turned = q_rev.T
    k_turned = kx_ref[...].T
    product = g_rev.astype(F32) * ctxf_ref[0]
    dvt_ref[...] = jnp.zeros_like(dvt_ref)
    dkt_ref[...] = jnp.zeros_like(dkt_ref)
    zero = jnp.zeros((TILE, TILE), BF)
    dq_main = [[], []]
    dq_parts = [None, None]
    dk_tiles = [[], []]

    def of_head(h):
        own = qcol if h == 0 else ~qcol
        inv = inv_ref[0, h]
        delta = jnp.sum(jnp.where(own, product, 0.0), axis=1, keepdims=True) * inv
        g_turned = (g_rev.astype(F32) * inv).astype(BF).T[h * HEAD_DIM : (h + 1) * HEAD_DIM]
        return jnp.where(own, g_rev, jnp.zeros_like(g_rev)), inv, delta, g_turned

    heads = [of_head(h) for h in range(2)]

    def errors(h, u):
        g_masked, inv, delta, g_turned = heads[h]
        part = slice(h * HEAD_DIM, (h + 1) * HEAD_DIM)
        at = slice(u * 2 * TILE, (u + 1) * 2 * TILE)
        window = slice(u * 2 * TILE, u * 2 * TILE + wide)
        prob = p_ref[0, h, u]
        g_probs = mm(g_masked[at], vx_ref[window], NT)
        inv_u = jnp.concatenate([inv[at]] * (span + 2), axis=1)
        delta_u = jnp.concatenate([delta[at]] * (span + 2), axis=1)
        e = (prob.astype(F32) * (g_probs * inv_u - delta_u)).astype(BF)
        e_ref[h, u] = e
        dvt_ref[part, window] += mm(g_turned[:, at], prob)
        dkt_ref[part, window] += mm(q_turned[part, at], e)
        dq_main[h].append(mm(e, kx_ref[window]))

    def error(h, t, d):
        a = t % 2
        return e_ref[h, t // 2, a * TILE : (a + 1) * TILE, (a + d) * TILE : (a + d + 1) * TILE]

    def distances(h, t):
        here = None
        for d in range(span + 1):
            block = pltpu.roll(error(h, t, d), 1, 1, stride=1, stride_axis=0)
            if d > 0:
                gc_ref[h, t * TILE : (t + 1) * TILE, (d - 1) * TILE : d * TILE] = jnp.where(over, block, here)
            here = block

    def end_queries(h):
        part = slice(h * HEAD_DIM, (h + 1) * HEAD_DIM)
        dq_parts[h] = jnp.concatenate(dq_main[h], axis=0) + mm(gc_ref[h], pk_ref[0])
        dpk_ref[0, part, :] = (mm(q_turned[part], gc_ref[h]) * scale).astype(BF)

    def keys(h, j):
        spun = {j - t: skew(error(h, t, j - t).T) for t in range(tiles) if 0 <= j - t <= span}
        low = max(min(spun) - 1, 0)
        high = min(max(spun), span - 1)
        at = slice(j * TILE, (j + 1) * TILE)
        for c in range(low, high + 1):
            gk_ref[h, at, c * TILE : (c + 1) * TILE] = jnp.where(under, spun.get(c + 1, zero), spun.get(c, zero))
        cols = slice(low * TILE, (high + 1) * TILE)
        dk_tiles[h].append(mm(gk_ref[h, at, cols], pq_ref[0, cols]))

    def end_keys(h):
        part = slice(h * HEAD_DIM, (h + 1) * HEAD_DIM)
        for c in range(0, span, 2):
            near = slice(c * TILE, (c + tiles + 2) * TILE)
            cols = slice(c * TILE, (c + 2) * TILE)
            dpq_ref[0, part, cols] = (mm(k_turned[part, near], gk_ref[h, near, cols]) * scale).astype(BF)

    for h in range(2):
        for u in range(tiles // 2):
            errors(h, u)
            distances(h, 2 * u)
            distances(h, 2 * u + 1)
        end_queries(h)
        for j in range(key_tiles):
            keys(h, j)
        end_keys(h)
    dk_parts = [jnp.concatenate(found, axis=0) for found in dk_tiles]
    dq = (jnp.where(qcol, dq_parts[0], dq_parts[1]) * scale).astype(BF)
    for t in range(tiles):
        at = slice(t * TILE, (t + 1) * TILE)
        dq_ref[0, at] = mm(flip, dq[at]).astype(BF)
    kcol = lanes((rows_k, TILE)) < HEAD_DIM
    dk = ((dkt_ref[...].T + jnp.where(kcol, dk_parts[0], dk_parts[1])) * scale).astype(BF)
    dv = dvt_ref[...].astype(BF).T
    for whole, own_ref, halo_ref in ((dk, dk_ref, dkh_ref), (dv, dv_ref, dvh_ref)):
        halo_ref[0, :HALF] = whole[:HALF]
        own_ref[0] = whole[HALF : HALF + rows_q]
        halo_ref[0, HALF:] = whole[HALF + rows_q :]


def attention_backward(q, k, k_halo, v, v_halo, pk, pq, probs, g, ctxf, inv, *layer):
    n, rq, width = q.shape
    off = 2 * HALF
    rk = rq + off
    pairs = width // TILE
    wide = off + 2 * TILE
    def col(r):
        return pl.BlockSpec((1, r, TILE), lambda s, p: (s, 0, p))
    def row(r):
        return pl.BlockSpec((1, TILE, r), lambda s, p: (s, p, 0))
    return pl.pallas_call(
        partial(backward_kernel, len(layer) > 0),
        grid=(n, pairs),
        in_specs=[col(rq), col(rq), col(off), col(rq), col(off), col(off), col(off),
                  pl.BlockSpec((1, 2, rq // (2 * TILE), 2 * TILE, wide), lambda s, p: (s, p, 0, 0, 0)),
                  col(rq), col(rq),
                  pl.BlockSpec((1, 2, rq, TILE), lambda s, p: (s, p, 0, 0))] + [col(rq)] * len(layer),
        out_specs=[col(rq)] * len(layer) + [col(rq), col(rq), col(off), col(rq), col(off), row(off), row(off)],
        out_shape=[jax.ShapeDtypeStruct(array.shape, array.dtype) for array in layer]
        + [jax.ShapeDtypeStruct((n, rq, width), BF),
                   jax.ShapeDtypeStruct((n, rq, width), BF),
                   jax.ShapeDtypeStruct((n, off, width), BF),
                   jax.ShapeDtypeStruct((n, rq, width), BF),
                   jax.ShapeDtypeStruct((n, off, width), BF),
                   jax.ShapeDtypeStruct((n, width, off), BF),
                   jax.ShapeDtypeStruct((n, width, off), BF)],
        scratch_shapes=[pltpu.VMEM((rk, TILE), BF), pltpu.VMEM((rk, TILE), BF), pltpu.VMEM((rq, TILE), BF), pltpu.VMEM((rq, TILE), BF),
                        pltpu.VMEM((2, rq // (2 * TILE), 2 * TILE, wide), BF),
                        pltpu.VMEM((2, rq, off), BF),
                        pltpu.VMEM((2, rk, off), BF),
                        pltpu.VMEM((TILE, rk), F32), pltpu.VMEM((TILE, rk), F32)],
        compiler_params=pltpu.CompilerParams(dimension_semantics=("arbitrary", "arbitrary"), vmem_limit_bytes=VMEM),
        name="attention_backward",
    )(q, k, k_halo, v, v_halo, pk, pq, probs, g, ctxf, inv, *layer)


def gather_rows(left, right):
    return lax.dot_general(left, right, (((0,), (0,)), ((), ())), preferred_element_type=F32)


def whereabouts(shape):
    groups, blocks = shape[:2]
    seq, head, core = lax.axis_index("seq"), lax.axis_index("head"), lax.axis_index("batch")
    return blocks * groups, seq * groups + head, lambda p: (p // groups, p % groups, core), (seq, head, core)


def signal(barrier, device):
    pl.semaphore_signal(barrier, inc=1, device_id=device, device_id_type=MESH)


def remote(source, target, send_sem, recv_sem, device):
    return pltpu.make_async_remote_copy(
        src_ref=source, dst_ref=target, send_sem=send_sem, recv_sem=recv_sem, device_id=device, device_id_type=MESH
    )


def each(first, end, step):
    lax.fori_loop(first, end, lambda k, carry: (step(k), carry)[1], 0)


def finish_kernel(shape, names, *refs):
    groups, blocks, cores, rank = shape
    r = SimpleNamespace(**dict(zip(names, refs)))
    peers, me, place, (seq, head, core) = whereabouts(shape)
    partner = (seq, head, 1 - core)
    width = r.table_out.shape[3]

    held = SimpleNamespace()
    for index, name in enumerate(names[:LOADS]):
        target = refs[len(refs) - LOADS + index]
        setattr(held, name, Loaded(refs[index], target, r.load_sems.at[index], start=index < FIRST_LOADS))

    barrier = pltpu.get_barrier_semaphore()
    signal(barrier, partner)
    each(1, peers, lambda k: signal(barrier, place((me + k) % peers)))

    def inner_grad(gradient, up):
        return (ADAPTER_SCALING * mm(gradient, up[...], NT)).astype(BF)

    halo_buf, halo_recv, halo_sems = r.halo_buf, r.halo_recv, r.halo_sems
    half = HALF // 2

    def crossing(side, piece):
        there = place(jnp.maximum(me - 1, 0) if side == 0 else jnp.minimum(me + 1, peers - 1))
        return remote(
            halo_buf.at[side, piece], halo_recv.at[1 - side, piece],
            halo_sems.at[4 * side + 2 * piece], halo_sems.at[4 * side + 2 * piece + 1], there,
        )

    def start_crossing(side, piece):
        @pl.when(me > 0 if side == 0 else me < peers - 1)
        def _():
            crossing(side, piece).start()
    key_halo, value_halo = held.key_halo(), held.value_halo()
    key_hu, value_hu = inner_grad(key_halo, r.key_b), inner_grad(value_halo, r.value_b)
    key_w, value_w = held.key_w(), held.value_w()
    for name in names[FIRST_LOADS:LOADS]:
        getattr(held, name).copy.start()

    def map_piece(piece):
        for side in range(2):
            start = side * HALF + piece * half
            at = slice(start, start + half)
            halo_buf[side, piece] = (
                mm(key_halo[at], key_w, NT)
                + mm(value_halo[at], value_w, NT)
                + mm(key_hu[at], r.key_a[...])
                + mm(value_hu[at], r.value_a[...])
            ).astype(BF)
            if piece == 0 and side == 0:
                pl.semaphore_wait(barrier, peers)
            start_crossing(side, piece)

    map_piece(0)

    def give_f(p):
        return remote(r.ff, r.ff_out.at[core, me], r.spread_f.at[p], r.arrive_f.at[me], place(p))

    def on_f(p):
        return remote(r.ff_out.at[core, p], r.ff_out.at[core, p], r.pass_f.at[p], r.other_f.at[p], partner)

    def got_f(k):
        p = (me + peers - k) % peers
        remote(r.ff, r.ff_out.at[core, p], r.spread_f.at[p], r.arrive_f.at[p], place(p)).wait_recv()
        on_f(p).start()

    def end_f(k):
        p = k - 1
        remote(r.ff_out.at[1 - core, p], r.ff_out.at[1 - core, p], r.pass_f.at[p], r.other_f.at[p], partner).wait_recv()
        on_f(p).wait_send()

    r.ff_out[core, me] = r.ff[...]
    each(1, peers, lambda k: give_f((me + k) % peers).start())
    on_f(me).start()

    table_ref, stage_ref, recv_ref, sum_ref = r.table, r.stage, r.recv, r.sum
    core_ref, core_sems = r.core, r.core_sems
    position_q = mm(held.back_hot(), held.query_rel_g(), NT).astype(BF)
    position_k = mm(held.key_hot(), held.key_rel_g(), NT).astype(BF)
    query_pg, key_pg = inner_grad(position_q, r.query_b), inner_grad(position_k, r.key_b)
    query_w = held.query_w()
    table = (
        mm(position_q, query_w, NT)
        + mm(position_k, key_w, NT)
        + mm(query_pg, r.query_a[...])
        + mm(key_pg, r.key_a[...])
    ).astype(BF)
    for group in range(groups):
        for block in range(blocks):
            for side in range(cores):
                start = ((group * blocks + block) * cores + side) * rank
                table_ref[side, block * groups + group] = table[start : start + rank]
    swap = remote(table_ref.at[1 - core], core_ref, core_sems.at[0], core_sems.at[1], partner)
    swap.start()
    r.ids_out[core] = r.own_id[...]
    tell = remote(r.own_id, r.ids_out.at[core], core_sems.at[2], core_sems.at[3], partner)
    tell.start()

    x, x_before, x_after, low = held.x(), held.x_before(), held.x_after(), held.low()
    query_g, key_g, value_g = held.query_g(), held.key_g(), held.value_g()
    query_gu, key_gu, value_gu = inner_grad(query_g, r.query_b), inner_grad(key_g, r.key_b), inner_grad(value_g, r.value_b)
    def of_halo(inner):
        return gather_rows(inner[:HALF], x_before) + gather_rows(inner[HALF:], x_after)

    pieces = [
        gather_rows(query_gu, x) + gather_rows(query_pg, low),
        gather_rows(key_gu, x) + of_halo(key_hu) + gather_rows(key_pg, low),
        gather_rows(value_gu, x) + of_halo(value_hu),
        r.out_ga[...],
        ADAPTER_SCALING * (gather_rows(r.query_u[...], query_g) + gather_rows(r.query_pu[...], position_q)),
        ADAPTER_SCALING
        * (
            gather_rows(r.key_u[...], key_g)
            + gather_rows(r.key_uh[...], key_halo)
            + gather_rows(r.key_pu[...], position_k)
        ),
        ADAPTER_SCALING * (gather_rows(r.value_u[...], value_g) + gather_rows(r.value_uh[...], value_halo)),
        r.out_gb[...],
    ]
    part = len(pieces) * width // peers
    per = width // part
    for index, piece in enumerate(pieces):
        for cut in range(per):
            stage_ref[index * per + cut, :, width : width + part] = piece[:, cut * part : (cut + 1) * part].astype(BF)

    send_sems, recv_sems = r.send_sems, r.recv_sems
    swap.wait()

    def to_peer(p):
        return remote(stage_ref.at[p], recv_ref.at[me], send_sems.at[p], recv_sems.at[me], place(p))

    def send(k):
        p = (me + k) % peers
        stage_ref[p, :, :width] = (table_ref[core, p].astype(F32) + core_ref[p].astype(F32)).astype(BF)
        to_peer(p).start()

    each(1, peers, send)
    map_piece(1)
    each(1, peers, got_f)
    sum_ref[:, :width] = table_ref[core, me].astype(F32) + core_ref[me].astype(F32)
    sum_ref[:, width:] = stage_ref[me, :, width:].astype(F32)

    grad_ref = r.grad_out
    grad_ref[...] = (
        held.grad_one()
        + mm(query_g, query_w, NT)
        + mm(key_g, key_w, NT)
        + mm(value_g, value_w, NT)
        + mm(query_gu, r.query_a[...])
        + mm(key_gu, r.key_a[...])
        + mm(value_gu, r.value_a[...])
    )

    def take(k):
        p = (me + peers - k) % peers
        remote(stage_ref.at[p], recv_ref.at[p], send_sems.at[p], recv_sems.at[p], place(p)).wait_recv()
        sum_ref[...] += recv_ref[p].astype(F32)

    each(1, peers, take)
    mine_t, mine_l, table_out, late_out = r.mine_t, r.mine_l, r.table_out, r.late_out
    mine_t[...] = sum_ref[:, :width].astype(BF)
    mine_l[...] = sum_ref[:, width:].astype(BF)
    late_out[core, me] = mine_l[...]
    table_out[seq, core] = mine_t[...]

    def give_l(p):
        return remote(mine_l, late_out.at[core, me], r.spread_l.at[p], r.arrive_l.at[me], place(p))

    def give_t(s):
        return remote(mine_t, table_out.at[seq, core], r.spread_t.at[s], r.arrive_t.at[seq], (s, head, core))

    each(1, peers, lambda k: give_l((me + k) % peers).start())
    each(1, blocks, lambda k: give_t((seq + k) % blocks).start())

    def on_l(p):
        return remote(late_out.at[core, p], late_out.at[core, p], r.pass_l.at[p], r.other_l.at[p], partner)

    def on_t(s):
        return remote(table_out.at[s, core], table_out.at[s, core], r.pass_t.at[s], r.other_t.at[s], partner)

    on_l(me).start()
    on_t(seq).start()

    def got_l(k):
        p = (me + peers - k) % peers
        remote(mine_l, late_out.at[core, p], r.spread_l.at[p], r.arrive_l.at[p], place(p)).wait_recv()
        on_l(p).start()

    def got_t(k):
        s = (seq + blocks - k) % blocks
        remote(mine_t, table_out.at[s, core], r.spread_t.at[s], r.arrive_t.at[s], (s, head, core)).wait_recv()
        on_t(s).start()

    each(1, peers, got_l)
    each(1, blocks, got_t)

    @pl.when(me > 0)
    def _():
        for piece in range(2):
            crossing(0, piece).wait_send()
            crossing(1, piece).wait_recv()
        grad_ref[...] += halo_recv[0].astype(F32).reshape(HALF, width)

    @pl.when(me < peers - 1)
    def _():
        for piece in range(2):
            crossing(1, piece).wait_send()
            crossing(0, piece).wait_recv()
        grad_ref[...] += halo_recv[1].astype(F32).reshape(HALF, width)

    def end_l(k):
        p = k - 1
        remote(late_out.at[1 - core, p], late_out.at[1 - core, p], r.pass_l.at[p], r.other_l.at[p], partner).wait_recv()
        on_l(p).wait_send()

    def end_t(k):
        s = k - 1
        remote(table_out.at[s, 1 - core], table_out.at[s, 1 - core], r.pass_t.at[s], r.other_t.at[s], partner).wait_recv()
        on_t(s).wait_send()

    tell.wait()
    each(1, peers + 1, end_f)
    each(1, peers + 1, end_l)
    each(1, blocks + 1, end_t)

    def sent(k):
        p = (me + k) % peers
        to_peer(p).wait_send()
        give_l(p).wait_send()
        give_f(p).wait_send()

    each(1, peers, sent)
    each(1, blocks, lambda k: give_t((seq + k) % blocks).wait_send())


LOADS = 17
FIRST_LOADS = 4


def finish(shape, **arrays):
    groups, blocks, cores, rank = shape
    peers = groups * blocks
    rows, width = arrays[list(arrays)[LOADS - 1]].shape
    share = 8 * width // peers
    ff = arrays[list(arrays)[-1]]
    vm = pl.BlockSpec(memory_space=pltpu.VMEM)
    hbm = pl.BlockSpec(memory_space=pltpu.HBM)
    dma = pltpu.SemaphoreType.DMA
    outputs = dict(
        grad_out=jax.ShapeDtypeStruct((rows, width), F32),
        table_out=jax.ShapeDtypeStruct((blocks, cores, rank, width), BF),
        late_out=jax.ShapeDtypeStruct((cores, peers, rank, share), BF),
        ids_out=jax.ShapeDtypeStruct((cores, 8, TILE), F32),
        ff_out=jax.ShapeDtypeStruct((cores, peers) + ff.shape, BF),
    )
    scratch = dict(
        load_sems=dma((LOADS,)),
        halo_buf=pltpu.VMEM((2, 2, HALF // 2, width), BF),
        halo_recv=pltpu.VMEM((2, 2, HALF // 2, width), BF),
        halo_sems=dma((8,)),
        table=pltpu.VMEM((cores, peers, rank, width), BF),
        core=pltpu.VMEM((peers, rank, width), BF),
        stage=pltpu.VMEM((peers, rank, width + share), BF),
        recv=pltpu.VMEM((peers, rank, width + share), BF),
        sum=pltpu.VMEM((rank, width + share), F32),
        mine_t=pltpu.VMEM((rank, width), BF),
        mine_l=pltpu.VMEM((rank, share), BF),
        core_sems=dma((4,)),
        send_sems=dma((peers,)),
        recv_sems=dma((peers,)),
        spread_l=dma((peers,)),
        arrive_l=dma((peers,)),
        pass_l=dma((peers,)),
        other_l=dma((peers,)),
        spread_t=dma((blocks,)),
        arrive_t=dma((blocks,)),
        pass_t=dma((blocks,)),
        other_t=dma((blocks,)),
        spread_f=dma((peers,)),
        arrive_f=dma((peers,)),
        pass_f=dma((peers,)),
        other_f=dma((peers,)),
    )
    names = (*arrays, *outputs, *scratch)
    kept = [pltpu.VMEM(array.shape, array.dtype) for array in list(arrays.values())[:LOADS]]
    return pl.pallas_call(
        partial(finish_kernel, shape, names),
        in_specs=[hbm] * LOADS + [vm] * (len(arrays) - LOADS),
        out_specs=[vm] * len(outputs),
        out_shape=list(outputs.values()),
        scratch_shapes=list(scratch.values()) + kept,
        compiler_params=pltpu.CompilerParams(
            collective_id=0, has_side_effects=True, vmem_limit_bytes=VMEM
        ),
        name="finish",
    )(*arrays.values())


def middle_kernel(seqs, shape, context_hbm, tokens_hbm, cotangent_hbm, out_w_hbm, up_w_hbm, down_w_hbm,
                  out_a_ref, out_b_ref, up_a_ref, up_b_ref, down_a_ref, down_b_ref, gain_one_ref, gain_two_ref,
                  layer_hbm, grad_one_hbm, grad_context_ref, out_ga_ref, out_gb_ref, result_ref,
                  out_w, up_w, down_w, hidden_ref, low_ref, work_ref, act_ref, slope_ref,
                  context_ref, tokens_ref, cotangent_ref, layer_ref, grad_one_ref, sems, *refs):
    if shape is None:
        ff_ref = result_ref
    else:
        ff_ref, stage_ref, recv_ref, send_sems, recv_sems = refs
        peers, me, place, _ = whereabouts(shape)
        barrier = pltpu.get_barrier_semaphore()
        each(1, peers, lambda k: signal(barrier, place((me + k) % peers)))

    def to_peer(p):
        return remote(stage_ref.at[p], recv_ref.at[me], send_sems.at[p], recv_sems.at[me], place(p))

    def send(first):
        if shape is None:
            return
        half = peers // 2
        part = stage_ref.shape[2]
        for p in range(first, first + half):
            stage_ref[p] = ff_ref[0, :, p * part : (p + 1) * part].astype(BF)

        def start(k):
            p = first + (me + k) % half

            @pl.when(p != me)
            def _():
                to_peer(p).start()

        each(0, half, start)

    rows, width = tokens_ref.shape
    ff = up_w.shape[1]
    share = rows // seqs
    chunk = 512
    context_in, out_in, tokens_in, up_in, down_in, cotangent_in = (
        Loaded(source, target, sems.at[index])
        for index, (source, target) in enumerate(
            (
                (context_hbm, context_ref),
                (out_w_hbm, out_w),
                (tokens_hbm, tokens_ref),
                (up_w_hbm, up_w),
                (down_w_hbm, down_w),
                (cotangent_hbm, cotangent_ref),
            )
        )
    )
    layer_out = Stored(layer_hbm, layer_ref, sems.at[6])
    grad_one_out = Stored(grad_one_hbm, grad_one_ref, sems.at[7])

    def parts(step):
        found = [step(s, slice(s * share, (s + 1) * share)) for s in range(seqs)]
        return found[0] if seqs == 1 else jnp.concatenate(found, axis=0)

    def inner(values, factor_ref, scale=1.0):
        return parts(lambda s, at: (scale * mm(values[at], factor_ref[s], NT)).astype(BF))

    def widened(inner_values, factor_ref, columns=slice(None)):
        return parts(lambda s, at: mm(inner_values[at], factor_ref[s, :, columns]))

    def factor_grad(left, right, s):
        at = slice(s * share, (s + 1) * share)
        return lax.dot_general(left[at], right[at], (((0,), (0,)), ((), ())), preferred_element_type=F32)

    def stats(values):
        centered = values - jnp.mean(values, axis=1, keepdims=True)
        inverse = lax.rsqrt(jnp.mean(centered * centered, axis=1, keepdims=True) + EPSILON)
        return centered * inverse, inverse

    def back(normed, inverse, gain, upstream):
        scaled = upstream * gain
        return inverse * (
            scaled
            - jnp.mean(scaled, axis=1, keepdims=True)
            - normed * jnp.mean(scaled * normed, axis=1, keepdims=True)
        )

    context = context_in()
    inner_out = inner(context, out_a_ref)
    out_in()
    attended = mm(context, out_w[...]) + ADAPTER_SCALING * widened(inner_out, out_b_ref)
    normed_one, inverse_one = stats(tokens_in() + attended)
    grad_one_ref[...] = normed_one
    hidden = normed_one * gain_one_ref[...]
    hidden_ref[...] = hidden
    low_ref[...] = hidden.astype(BF)
    low = low_ref[...]
    inner_up = inner(low, up_a_ref)
    up_in()
    for start in range(0, ff, chunk):
        columns = slice(start, start + chunk)
        pre = mm(low, up_w[:, columns]) + ADAPTER_SCALING * widened(inner_up, up_b_ref, columns)
        below = 0.5 + 0.5 * lax.erf(pre * math.sqrt(0.5))
        act_ref[:, columns] = (pre * below).astype(BF)
        density = jnp.exp(pre * pre * -0.5) * (1.0 / math.sqrt(2.0 * math.pi))
        slope_ref[:, columns] = (below + pre * density).astype(BF)
    act = act_ref[...]
    inner_down = inner(act, down_a_ref)
    down_in()
    branch = mm(act, down_w[...]) + ADAPTER_SCALING * widened(inner_down, down_b_ref)
    normed_two, inverse_two = stats(hidden_ref[...] + branch)
    layer_out.put(normed_two * gain_two_ref[...])
    work_ref[...] = back(normed_two, inverse_two, gain_two_ref[...], cotangent_in())
    grad_low = work_ref[...].astype(BF)
    grad_inner = inner(grad_low, down_b_ref, ADAPTER_SCALING)
    for s in range(seqs):
        ff_ref[s, :, width + 2 * ff:] = ADAPTER_SCALING * factor_grad(inner_down, grad_low, s)
        ff_ref[s, :, width + ff:width + 2 * ff] = factor_grad(grad_inner, act, s)
    if shape is not None:
        pl.semaphore_wait(barrier, peers - 1)
        send(peers // 2)
    for start in range(0, ff, chunk):
        columns = slice(start, start + chunk)
        grad_act = mm(grad_low, down_w[columns, :], NT) + widened(grad_inner, down_a_ref, columns)
        slope_ref[:, columns] = (grad_act.astype(BF).astype(F32) * slope_ref[:, columns].astype(F32)).astype(BF)
    grad_pre = slope_ref[...]
    grad_inner = inner(grad_pre, up_b_ref, ADAPTER_SCALING)
    for s in range(seqs):
        ff_ref[s, :, width:width + ff] = ADAPTER_SCALING * factor_grad(inner_up, grad_pre, s)
        ff_ref[s, :, :width] = factor_grad(grad_inner, low, s)
    send(0)
    grad_hidden = mm(grad_pre, up_w[...], NT) + widened(grad_inner, up_a_ref)
    grad_one = back(grad_one_ref[...], inverse_one, gain_one_ref[...], grad_hidden + work_ref[...])
    grad_one_out.put(grad_one)
    grad_low = grad_one.astype(BF)
    grad_inner = inner(grad_low, out_b_ref, ADAPTER_SCALING)
    for s in range(seqs):
        out_gb_ref[s] = ADAPTER_SCALING * factor_grad(inner_out, grad_low, s)
        out_ga_ref[s] = factor_grad(grad_inner, context, s)
    grad_context_ref[...] = (mm(grad_low, out_w[...], NT) + widened(grad_inner, out_a_ref)).astype(BF)
    layer_out.wait()
    grad_one_out.wait()
    if shape is not None:
        ff_ref[0, :, : stage_ref.shape[2]] = stage_ref[me].astype(F32)

        def take(k):
            p = (me + peers - k) % peers
            remote(stage_ref.at[p], recv_ref.at[p], send_sems.at[p], recv_sems.at[p], place(p)).wait_recv()
            ff_ref[0, :, : stage_ref.shape[2]] += recv_ref[p].astype(F32)

        each(1, peers, take)
        result_ref[...] = ff_ref[0, :, : stage_ref.shape[2]].astype(BF)
        each(1, peers, lambda k: to_peer((me + k) % peers).wait_send())


def middle(context, tokens, cotangent, out_weight, up_weight, down_weight, factors, gain_one, gain_two, shape=None):
    seqs, share, width = tokens.shape
    rows = seqs * share
    ff = up_weight.shape[1]
    rank = factors[0].shape[1]
    vm = pl.BlockSpec(memory_space=pltpu.VMEM)
    hbm = pl.BlockSpec(memory_space=pltpu.HBM)
    wide = jax.ShapeDtypeStruct((rows, width), F32)
    factor = jax.ShapeDtypeStruct((seqs, rank, width), F32)
    columns = 2 * width + 2 * ff
    result = jax.ShapeDtypeStruct((seqs, rank, columns), F32)
    extra = []
    params = pltpu.CompilerParams(vmem_limit_bytes=VMEM)
    if shape is not None:
        peers = shape[0] * shape[1]
        result = jax.ShapeDtypeStruct((rank, columns // peers), BF)
        extra = [pltpu.VMEM((seqs, rank, columns), F32)] + [pltpu.VMEM((peers, rank, columns // peers), BF)] * 2
        extra += [pltpu.SemaphoreType.DMA((peers,))] * 2
        params = pltpu.CompilerParams(vmem_limit_bytes=VMEM, collective_id=1, has_side_effects=True)
    found = pl.pallas_call(
        partial(middle_kernel, seqs, shape),
        in_specs=[hbm] * 6 + [vm] * 8,
        out_specs=[hbm] * 2 + [vm] * 4,
        out_shape=[wide, wide, jax.ShapeDtypeStruct((rows, width), BF), factor, factor, result],
        scratch_shapes=[
            pltpu.VMEM(out_weight.shape, BF), pltpu.VMEM(up_weight.shape, BF), pltpu.VMEM(down_weight.shape, BF),
            pltpu.VMEM((rows, width), F32), pltpu.VMEM((rows, width), BF), pltpu.VMEM((rows, width), F32),
            pltpu.VMEM((rows, ff), BF), pltpu.VMEM((rows, ff), BF),
            pltpu.VMEM((rows, width), BF), *[pltpu.VMEM((rows, width), F32)] * 4, pltpu.SemaphoreType.DMA((8,)),
        ] + extra,
        compiler_params=params,
        cost_estimate=pl.CostEstimate(flops=36 * rows * width * width, bytes_accessed=24 * width * width, transcendentals=rows * ff),
        name="middle",
    )(context.reshape(rows, width), tokens.reshape(rows, width), cotangent.reshape(rows, width),
      out_weight, up_weight, down_weight, *factors, gain_one.reshape(1, width), gain_two.reshape(1, width))
    return [array.reshape(seqs, share, width) for array in found[:3]] + list(found[3:])


def shifted(value, axes, steps):
    count = math.prod(lax.axis_size(axis) for axis in axes)
    initial, last = (max(0, -steps), min(count, count - steps))
    return lax.ppermute(value, axes, [(source, source + steps) for source in range(initial, last)])


def bucket_of(offset, buckets, distance_cap):
    middle = buckets // 2
    sign_of = np.sign(offset)
    magnitude = np.where((offset < middle) & (offset > -middle), middle - 1, np.abs(offset))
    log_place = (
        np.ceil(np.log(magnitude / middle) / np.log((distance_cap - 1) / middle) * (middle - 1))
        + middle
    )
    return np.where(np.abs(offset) <= middle, offset, log_place * sign_of).astype(np.int32)


def offset_tables():
    place = np.arange(2 * HALF)

    def hot(distance, sign):
        clipped = np.clip(distance, 1 - HALF, HALF - 1)
        bucket = np.clip(BUCK + sign * bucket_of(clipped, BUCK, SPAN), 0, 2 * BUCK - 1)
        return np.eye(2 * BUCK, dtype=np.float32)[bucket]

    return hot(HALF - place, 1), hot(place - HALF, -1), hot(HALF - 1 - place, -1)


def segment_ids(lengths, positions):
    bounds = jnp.cumsum(lengths, axis=-1, dtype=jnp.int32)
    return jnp.sum(
        (bounds[..., None, :] <= positions[:, None]).astype(jnp.int32), axis=-1, dtype=jnp.int32
    )


def product(pattern, left_side, right_side):
    return jnp.einsum(pattern, left_side, right_side, preferred_element_type=F32)


def norm_stats(values):
    centered = values - jnp.mean(values, axis=-1, keepdims=True)
    inverse = lax.rsqrt(jnp.mean(centered * centered, axis=-1, keepdims=True) + EPSILON)
    return (centered * inverse, inverse)


def norm_back(normed, inverse, scale_gain, upstream):
    scaled = upstream * scale_gain
    return inverse * (
        scaled
        - jnp.mean(scaled, axis=-1, keepdims=True)
        - normed * jnp.mean(scaled * normed, axis=-1, keepdims=True)
    )


def adapter_forward(rows_in, weight, down, up):
    inner = product("sti,sir->str", rows_in, down).astype(BF)
    mapped = product("sti,io->sto", rows_in, weight) + ADAPTER_SCALING * product(
        "str,sro->sto", inner, up
    )
    return (mapped, inner)


def adapter_back(rows_in, inner, weight, down, up, gradient):
    grad_up = ADAPTER_SCALING * product("str,sto->sro", inner, gradient)
    grad_inner = (ADAPTER_SCALING * product("sto,sro->str", gradient, up)).astype(BF)
    grad_down = product("sti,str->sir", rows_in, grad_inner)
    grad_in = product("sto,io->sti", gradient, weight) + product("str,sir->sti", grad_inner, down)
    return (grad_in, grad_down, grad_up)


def body(
    tokens,
    cotangent,
    doc_lengths,
    adapter_ids,
    query_weight,
    key_weight,
    value_weight,
    output_weight,
    up_weight,
    down_weight,
    attention_gain,
    feedforward_gain,
    position_gain,
    position_table,
    attention_down,
    attention_up,
    expand_down,
    expand_up,
    reduce_down,
    reduce_up,
):
    seqs, row_count, width = tokens.shape
    head_groups = lax.axis_size("head")
    head_index = lax.axis_index("head")
    seq_index = lax.axis_index("seq")
    by_rows = seqs == 1 and row_count == HALF

    def turned(array):
        return jnp.swapaxes(array, -1, -2)

    token_low = lax.optimization_barrier(tokens.astype(BF))
    frozen = (query_weight, key_weight, value_weight)

    def columns(matrix):
        if by_rows:
            return matrix
        local = width // head_groups
        return lax.dynamic_slice_in_dim(matrix, head_index * local, local, matrix.ndim - 1)

    if by_rows:
        block_axes = ("seq", "head")
        block_index = seq_index * head_groups + head_index
        query_count = row_count
    else:
        block_axes = ("seq",)
        block_index = seq_index
        query_count = row_count * head_groups
    blocks = math.prod(lax.axis_size(axis) for axis in block_axes)

    first_place = block_index * query_count - HALF
    factors, query_seg, key_bias = prepare(
        adapter_ids,
        doc_lengths,
        jnp.stack([first_place, query_count * blocks]).astype(jnp.int32),
        [turned(attention_down), attention_up, turned(expand_down), expand_up, turned(reduce_down), reduce_up],
        query_count,
    )
    downs, att_up = factors[:4], factors[4:8]
    att_down = [turned(factor) for factor in downs]

    def halo(array):
        before = shifted(array[:, query_count - HALF :], block_axes, 1)
        after = shifted(array[:, :HALF], block_axes, -1)
        return before, after

    hots = [jnp.asarray(hot, BF) for hot in offset_tables()]
    if by_rows:
        before, after = halo(token_low)
        (query, key, value), (query_rel, query_back, key_rel), table_low, inners, position_inners = begin(
            token_low[0],
            position_table,
            position_gain,
            frozen,
            [down[0] for down in downs[:3]],
            [up[0] for up in att_up[:3]],
            hots,
        )
        queries, keys, values, key_rel, query_rel, query_back = (
            array[None] for array in (query, key, value, key_rel, query_rel, query_back)
        )
    else:
        projected = []
        inners = []
        for member in range(3):
            mapped, inner = adapter_forward(
                token_low, frozen[member], att_down[member], att_up[member]
            )
            projected.append(mapped.astype(BF))
            inners.append(inner)
        queries, keys, values = lax.all_to_all(
            jnp.stack(projected), "head", split_axis=3, concat_axis=2, tiled=True
        )
        keys_halo, values_halo = (jnp.concatenate(halo(array), axis=1) for array in (keys, values))
        table_low = (norm_stats(position_table)[0] * position_gain).astype(BF)
        position_inners = []
        tables = []
        for member in range(2):
            inner = product("pi,sir->spr", table_low, att_down[member]).astype(BF)
            mapped = product("pi,io->po", table_low, columns(frozen[member]))[
                None
            ] + ADAPTER_SCALING * product("spr,sro->spo", inner, columns(att_up[member]))
            position_inners.append(inner)
            tables.append(mapped.astype(BF))
        key_rel = product("cp,spo->sco", hots[0], tables[1]).astype(BF)
        query_rel = product("cp,spo->sco", hots[1], tables[0]).astype(BF)
        query_back = product("cp,spo->sco", hots[2], tables[0]).astype(BF)

    query_scores, key_scores = relative_scores(queries, keys, key_rel, query_rel)
    if by_rows:
        sides = (before[0], after[0], *frozen[1:], downs[1][0], downs[2][0], att_up[1][0], att_up[2][0])
    else:
        sides = (keys_halo, values_halo)
    context, probs, context_wide, inverse_total, *made = attention_forward(
        queries, keys, values, query_rel, query_seg, key_bias, query_scores, key_scores, sides
    )
    if by_rows:
        keys_halo, values_halo, *inners_halo = made
    if by_rows:
        context_rows = context
    else:
        context_rows = lax.all_to_all(context, "head", split_axis=1, concat_axis=2, tiled=True)

    ff_width = up_weight.shape[1]
    rank = attention_up.shape[2]
    peers = lax.axis_size("seq") * head_groups
    cores = lax.axis_size("batch")
    table_rows = position_table.shape[0]
    direct = by_rows and cores == 2 and table_rows == peers * cores * rank
    shape = (head_groups, peers // head_groups, cores, rank) if direct else None
    layer_output, grad_one, grad_context, grad_out_down, grad_out_up, grad_ff = middle(
        context_rows,
        tokens,
        cotangent,
        output_weight,
        up_weight,
        down_weight,
        (downs[3], att_up[3], *factors[8:]),
        attention_gain,
        feedforward_gain,
        shape,
    )
    if not by_rows:
        grad_context = lax.all_to_all(grad_context, "head", split_axis=2, concat_axis=1, tiled=True)

    group = ADAPTERS // head_groups
    def spread(array):
        chosen_by = select.reshape(select.shape + (1,) * (array.ndim - 1))
        return jnp.sum(chosen_by * array[:, None], axis=0)

    def unflat(array, widths):
        return jnp.split(array, np.cumsum(widths)[:-1].tolist(), axis=-1)

    *handed, grad_q, grad_k, grad_k_halo, grad_v, grad_v_halo, grad_key_rel, grad_query_rel = attention_backward(
        queries,
        keys,
        keys_halo,
        values,
        values_halo,
        key_rel,
        query_back,
        probs,
        grad_context,
        context_wide,
        inverse_total,
        *([layer_output] if direct else []),
    )
    if direct:
        layer_output = handed[0]

    def joined(total, from_above, from_below):
        if query_count == HALF:
            return total + from_above + from_below
        total = total.at[:, query_count - HALF :].add(from_above)
        return total.at[:, :HALF].add(from_below)

    def fold(total, halo_part):
        from_above = shifted(halo_part[:, :HALF], block_axes, -1).astype(F32)
        from_below = shifted(halo_part[:, HALF:], block_axes, 1).astype(F32)
        return joined(total.astype(F32), from_above, from_below)

    if direct:
        grad_tokens, table_total, late, both_ids, ff_total = finish(
            shape,
            key_halo=grad_k_halo[0],
            value_halo=grad_v_halo[0],
            key_w=key_weight,
            value_w=value_weight,
            back_hot=hots[2].T,
            query_rel_g=grad_query_rel[0],
            key_hot=hots[0].T,
            key_rel_g=grad_key_rel[0],
            query_w=query_weight,
            x=token_low[0],
            x_before=before[0],
            x_after=after[0],
            low=table_low,
            query_g=grad_q[0],
            key_g=grad_k[0],
            value_g=grad_v[0],
            grad_one=grad_one[0],
            query_a=downs[0][0],
            key_a=downs[1][0],
            value_a=downs[2][0],
            query_b=att_up[0][0],
            key_b=att_up[1][0],
            value_b=att_up[2][0],
            query_u=inners[0],
            key_u=inners[1],
            value_u=inners[2],
            key_uh=inners_halo[0],
            value_uh=inners_halo[1],
            query_pu=position_inners[0],
            key_pu=position_inners[1],
            own_id=jnp.broadcast_to(adapter_ids.astype(F32)[:, None], (8, TILE)),
            out_ga=grad_out_down[0],
            out_gb=grad_out_up[0],
            ff=grad_ff,
        )
        table_grad, down_grad, up_grad, *ff_grads, input_grad = spread_all(
            group,
            head_index.astype(jnp.int32).reshape(1),
            both_ids,
            late,
            ff_total,
            table_total,
            position_table,
            grad_tokens,
            position_gain,
            ff_width,
        )
        return (
            layer_output,
            input_grad[None],
            table_grad,
            turned(down_grad),
            up_grad,
            turned(ff_grads[0]),
            ff_grads[1],
            turned(ff_grads[2]),
            ff_grads[3],
        )
    else:
        ids = lax.all_gather(adapter_ids, "batch", axis=0, tiled=True)
        slots = head_index * group + jnp.arange(group, dtype=jnp.int32)
        select = (ids[:, None] == slots[None, :]).astype(F32)
        down_grads = []
        up_grads = []
        if by_rows:
            input_grad = grad_one
            grad_halo = 0.0
            rows_halo = jnp.concatenate([before, after], axis=1)
            for member, pieces in enumerate(
                (
                    ((token_low, inners[0][None], grad_q),),
                    ((token_low, inners[1][None], grad_k), (rows_halo, inners_halo[0][None], grad_k_halo)),
                    ((token_low, inners[2][None], grad_v), (rows_halo, inners_halo[1][None], grad_v_halo)),
                )
            ):
                found = [
                    adapter_back(rows, inner, frozen[member], att_down[member], att_up[member], gradient)
                    for rows, inner, gradient in pieces
                ]
                input_grad = input_grad + found[0][0]
                if member > 0:
                    grad_halo = grad_halo + found[1][0]
                down_grads.append(sum(turned(one[1]) for one in found))
                up_grads.append(sum(one[2] for one in found))
            input_grad = fold(input_grad, grad_halo.astype(BF))
            position_inners = [inner[None] for inner in position_inners]
        else:
            grad_qkv = jnp.stack(
                [grad_q, fold(grad_k, grad_k_halo).astype(BF), fold(grad_v, grad_v_halo).astype(BF)]
            )
            grad_qkv = lax.all_to_all(grad_qkv, "head", split_axis=2, concat_axis=3, tiled=True)
            input_grad = grad_one
            for member in range(3):
                grad_in, grad_dn, grad_upper = adapter_back(
                    token_low,
                    inners[member],
                    frozen[member],
                    att_down[member],
                    att_up[member],
                    grad_qkv[member],
                )
                input_grad = input_grad + grad_in
                down_grads.append(turned(grad_dn))
                up_grads.append(grad_upper)
        down_grads.append(grad_out_down)
        up_grads.append(grad_out_up)
        position_grads = (
            product("cb,soc->sbo", hots[2], grad_query_rel),
            product("cb,soc->sbo", hots[0], grad_key_rel),
        )
        grad_table_low = jnp.zeros(position_table.shape, F32)
        for member in range(2):
            gradient = position_grads[member].astype(BF)
            up = columns(att_up[member])
            grad_columns = ADAPTER_SCALING * product(
                "spr,spo->sro", position_inners[member], gradient
            )
            grad_inner = (ADAPTER_SCALING * product("spo,sro->spr", gradient, up)).astype(BF)
            grad_table_low = (
                grad_table_low
                + product("spo,io->pi", gradient, columns(frozen[member]))
                + product("spr,sir->pi", grad_inner, att_down[member])
            )
            down_grads[member] = down_grads[member] + product("spr,pi->sri", grad_inner, table_low)
            if not by_rows:
                grad_columns = lax.dynamic_update_slice_in_dim(
                    jnp.zeros_like(up_grads[member]),
                    grad_columns,
                    head_index * (width // head_groups),
                    2,
                )
            up_grads[member] = up_grads[member] + grad_columns
        late = jnp.concatenate(down_grads + up_grads, axis=-1)
        late = lax.all_gather(lax.psum(late, ("seq", "head")), "batch", axis=0, tiled=True)
        early = lax.all_gather(lax.psum(grad_ff, ("seq", "head")), "batch", axis=0, tiled=True)
        table_total = lax.psum(grad_table_low, ("seq", "batch"))
        table_total = lax.psum_scatter(table_total, "head", scatter_dimension=0, tiled=True)
    own_rows = table_rows // head_groups

    def head_rows(array):
        return lax.dynamic_slice_in_dim(array, head_index * own_rows, own_rows, 0)

    table_normed, table_inverse = norm_stats(head_rows(position_table))
    table_grad = norm_back(table_normed, table_inverse, position_gain, table_total)
    early = [spread(part) for part in unflat(early, [width, ff_width, ff_width, width])]
    late = [spread(part) for part in unflat(late, [width] * 8)]
    return (
        layer_output,
        input_grad,
        table_grad,
        jnp.stack([turned(part) for part in late[:4]]),
        jnp.stack(late[4:]),
        turned(early[0]),
        early[1],
        turned(early[2]),
        early[3],
    )


def solution(mesh):
    rows = P("batch", ("seq", "head"), None)
    return jax.shard_map(
        body,
        mesh=mesh,
        in_specs=(rows, rows, P("batch", None), P("batch")) + (P(),) * 16,
        out_specs=(
            rows,
            rows,
            P("head", None),
            P(None, "head", None, None),
            P(None, "head", None, None),
            P("head", None, None),
            P("head", None, None),
            P("head", None, None),
            P("head", None, None),
        ),
        check_vma=False,
    )
```

```python
from functools import partial
import math
from types import SimpleNamespace

import jax
import jax.numpy as jnp
import numpy as np
from jax import lax
from jax.experimental import pallas as pl
from jax.experimental.pallas import tpu as pltpu
from jax.sharding import PartitionSpec as P

HEADS = 16
HEAD_DIM = 64
BUCK = 256
SPAN = 512
ADAPTERS = 8
HALF = 512
DOCS = 8

EPSILON = 1e-07
ADAPTER_SCALING = 2.0
NEGATIVE = -1e30
PRECISE = lax.Precision.HIGHEST
TILE = 128
BF = jnp.bfloat16
F32 = jnp.float32
MESH = pl.DeviceIdType.MESH
VMEM = 63 * 2**20
NN = (((1,), (0,)), ((), ()))
NT = (((1,), (1,)), ((), ()))


def mm(a, b, dims=NN):
    return lax.dot_general(a, b, dims, preferred_element_type=F32)

def lanes(shape=(TILE, TILE)):
    return lax.broadcasted_iota(jnp.int32, shape, 1)

def rows(shape=(TILE, TILE)):
    return lax.broadcasted_iota(jnp.int32, shape, 0)

def skew(tile):
    return pltpu.roll(tile, 0, 1, stride=1, stride_axis=0)

def flip_matrix():
    return jnp.where(lanes() + rows() == TILE - 1, 1.0, 0.0).astype(BF)


class Loaded:
    def __init__(self, source, target, sem, start=True):
        self.target = target
        self.copy = pltpu.make_async_copy(source, target, sem)
        if start:
            self.copy.start()

    def __call__(self):
        if self.copy is not None:
            self.copy.wait()
            self.copy = None
        return self.target[...]


def with_halo(own_ref, halo_ref):
    return jnp.concatenate([halo_ref[0, :HALF], own_ref[0], halo_ref[0, HALF:]], axis=0)


class Stored:
    def __init__(self, target, buffer, sem):
        self.buffer = buffer
        self.copy = pltpu.make_async_copy(buffer, target, sem)

    def put(self, value):
        self.buffer[...] = value
        self.copy.start()

    def wait(self):
        self.copy.wait()


def prepare_kernel(seqs, ids_ref, lengths_ref, base_ref, *refs):
    stacks = [stack.at[member] for stack in refs[:2] for member in range(4)] + list(refs[2:6])
    count = len(stacks)
    refs = refs[6:]
    outs = refs[: count + 2]
    buffers = refs[count + 2 : 2 * count + 2]
    made = refs[2 * count + 2 : 3 * count + 4]
    sems, out_sems = refs[3 * count + 4 :]
    outs = [Stored(target, buffer, out_sems.at[i]) for i, (target, buffer) in enumerate(zip(outs, made))]
    query_seg_ref, key_bias_ref = made[count:]
    copies = []
    for s in range(seqs):
        for index, (stack, buffer) in enumerate(zip(stacks, buffers)):
            copy = pltpu.make_async_copy(stack.at[ids_ref[s]], buffer.at[s], sems.at[s, index])
            copy.start()
            copies.append(copy)
    rows_k = key_bias_ref.shape[1]
    rows_q = query_seg_ref.shape[1]
    place = base_ref[0] + rows((rows_k, TILE))
    slot = lanes((rows_k, TILE)) % HEAD_DIM
    inside = (place >= 0) & (place < base_ref[1])
    for s in range(seqs):
        segment = jnp.zeros((rows_k, TILE), jnp.int32)
        bound = jnp.int32(0)
        for document in range(DOCS):
            bound = bound + lengths_ref[s, document]
            segment += jnp.where(place >= bound, 1, 0)
        segment = jnp.where(inside, segment, DOCS)
        same = slot == segment
        query_seg_ref[s] = jnp.where(same, 1.0, 0.0)[HALF : HALF + rows_q].astype(BF)
        open_slot = (same & (segment < DOCS)) | (slot > DOCS)
        key_bias_ref[s] = jnp.where(open_slot, 0.0, NEGATIVE).astype(BF)
    for out in outs[count:]:
        out.copy.start()
    for copy in copies:
        copy.wait()
    for buffer, out in zip(buffers, outs):
        out.put(buffer[...].astype(BF))
    for out in outs:
        out.wait()


def prepare(adapter_ids, lengths, base, stacks, query_count):
    seqs = adapter_ids.shape[0]
    hbm = pl.BlockSpec(memory_space=pltpu.HBM)
    sm = pl.BlockSpec(memory_space=pltpu.SMEM)
    shapes = [(seqs,) + stack.shape[2:] for stack in stacks[:2] for _ in range(4)]
    shapes += [(seqs,) + stack.shape[1:] for stack in stacks[2:]]
    count = len(shapes)
    columns = [(seqs, query_count, TILE), (seqs, query_count + 2 * HALF, TILE)]
    found = pl.pallas_call(
        partial(prepare_kernel, seqs),
        in_specs=[sm] * 3 + [hbm] * len(stacks),
        out_specs=[hbm] * (count + 2),
        out_shape=[jax.ShapeDtypeStruct(shape, BF) for shape in shapes + columns],
        scratch_shapes=[pltpu.VMEM(shape, F32) for shape in shapes]
        + [pltpu.VMEM(shape, BF) for shape in shapes + columns]
        + [pltpu.SemaphoreType.DMA((seqs, count)), pltpu.SemaphoreType.DMA((count + 2,))],
        compiler_params=pltpu.CompilerParams(vmem_limit_bytes=VMEM),
        cost_estimate=pl.CostEstimate(flops=10**6, bytes_accessed=6 * 10**6, transcendentals=0),
        name="prepare",
    )(adapter_ids, lengths, base, *stacks)
    return found[:count], found[count], found[count + 1]


def adapted(x, weight, inner, up):
    return (mm(x, weight) + ADAPTER_SCALING * mm(inner, up)).astype(BF)


def begin_kernel(x_ref, table_ref, gain_ref, query_a, key_a, value_a, query_b, key_b, value_b,
                 query_w, key_w, value_w, query_hot, back_hot, key_hot,
                 query_out, key_out, value_out, query_rel_out, back_rel_out, key_rel_out, low_out,
                 query_u, key_u, value_u, query_pu, key_pu, *scratch):
    loaded = scratch[:6]
    stored = scratch[6:13]
    load_sems, store_sems = scratch[13:]
    query_w, key_w, value_w, query_hot, back_hot, key_hot = (
        Loaded(source, target, load_sems.at[index])
        for index, (source, target) in enumerate(zip((query_w, key_w, value_w, query_hot, back_hot, key_hot), loaded))
    )
    outs = [
        Stored(target, buffer, store_sems.at[index])
        for index, (target, buffer) in enumerate(
            zip((query_out, key_out, value_out, query_rel_out, back_rel_out, key_rel_out, low_out), stored)
        )
    ]
    x = x_ref[...]
    query_u[...] = mm(x, query_a[...], NT).astype(BF)
    key_u[...] = mm(x, key_a[...], NT).astype(BF)
    value_u[...] = mm(x, value_a[...], NT).astype(BF)
    values = table_ref[...]
    centered = values - jnp.mean(values, axis=1, keepdims=True)
    inverse = lax.rsqrt(jnp.mean(centered * centered, axis=1, keepdims=True) + EPSILON)
    low = (centered * inverse * gain_ref[...]).astype(BF)
    outs[6].put(low)
    query_pu[...] = mm(low, query_a[...], NT).astype(BF)
    key_pu[...] = mm(low, key_a[...], NT).astype(BF)
    outs[0].put(adapted(x, query_w(), query_u[...], query_b[...]))
    position_q = adapted(low, query_w(), query_pu[...], query_b[...])
    outs[1].put(adapted(x, key_w(), key_u[...], key_b[...]))
    position_k = adapted(low, key_w(), key_pu[...], key_b[...])
    outs[2].put(adapted(x, value_w(), value_u[...], value_b[...]))
    outs[3].put(mm(query_hot(), position_q).astype(BF))
    outs[4].put(mm(back_hot(), position_q).astype(BF))
    outs[5].put(mm(key_hot(), position_k).astype(BF))
    for out in outs:
        out.wait()


def begin(x, table, gain, weights, downs, ups, hots):
    rows_x, width = x.shape
    rank = ups[0].shape[0]
    places = table.shape[0]
    spans = hots[0].shape[0]
    vm = pl.BlockSpec(memory_space=pltpu.VMEM)
    hbm = pl.BlockSpec(memory_space=pltpu.HBM)
    large = [(rows_x, width)] * 3 + [(spans, width)] * 3 + [(places, width)]
    inner = jax.ShapeDtypeStruct((rows_x, rank), BF)
    position_inner = jax.ShapeDtypeStruct((places, rank), BF)
    sources = (*weights, hots[1], hots[2], hots[0])
    found = pl.pallas_call(
        begin_kernel,
        in_specs=[vm] * 9 + [hbm] * 6,
        out_specs=[hbm] * 7 + [vm] * 5,
        out_shape=[jax.ShapeDtypeStruct(shape, BF) for shape in large] + [inner] * 3 + [position_inner] * 2,
        scratch_shapes=[pltpu.VMEM(source.shape, BF) for source in sources]
        + [pltpu.VMEM(shape, BF) for shape in large]
        + [pltpu.SemaphoreType.DMA((6,)), pltpu.SemaphoreType.DMA((7,))],
        compiler_params=pltpu.CompilerParams(vmem_limit_bytes=VMEM),
        cost_estimate=pl.CostEstimate(
            flops=6 * rows_x * width * width + 10 * places * width * width,
            bytes_accessed=24 * places * width + 6 * width * width,
            transcendentals=0,
        ),
        name="begin",
    )(x, table, gain.reshape(1, width), *downs, *ups, *sources)
    return found[:3], found[3:6], found[6], found[7:10], found[10:]


def relative_kernel(q_ref, k_ref, pk_ref, pq_ref, qs_ref, ks_ref):
    tiles = HALF // TILE
    span = 2 * tiles
    below = lanes() + rows() < TILE
    column = lanes((HALF, TILE)) < HEAD_DIM
    for h in range(2):
        own = column if h == 0 else ~column
        km = jnp.where(own, k_ref[0], jnp.zeros_like(k_ref[0]))
        qm = jnp.where(own, q_ref[0], jnp.zeros_like(q_ref[0]))
        for d in range(1, span):
            pairs = [(t, d + t - tiles) for t in range(tiles) if 0 <= d + t - tiles < tiles]
            first, last = pairs[0][1], pairs[-1][1]
            key_rel = mm(
                km[first * TILE : (last + 1) * TILE], pq_ref[0, (span - 1 - d) * TILE : (span + 1 - d) * TILE, :], NT
            ).astype(BF)
            for t, j in pairs:
                part = key_rel[(j - first) * TILE : (j - first + 1) * TILE]
                ks_ref[0, h, t, :, j * TILE : (j + 1) * TILE] = skew(
                    jnp.where(below, part[:, TILE:], part[:, :TILE])
                ).T
        query_rel = mm(qm, pk_ref[0], NT).astype(BF)
        for t in range(tiles):
            part = query_rel[t * TILE : (t + 1) * TILE]
            for d in range(span + 1):
                here = part[:, min(d, span - 1) * TILE : (min(d, span - 1) + 1) * TILE]
                if 0 < d < span:
                    here = jnp.where(below, here, part[:, (d - 1) * TILE : d * TILE])
                qs_ref[0, h, t, :, d * TILE : (d + 1) * TILE] = skew(here)


def relative_scores(q, k, pk, pq):
    n, rq, width = q.shape
    pairs = width // TILE
    off = 2 * HALF
    tiles = rq // TILE
    return pl.pallas_call(
        relative_kernel,
        grid=(n, pairs),
        in_specs=[column_spec(rq), column_spec(rq), column_spec(off), column_spec(off)],
        out_specs=[head_spec(tiles, TILE, off + TILE), head_spec(tiles, TILE, HALF)],
        out_shape=[jax.ShapeDtypeStruct((n, 2 * pairs, tiles, TILE, off + TILE), BF),
                   jax.ShapeDtypeStruct((n, 2 * pairs, tiles, TILE, HALF), BF)],
        compiler_params=pltpu.CompilerParams(dimension_semantics=("arbitrary", "arbitrary"), vmem_limit_bytes=VMEM),
        cost_estimate=pl.CostEstimate(
            flops=16 * n * rq * off * width, bytes_accessed=60 * 10**6, transcendentals=0
        ),
        name="relative_scores",
    )(q, k, pk, pq)


def column_spec(r):
    return pl.BlockSpec((1, r, TILE), lambda s, p: (s, 0, p))


def head_spec(*shape):
    return pl.BlockSpec((1, 2) + shape, lambda s, p: (s, p) + (0,) * len(shape))


def forward_kernel(mapped, pairs, q_ref, k_ref, v_ref, pq_ref, qhot_ref, kbias_ref, qs_ref, ko_ref, *refs):
    if mapped:
        kh_ref, vh_ref, ctx_ref, p_ref, ctxf_ref, inv_ref = refs[:6]
    else:
        before, after, key_w, value_w, key_a, value_a, key_b, value_b = refs[:8]
        ctx_ref, p_ref, ctxf_ref, inv_ref, kh_ref, vh_ref, key_u, value_u = refs[8:16]
    prepared = (refs[-7:-4], refs[-4:-1])
    s_ref = refs[-1]
    step = pl.program_id(1)
    tiles = HALF // TILE
    span = 2 * tiles
    width = (span + 1) * TILE
    flip = flip_matrix()
    flips = jnp.concatenate([flip, flip], axis=1)
    factor = math.log2(math.e) / math.sqrt(3 * HEAD_DIM)
    below = lanes() + rows() < TILE
    place = lanes() + rows()
    tcol = lanes() < HEAD_DIM

    def halo_inners():
        for side, x in ((0, before), (1, after)):
            at = slice(side * HALF, (side + 1) * HALF)
            key_u[at] = mm(x[...], key_a[...], NT).astype(BF)
            value_u[at] = mm(x[...], value_a[...], NT).astype(BF)

    def halo_map(side):
        weights = jnp.concatenate([key_w[...], value_w[...]], axis=1)
        nothing = jnp.zeros_like(key_b[...])
        ups = jnp.concatenate(
            [jnp.concatenate([key_b[...], nothing], axis=1), jnp.concatenate([nothing, value_b[...]], axis=1)], axis=0
        )
        at = slice(side * HALF, (side + 1) * HALF)
        inner = jnp.concatenate([key_u[at], value_u[at]], axis=1)
        both = adapted((before, after)[side][...], weights, inner, ups)
        kh_ref[0, at] = both[:, :TILE]
        vh_ref[0, at] = both[:, TILE:]

    def prepare_head(h, target):
        kz_ref, vz_ref, ks_ref = target
        k = with_halo(k_ref, kh_ref)
        v = with_halo(v_ref, vh_ref)
        own = lanes(k.shape) < HEAD_DIM
        halo_own = lanes(kh_ref.shape[1:]) < HEAD_DIM
        if h == 1:
            own, halo_own = ~own, ~halo_own
        kz_ref[h] = jnp.where(own, k, kbias_ref[0])
        vz_ref[h] = jnp.where(own, v, jnp.ones_like(v))
        km = jnp.where(halo_own, kh_ref[0], jnp.zeros_like(kh_ref[0]))
        for d in range(span + 1):
            seen = [(t, d + t if d + t < tiles else d + t - tiles) for t in range(tiles) if not tiles <= d + t < 2 * tiles]
            if not seen:
                continue
            low = max(span - 1 - d, 0) * TILE
            high = min(span + 1 - d, span) * TILE
            first, last = seen[0][1], seen[-1][1]
            key_rel = mm(km[first * TILE : (last + 1) * TILE], pq_ref[0, low:high, :], NT).astype(BF)
            for t, j in seen:
                part = key_rel[(j - first) * TILE : (j - first + 1) * TILE]
                if 0 < d < span:
                    part = jnp.where(below, part[:, TILE:], part[:, :TILE])
                w = d if d < tiles else d - tiles
                ks_ref[h, t, :, w * TILE : (w + 1) * TILE] = skew(part).T

    def scores(t, h, source):
        kz_ref, _, ks_ref = source
        at = slice(t * TILE, (t + 1) * TILE)
        edge = (tiles - t) * TILE
        q_side = mm(flip, jnp.where(tcol if h == 0 else ~tcol, q_ref[0, at, :], qhot_ref[0, at, :])).astype(BF)
        key_side = jnp.concatenate([ks_ref[h, t, :, :edge], ko_ref[0, h, t], ks_ref[h, t, :, edge:]], axis=1)
        relative = jnp.concatenate([qs_ref[0, h, t], key_side], axis=0)
        s_ref[2 * (t % 2) + h] = mm(q_side, kz_ref[h, t * TILE : t * TILE + width, :], NT) + mm(flips, relative)

    def softmax(t, h, source):
        slot = 2 * (t % 2) + h
        at = slice(t * TILE, (t + 1) * TILE)
        own = tcol if h == 0 else ~tcol
        s_ref[slot, :, :TILE] = jnp.where(place > TILE - 1, s_ref[slot, :, :TILE], NEGATIVE)
        s_ref[slot, :, span * TILE :] = jnp.where(place < TILE - 1, s_ref[slot, :, span * TILE :], NEGATIVE)
        middle = s_ref[slot, :, tiles * TILE : (tiles + 1) * TILE]
        s_ref[slot, :, tiles * TILE : (tiles + 1) * TILE] = jnp.where(
            (place == TILE - 1) & (middle < 0.1 * NEGATIVE), 0.0, middle
        )
        top = s_ref[slot, :, :TILE]
        for d in range(1, span + 1):
            top = jnp.maximum(top, s_ref[slot, :, d * TILE : (d + 1) * TILE])
        peak = jnp.max(top, axis=1, keepdims=True)
        prob = jnp.exp2((s_ref[slot] - peak) * factor).astype(BF)
        a = t % 2
        row_at = slice(a * TILE, (a + 1) * TILE)
        p_ref[0, h, t // 2, row_at, a * TILE : a * TILE + width] = prob
        p_ref[0, h, t // 2, row_at, (1 - a) * width : (1 - a) * width + TILE] = jnp.zeros((TILE, TILE), BF)
        total = mm(prob, source[1][h, t * TILE : t * TILE + width, :])
        inv = 1.0 / jnp.where(own, pltpu.roll(total, HEAD_DIM, 1), total)
        inv_ref[0, h, at, :] = inv
        return total * inv

    @pl.when(step == 0)
    def _():
        if not mapped:
            halo_inners()
            halo_map(0)
            halo_map(1)
        for h in range(2):
            prepare_head(h, prepared[0])

    def both(target, source):
        between = []
        if target is not None:
            between = [lambda: prepare_head(0, target), lambda: prepare_head(1, target)]
        if target is not None and not mapped:
            between = [lambda: (halo_map(0), halo_map(1))] + between
        for h in range(2):
            scores(0, h, source)
        for t in range(tiles):
            outs = []
            for h in range(2):
                if t + 1 < tiles:
                    scores(t + 1, h, source)
                outs.append(softmax(t, h, source))
            if between:
                between.pop(0)()
            at = slice(t * TILE, (t + 1) * TILE)
            ctx = jnp.where(tcol, outs[0], outs[1])
            ctxf_ref[0, at, :] = ctx
            ctx_ref[0, at, :] = mm(flip, ctx.astype(BF)).astype(BF)

    for parity in range(2):

        @pl.when((step > 0) & (step < pairs) & (step % 2 == parity))
        def _():
            both(prepared[parity], prepared[1 - parity])

    @pl.when(step == pairs)
    def _():
        both(None, prepared[(pairs - 1) % 2])


def attention_forward(q, k, v, pq, qhot, kbias, query_scores, key_scores, halo):
    n, rq, width = q.shape
    off = 2 * HALF
    rk = rq + off
    pairs = width // TILE
    tiles = rq // TILE

    def coming(r):
        return pl.BlockSpec((1, r, TILE), lambda s, p: (s, 0, jnp.minimum(p, pairs - 1)))

    def current(r):
        return pl.BlockSpec((1, r, TILE), lambda s, p: (s, 0, jnp.maximum(p - 1, 0)))

    def current_heads(*shape):
        return pl.BlockSpec((1, 2) + shape, lambda s, p: (s, jnp.maximum(p - 1, 0)) + (0,) * len(shape))

    def whole(r):
        return pl.BlockSpec((1, r, TILE), lambda s, p: (s, 0, 0))

    mapped = len(halo) == 2
    in_specs = [current(rq), coming(rq), coming(rq), coming(off), whole(rq), whole(rk),
                current_heads(tiles, TILE, off + TILE), current_heads(tiles, TILE, HALF)]
    out_specs = [current(rq), current_heads(tiles // 2, 2 * TILE, off + 2 * TILE), current(rq), current_heads(rq, TILE)]
    out_shape = [jax.ShapeDtypeStruct((n, rq, width), BF),
                 jax.ShapeDtypeStruct((n, 2 * pairs, tiles // 2, 2 * TILE, off + 2 * TILE), BF),
                 jax.ShapeDtypeStruct((n, rq, width), F32),
                 jax.ShapeDtypeStruct((n, 2 * pairs, rq, TILE), F32)]
    if mapped:
        in_specs += [coming(off)] * 2
    else:
        rank = halo[4].shape[0]

        def once(*shape):
            return pl.BlockSpec(shape, lambda s, p: (0,) * len(shape))

        def columns(r):
            return pl.BlockSpec((r, TILE), lambda s, p: (0, jnp.minimum(p, pairs - 1)))

        in_specs += [once(HALF, width)] * 2 + [columns(width)] * 2 + [once(rank, width)] * 2 + [columns(rank)] * 2
        out_specs += [coming(off)] * 2 + [once(off, rank)] * 2
        out_shape += [jax.ShapeDtypeStruct((n, off, width), BF)] * 2 + [jax.ShapeDtypeStruct((off, rank), BF)] * 2
    return pl.pallas_call(
        partial(forward_kernel, mapped, pairs),
        grid=(n, pairs + 1),
        in_specs=in_specs,
        out_specs=out_specs,
        out_shape=out_shape,
        scratch_shapes=[pltpu.VMEM((2, rk, TILE), BF), pltpu.VMEM((2, rk, TILE), BF),
                        pltpu.VMEM((2, tiles, TILE, HALF + TILE), BF)] * 2
        + [pltpu.VMEM((4, TILE, off + TILE), F32)],
        compiler_params=pltpu.CompilerParams(dimension_semantics=("arbitrary", "arbitrary"), vmem_limit_bytes=VMEM),
        cost_estimate=pl.CostEstimate(
            flops=32 * n * rq * off * width, bytes_accessed=60 * 10**6, transcendentals=0
        ),
        name="attention_forward",
    )(q, k, v, pq, qhot, kbias, query_scores, key_scores, *halo)


def spread_kernel(group, head_ref, ids_ref, late_ref, ff_ref, table_ref, places_hbm, grad_hbm, gain_ref,
                  table_out, down_out, up_out, expand_down, expand_up, reduce_down, reduce_up, grad_out, places_ref, grad_ref, sems):
    cores, peers, rank, part = late_ref.shape
    grad_in = Loaded(grad_hbm, grad_ref, sems.at[1])
    grad_done = Stored(grad_out, grad_ref, sems.at[2])
    width = table_ref.shape[3]
    ff = expand_up.shape[2]
    rest = ff_ref.shape[3]
    count = places_ref.shape[0]
    fetch = pltpu.make_async_copy(places_hbm.at[pl.ds(pl.multiple_of(head_ref[0] * count, count), count)], places_ref, sems.at[0])
    fetch.start()
    first = head_ref[0] * group
    weights = [
        [jnp.where(ids_ref[s, :1, :1] == (first + a).astype(F32), 1.0, 0.0) for a in range(group)] for s in range(cores)
    ]

    def fill(out, a, source, pieces):
        for column, piece in pieces:
            value = sum(weights[s][a] * source[s, piece[0], :, piece[1]].astype(F32) for s in range(cores))
            out[:, column] = value

    per = width // part
    starts = ((expand_down, 0, width), (expand_up, width, ff), (reduce_down, width + ff, ff), (reduce_up, width + 2 * ff, width))
    for a in range(group):
        for member in range(8):
            out = (down_out if member < 4 else up_out).at[member % 4, a]
            fill(out, a, late_ref, [
                (slice(half * part, (half + 1) * part), (member * per + half, slice(0, part))) for half in range(per)
            ])
        for out, start, count in starts:
            pieces = []
            at = start
            while at < start + count:
                peer, offset = at // rest, at % rest
                length = min(rest - offset, start + count - at)
                pieces.append((slice(at - start, at - start + length), (peer, slice(offset, offset + length))))
                at += length
            fill(out.at[a], a, ff_ref, pieces)
    grad_in()
    grad_done.copy.start()
    fetch.wait()
    values = places_ref[...]
    centered = values - jnp.mean(values, axis=1, keepdims=True)
    inverse = lax.rsqrt(jnp.mean(centered * centered, axis=1, keepdims=True) + EPSILON)
    normed = centered * inverse
    upstream = table_ref[...].reshape(values.shape).astype(F32) * gain_ref[...]
    table_out[...] = inverse * (
        upstream
        - jnp.mean(upstream, axis=1, keepdims=True)
        - normed * jnp.mean(upstream * normed, axis=1, keepdims=True)
    )
    grad_done.wait()


def spread_all(group, head, ids, late, ff_late, table, places, grad, gain, ff):
    rank = late.shape[2]
    width = table.shape[3]
    own = (places.shape[0] * group // ADAPTERS, width)
    vm = pl.BlockSpec(memory_space=pltpu.VMEM)
    sm = pl.BlockSpec(memory_space=pltpu.SMEM)
    hbm = pl.BlockSpec(memory_space=pltpu.HBM)

    def out(*shape):
        return jax.ShapeDtypeStruct(shape, F32)

    return pl.pallas_call(
        partial(spread_kernel, group),
        in_specs=[sm, vm, vm, vm, vm, hbm, hbm, vm],
        out_specs=[vm] * 7 + [hbm],
        out_shape=[out(*own), out(4, group, rank, width), out(4, group, rank, width), out(group, rank, width),
                   out(group, rank, ff), out(group, rank, ff), out(group, rank, width), out(*grad.shape)],
        scratch_shapes=[pltpu.VMEM(own, F32), pltpu.VMEM(grad.shape, F32), pltpu.SemaphoreType.DMA((3,))],
        compiler_params=pltpu.CompilerParams(vmem_limit_bytes=VMEM),
        name="spread_all",
    )(head, ids, late, ff_late, table, places, grad, gain.reshape(1, width))


def backward_kernel(handed, q_ref, k_ref, kh_ref, v_ref, vh_ref, pk_ref, pq_ref, p_ref, g_ref, ctxf_ref, inv_ref, *refs):
    if handed:
        layer_ref, layer_out, *refs = refs
        layer_out[...] = layer_ref[...]
    dq_ref, dk_ref, dkh_ref, dv_ref, dvh_ref, dpk_ref, dpq_ref, kx_ref, vx_ref = refs[:9]
    qr_ref, gr_ref, e_ref, gc_ref, gk_ref, dvt_ref, dkt_ref = refs[9:]
    rows_q = q_ref.shape[1]
    rows_k = kx_ref.shape[0]
    kx_ref[...] = with_halo(k_ref, kh_ref)
    vx_ref[...] = with_halo(v_ref, vh_ref)
    tiles = rows_q // TILE
    key_tiles = rows_k // TILE
    span = 2 * HALF // TILE
    wide = (span + 2) * TILE
    flip = flip_matrix()
    scale = 1.0 / math.sqrt(3 * HEAD_DIM)
    tcol = lanes() < HEAD_DIM
    qcol = lanes((rows_q, TILE)) < HEAD_DIM
    over = lanes() > rows()
    under = lanes() >= rows()

    @pl.when((pl.program_id(0) == 0) & (pl.program_id(1) == 0))
    def _():
        gk_ref[...] = jnp.zeros_like(gk_ref)

    for t in range(tiles):
        at = slice(t * TILE, (t + 1) * TILE)
        qr_ref[at] = mm(flip, q_ref[0, at]).astype(BF)
        gr_ref[at] = mm(flip, g_ref[0, at]).astype(BF)
    q_rev = qr_ref[...]
    g_rev = gr_ref[...]
    q_turned = q_rev.T
    k_turned = kx_ref[...].T
    product = g_rev.astype(F32) * ctxf_ref[0]
    dvt_ref[...] = jnp.zeros_like(dvt_ref)
    dkt_ref[...] = jnp.zeros_like(dkt_ref)
    zero = jnp.zeros((TILE, TILE), BF)
    dq_main = [[], []]
    dq_parts = [None, None]
    dk_tiles = [[], []]

    def of_head(h):
        own = qcol if h == 0 else ~qcol
        inv = inv_ref[0, h]
        delta = jnp.sum(jnp.where(own, product, 0.0), axis=1, keepdims=True) * inv
        g_turned = (g_rev.astype(F32) * inv).astype(BF).T[h * HEAD_DIM : (h + 1) * HEAD_DIM]
        return jnp.where(own, g_rev, jnp.zeros_like(g_rev)), inv, delta, g_turned

    heads = [of_head(h) for h in range(2)]

    def errors(h, u):
        g_masked, inv, delta, g_turned = heads[h]
        part = slice(h * HEAD_DIM, (h + 1) * HEAD_DIM)
        at = slice(u * 2 * TILE, (u + 1) * 2 * TILE)
        window = slice(u * 2 * TILE, u * 2 * TILE + wide)
        prob = p_ref[0, h, u]
        g_probs = mm(g_masked[at], vx_ref[window], NT)
        inv_u = jnp.concatenate([inv[at]] * (span + 2), axis=1)
        delta_u = jnp.concatenate([delta[at]] * (span + 2), axis=1)
        e = (prob.astype(F32) * (g_probs * inv_u - delta_u)).astype(BF)
        e_ref[h, u] = e
        dvt_ref[part, window] += mm(g_turned[:, at], prob)
        dkt_ref[part, window] += mm(q_turned[part, at], e)
        dq_main[h].append(mm(e, kx_ref[window]))

    def error(h, t, d):
        a = t % 2
        return e_ref[h, t // 2, a * TILE : (a + 1) * TILE, (a + d) * TILE : (a + d + 1) * TILE]

    def distances(h, t):
        here = None
        for d in range(span + 1):
            block = pltpu.roll(error(h, t, d), 1, 1, stride=1, stride_axis=0)
            if d > 0:
                gc_ref[h, t * TILE : (t + 1) * TILE, (d - 1) * TILE : d * TILE] = jnp.where(over, block, here)
            here = block

    def end_queries(h):
        part = slice(h * HEAD_DIM, (h + 1) * HEAD_DIM)
        dq_parts[h] = jnp.concatenate(dq_main[h], axis=0) + mm(gc_ref[h], pk_ref[0])
        dpk_ref[0, part, :] = (mm(q_turned[part], gc_ref[h]) * scale).astype(BF)

    def keys(h, j):
        spun = {j - t: skew(error(h, t, j - t).T) for t in range(tiles) if 0 <= j - t <= span}
        low = max(min(spun) - 1, 0)
        high = min(max(spun), span - 1)
        at = slice(j * TILE, (j + 1) * TILE)
        for c in range(low, high + 1):
            gk_ref[h, at, c * TILE : (c + 1) * TILE] = jnp.where(under, spun.get(c + 1, zero), spun.get(c, zero))
        cols = slice(low * TILE, (high + 1) * TILE)
        dk_tiles[h].append(mm(gk_ref[h, at, cols], pq_ref[0, cols]))

    def end_keys(h):
        part = slice(h * HEAD_DIM, (h + 1) * HEAD_DIM)
        for c in range(0, span, 2):
            near = slice(c * TILE, (c + tiles + 2) * TILE)
            cols = slice(c * TILE, (c + 2) * TILE)
            dpq_ref[0, part, cols] = (mm(k_turned[part, near], gk_ref[h, near, cols]) * scale).astype(BF)

    for h in range(2):
        for u in range(tiles // 2):
            errors(h, u)
            distances(h, 2 * u)
            distances(h, 2 * u + 1)
        end_queries(h)
        for j in range(key_tiles):
            keys(h, j)
        end_keys(h)
    dk_parts = [jnp.concatenate(found, axis=0) for found in dk_tiles]
    dq = (jnp.where(qcol, dq_parts[0], dq_parts[1]) * scale).astype(BF)
    for t in range(tiles):
        at = slice(t * TILE, (t + 1) * TILE)
        dq_ref[0, at] = mm(flip, dq[at]).astype(BF)
    kcol = lanes((rows_k, TILE)) < HEAD_DIM
    dk = ((dkt_ref[...].T + jnp.where(kcol, dk_parts[0], dk_parts[1])) * scale).astype(BF)
    dv = dvt_ref[...].astype(BF).T
    for whole, own_ref, halo_ref in ((dk, dk_ref, dkh_ref), (dv, dv_ref, dvh_ref)):
        halo_ref[0, :HALF] = whole[:HALF]
        own_ref[0] = whole[HALF : HALF + rows_q]
        halo_ref[0, HALF:] = whole[HALF + rows_q :]


def attention_backward(q, k, k_halo, v, v_halo, pk, pq, probs, g, ctxf, inv, *layer):
    n, rq, width = q.shape
    off = 2 * HALF
    rk = rq + off
    pairs = width // TILE
    wide = off + 2 * TILE
    def col(r):
        return pl.BlockSpec((1, r, TILE), lambda s, p: (s, 0, p))
    def row(r):
        return pl.BlockSpec((1, TILE, r), lambda s, p: (s, p, 0))
    return pl.pallas_call(
        partial(backward_kernel, len(layer) > 0),
        grid=(n, pairs),
        in_specs=[col(rq), col(rq), col(off), col(rq), col(off), col(off), col(off),
                  pl.BlockSpec((1, 2, rq // (2 * TILE), 2 * TILE, wide), lambda s, p: (s, p, 0, 0, 0)),
                  col(rq), col(rq),
                  pl.BlockSpec((1, 2, rq, TILE), lambda s, p: (s, p, 0, 0))] + [col(rq)] * len(layer),
        out_specs=[col(rq)] * len(layer) + [col(rq), col(rq), col(off), col(rq), col(off), row(off), row(off)],
        out_shape=[jax.ShapeDtypeStruct(array.shape, array.dtype) for array in layer]
        + [jax.ShapeDtypeStruct((n, rq, width), BF),
                   jax.ShapeDtypeStruct((n, rq, width), BF),
                   jax.ShapeDtypeStruct((n, off, width), BF),
                   jax.ShapeDtypeStruct((n, rq, width), BF),
                   jax.ShapeDtypeStruct((n, off, width), BF),
                   jax.ShapeDtypeStruct((n, width, off), BF),
                   jax.ShapeDtypeStruct((n, width, off), BF)],
        scratch_shapes=[pltpu.VMEM((rk, TILE), BF), pltpu.VMEM((rk, TILE), BF), pltpu.VMEM((rq, TILE), BF), pltpu.VMEM((rq, TILE), BF),
                        pltpu.VMEM((2, rq // (2 * TILE), 2 * TILE, wide), BF),
                        pltpu.VMEM((2, rq, off), BF),
                        pltpu.VMEM((2, rk, off), BF),
                        pltpu.VMEM((TILE, rk), F32), pltpu.VMEM((TILE, rk), F32)],
        compiler_params=pltpu.CompilerParams(dimension_semantics=("arbitrary", "arbitrary"), vmem_limit_bytes=VMEM),
        name="attention_backward",
    )(q, k, k_halo, v, v_halo, pk, pq, probs, g, ctxf, inv, *layer)


def gather_rows(left, right):
    return lax.dot_general(left, right, (((0,), (0,)), ((), ())), preferred_element_type=F32)


def whereabouts(shape):
    groups, blocks = shape[:2]
    seq, head, core = lax.axis_index("seq"), lax.axis_index("head"), lax.axis_index("batch")
    return blocks * groups, seq * groups + head, lambda p: (p // groups, p % groups, core), (seq, head, core)


def signal(barrier, device):
    pl.semaphore_signal(barrier, inc=1, device_id=device, device_id_type=MESH)


def remote(source, target, send_sem, recv_sem, device):
    return pltpu.make_async_remote_copy(
        src_ref=source, dst_ref=target, send_sem=send_sem, recv_sem=recv_sem, device_id=device, device_id_type=MESH
    )


def each(first, end, step):
    lax.fori_loop(first, end, lambda k, carry: (step(k), carry)[1], 0)


def finish_kernel(shape, names, *refs):
    groups, blocks, cores, rank = shape
    r = SimpleNamespace(**dict(zip(names, refs)))
    peers, me, place, (seq, head, core) = whereabouts(shape)
    partner = (seq, head, 1 - core)
    width = r.table_out.shape[3]

    held = SimpleNamespace()
    for index, name in enumerate(names[:LOADS]):
        target = refs[len(refs) - LOADS + index]
        setattr(held, name, Loaded(refs[index], target, r.load_sems.at[index], start=index < FIRST_LOADS))

    barrier = pltpu.get_barrier_semaphore()
    signal(barrier, partner)
    each(1, peers, lambda k: signal(barrier, place((me + k) % peers)))

    def inner_grad(gradient, up):
        return (ADAPTER_SCALING * mm(gradient, up[...], NT)).astype(BF)

    halo_buf, halo_recv, halo_sems = r.halo_buf, r.halo_recv, r.halo_sems
    half = HALF // 2

    def crossing(side, piece):
        there = place(jnp.maximum(me - 1, 0) if side == 0 else jnp.minimum(me + 1, peers - 1))
        return remote(
            halo_buf.at[side, piece], halo_recv.at[1 - side, piece],
            halo_sems.at[4 * side + 2 * piece], halo_sems.at[4 * side + 2 * piece + 1], there,
        )

    def start_crossing(side, piece):
        @pl.when(me > 0 if side == 0 else me < peers - 1)
        def _():
            crossing(side, piece).start()
    key_halo, value_halo = held.key_halo(), held.value_halo()
    key_hu, value_hu = inner_grad(key_halo, r.key_b), inner_grad(value_halo, r.value_b)
    key_w, value_w = held.key_w(), held.value_w()
    for name in names[FIRST_LOADS:LOADS]:
        getattr(held, name).copy.start()

    def map_piece(piece):
        for side in range(2):
            start = side * HALF + piece * half
            at = slice(start, start + half)
            halo_buf[side, piece] = (
                mm(key_halo[at], key_w, NT)
                + mm(value_halo[at], value_w, NT)
                + mm(key_hu[at], r.key_a[...])
                + mm(value_hu[at], r.value_a[...])
            ).astype(BF)
            if piece == 0 and side == 0:
                pl.semaphore_wait(barrier, peers)
            start_crossing(side, piece)

    map_piece(0)

    def give_f(p):
        return remote(r.ff, r.ff_out.at[core, me], r.spread_f.at[p], r.arrive_f.at[me], place(p))

    def on_f(p):
        return remote(r.ff_out.at[core, p], r.ff_out.at[core, p], r.pass_f.at[p], r.other_f.at[p], partner)

    def got_f(k):
        p = (me + peers - k) % peers
        remote(r.ff, r.ff_out.at[core, p], r.spread_f.at[p], r.arrive_f.at[p], place(p)).wait_recv()
        on_f(p).start()

    def end_f(k):
        p = k - 1
        remote(r.ff_out.at[1 - core, p], r.ff_out.at[1 - core, p], r.pass_f.at[p], r.other_f.at[p], partner).wait_recv()
        on_f(p).wait_send()

    r.ff_out[core, me] = r.ff[...]
    each(1, peers, lambda k: give_f((me + k) % peers).start())
    on_f(me).start()

    table_ref, stage_ref, recv_ref, sum_ref = r.table, r.stage, r.recv, r.sum
    core_ref, core_sems = r.core, r.core_sems
    position_q = mm(held.back_hot(), held.query_rel_g(), NT).astype(BF)
    position_k = mm(held.key_hot(), held.key_rel_g(), NT).astype(BF)
    query_pg, key_pg = inner_grad(position_q, r.query_b), inner_grad(position_k, r.key_b)
    query_w = held.query_w()
    table = (
        mm(position_q, query_w, NT)
        + mm(position_k, key_w, NT)
        + mm(query_pg, r.query_a[...])
        + mm(key_pg, r.key_a[...])
    ).astype(BF)
    for group in range(groups):
        for block in range(blocks):
            for side in range(cores):
                start = ((group * blocks + block) * cores + side) * rank
                table_ref[side, block * groups + group] = table[start : start + rank]
    swap = remote(table_ref.at[1 - core], core_ref, core_sems.at[0], core_sems.at[1], partner)
    swap.start()
    r.ids_out[core] = r.own_id[...]
    tell = remote(r.own_id, r.ids_out.at[core], core_sems.at[2], core_sems.at[3], partner)
    tell.start()

    x, x_before, x_after, low = held.x(), held.x_before(), held.x_after(), held.low()
    query_g, key_g, value_g = held.query_g(), held.key_g(), held.value_g()
    query_gu, key_gu, value_gu = inner_grad(query_g, r.query_b), inner_grad(key_g, r.key_b), inner_grad(value_g, r.value_b)
    def of_halo(inner):
        return gather_rows(inner[:HALF], x_before) + gather_rows(inner[HALF:], x_after)

    pieces = [
        gather_rows(query_gu, x) + gather_rows(query_pg, low),
        gather_rows(key_gu, x) + of_halo(key_hu) + gather_rows(key_pg, low),
        gather_rows(value_gu, x) + of_halo(value_hu),
        r.out_ga[...],
        ADAPTER_SCALING * (gather_rows(r.query_u[...], query_g) + gather_rows(r.query_pu[...], position_q)),
        ADAPTER_SCALING
        * (
            gather_rows(r.key_u[...], key_g)
            + gather_rows(r.key_uh[...], key_halo)
            + gather_rows(r.key_pu[...], position_k)
        ),
        ADAPTER_SCALING * (gather_rows(r.value_u[...], value_g) + gather_rows(r.value_uh[...], value_halo)),
        r.out_gb[...],
    ]
    part = len(pieces) * width // peers
    per = width // part
    for index, piece in enumerate(pieces):
        for cut in range(per):
            stage_ref[index * per + cut, :, width : width + part] = piece[:, cut * part : (cut + 1) * part].astype(BF)

    send_sems, recv_sems = r.send_sems, r.recv_sems
    swap.wait()

    def to_peer(p):
        return remote(stage_ref.at[p], recv_ref.at[me], send_sems.at[p], recv_sems.at[me], place(p))

    def send(k):
        p = (me + k) % peers
        stage_ref[p, :, :width] = (table_ref[core, p].astype(F32) + core_ref[p].astype(F32)).astype(BF)
        to_peer(p).start()

    each(1, peers, send)
    map_piece(1)
    each(1, peers, got_f)
    sum_ref[:, :width] = table_ref[core, me].astype(F32) + core_ref[me].astype(F32)
    sum_ref[:, width:] = stage_ref[me, :, width:].astype(F32)

    grad_ref = r.grad_out
    grad_ref[...] = (
        held.grad_one()
        + mm(query_g, query_w, NT)
        + mm(key_g, key_w, NT)
        + mm(value_g, value_w, NT)
        + mm(query_gu, r.query_a[...])
        + mm(key_gu, r.key_a[...])
        + mm(value_gu, r.value_a[...])
    )

    def take(k):
        p = (me + peers - k) % peers
        remote(stage_ref.at[p], recv_ref.at[p], send_sems.at[p], recv_sems.at[p], place(p)).wait_recv()
        sum_ref[...] += recv_ref[p].astype(F32)

    each(1, peers, take)
    mine_t, mine_l, table_out, late_out = r.mine_t, r.mine_l, r.table_out, r.late_out
    mine_t[...] = sum_ref[:, :width].astype(BF)
    mine_l[...] = sum_ref[:, width:].astype(BF)
    late_out[core, me] = mine_l[...]
    table_out[seq, core] = mine_t[...]

    def give_l(p):
        return remote(mine_l, late_out.at[core, me], r.spread_l.at[p], r.arrive_l.at[me], place(p))

    def give_t(s):
        return remote(mine_t, table_out.at[seq, core], r.spread_t.at[s], r.arrive_t.at[seq], (s, head, core))

    each(1, peers, lambda k: give_l((me + k) % peers).start())
    each(1, blocks, lambda k: give_t((seq + k) % blocks).start())

    def on_l(p):
        return remote(late_out.at[core, p], late_out.at[core, p], r.pass_l.at[p], r.other_l.at[p], partner)

    def on_t(s):
        return remote(table_out.at[s, core], table_out.at[s, core], r.pass_t.at[s], r.other_t.at[s], partner)

    on_l(me).start()
    on_t(seq).start()

    def got_l(k):
        p = (me + peers - k) % peers
        remote(mine_l, late_out.at[core, p], r.spread_l.at[p], r.arrive_l.at[p], place(p)).wait_recv()
        on_l(p).start()

    def got_t(k):
        s = (seq + blocks - k) % blocks
        remote(mine_t, table_out.at[s, core], r.spread_t.at[s], r.arrive_t.at[s], (s, head, core)).wait_recv()
        on_t(s).start()

    each(1, peers, got_l)
    each(1, blocks, got_t)

    @pl.when(me > 0)
    def _():
        for piece in range(2):
            crossing(0, piece).wait_send()
            crossing(1, piece).wait_recv()
        grad_ref[...] += halo_recv[0].astype(F32).reshape(HALF, width)

    @pl.when(me < peers - 1)
    def _():
        for piece in range(2):
            crossing(1, piece).wait_send()
            crossing(0, piece).wait_recv()
        grad_ref[...] += halo_recv[1].astype(F32).reshape(HALF, width)

    def end_l(k):
        p = k - 1
        remote(late_out.at[1 - core, p], late_out.at[1 - core, p], r.pass_l.at[p], r.other_l.at[p], partner).wait_recv()
        on_l(p).wait_send()

    def end_t(k):
        s = k - 1
        remote(table_out.at[s, 1 - core], table_out.at[s, 1 - core], r.pass_t.at[s], r.other_t.at[s], partner).wait_recv()
        on_t(s).wait_send()

    tell.wait()
    each(1, peers + 1, end_f)
    each(1, peers + 1, end_l)
    each(1, blocks + 1, end_t)

    def sent(k):
        p = (me + k) % peers
        to_peer(p).wait_send()
        give_l(p).wait_send()
        give_f(p).wait_send()

    each(1, peers, sent)
    each(1, blocks, lambda k: give_t((seq + k) % blocks).wait_send())


LOADS = 17
FIRST_LOADS = 4


def finish(shape, **arrays):
    groups, blocks, cores, rank = shape
    peers = groups * blocks
    rows, width = arrays[list(arrays)[LOADS - 1]].shape
    share = 8 * width // peers
    ff = arrays[list(arrays)[-1]]
    vm = pl.BlockSpec(memory_space=pltpu.VMEM)
    hbm = pl.BlockSpec(memory_space=pltpu.HBM)
    dma = pltpu.SemaphoreType.DMA
    outputs = dict(
        grad_out=jax.ShapeDtypeStruct((rows, width), F32),
        table_out=jax.ShapeDtypeStruct((blocks, cores, rank, width), BF),
        late_out=jax.ShapeDtypeStruct((cores, peers, rank, share), BF),
        ids_out=jax.ShapeDtypeStruct((cores, 8, TILE), F32),
        ff_out=jax.ShapeDtypeStruct((cores, peers) + ff.shape, BF),
    )
    scratch = dict(
        load_sems=dma((LOADS,)),
        halo_buf=pltpu.VMEM((2, 2, HALF // 2, width), BF),
        halo_recv=pltpu.VMEM((2, 2, HALF // 2, width), BF),
        halo_sems=dma((8,)),
        table=pltpu.VMEM((cores, peers, rank, width), BF),
        core=pltpu.VMEM((peers, rank, width), BF),
        stage=pltpu.VMEM((peers, rank, width + share), BF),
        recv=pltpu.VMEM((peers, rank, width + share), BF),
        sum=pltpu.VMEM((rank, width + share), F32),
        mine_t=pltpu.VMEM((rank, width), BF),
        mine_l=pltpu.VMEM((rank, share), BF),
        core_sems=dma((4,)),
        send_sems=dma((peers,)),
        recv_sems=dma((peers,)),
        spread_l=dma((peers,)),
        arrive_l=dma((peers,)),
        pass_l=dma((peers,)),
        other_l=dma((peers,)),
        spread_t=dma((blocks,)),
        arrive_t=dma((blocks,)),
        pass_t=dma((blocks,)),
        other_t=dma((blocks,)),
        spread_f=dma((peers,)),
        arrive_f=dma((peers,)),
        pass_f=dma((peers,)),
        other_f=dma((peers,)),
    )
    names = (*arrays, *outputs, *scratch)
    kept = [pltpu.VMEM(array.shape, array.dtype) for array in list(arrays.values())[:LOADS]]
    return pl.pallas_call(
        partial(finish_kernel, shape, names),
        in_specs=[hbm] * LOADS + [vm] * (len(arrays) - LOADS),
        out_specs=[vm] * len(outputs),
        out_shape=list(outputs.values()),
        scratch_shapes=list(scratch.values()) + kept,
        compiler_params=pltpu.CompilerParams(
            collective_id=0, has_side_effects=True, vmem_limit_bytes=VMEM
        ),
        name="finish",
    )(*arrays.values())


def middle_kernel(seqs, shape, context_hbm, tokens_hbm, cotangent_hbm, out_w_hbm, up_w_hbm, down_w_hbm,
                  out_a_ref, out_b_ref, up_a_ref, up_b_ref, down_a_ref, down_b_ref, gain_one_ref, gain_two_ref,
                  layer_hbm, grad_one_hbm, grad_context_ref, out_ga_ref, out_gb_ref, result_ref,
                  out_w, up_w, down_w, hidden_ref, low_ref, work_ref, act_ref, slope_ref,
                  context_ref, tokens_ref, cotangent_ref, layer_ref, grad_one_ref, sems, *refs):
    if shape is None:
        ff_ref = result_ref
    else:
        ff_ref, stage_ref, recv_ref, send_sems, recv_sems = refs
        peers, me, place, _ = whereabouts(shape)
        barrier = pltpu.get_barrier_semaphore()
        each(1, peers, lambda k: signal(barrier, place((me + k) % peers)))

    def to_peer(p):
        return remote(stage_ref.at[p], recv_ref.at[me], send_sems.at[p], recv_sems.at[me], place(p))

    def send(first):
        if shape is None:
            return
        half = peers // 2
        part = stage_ref.shape[2]
        for p in range(first, first + half):
            stage_ref[p] = ff_ref[0, :, p * part : (p + 1) * part].astype(BF)

        def start(k):
            p = first + (me + k) % half

            @pl.when(p != me)
            def _():
                to_peer(p).start()

        each(0, half, start)

    rows, width = tokens_ref.shape
    ff = up_w.shape[1]
    share = rows // seqs
    chunk = 512
    context_in, out_in, tokens_in, up_in, down_in, cotangent_in = (
        Loaded(source, target, sems.at[index])
        for index, (source, target) in enumerate(
            (
                (context_hbm, context_ref),
                (out_w_hbm, out_w),
                (tokens_hbm, tokens_ref),
                (up_w_hbm, up_w),
                (down_w_hbm, down_w),
                (cotangent_hbm, cotangent_ref),
            )
        )
    )
    layer_out = Stored(layer_hbm, layer_ref, sems.at[6])
    grad_one_out = Stored(grad_one_hbm, grad_one_ref, sems.at[7])

    half = rows // 2
    sides = (slice(0, half), slice(half, rows))

    def parts(side, step):
        if seqs == 1:
            return step(0, slice(0, half))
        per = seqs // 2
        return jnp.concatenate(
            [step(side * per + s, slice(s * share, (s + 1) * share)) for s in range(per)], axis=0
        )

    def inner(side, values, factor_ref, scale=1.0):
        return parts(side, lambda s, at: (scale * mm(values[at], factor_ref[s], NT)).astype(BF))

    def widened(side, inner_values, factor_ref, columns=slice(None)):
        return parts(side, lambda s, at: mm(inner_values[at], factor_ref[s, :, columns]))

    def factor_grad(left, right, s):
        at = slice(s * share, (s + 1) * share)
        return gather_rows(left[at], right[at])

    def joined(pair):
        return jnp.concatenate(pair, axis=0)

    def stats(values):
        centered = values - jnp.mean(values, axis=1, keepdims=True)
        inverse = lax.rsqrt(jnp.mean(centered * centered, axis=1, keepdims=True) + EPSILON)
        return centered * inverse, inverse

    def back(normed, inverse, gain, upstream):
        scaled = upstream * gain
        return inverse * (
            scaled
            - jnp.mean(scaled, axis=1, keepdims=True)
            - normed * jnp.mean(scaled * normed, axis=1, keepdims=True)
        )

    context = context_in()
    inner_out = [inner(side, context[at], out_a_ref) for side, at in enumerate(sides)]
    out_in()
    attended = [
        mm(context[at], out_w[...]) + ADAPTER_SCALING * widened(side, inner_out[side], out_b_ref)
        for side, at in enumerate(sides)
    ]
    tokens_in()
    inverse_one = [None, None]
    inner_up = [None, None]

    def norm_one(side):
        at = sides[side]
        normed, inverse_one[side] = stats(tokens_ref[at] + attended[side])
        grad_one_ref[at] = normed
        hidden = normed * gain_one_ref[...]
        hidden_ref[at] = hidden
        low_ref[at] = hidden.astype(BF)
        inner_up[side] = inner(side, low_ref[at], up_a_ref)

    def activate(side, start):
        at = sides[side]
        columns = slice(start, start + chunk)
        pre = mm(low_ref[at], up_w[:, columns]) + ADAPTER_SCALING * widened(side, inner_up[side], up_b_ref, columns)
        below = 0.5 + 0.5 * lax.erf(pre * math.sqrt(0.5))
        act_ref[at, columns] = (pre * below).astype(BF)
        density = jnp.exp(pre * pre * -0.5) * (1.0 / math.sqrt(2.0 * math.pi))
        slope_ref[at, columns] = (below + pre * density).astype(BF)

    norm_one(0)
    up_in()
    activate(0, 0)
    norm_one(1)
    for start in range(chunk, ff, chunk):
        activate(0, start)
    for start in range(0, ff, chunk):
        activate(1, start)
    down_in()
    inner_down = [None, None]
    branch = [None, None]
    for side, at in enumerate(sides):
        inner_down[side] = inner(side, act_ref[at], down_a_ref)
        branch[side] = mm(act_ref[at], down_w[...]) + ADAPTER_SCALING * widened(side, inner_down[side], down_b_ref)
    cotangent_in()
    grad_two = [None, None]
    grad_inner = [None, None]

    def norm_two(side):
        at = sides[side]
        normed, inverse = stats(hidden_ref[at] + branch[side])
        layer_ref[at] = normed * gain_two_ref[...]
        work_ref[at] = back(normed, inverse, gain_two_ref[...], cotangent_ref[at])
        grad_two[side] = work_ref[at].astype(BF)
        grad_inner[side] = inner(side, grad_two[side], down_b_ref, ADAPTER_SCALING)

    def back_activate(side, start):
        at = sides[side]
        columns = slice(start, start + chunk)
        grad_act = mm(grad_two[side], down_w[columns, :], NT) + widened(side, grad_inner[side], down_a_ref, columns)
        slope_ref[at, columns] = (grad_act.astype(BF).astype(F32) * slope_ref[at, columns].astype(F32)).astype(BF)

    norm_two(0)
    back_activate(0, 0)
    norm_two(1)
    layer_out.copy.start()
    for start in range(chunk, ff, chunk):
        back_activate(0, start)
    all_two, all_inner, all_down = joined(grad_two), joined(grad_inner), joined(inner_down)
    for s in range(seqs):
        ff_ref[s, :, width + 2 * ff:] = ADAPTER_SCALING * factor_grad(all_down, all_two, s)
        ff_ref[s, :, width + ff:width + 2 * ff] = factor_grad(all_inner, act_ref, s)
    if shape is not None:
        pl.semaphore_wait(barrier, peers - 1)
        send(peers // 2)
    for start in range(0, ff, chunk):
        back_activate(1, start)
    grad_inner = [inner(side, slope_ref[at], up_b_ref, ADAPTER_SCALING) for side, at in enumerate(sides)]
    all_inner, all_up = joined(grad_inner), joined(inner_up)
    for s in range(seqs):
        ff_ref[s, :, width:width + ff] = ADAPTER_SCALING * factor_grad(all_up, slope_ref, s)
        ff_ref[s, :, :width] = factor_grad(all_inner, low_ref, s)
    send(0)
    grad_hidden = [
        mm(slope_ref[at], up_w[...], NT) + widened(side, grad_inner[side], up_a_ref) for side, at in enumerate(sides)
    ]
    grad_low = [None, None]
    for side, at in enumerate(sides):
        grad_one = back(grad_one_ref[at], inverse_one[side], gain_one_ref[...], grad_hidden[side] + work_ref[at])
        grad_one_ref[at] = grad_one
        grad_low[side] = grad_one.astype(BF)
        grad_inner[side] = inner(side, grad_low[side], out_b_ref, ADAPTER_SCALING)
        grad_context_ref[at] = (
            mm(grad_low[side], out_w[...], NT) + widened(side, grad_inner[side], out_a_ref)
        ).astype(BF)
    grad_one_out.copy.start()
    all_low, all_inner, all_out = joined(grad_low), joined(grad_inner), joined(inner_out)
    for s in range(seqs):
        out_gb_ref[s] = ADAPTER_SCALING * factor_grad(all_out, all_low, s)
        out_ga_ref[s] = factor_grad(all_inner, context, s)
    layer_out.wait()
    grad_one_out.wait()
    if shape is not None:
        ff_ref[0, :, : stage_ref.shape[2]] = stage_ref[me].astype(F32)

        def take(k):
            p = (me + peers - k) % peers
            remote(stage_ref.at[p], recv_ref.at[p], send_sems.at[p], recv_sems.at[p], place(p)).wait_recv()
            ff_ref[0, :, : stage_ref.shape[2]] += recv_ref[p].astype(F32)

        each(1, peers, take)
        result_ref[...] = ff_ref[0, :, : stage_ref.shape[2]].astype(BF)
        each(1, peers, lambda k: to_peer((me + k) % peers).wait_send())


def middle(context, tokens, cotangent, out_weight, up_weight, down_weight, factors, gain_one, gain_two, shape=None):
    seqs, share, width = tokens.shape
    rows = seqs * share
    ff = up_weight.shape[1]
    rank = factors[0].shape[1]
    vm = pl.BlockSpec(memory_space=pltpu.VMEM)
    hbm = pl.BlockSpec(memory_space=pltpu.HBM)
    wide = jax.ShapeDtypeStruct((rows, width), F32)
    factor = jax.ShapeDtypeStruct((seqs, rank, width), F32)
    columns = 2 * width + 2 * ff
    result = jax.ShapeDtypeStruct((seqs, rank, columns), F32)
    extra = []
    params = pltpu.CompilerParams(vmem_limit_bytes=VMEM)
    if shape is not None:
        peers = shape[0] * shape[1]
        result = jax.ShapeDtypeStruct((rank, columns // peers), BF)
        extra = [pltpu.VMEM((seqs, rank, columns), F32)] + [pltpu.VMEM((peers, rank, columns // peers), BF)] * 2
        extra += [pltpu.SemaphoreType.DMA((peers,))] * 2
        params = pltpu.CompilerParams(vmem_limit_bytes=VMEM, collective_id=1, has_side_effects=True)
    found = pl.pallas_call(
        partial(middle_kernel, seqs, shape),
        in_specs=[hbm] * 6 + [vm] * 8,
        out_specs=[hbm] * 2 + [vm] * 4,
        out_shape=[wide, wide, jax.ShapeDtypeStruct((rows, width), BF), factor, factor, result],
        scratch_shapes=[
            pltpu.VMEM(out_weight.shape, BF), pltpu.VMEM(up_weight.shape, BF), pltpu.VMEM(down_weight.shape, BF),
            pltpu.VMEM((rows, width), F32), pltpu.VMEM((rows, width), BF), pltpu.VMEM((rows, width), F32),
            pltpu.VMEM((rows, ff), BF), pltpu.VMEM((rows, ff), BF),
            pltpu.VMEM((rows, width), BF), *[pltpu.VMEM((rows, width), F32)] * 4, pltpu.SemaphoreType.DMA((8,)),
        ] + extra,
        compiler_params=params,
        cost_estimate=pl.CostEstimate(flops=36 * rows * width * width, bytes_accessed=24 * width * width, transcendentals=rows * ff),
        name="middle",
    )(context.reshape(rows, width), tokens.reshape(rows, width), cotangent.reshape(rows, width),
      out_weight, up_weight, down_weight, *factors, gain_one.reshape(1, width), gain_two.reshape(1, width))
    return [array.reshape(seqs, share, width) for array in found[:3]] + list(found[3:])


def shifted(value, axes, steps):
    count = math.prod(lax.axis_size(axis) for axis in axes)
    initial, last = (max(0, -steps), min(count, count - steps))
    return lax.ppermute(value, axes, [(source, source + steps) for source in range(initial, last)])


def bucket_of(offset, buckets, distance_cap):
    middle = buckets // 2
    sign_of = np.sign(offset)
    magnitude = np.where((offset < middle) & (offset > -middle), middle - 1, np.abs(offset))
    log_place = (
        np.ceil(np.log(magnitude / middle) / np.log((distance_cap - 1) / middle) * (middle - 1))
        + middle
    )
    return np.where(np.abs(offset) <= middle, offset, log_place * sign_of).astype(np.int32)


def offset_tables():
    place = np.arange(2 * HALF)

    def hot(distance, sign):
        clipped = np.clip(distance, 1 - HALF, HALF - 1)
        bucket = np.clip(BUCK + sign * bucket_of(clipped, BUCK, SPAN), 0, 2 * BUCK - 1)
        return np.eye(2 * BUCK, dtype=np.float32)[bucket]

    return hot(HALF - place, 1), hot(place - HALF, -1), hot(HALF - 1 - place, -1)


def segment_ids(lengths, positions):
    bounds = jnp.cumsum(lengths, axis=-1, dtype=jnp.int32)
    return jnp.sum(
        (bounds[..., None, :] <= positions[:, None]).astype(jnp.int32), axis=-1, dtype=jnp.int32
    )


def product(pattern, left_side, right_side):
    return jnp.einsum(pattern, left_side, right_side, preferred_element_type=F32)


def norm_stats(values):
    centered = values - jnp.mean(values, axis=-1, keepdims=True)
    inverse = lax.rsqrt(jnp.mean(centered * centered, axis=-1, keepdims=True) + EPSILON)
    return (centered * inverse, inverse)


def norm_back(normed, inverse, scale_gain, upstream):
    scaled = upstream * scale_gain
    return inverse * (
        scaled
        - jnp.mean(scaled, axis=-1, keepdims=True)
        - normed * jnp.mean(scaled * normed, axis=-1, keepdims=True)
    )


def adapter_forward(rows_in, weight, down, up):
    inner = product("sti,sir->str", rows_in, down).astype(BF)
    mapped = product("sti,io->sto", rows_in, weight) + ADAPTER_SCALING * product(
        "str,sro->sto", inner, up
    )
    return (mapped, inner)


def adapter_back(rows_in, inner, weight, down, up, gradient):
    grad_up = ADAPTER_SCALING * product("str,sto->sro", inner, gradient)
    grad_inner = (ADAPTER_SCALING * product("sto,sro->str", gradient, up)).astype(BF)
    grad_down = product("sti,str->sir", rows_in, grad_inner)
    grad_in = product("sto,io->sti", gradient, weight) + product("str,sir->sti", grad_inner, down)
    return (grad_in, grad_down, grad_up)


def body(
    tokens,
    cotangent,
    doc_lengths,
    adapter_ids,
    query_weight,
    key_weight,
    value_weight,
    output_weight,
    up_weight,
    down_weight,
    attention_gain,
    feedforward_gain,
    position_gain,
    position_table,
    attention_down,
    attention_up,
    expand_down,
    expand_up,
    reduce_down,
    reduce_up,
):
    seqs, row_count, width = tokens.shape
    head_groups = lax.axis_size("head")
    head_index = lax.axis_index("head")
    seq_index = lax.axis_index("seq")
    by_rows = seqs == 1 and row_count == HALF

    def turned(array):
        return jnp.swapaxes(array, -1, -2)

    token_low = lax.optimization_barrier(tokens.astype(BF))
    frozen = (query_weight, key_weight, value_weight)

    def columns(matrix):
        if by_rows:
            return matrix
        local = width // head_groups
        return lax.dynamic_slice_in_dim(matrix, head_index * local, local, matrix.ndim - 1)

    if by_rows:
        block_axes = ("seq", "head")
        block_index = seq_index * head_groups + head_index
        query_count = row_count
    else:
        block_axes = ("seq",)
        block_index = seq_index
        query_count = row_count * head_groups
    blocks = math.prod(lax.axis_size(axis) for axis in block_axes)

    first_place = block_index * query_count - HALF
    factors, query_seg, key_bias = prepare(
        adapter_ids,
        doc_lengths,
        jnp.stack([first_place, query_count * blocks]).astype(jnp.int32),
        [turned(attention_down), attention_up, turned(expand_down), expand_up, turned(reduce_down), reduce_up],
        query_count,
    )
    downs, att_up = factors[:4], factors[4:8]
    att_down = [turned(factor) for factor in downs]

    def halo(array):
        before = shifted(array[:, query_count - HALF :], block_axes, 1)
        after = shifted(array[:, :HALF], block_axes, -1)
        return before, after

    hots = [jnp.asarray(hot, BF) for hot in offset_tables()]
    if by_rows:
        before, after = halo(token_low)
        (query, key, value), (query_rel, query_back, key_rel), table_low, inners, position_inners = begin(
            token_low[0],
            position_table,
            position_gain,
            frozen,
            [down[0] for down in downs[:3]],
            [up[0] for up in att_up[:3]],
            hots,
        )
        queries, keys, values, key_rel, query_rel, query_back = (
            array[None] for array in (query, key, value, key_rel, query_rel, query_back)
        )
    else:
        projected = []
        inners = []
        for member in range(3):
            mapped, inner = adapter_forward(
                token_low, frozen[member], att_down[member], att_up[member]
            )
            projected.append(mapped.astype(BF))
            inners.append(inner)
        queries, keys, values = lax.all_to_all(
            jnp.stack(projected), "head", split_axis=3, concat_axis=2, tiled=True
        )
        keys_halo, values_halo = (jnp.concatenate(halo(array), axis=1) for array in (keys, values))
        table_low = (norm_stats(position_table)[0] * position_gain).astype(BF)
        position_inners = []
        tables = []
        for member in range(2):
            inner = product("pi,sir->spr", table_low, att_down[member]).astype(BF)
            mapped = product("pi,io->po", table_low, columns(frozen[member]))[
                None
            ] + ADAPTER_SCALING * product("spr,sro->spo", inner, columns(att_up[member]))
            position_inners.append(inner)
            tables.append(mapped.astype(BF))
        key_rel = product("cp,spo->sco", hots[0], tables[1]).astype(BF)
        query_rel = product("cp,spo->sco", hots[1], tables[0]).astype(BF)
        query_back = product("cp,spo->sco", hots[2], tables[0]).astype(BF)

    query_scores, key_scores = relative_scores(queries, keys, key_rel, query_rel)
    if by_rows:
        sides = (before[0], after[0], *frozen[1:], downs[1][0], downs[2][0], att_up[1][0], att_up[2][0])
    else:
        sides = (keys_halo, values_halo)
    context, probs, context_wide, inverse_total, *made = attention_forward(
        queries, keys, values, query_rel, query_seg, key_bias, query_scores, key_scores, sides
    )
    if by_rows:
        keys_halo, values_halo, *inners_halo = made
    if by_rows:
        context_rows = context
    else:
        context_rows = lax.all_to_all(context, "head", split_axis=1, concat_axis=2, tiled=True)

    ff_width = up_weight.shape[1]
    rank = attention_up.shape[2]
    peers = lax.axis_size("seq") * head_groups
    cores = lax.axis_size("batch")
    table_rows = position_table.shape[0]
    direct = by_rows and cores == 2 and table_rows == peers * cores * rank
    shape = (head_groups, peers // head_groups, cores, rank) if direct else None
    layer_output, grad_one, grad_context, grad_out_down, grad_out_up, grad_ff = middle(
        context_rows,
        tokens,
        cotangent,
        output_weight,
        up_weight,
        down_weight,
        (downs[3], att_up[3], *factors[8:]),
        attention_gain,
        feedforward_gain,
        shape,
    )
    if not by_rows:
        grad_context = lax.all_to_all(grad_context, "head", split_axis=2, concat_axis=1, tiled=True)

    group = ADAPTERS // head_groups
    def spread(array):
        chosen_by = select.reshape(select.shape + (1,) * (array.ndim - 1))
        return jnp.sum(chosen_by * array[:, None], axis=0)

    def unflat(array, widths):
        return jnp.split(array, np.cumsum(widths)[:-1].tolist(), axis=-1)

    *handed, grad_q, grad_k, grad_k_halo, grad_v, grad_v_halo, grad_key_rel, grad_query_rel = attention_backward(
        queries,
        keys,
        keys_halo,
        values,
        values_halo,
        key_rel,
        query_back,
        probs,
        grad_context,
        context_wide,
        inverse_total,
        *([layer_output] if direct else []),
    )
    if direct:
        layer_output = handed[0]

    def joined(total, from_above, from_below):
        if query_count == HALF:
            return total + from_above + from_below
        total = total.at[:, query_count - HALF :].add(from_above)
        return total.at[:, :HALF].add(from_below)

    def fold(total, halo_part):
        from_above = shifted(halo_part[:, :HALF], block_axes, -1).astype(F32)
        from_below = shifted(halo_part[:, HALF:], block_axes, 1).astype(F32)
        return joined(total.astype(F32), from_above, from_below)

    if direct:
        grad_tokens, table_total, late, both_ids, ff_total = finish(
            shape,
            key_halo=grad_k_halo[0],
            value_halo=grad_v_halo[0],
            key_w=key_weight,
            value_w=value_weight,
            back_hot=hots[2].T,
            query_rel_g=grad_query_rel[0],
            key_hot=hots[0].T,
            key_rel_g=grad_key_rel[0],
            query_w=query_weight,
            x=token_low[0],
            x_before=before[0],
            x_after=after[0],
            low=table_low,
            query_g=grad_q[0],
            key_g=grad_k[0],
            value_g=grad_v[0],
            grad_one=grad_one[0],
            query_a=downs[0][0],
            key_a=downs[1][0],
            value_a=downs[2][0],
            query_b=att_up[0][0],
            key_b=att_up[1][0],
            value_b=att_up[2][0],
            query_u=inners[0],
            key_u=inners[1],
            value_u=inners[2],
            key_uh=inners_halo[0],
            value_uh=inners_halo[1],
            query_pu=position_inners[0],
            key_pu=position_inners[1],
            own_id=jnp.broadcast_to(adapter_ids.astype(F32)[:, None], (8, TILE)),
            out_ga=grad_out_down[0],
            out_gb=grad_out_up[0],
            ff=grad_ff,
        )
        table_grad, down_grad, up_grad, *ff_grads, input_grad = spread_all(
            group,
            head_index.astype(jnp.int32).reshape(1),
            both_ids,
            late,
            ff_total,
            table_total,
            position_table,
            grad_tokens,
            position_gain,
            ff_width,
        )
        return (
            layer_output,
            input_grad[None],
            table_grad,
            turned(down_grad),
            up_grad,
            turned(ff_grads[0]),
            ff_grads[1],
            turned(ff_grads[2]),
            ff_grads[3],
        )
    else:
        ids = lax.all_gather(adapter_ids, "batch", axis=0, tiled=True)
        slots = head_index * group + jnp.arange(group, dtype=jnp.int32)
        select = (ids[:, None] == slots[None, :]).astype(F32)
        down_grads = []
        up_grads = []
        if by_rows:
            input_grad = grad_one
            grad_halo = 0.0
            rows_halo = jnp.concatenate([before, after], axis=1)
            for member, pieces in enumerate(
                (
                    ((token_low, inners[0][None], grad_q),),
                    ((token_low, inners[1][None], grad_k), (rows_halo, inners_halo[0][None], grad_k_halo)),
                    ((token_low, inners[2][None], grad_v), (rows_halo, inners_halo[1][None], grad_v_halo)),
                )
            ):
                found = [
                    adapter_back(rows, inner, frozen[member], att_down[member], att_up[member], gradient)
                    for rows, inner, gradient in pieces
                ]
                input_grad = input_grad + found[0][0]
                if member > 0:
                    grad_halo = grad_halo + found[1][0]
                down_grads.append(sum(turned(one[1]) for one in found))
                up_grads.append(sum(one[2] for one in found))
            input_grad = fold(input_grad, grad_halo.astype(BF))
            position_inners = [inner[None] for inner in position_inners]
        else:
            grad_qkv = jnp.stack(
                [grad_q, fold(grad_k, grad_k_halo).astype(BF), fold(grad_v, grad_v_halo).astype(BF)]
            )
            grad_qkv = lax.all_to_all(grad_qkv, "head", split_axis=2, concat_axis=3, tiled=True)
            input_grad = grad_one
            for member in range(3):
                grad_in, grad_dn, grad_upper = adapter_back(
                    token_low,
                    inners[member],
                    frozen[member],
                    att_down[member],
                    att_up[member],
                    grad_qkv[member],
                )
                input_grad = input_grad + grad_in
                down_grads.append(turned(grad_dn))
                up_grads.append(grad_upper)
        down_grads.append(grad_out_down)
        up_grads.append(grad_out_up)
        position_grads = (
            product("cb,soc->sbo", hots[2], grad_query_rel),
            product("cb,soc->sbo", hots[0], grad_key_rel),
        )
        grad_table_low = jnp.zeros(position_table.shape, F32)
        for member in range(2):
            gradient = position_grads[member].astype(BF)
            up = columns(att_up[member])
            grad_columns = ADAPTER_SCALING * product(
                "spr,spo->sro", position_inners[member], gradient
            )
            grad_inner = (ADAPTER_SCALING * product("spo,sro->spr", gradient, up)).astype(BF)
            grad_table_low = (
                grad_table_low
                + product("spo,io->pi", gradient, columns(frozen[member]))
                + product("spr,sir->pi", grad_inner, att_down[member])
            )
            down_grads[member] = down_grads[member] + product("spr,pi->sri", grad_inner, table_low)
            if not by_rows:
                grad_columns = lax.dynamic_update_slice_in_dim(
                    jnp.zeros_like(up_grads[member]),
                    grad_columns,
                    head_index * (width // head_groups),
                    2,
                )
            up_grads[member] = up_grads[member] + grad_columns
        late = jnp.concatenate(down_grads + up_grads, axis=-1)
        late = lax.all_gather(lax.psum(late, ("seq", "head")), "batch", axis=0, tiled=True)
        early = lax.all_gather(lax.psum(grad_ff, ("seq", "head")), "batch", axis=0, tiled=True)
        table_total = lax.psum(grad_table_low, ("seq", "batch"))
        table_total = lax.psum_scatter(table_total, "head", scatter_dimension=0, tiled=True)
    own_rows = table_rows // head_groups

    def head_rows(array):
        return lax.dynamic_slice_in_dim(array, head_index * own_rows, own_rows, 0)

    table_normed, table_inverse = norm_stats(head_rows(position_table))
    table_grad = norm_back(table_normed, table_inverse, position_gain, table_total)
    early = [spread(part) for part in unflat(early, [width, ff_width, ff_width, width])]
    late = [spread(part) for part in unflat(late, [width] * 8)]
    return (
        layer_output,
        input_grad,
        table_grad,
        jnp.stack([turned(part) for part in late[:4]]),
        jnp.stack(late[4:]),
        turned(early[0]),
        early[1],
        turned(early[2]),
        early[3],
    )


def solution(mesh):
    rows = P("batch", ("seq", "head"), None)
    return jax.shard_map(
        body,
        mesh=mesh,
        in_specs=(rows, rows, P("batch", None), P("batch")) + (P(),) * 16,
        out_specs=(
            rows,
            rows,
            P("head", None),
            P(None, "head", None, None),
            P(None, "head", None, None),
            P("head", None, None),
            P("head", None, None),
            P("head", None, None),
            P("head", None, None),
        ),
        check_vma=False,
    )
```

```python
from functools import partial
import math
from types import SimpleNamespace

import jax
import jax.numpy as jnp
import numpy as np
from jax import lax
from jax.experimental import pallas as pl
from jax.experimental.pallas import tpu as pltpu
from jax.sharding import PartitionSpec as P

HEADS = 16
HEAD_DIM = 64
BUCK = 256
SPAN = 512
ADAPTERS = 8
HALF = 512
DOCS = 8

EPSILON = 1e-07
ADAPTER_SCALING = 2.0
NEGATIVE = -1e30
PRECISE = lax.Precision.HIGHEST
TILE = 128
BF = jnp.bfloat16
F32 = jnp.float32
MESH = pl.DeviceIdType.MESH
VMEM = 63 * 2**20
NN = (((1,), (0,)), ((), ()))
NT = (((1,), (1,)), ((), ()))


def mm(a, b, dims=NN):
    return lax.dot_general(a, b, dims, preferred_element_type=F32)

def lanes(shape=(TILE, TILE)):
    return lax.broadcasted_iota(jnp.int32, shape, 1)

def rows(shape=(TILE, TILE)):
    return lax.broadcasted_iota(jnp.int32, shape, 0)

def skew(tile):
    return pltpu.roll(tile, 0, 1, stride=1, stride_axis=0)

def flip_matrix():
    return jnp.where(lanes() + rows() == TILE - 1, 1.0, 0.0).astype(BF)


class Loaded:
    def __init__(self, source, target, sem, start=True):
        self.target = target
        self.copy = pltpu.make_async_copy(source, target, sem)
        if start:
            self.copy.start()

    def __call__(self):
        if self.copy is not None:
            self.copy.wait()
            self.copy = None
        return self.target[...]


def with_halo(own_ref, halo_ref):
    return jnp.concatenate([halo_ref[0, :HALF], own_ref[0], halo_ref[0, HALF:]], axis=0)


class Stored:
    def __init__(self, target, buffer, sem):
        self.buffer = buffer
        self.copy = pltpu.make_async_copy(buffer, target, sem)

    def put(self, value):
        self.buffer[...] = value
        self.copy.start()

    def wait(self):
        self.copy.wait()


def prepare_kernel(seqs, ids_ref, lengths_ref, base_ref, *refs):
    stacks = [stack.at[member] for stack in refs[:2] for member in range(4)] + list(refs[2:6])
    count = len(stacks)
    refs = refs[6:]
    outs = refs[: count + 2]
    buffers = refs[count + 2 : 2 * count + 2]
    made = refs[2 * count + 2 : 3 * count + 4]
    sems, out_sems = refs[3 * count + 4 :]
    outs = [Stored(target, buffer, out_sems.at[i]) for i, (target, buffer) in enumerate(zip(outs, made))]
    query_seg_ref, key_bias_ref = made[count:]
    copies = []
    for s in range(seqs):
        for index, (stack, buffer) in enumerate(zip(stacks, buffers)):
            copy = pltpu.make_async_copy(stack.at[ids_ref[s]], buffer.at[s], sems.at[s, index])
            copy.start()
            copies.append(copy)
    rows_k = key_bias_ref.shape[1]
    rows_q = query_seg_ref.shape[1]
    place = base_ref[0] + rows((rows_k, TILE))
    slot = lanes((rows_k, TILE)) % HEAD_DIM
    inside = (place >= 0) & (place < base_ref[1])
    for s in range(seqs):
        segment = jnp.zeros((rows_k, TILE), jnp.int32)
        bound = jnp.int32(0)
        for document in range(DOCS):
            bound = bound + lengths_ref[s, document]
            segment += jnp.where(place >= bound, 1, 0)
        segment = jnp.where(inside, segment, DOCS)
        same = slot == segment
        query_seg_ref[s] = jnp.where(same, 1.0, 0.0)[HALF : HALF + rows_q].astype(BF)
        open_slot = (same & (segment < DOCS)) | (slot > DOCS)
        key_bias_ref[s] = jnp.where(open_slot, 0.0, NEGATIVE).astype(BF)
    for out in outs[count:]:
        out.copy.start()
    for copy in copies:
        copy.wait()
    for buffer, out in zip(buffers, outs):
        out.put(buffer[...].astype(BF))
    for out in outs:
        out.wait()


def prepare(adapter_ids, lengths, base, stacks, query_count):
    seqs = adapter_ids.shape[0]
    hbm = pl.BlockSpec(memory_space=pltpu.HBM)
    sm = pl.BlockSpec(memory_space=pltpu.SMEM)
    shapes = [(seqs,) + stack.shape[2:] for stack in stacks[:2] for _ in range(4)]
    shapes += [(seqs,) + stack.shape[1:] for stack in stacks[2:]]
    count = len(shapes)
    columns = [(seqs, query_count, TILE), (seqs, query_count + 2 * HALF, TILE)]
    found = pl.pallas_call(
        partial(prepare_kernel, seqs),
        in_specs=[sm] * 3 + [hbm] * len(stacks),
        out_specs=[hbm] * (count + 2),
        out_shape=[jax.ShapeDtypeStruct(shape, BF) for shape in shapes + columns],
        scratch_shapes=[pltpu.VMEM(shape, F32) for shape in shapes]
        + [pltpu.VMEM(shape, BF) for shape in shapes + columns]
        + [pltpu.SemaphoreType.DMA((seqs, count)), pltpu.SemaphoreType.DMA((count + 2,))],
        compiler_params=pltpu.CompilerParams(vmem_limit_bytes=VMEM),
        cost_estimate=pl.CostEstimate(flops=10**6, bytes_accessed=6 * 10**6, transcendentals=0),
        name="prepare",
    )(adapter_ids, lengths, base, *stacks)
    return found[:count], found[count], found[count + 1]


def adapted(x, weight, inner, up):
    return (mm(x, weight) + ADAPTER_SCALING * mm(inner, up)).astype(BF)


def begin_kernel(x_ref, table_ref, gain_ref, query_a, key_a, value_a, query_b, key_b, value_b,
                 query_w, key_w, value_w, query_hot, back_hot, key_hot,
                 query_out, key_out, value_out, query_rel_out, back_rel_out, key_rel_out, low_out,
                 query_u, key_u, value_u, query_pu, key_pu, *scratch):
    loaded = scratch[:6]
    stored = scratch[6:13]
    load_sems, store_sems = scratch[13:]
    query_w, key_w, value_w, query_hot, back_hot, key_hot = (
        Loaded(source, target, load_sems.at[index])
        for index, (source, target) in enumerate(zip((query_w, key_w, value_w, query_hot, back_hot, key_hot), loaded))
    )
    outs = [
        Stored(target, buffer, store_sems.at[index])
        for index, (target, buffer) in enumerate(
            zip((query_out, key_out, value_out, query_rel_out, back_rel_out, key_rel_out, low_out), stored)
        )
    ]
    x = x_ref[...]
    query_u[...] = mm(x, query_a[...], NT).astype(BF)
    key_u[...] = mm(x, key_a[...], NT).astype(BF)
    value_u[...] = mm(x, value_a[...], NT).astype(BF)
    values = table_ref[...]
    centered = values - jnp.mean(values, axis=1, keepdims=True)
    inverse = lax.rsqrt(jnp.mean(centered * centered, axis=1, keepdims=True) + EPSILON)
    low = (centered * inverse * gain_ref[...]).astype(BF)
    outs[6].put(low)
    query_pu[...] = mm(low, query_a[...], NT).astype(BF)
    key_pu[...] = mm(low, key_a[...], NT).astype(BF)
    outs[0].put(adapted(x, query_w(), query_u[...], query_b[...]))
    position_q = adapted(low, query_w(), query_pu[...], query_b[...])
    outs[1].put(adapted(x, key_w(), key_u[...], key_b[...]))
    position_k = adapted(low, key_w(), key_pu[...], key_b[...])
    outs[2].put(adapted(x, value_w(), value_u[...], value_b[...]))
    outs[3].put(mm(query_hot(), position_q).astype(BF))
    outs[4].put(mm(back_hot(), position_q).astype(BF))
    outs[5].put(mm(key_hot(), position_k).astype(BF))
    for out in outs:
        out.wait()


def begin(x, table, gain, weights, downs, ups, hots):
    rows_x, width = x.shape
    rank = ups[0].shape[0]
    places = table.shape[0]
    spans = hots[0].shape[0]
    vm = pl.BlockSpec(memory_space=pltpu.VMEM)
    hbm = pl.BlockSpec(memory_space=pltpu.HBM)
    large = [(rows_x, width)] * 3 + [(spans, width)] * 3 + [(places, width)]
    inner = jax.ShapeDtypeStruct((rows_x, rank), BF)
    position_inner = jax.ShapeDtypeStruct((places, rank), BF)
    sources = (*weights, hots[1], hots[2], hots[0])
    found = pl.pallas_call(
        begin_kernel,
        in_specs=[vm] * 9 + [hbm] * 6,
        out_specs=[hbm] * 7 + [vm] * 5,
        out_shape=[jax.ShapeDtypeStruct(shape, BF) for shape in large] + [inner] * 3 + [position_inner] * 2,
        scratch_shapes=[pltpu.VMEM(source.shape, BF) for source in sources]
        + [pltpu.VMEM(shape, BF) for shape in large]
        + [pltpu.SemaphoreType.DMA((6,)), pltpu.SemaphoreType.DMA((7,))],
        compiler_params=pltpu.CompilerParams(vmem_limit_bytes=VMEM),
        cost_estimate=pl.CostEstimate(
            flops=6 * rows_x * width * width + 10 * places * width * width,
            bytes_accessed=24 * places * width + 6 * width * width,
            transcendentals=0,
        ),
        name="begin",
    )(x, table, gain.reshape(1, width), *downs, *ups, *sources)
    return found[:3], found[3:6], found[6], found[7:10], found[10:]


def relative_kernel(q_ref, k_ref, pk_ref, pq_ref, qs_ref, ks_ref):
    tiles = HALF // TILE
    span = 2 * tiles
    below = lanes() + rows() < TILE
    column = lanes((HALF, TILE)) < HEAD_DIM
    for h in range(2):
        own = column if h == 0 else ~column
        km = jnp.where(own, k_ref[0], jnp.zeros_like(k_ref[0]))
        qm = jnp.where(own, q_ref[0], jnp.zeros_like(q_ref[0]))
        for d in range(1, span):
            pairs = [(t, d + t - tiles) for t in range(tiles) if 0 <= d + t - tiles < tiles]
            first, last = pairs[0][1], pairs[-1][1]
            key_rel = mm(
                km[first * TILE : (last + 1) * TILE], pq_ref[0, (span - 1 - d) * TILE : (span + 1 - d) * TILE, :], NT
            ).astype(BF)
            for t, j in pairs:
                part = key_rel[(j - first) * TILE : (j - first + 1) * TILE]
                ks_ref[0, h, t, :, j * TILE : (j + 1) * TILE] = skew(
                    jnp.where(below, part[:, TILE:], part[:, :TILE])
                ).T
        query_rel = mm(qm, pk_ref[0], NT).astype(BF)
        for t in range(tiles):
            part = query_rel[t * TILE : (t + 1) * TILE]
            for d in range(span + 1):
                here = part[:, min(d, span - 1) * TILE : (min(d, span - 1) + 1) * TILE]
                if 0 < d < span:
                    here = jnp.where(below, here, part[:, (d - 1) * TILE : d * TILE])
                qs_ref[0, h, t, :, d * TILE : (d + 1) * TILE] = skew(here)


def relative_scores(q, k, pk, pq):
    n, rq, width = q.shape
    pairs = width // TILE
    off = 2 * HALF
    tiles = rq // TILE
    return pl.pallas_call(
        relative_kernel,
        grid=(n, pairs),
        in_specs=[column_spec(rq), column_spec(rq), column_spec(off), column_spec(off)],
        out_specs=[head_spec(tiles, TILE, off + TILE), head_spec(tiles, TILE, HALF)],
        out_shape=[jax.ShapeDtypeStruct((n, 2 * pairs, tiles, TILE, off + TILE), BF),
                   jax.ShapeDtypeStruct((n, 2 * pairs, tiles, TILE, HALF), BF)],
        compiler_params=pltpu.CompilerParams(dimension_semantics=("arbitrary", "arbitrary"), vmem_limit_bytes=VMEM),
        cost_estimate=pl.CostEstimate(
            flops=16 * n * rq * off * width, bytes_accessed=60 * 10**6, transcendentals=0
        ),
        name="relative_scores",
    )(q, k, pk, pq)


def column_spec(r):
    return pl.BlockSpec((1, r, TILE), lambda s, p: (s, 0, p))


def head_spec(*shape):
    return pl.BlockSpec((1, 2) + shape, lambda s, p: (s, p) + (0,) * len(shape))


def forward_kernel(mapped, pairs, q_ref, k_ref, v_ref, pq_ref, qhot_ref, kbias_ref, qs_ref, ko_ref, *refs):
    if mapped:
        kh_ref, vh_ref, ctx_ref, p_ref, ctxf_ref, inv_ref = refs[:6]
    else:
        before, after, key_w, value_w, key_a, value_a, key_b, value_b = refs[:8]
        ctx_ref, p_ref, ctxf_ref, inv_ref, kh_ref, vh_ref, key_u, value_u = refs[8:16]
    prepared = (refs[-7:-4], refs[-4:-1])
    s_ref = refs[-1]
    step = pl.program_id(1)
    tiles = HALF // TILE
    span = 2 * tiles
    width = (span + 1) * TILE
    flip = flip_matrix()
    flips = jnp.concatenate([flip, flip], axis=1)
    factor = math.log2(math.e) / math.sqrt(3 * HEAD_DIM)
    below = lanes() + rows() < TILE
    place = lanes() + rows()
    tcol = lanes() < HEAD_DIM

    def halo_inners():
        for side, x in ((0, before), (1, after)):
            at = slice(side * HALF, (side + 1) * HALF)
            key_u[at] = mm(x[...], key_a[...], NT).astype(BF)
            value_u[at] = mm(x[...], value_a[...], NT).astype(BF)

    def halo_map(side):
        weights = jnp.concatenate([key_w[...], value_w[...]], axis=1)
        nothing = jnp.zeros_like(key_b[...])
        ups = jnp.concatenate(
            [jnp.concatenate([key_b[...], nothing], axis=1), jnp.concatenate([nothing, value_b[...]], axis=1)], axis=0
        )
        at = slice(side * HALF, (side + 1) * HALF)
        inner = jnp.concatenate([key_u[at], value_u[at]], axis=1)
        both = adapted((before, after)[side][...], weights, inner, ups)
        kh_ref[0, at] = both[:, :TILE]
        vh_ref[0, at] = both[:, TILE:]

    def prepare_head(h, target):
        kz_ref, vz_ref, ks_ref = target
        k = with_halo(k_ref, kh_ref)
        v = with_halo(v_ref, vh_ref)
        own = lanes(k.shape) < HEAD_DIM
        halo_own = lanes(kh_ref.shape[1:]) < HEAD_DIM
        if h == 1:
            own, halo_own = ~own, ~halo_own
        kz_ref[h] = jnp.where(own, k, kbias_ref[0])
        vz_ref[h] = jnp.where(own, v, jnp.ones_like(v))
        km = jnp.where(halo_own, kh_ref[0], jnp.zeros_like(kh_ref[0]))
        for d in range(span + 1):
            seen = [(t, d + t if d + t < tiles else d + t - tiles) for t in range(tiles) if not tiles <= d + t < 2 * tiles]
            if not seen:
                continue
            low = max(span - 1 - d, 0) * TILE
            high = min(span + 1 - d, span) * TILE
            first, last = seen[0][1], seen[-1][1]
            key_rel = mm(km[first * TILE : (last + 1) * TILE], pq_ref[0, low:high, :], NT).astype(BF)
            for t, j in seen:
                part = key_rel[(j - first) * TILE : (j - first + 1) * TILE]
                if 0 < d < span:
                    part = jnp.where(below, part[:, TILE:], part[:, :TILE])
                w = d if d < tiles else d - tiles
                ks_ref[h, t, :, w * TILE : (w + 1) * TILE] = skew(part).T

    def scores(t, h, source):
        kz_ref, _, ks_ref = source
        at = slice(t * TILE, (t + 1) * TILE)
        edge = (tiles - t) * TILE
        q_side = mm(flip, jnp.where(tcol if h == 0 else ~tcol, q_ref[0, at, :], qhot_ref[0, at, :])).astype(BF)
        key_side = jnp.concatenate([ks_ref[h, t, :, :edge], ko_ref[0, h, t], ks_ref[h, t, :, edge:]], axis=1)
        relative = jnp.concatenate([qs_ref[0, h, t], key_side], axis=0)
        s_ref[2 * (t % 2) + h] = mm(q_side, kz_ref[h, t * TILE : t * TILE + width, :], NT) + mm(flips, relative)

    def softmax(t, h, source):
        slot = 2 * (t % 2) + h
        at = slice(t * TILE, (t + 1) * TILE)
        own = tcol if h == 0 else ~tcol
        s_ref[slot, :, :TILE] = jnp.where(place > TILE - 1, s_ref[slot, :, :TILE], NEGATIVE)
        s_ref[slot, :, span * TILE :] = jnp.where(place < TILE - 1, s_ref[slot, :, span * TILE :], NEGATIVE)
        middle = s_ref[slot, :, tiles * TILE : (tiles + 1) * TILE]
        s_ref[slot, :, tiles * TILE : (tiles + 1) * TILE] = jnp.where(
            (place == TILE - 1) & (middle < 0.1 * NEGATIVE), 0.0, middle
        )
        top = s_ref[slot, :, :TILE]
        for d in range(1, span + 1):
            top = jnp.maximum(top, s_ref[slot, :, d * TILE : (d + 1) * TILE])
        peak = jnp.max(top, axis=1, keepdims=True)
        prob = jnp.exp2((s_ref[slot] - peak) * factor).astype(BF)
        a = t % 2
        row_at = slice(a * TILE, (a + 1) * TILE)
        p_ref[0, h, t // 2, row_at, a * TILE : a * TILE + width] = prob
        p_ref[0, h, t // 2, row_at, (1 - a) * width : (1 - a) * width + TILE] = jnp.zeros((TILE, TILE), BF)
        total = mm(prob, source[1][h, t * TILE : t * TILE + width, :])
        inv = 1.0 / jnp.where(own, pltpu.roll(total, HEAD_DIM, 1), total)
        inv_ref[0, h, at, :] = inv
        return total * inv

    @pl.when(step == 0)
    def _():
        if not mapped:
            halo_inners()
            halo_map(0)
            halo_map(1)
        for h in range(2):
            prepare_head(h, prepared[0])

    def both(target, source):
        between = []
        if target is not None:
            between = [lambda: prepare_head(0, target), lambda: prepare_head(1, target)]
        if target is not None and not mapped:
            between = [lambda: (halo_map(0), halo_map(1))] + between
        for h in range(2):
            scores(0, h, source)
        for t in range(tiles):
            outs = []
            for h in range(2):
                if t + 1 < tiles:
                    scores(t + 1, h, source)
                outs.append(softmax(t, h, source))
            if between:
                between.pop(0)()
            at = slice(t * TILE, (t + 1) * TILE)
            ctx = jnp.where(tcol, outs[0], outs[1])
            ctxf_ref[0, at, :] = ctx
            ctx_ref[0, at, :] = mm(flip, ctx.astype(BF)).astype(BF)

    for parity in range(2):

        @pl.when((step > 0) & (step < pairs) & (step % 2 == parity))
        def _():
            both(prepared[parity], prepared[1 - parity])

    @pl.when(step == pairs)
    def _():
        both(None, prepared[(pairs - 1) % 2])


def attention_forward(q, k, v, pq, qhot, kbias, query_scores, key_scores, halo):
    n, rq, width = q.shape
    off = 2 * HALF
    rk = rq + off
    pairs = width // TILE
    tiles = rq // TILE

    def coming(r):
        return pl.BlockSpec((1, r, TILE), lambda s, p: (s, 0, jnp.minimum(p, pairs - 1)))

    def current(r):
        return pl.BlockSpec((1, r, TILE), lambda s, p: (s, 0, jnp.maximum(p - 1, 0)))

    def current_heads(*shape):
        return pl.BlockSpec((1, 2) + shape, lambda s, p: (s, jnp.maximum(p - 1, 0)) + (0,) * len(shape))

    def whole(r):
        return pl.BlockSpec((1, r, TILE), lambda s, p: (s, 0, 0))

    mapped = len(halo) == 2
    in_specs = [current(rq), coming(rq), coming(rq), coming(off), whole(rq), whole(rk),
                current_heads(tiles, TILE, off + TILE), current_heads(tiles, TILE, HALF)]
    out_specs = [current(rq), current_heads(tiles // 2, 2 * TILE, off + 2 * TILE), current(rq), current_heads(rq, TILE)]
    out_shape = [jax.ShapeDtypeStruct((n, rq, width), BF),
                 jax.ShapeDtypeStruct((n, 2 * pairs, tiles // 2, 2 * TILE, off + 2 * TILE), BF),
                 jax.ShapeDtypeStruct((n, rq, width), F32),
                 jax.ShapeDtypeStruct((n, 2 * pairs, rq, TILE), F32)]
    if mapped:
        in_specs += [coming(off)] * 2
    else:
        rank = halo[4].shape[0]

        def once(*shape):
            return pl.BlockSpec(shape, lambda s, p: (0,) * len(shape))

        def columns(r):
            return pl.BlockSpec((r, TILE), lambda s, p: (0, jnp.minimum(p, pairs - 1)))

        in_specs += [once(HALF, width)] * 2 + [columns(width)] * 2 + [once(rank, width)] * 2 + [columns(rank)] * 2
        out_specs += [coming(off)] * 2 + [once(off, rank)] * 2
        out_shape += [jax.ShapeDtypeStruct((n, off, width), BF)] * 2 + [jax.ShapeDtypeStruct((off, rank), BF)] * 2
    return pl.pallas_call(
        partial(forward_kernel, mapped, pairs),
        grid=(n, pairs + 1),
        in_specs=in_specs,
        out_specs=out_specs,
        out_shape=out_shape,
        scratch_shapes=[pltpu.VMEM((2, rk, TILE), BF), pltpu.VMEM((2, rk, TILE), BF),
                        pltpu.VMEM((2, tiles, TILE, HALF + TILE), BF)] * 2
        + [pltpu.VMEM((4, TILE, off + TILE), F32)],
        compiler_params=pltpu.CompilerParams(dimension_semantics=("arbitrary", "arbitrary"), vmem_limit_bytes=VMEM),
        cost_estimate=pl.CostEstimate(
            flops=32 * n * rq * off * width, bytes_accessed=60 * 10**6, transcendentals=0
        ),
        name="attention_forward",
    )(q, k, v, pq, qhot, kbias, query_scores, key_scores, *halo)


def spread_kernel(group, head_ref, ids_ref, late_hbm, ff_hbm, table_hbm, places_hbm, grad_hbm, gain_ref,
                  table_out, down_out, up_out, expand_down, expand_up, reduce_down, reduce_up, grad_out,
                  late_ref, ff_ref, table_ref, places_ref, grad_ref, table_made, down_made, up_made,
                  expand_down_made, expand_up_made, reduce_down_made, reduce_up_made, sems, out_sems):
    cores, peers, rank, part = late_ref.shape
    late_in = Loaded(late_hbm, late_ref, sems.at[3])
    ff_in = Loaded(ff_hbm, ff_ref, sems.at[4])
    table_in = Loaded(table_hbm, table_ref, sems.at[5])
    grad_in = Loaded(grad_hbm, grad_ref, sems.at[1])
    grad_done = Stored(grad_out, grad_ref, sems.at[2])
    down_done = Stored(down_out, down_made, out_sems.at[0])
    up_done = Stored(up_out, up_made, out_sems.at[1])
    table_done = Stored(table_out, table_made, out_sems.at[2])
    ff_done = [
        Stored(target, made, out_sems.at[3 + index])
        for index, (target, made) in enumerate(
            (
                (expand_down, expand_down_made),
                (expand_up, expand_up_made),
                (reduce_down, reduce_down_made),
                (reduce_up, reduce_up_made),
            )
        )
    ]
    width = table_ref.shape[3]
    ff = expand_up_made.shape[2]
    rest = ff_ref.shape[3]
    own = places_ref.shape[0]
    fetch = pltpu.make_async_copy(places_hbm.at[pl.ds(pl.multiple_of(head_ref[0] * own, own), own)], places_ref, sems.at[0])
    fetch.start()
    first = head_ref[0] * group
    weights = [
        [jnp.where(ids_ref[s, :1, :1] == (first + a).astype(F32), 1.0, 0.0) for a in range(group)] for s in range(cores)
    ]

    def fill(out, a, source, pieces):
        for column, piece in pieces:
            value = sum(weights[s][a] * source[s, piece[0], :, piece[1]].astype(F32) for s in range(cores))
            out[:, column] = value

    per = width // part
    starts = (0, width, width + ff, width + 2 * ff)
    late_in()
    for member in range(8):
        for a in range(group):
            out = (down_made if member < 4 else up_made).at[member % 4, a]
            fill(out, a, late_ref, [
                (slice(half * part, (half + 1) * part), (member * per + half, slice(0, part))) for half in range(per)
            ])
        if member == 3:
            down_done.copy.start()
    up_done.copy.start()
    ff_in()
    for done, start in zip(ff_done, starts):
        count = done.buffer.shape[2]
        pieces = []
        at = start
        while at < start + count:
            peer, offset = at // rest, at % rest
            length = min(rest - offset, start + count - at)
            pieces.append((slice(at - start, at - start + length), (peer, slice(offset, offset + length))))
            at += length
        for a in range(group):
            fill(done.buffer.at[a], a, ff_ref, pieces)
        done.copy.start()
    table_in()
    grad_in()
    grad_done.copy.start()
    fetch.wait()
    values = places_ref[...]
    centered = values - jnp.mean(values, axis=1, keepdims=True)
    inverse = lax.rsqrt(jnp.mean(centered * centered, axis=1, keepdims=True) + EPSILON)
    normed = centered * inverse
    upstream = table_ref[...].reshape(values.shape).astype(F32) * gain_ref[...]
    table_made[...] = inverse * (
        upstream
        - jnp.mean(upstream, axis=1, keepdims=True)
        - normed * jnp.mean(upstream * normed, axis=1, keepdims=True)
    )
    table_done.copy.start()
    for done in (grad_done, down_done, up_done, table_done, *ff_done):
        done.wait()


def spread_all(group, head, ids, late, ff_late, table, places, grad, gain, ff):
    rank = late.shape[2]
    width = table.shape[3]
    own = (places.shape[0] * group // ADAPTERS, width)
    vm = pl.BlockSpec(memory_space=pltpu.VMEM)
    sm = pl.BlockSpec(memory_space=pltpu.SMEM)
    hbm = pl.BlockSpec(memory_space=pltpu.HBM)

    shapes = [own] + [(4, group, rank, width)] * 2
    shapes += [(group, rank, width), (group, rank, ff), (group, rank, ff), (group, rank, width)]

    def out(*shape):
        return jax.ShapeDtypeStruct(shape, F32)

    return pl.pallas_call(
        partial(spread_kernel, group),
        in_specs=[sm, vm] + [hbm] * 5 + [vm],
        out_specs=[hbm] * 8,
        out_shape=[out(*shape) for shape in shapes] + [out(*grad.shape)],
        scratch_shapes=[pltpu.VMEM(array.shape, BF) for array in (late, ff_late, table)]
        + [pltpu.VMEM(own, F32), pltpu.VMEM(grad.shape, F32)]
        + [pltpu.VMEM(shape, F32) for shape in shapes]
        + [pltpu.SemaphoreType.DMA((6,)), pltpu.SemaphoreType.DMA((7,))],
        compiler_params=pltpu.CompilerParams(vmem_limit_bytes=VMEM),
        name="spread_all",
    )(head, ids, late, ff_late, table, places, grad, gain.reshape(1, width))


def backward_kernel(handed, q_ref, k_ref, kh_ref, v_ref, vh_ref, pk_ref, pq_ref, p_ref, g_ref, ctxf_ref, inv_ref, *refs):
    if handed:
        layer_ref, layer_out, *refs = refs
        layer_out[...] = layer_ref[...]
    dq_ref, dk_ref, dkh_ref, dv_ref, dvh_ref, dpk_ref, dpq_ref, kx_ref, vx_ref = refs[:9]
    qr_ref, gr_ref, e_ref, gc_ref, gk_ref, dvt_ref, dkt_ref = refs[9:]
    rows_q = q_ref.shape[1]
    rows_k = kx_ref.shape[0]
    kx_ref[...] = with_halo(k_ref, kh_ref)
    vx_ref[...] = with_halo(v_ref, vh_ref)
    tiles = rows_q // TILE
    key_tiles = rows_k // TILE
    span = 2 * HALF // TILE
    wide = (span + 2) * TILE
    flip = flip_matrix()
    scale = 1.0 / math.sqrt(3 * HEAD_DIM)
    tcol = lanes() < HEAD_DIM
    qcol = lanes((rows_q, TILE)) < HEAD_DIM
    over = lanes() > rows()
    under = lanes() >= rows()

    @pl.when((pl.program_id(0) == 0) & (pl.program_id(1) == 0))
    def _():
        gk_ref[...] = jnp.zeros_like(gk_ref)

    for t in range(tiles):
        at = slice(t * TILE, (t + 1) * TILE)
        qr_ref[at] = mm(flip, q_ref[0, at]).astype(BF)
        gr_ref[at] = mm(flip, g_ref[0, at]).astype(BF)
    q_rev = qr_ref[...]
    g_rev = gr_ref[...]
    q_turned = q_rev.T
    k_turned = kx_ref[...].T
    product = g_rev.astype(F32) * ctxf_ref[0]
    dvt_ref[...] = jnp.zeros_like(dvt_ref)
    dkt_ref[...] = jnp.zeros_like(dkt_ref)
    zero = jnp.zeros((TILE, TILE), BF)
    dq_main = [[], []]
    dq_parts = [None, None]
    dk_tiles = [[], []]

    def of_head(h):
        own = qcol if h == 0 else ~qcol
        inv = inv_ref[0, h]
        delta = jnp.sum(jnp.where(own, product, 0.0), axis=1, keepdims=True) * inv
        g_turned = (g_rev.astype(F32) * inv).astype(BF).T[h * HEAD_DIM : (h + 1) * HEAD_DIM]
        return jnp.where(own, g_rev, jnp.zeros_like(g_rev)), inv, delta, g_turned

    heads = [of_head(h) for h in range(2)]

    def errors(h, u):
        g_masked, inv, delta, g_turned = heads[h]
        part = slice(h * HEAD_DIM, (h + 1) * HEAD_DIM)
        at = slice(u * 2 * TILE, (u + 1) * 2 * TILE)
        window = slice(u * 2 * TILE, u * 2 * TILE + wide)
        prob = p_ref[0, h, u]
        g_probs = mm(g_masked[at], vx_ref[window], NT)
        inv_u = jnp.concatenate([inv[at]] * (span + 2), axis=1)
        delta_u = jnp.concatenate([delta[at]] * (span + 2), axis=1)
        e = (prob.astype(F32) * (g_probs * inv_u - delta_u)).astype(BF)
        e_ref[h, u] = e
        dvt_ref[part, window] += mm(g_turned[:, at], prob)
        dkt_ref[part, window] += mm(q_turned[part, at], e)
        dq_main[h].append(mm(e, kx_ref[window]))

    def error(h, t, d):
        a = t % 2
        return e_ref[h, t // 2, a * TILE : (a + 1) * TILE, (a + d) * TILE : (a + d + 1) * TILE]

    def distances(h, t):
        here = None
        for d in range(span + 1):
            block = pltpu.roll(error(h, t, d), 1, 1, stride=1, stride_axis=0)
            if d > 0:
                gc_ref[h, t * TILE : (t + 1) * TILE, (d - 1) * TILE : d * TILE] = jnp.where(over, block, here)
            here = block

    def end_queries(h):
        part = slice(h * HEAD_DIM, (h + 1) * HEAD_DIM)
        dq_parts[h] = jnp.concatenate(dq_main[h], axis=0) + mm(gc_ref[h], pk_ref[0])
        dpk_ref[0, part, :] = (mm(q_turned[part], gc_ref[h]) * scale).astype(BF)

    def keys(h, j):
        spun = {j - t: skew(error(h, t, j - t).T) for t in range(tiles) if 0 <= j - t <= span}
        low = max(min(spun) - 1, 0)
        high = min(max(spun), span - 1)
        at = slice(j * TILE, (j + 1) * TILE)
        for c in range(low, high + 1):
            gk_ref[h, at, c * TILE : (c + 1) * TILE] = jnp.where(under, spun.get(c + 1, zero), spun.get(c, zero))
        cols = slice(low * TILE, (high + 1) * TILE)
        dk_tiles[h].append(mm(gk_ref[h, at, cols], pq_ref[0, cols]))

    def end_keys(h):
        part = slice(h * HEAD_DIM, (h + 1) * HEAD_DIM)
        for c in range(0, span, 2):
            near = slice(c * TILE, (c + tiles + 2) * TILE)
            cols = slice(c * TILE, (c + 2) * TILE)
            dpq_ref[0, part, cols] = (mm(k_turned[part, near], gk_ref[h, near, cols]) * scale).astype(BF)

    for h in range(2):
        for u in range(tiles // 2):
            errors(h, u)
            distances(h, 2 * u)
            distances(h, 2 * u + 1)
        end_queries(h)
        for j in range(key_tiles):
            keys(h, j)
        end_keys(h)
    dk_parts = [jnp.concatenate(found, axis=0) for found in dk_tiles]
    dq = (jnp.where(qcol, dq_parts[0], dq_parts[1]) * scale).astype(BF)
    for t in range(tiles):
        at = slice(t * TILE, (t + 1) * TILE)
        dq_ref[0, at] = mm(flip, dq[at]).astype(BF)
    kcol = lanes((rows_k, TILE)) < HEAD_DIM
    dk = ((dkt_ref[...].T + jnp.where(kcol, dk_parts[0], dk_parts[1])) * scale).astype(BF)
    dv = dvt_ref[...].astype(BF).T
    for whole, own_ref, halo_ref in ((dk, dk_ref, dkh_ref), (dv, dv_ref, dvh_ref)):
        halo_ref[0, :HALF] = whole[:HALF]
        own_ref[0] = whole[HALF : HALF + rows_q]
        halo_ref[0, HALF:] = whole[HALF + rows_q :]


def attention_backward(q, k, k_halo, v, v_halo, pk, pq, probs, g, ctxf, inv, *layer):
    n, rq, width = q.shape
    off = 2 * HALF
    rk = rq + off
    pairs = width // TILE
    wide = off + 2 * TILE
    def col(r):
        return pl.BlockSpec((1, r, TILE), lambda s, p: (s, 0, p))
    def row(r):
        return pl.BlockSpec((1, TILE, r), lambda s, p: (s, p, 0))
    return pl.pallas_call(
        partial(backward_kernel, len(layer) > 0),
        grid=(n, pairs),
        in_specs=[col(rq), col(rq), col(off), col(rq), col(off), col(off), col(off),
                  pl.BlockSpec((1, 2, rq // (2 * TILE), 2 * TILE, wide), lambda s, p: (s, p, 0, 0, 0)),
                  col(rq), col(rq),
                  pl.BlockSpec((1, 2, rq, TILE), lambda s, p: (s, p, 0, 0))] + [col(rq)] * len(layer),
        out_specs=[col(rq)] * len(layer) + [col(rq), col(rq), col(off), col(rq), col(off), row(off), row(off)],
        out_shape=[jax.ShapeDtypeStruct(array.shape, array.dtype) for array in layer]
        + [jax.ShapeDtypeStruct((n, rq, width), BF),
                   jax.ShapeDtypeStruct((n, rq, width), BF),
                   jax.ShapeDtypeStruct((n, off, width), BF),
                   jax.ShapeDtypeStruct((n, rq, width), BF),
                   jax.ShapeDtypeStruct((n, off, width), BF),
                   jax.ShapeDtypeStruct((n, width, off), BF),
                   jax.ShapeDtypeStruct((n, width, off), BF)],
        scratch_shapes=[pltpu.VMEM((rk, TILE), BF), pltpu.VMEM((rk, TILE), BF), pltpu.VMEM((rq, TILE), BF), pltpu.VMEM((rq, TILE), BF),
                        pltpu.VMEM((2, rq // (2 * TILE), 2 * TILE, wide), BF),
                        pltpu.VMEM((2, rq, off), BF),
                        pltpu.VMEM((2, rk, off), BF),
                        pltpu.VMEM((TILE, rk), F32), pltpu.VMEM((TILE, rk), F32)],
        compiler_params=pltpu.CompilerParams(dimension_semantics=("arbitrary", "arbitrary"), vmem_limit_bytes=VMEM),
        name="attention_backward",
    )(q, k, k_halo, v, v_halo, pk, pq, probs, g, ctxf, inv, *layer)


def gather_rows(left, right):
    return lax.dot_general(left, right, (((0,), (0,)), ((), ())), preferred_element_type=F32)


def whereabouts(shape):
    groups, blocks = shape[:2]
    seq, head, core = lax.axis_index("seq"), lax.axis_index("head"), lax.axis_index("batch")
    return blocks * groups, seq * groups + head, lambda p: (p // groups, p % groups, core), (seq, head, core)


def signal(barrier, device):
    pl.semaphore_signal(barrier, inc=1, device_id=device, device_id_type=MESH)


def remote(source, target, send_sem, recv_sem, device):
    return pltpu.make_async_remote_copy(
        src_ref=source, dst_ref=target, send_sem=send_sem, recv_sem=recv_sem, device_id=device, device_id_type=MESH
    )


def each(first, end, step):
    lax.fori_loop(first, end, lambda k, carry: (step(k), carry)[1], 0)


def finish_kernel(shape, names, *refs):
    groups, blocks, cores, rank = shape
    r = SimpleNamespace(**dict(zip(names, refs)))
    peers, me, place, (seq, head, core) = whereabouts(shape)
    partner = (seq, head, 1 - core)
    width = r.table_out.shape[3]

    held = SimpleNamespace()
    for index, name in enumerate(names[:LOADS]):
        target = refs[len(refs) - LOADS + index]
        setattr(held, name, Loaded(refs[index], target, r.load_sems.at[index], start=index < FIRST_LOADS))

    barrier = pltpu.get_barrier_semaphore()
    signal(barrier, partner)
    each(1, peers, lambda k: signal(barrier, place((me + k) % peers)))

    def inner_grad(gradient, up):
        return (ADAPTER_SCALING * mm(gradient, up[...], NT)).astype(BF)

    halo_buf, halo_recv, halo_sems = r.halo_buf, r.halo_recv, r.halo_sems
    half = HALF // 2

    def crossing(side, piece):
        there = place(jnp.maximum(me - 1, 0) if side == 0 else jnp.minimum(me + 1, peers - 1))
        return remote(
            halo_buf.at[side, piece], halo_recv.at[1 - side, piece],
            halo_sems.at[4 * side + 2 * piece], halo_sems.at[4 * side + 2 * piece + 1], there,
        )

    def start_crossing(side, piece):
        @pl.when(me > 0 if side == 0 else me < peers - 1)
        def _():
            crossing(side, piece).start()
    key_halo, value_halo = held.key_halo(), held.value_halo()
    key_hu, value_hu = inner_grad(key_halo, r.key_b), inner_grad(value_halo, r.value_b)
    key_w, value_w = held.key_w(), held.value_w()
    for name in names[FIRST_LOADS:LOADS]:
        getattr(held, name).copy.start()

    def map_piece(piece):
        for side in range(2):
            start = side * HALF + piece * half
            at = slice(start, start + half)
            halo_buf[side, piece] = (
                mm(key_halo[at], key_w, NT)
                + mm(value_halo[at], value_w, NT)
                + mm(key_hu[at], r.key_a[...])
                + mm(value_hu[at], r.value_a[...])
            ).astype(BF)
            if piece == 0 and side == 0:
                pl.semaphore_wait(barrier, peers)
            start_crossing(side, piece)

    map_piece(0)

    def give_f(p):
        return remote(r.ff, r.ff_out.at[core, me], r.spread_f.at[p], r.arrive_f.at[me], place(p))

    def on_f(p):
        return remote(r.ff_out.at[core, p], r.ff_out.at[core, p], r.pass_f.at[p], r.other_f.at[p], partner)

    def got_f(k):
        p = (me + peers - k) % peers
        remote(r.ff, r.ff_out.at[core, p], r.spread_f.at[p], r.arrive_f.at[p], place(p)).wait_recv()
        on_f(p).start()

    def end_f(k):
        p = k - 1
        remote(r.ff_out.at[1 - core, p], r.ff_out.at[1 - core, p], r.pass_f.at[p], r.other_f.at[p], partner).wait_recv()
        on_f(p).wait_send()

    r.ff_out[core, me] = r.ff[...]
    each(1, peers, lambda k: give_f((me + k) % peers).start())
    on_f(me).start()

    table_ref, stage_ref, recv_ref, sum_ref = r.table, r.stage, r.recv, r.sum
    core_ref, core_sems = r.core, r.core_sems
    position_q = mm(held.back_hot(), held.query_rel_g(), NT).astype(BF)
    position_k = mm(held.key_hot(), held.key_rel_g(), NT).astype(BF)
    query_pg, key_pg = inner_grad(position_q, r.query_b), inner_grad(position_k, r.key_b)
    query_w = held.query_w()
    table = (
        mm(position_q, query_w, NT)
        + mm(position_k, key_w, NT)
        + mm(query_pg, r.query_a[...])
        + mm(key_pg, r.key_a[...])
    ).astype(BF)
    for group in range(groups):
        for block in range(blocks):
            for side in range(cores):
                start = ((group * blocks + block) * cores + side) * rank
                table_ref[side, block * groups + group] = table[start : start + rank]
    swap = remote(table_ref.at[1 - core], core_ref, core_sems.at[0], core_sems.at[1], partner)
    swap.start()
    r.ids_out[core] = r.own_id[...]
    tell = remote(r.own_id, r.ids_out.at[core], core_sems.at[2], core_sems.at[3], partner)
    tell.start()

    x, x_before, x_after, low = held.x(), held.x_before(), held.x_after(), held.low()
    query_g, key_g, value_g = held.query_g(), held.key_g(), held.value_g()
    query_gu, key_gu, value_gu = inner_grad(query_g, r.query_b), inner_grad(key_g, r.key_b), inner_grad(value_g, r.value_b)
    def of_halo(inner):
        return gather_rows(inner[:HALF], x_before) + gather_rows(inner[HALF:], x_after)

    pieces = [
        gather_rows(query_gu, x) + gather_rows(query_pg, low),
        gather_rows(key_gu, x) + of_halo(key_hu) + gather_rows(key_pg, low),
        gather_rows(value_gu, x) + of_halo(value_hu),
        r.out_ga[...],
        ADAPTER_SCALING * (gather_rows(r.query_u[...], query_g) + gather_rows(r.query_pu[...], position_q)),
        ADAPTER_SCALING
        * (
            gather_rows(r.key_u[...], key_g)
            + gather_rows(r.key_uh[...], key_halo)
            + gather_rows(r.key_pu[...], position_k)
        ),
        ADAPTER_SCALING * (gather_rows(r.value_u[...], value_g) + gather_rows(r.value_uh[...], value_halo)),
        r.out_gb[...],
    ]
    part = len(pieces) * width // peers
    per = width // part
    for index, piece in enumerate(pieces):
        for cut in range(per):
            stage_ref[index * per + cut, :, width : width + part] = piece[:, cut * part : (cut + 1) * part].astype(BF)

    send_sems, recv_sems = r.send_sems, r.recv_sems
    swap.wait()

    def to_peer(p):
        return remote(stage_ref.at[p], recv_ref.at[me], send_sems.at[p], recv_sems.at[me], place(p))

    def send(k):
        p = (me + k) % peers
        stage_ref[p, :, :width] = (table_ref[core, p].astype(F32) + core_ref[p].astype(F32)).astype(BF)
        to_peer(p).start()

    each(1, peers, send)
    map_piece(1)
    each(1, peers, got_f)
    sum_ref[:, :width] = table_ref[core, me].astype(F32) + core_ref[me].astype(F32)
    sum_ref[:, width:] = stage_ref[me, :, width:].astype(F32)

    grad_ref = r.grad_out
    grad_ref[...] = (
        held.grad_one()
        + mm(query_g, query_w, NT)
        + mm(key_g, key_w, NT)
        + mm(value_g, value_w, NT)
        + mm(query_gu, r.query_a[...])
        + mm(key_gu, r.key_a[...])
        + mm(value_gu, r.value_a[...])
    )

    def take(k):
        p = (me + peers - k) % peers
        remote(stage_ref.at[p], recv_ref.at[p], send_sems.at[p], recv_sems.at[p], place(p)).wait_recv()
        sum_ref[...] += recv_ref[p].astype(F32)

    each(1, peers, take)
    mine_t, mine_l, table_out, late_out = r.mine_t, r.mine_l, r.table_out, r.late_out
    mine_t[...] = sum_ref[:, :width].astype(BF)
    mine_l[...] = sum_ref[:, width:].astype(BF)
    late_out[core, me] = mine_l[...]
    table_out[seq, core] = mine_t[...]

    def give_l(p):
        return remote(mine_l, late_out.at[core, me], r.spread_l.at[p], r.arrive_l.at[me], place(p))

    def give_t(s):
        return remote(mine_t, table_out.at[seq, core], r.spread_t.at[s], r.arrive_t.at[seq], (s, head, core))

    each(1, peers, lambda k: give_l((me + k) % peers).start())
    each(1, blocks, lambda k: give_t((seq + k) % blocks).start())

    def on_l(p):
        return remote(late_out.at[core, p], late_out.at[core, p], r.pass_l.at[p], r.other_l.at[p], partner)

    def on_t(s):
        return remote(table_out.at[s, core], table_out.at[s, core], r.pass_t.at[s], r.other_t.at[s], partner)

    on_l(me).start()
    on_t(seq).start()

    def got_l(k):
        p = (me + peers - k) % peers
        remote(mine_l, late_out.at[core, p], r.spread_l.at[p], r.arrive_l.at[p], place(p)).wait_recv()
        on_l(p).start()

    def got_t(k):
        s = (seq + blocks - k) % blocks
        remote(mine_t, table_out.at[s, core], r.spread_t.at[s], r.arrive_t.at[s], (s, head, core)).wait_recv()
        on_t(s).start()

    each(1, peers, got_l)
    each(1, blocks, got_t)

    @pl.when(me > 0)
    def _():
        for piece in range(2):
            crossing(0, piece).wait_send()
            crossing(1, piece).wait_recv()
        grad_ref[...] += halo_recv[0].astype(F32).reshape(HALF, width)

    @pl.when(me < peers - 1)
    def _():
        for piece in range(2):
            crossing(1, piece).wait_send()
            crossing(0, piece).wait_recv()
        grad_ref[...] += halo_recv[1].astype(F32).reshape(HALF, width)

    def end_l(k):
        p = k - 1
        remote(late_out.at[1 - core, p], late_out.at[1 - core, p], r.pass_l.at[p], r.other_l.at[p], partner).wait_recv()
        on_l(p).wait_send()

    def end_t(k):
        s = k - 1
        remote(table_out.at[s, 1 - core], table_out.at[s, 1 - core], r.pass_t.at[s], r.other_t.at[s], partner).wait_recv()
        on_t(s).wait_send()

    tell.wait()
    each(1, peers + 1, end_f)
    each(1, peers + 1, end_l)
    each(1, blocks + 1, end_t)

    def sent(k):
        p = (me + k) % peers
        to_peer(p).wait_send()
        give_l(p).wait_send()
        give_f(p).wait_send()

    each(1, peers, sent)
    each(1, blocks, lambda k: give_t((seq + k) % blocks).wait_send())


LOADS = 17
FIRST_LOADS = 4


def finish(shape, **arrays):
    groups, blocks, cores, rank = shape
    peers = groups * blocks
    rows, width = arrays[list(arrays)[LOADS - 1]].shape
    share = 8 * width // peers
    ff = arrays[list(arrays)[-1]]
    vm = pl.BlockSpec(memory_space=pltpu.VMEM)
    hbm = pl.BlockSpec(memory_space=pltpu.HBM)
    dma = pltpu.SemaphoreType.DMA
    outputs = dict(
        grad_out=jax.ShapeDtypeStruct((rows, width), F32),
        table_out=jax.ShapeDtypeStruct((blocks, cores, rank, width), BF),
        late_out=jax.ShapeDtypeStruct((cores, peers, rank, share), BF),
        ids_out=jax.ShapeDtypeStruct((cores, 8, TILE), F32),
        ff_out=jax.ShapeDtypeStruct((cores, peers) + ff.shape, BF),
    )
    scratch = dict(
        load_sems=dma((LOADS,)),
        halo_buf=pltpu.VMEM((2, 2, HALF // 2, width), BF),
        halo_recv=pltpu.VMEM((2, 2, HALF // 2, width), BF),
        halo_sems=dma((8,)),
        table=pltpu.VMEM((cores, peers, rank, width), BF),
        core=pltpu.VMEM((peers, rank, width), BF),
        stage=pltpu.VMEM((peers, rank, width + share), BF),
        recv=pltpu.VMEM((peers, rank, width + share), BF),
        sum=pltpu.VMEM((rank, width + share), F32),
        mine_t=pltpu.VMEM((rank, width), BF),
        mine_l=pltpu.VMEM((rank, share), BF),
        core_sems=dma((4,)),
        send_sems=dma((peers,)),
        recv_sems=dma((peers,)),
        spread_l=dma((peers,)),
        arrive_l=dma((peers,)),
        pass_l=dma((peers,)),
        other_l=dma((peers,)),
        spread_t=dma((blocks,)),
        arrive_t=dma((blocks,)),
        pass_t=dma((blocks,)),
        other_t=dma((blocks,)),
        spread_f=dma((peers,)),
        arrive_f=dma((peers,)),
        pass_f=dma((peers,)),
        other_f=dma((peers,)),
    )
    names = (*arrays, *outputs, *scratch)
    kept = [pltpu.VMEM(array.shape, array.dtype) for array in list(arrays.values())[:LOADS]]
    return pl.pallas_call(
        partial(finish_kernel, shape, names),
        in_specs=[hbm] * LOADS + [vm] * (len(arrays) - LOADS),
        out_specs=[vm] * len(outputs),
        out_shape=list(outputs.values()),
        scratch_shapes=list(scratch.values()) + kept,
        compiler_params=pltpu.CompilerParams(
            collective_id=0, has_side_effects=True, vmem_limit_bytes=VMEM
        ),
        name="finish",
    )(*arrays.values())


def middle_kernel(seqs, shape, context_hbm, tokens_hbm, cotangent_hbm, out_w_hbm, up_w_hbm, down_w_hbm,
                  out_a_ref, out_b_ref, up_a_ref, up_b_ref, down_a_ref, down_b_ref, gain_one_ref, gain_two_ref,
                  layer_hbm, grad_one_hbm, grad_context_ref, out_ga_ref, out_gb_ref, result_ref,
                  out_w, up_w, down_w, hidden_ref, low_ref, work_ref, act_ref, slope_ref,
                  context_ref, tokens_ref, cotangent_ref, layer_ref, grad_one_ref, sems, *refs):
    if shape is None:
        ff_ref = result_ref
    else:
        ff_ref, stage_ref, recv_ref, send_sems, recv_sems = refs
        peers, me, place, _ = whereabouts(shape)
        barrier = pltpu.get_barrier_semaphore()
        each(1, peers, lambda k: signal(barrier, place((me + k) % peers)))

    def to_peer(p):
        return remote(stage_ref.at[p], recv_ref.at[me], send_sems.at[p], recv_sems.at[me], place(p))

    def send(first):
        if shape is None:
            return
        half = peers // 2
        part = stage_ref.shape[2]
        for p in range(first, first + half):
            stage_ref[p] = ff_ref[0, :, p * part : (p + 1) * part].astype(BF)

        def start(k):
            p = first + (me + k) % half

            @pl.when(p != me)
            def _():
                to_peer(p).start()

        each(0, half, start)

    rows, width = tokens_ref.shape
    ff = up_w.shape[1]
    share = rows // seqs
    chunk = 512
    context_in, out_in, tokens_in, up_in, down_in, cotangent_in = (
        Loaded(source, target, sems.at[index])
        for index, (source, target) in enumerate(
            (
                (context_hbm, context_ref),
                (out_w_hbm, out_w),
                (tokens_hbm, tokens_ref),
                (up_w_hbm, up_w),
                (down_w_hbm, down_w),
                (cotangent_hbm, cotangent_ref),
            )
        )
    )
    layer_out = Stored(layer_hbm, layer_ref, sems.at[6])
    grad_one_out = Stored(grad_one_hbm, grad_one_ref, sems.at[7])

    half = rows // 2
    sides = (slice(0, half), slice(half, rows))

    def parts(side, step):
        if seqs == 1:
            return step(0, slice(0, half))
        per = seqs // 2
        return jnp.concatenate(
            [step(side * per + s, slice(s * share, (s + 1) * share)) for s in range(per)], axis=0
        )

    def inner(side, values, factor_ref, scale=1.0):
        return parts(side, lambda s, at: (scale * mm(values[at], factor_ref[s], NT)).astype(BF))

    def widened(side, inner_values, factor_ref, columns=slice(None)):
        return parts(side, lambda s, at: mm(inner_values[at], factor_ref[s, :, columns]))

    def factor_grad(left, right, s):
        at = slice(s * share, (s + 1) * share)
        return gather_rows(left[at], right[at])

    def joined(pair):
        return jnp.concatenate(pair, axis=0)

    def stats(values):
        centered = values - jnp.mean(values, axis=1, keepdims=True)
        inverse = lax.rsqrt(jnp.mean(centered * centered, axis=1, keepdims=True) + EPSILON)
        return centered * inverse, inverse

    def back(normed, inverse, gain, upstream):
        scaled = upstream * gain
        return inverse * (
            scaled
            - jnp.mean(scaled, axis=1, keepdims=True)
            - normed * jnp.mean(scaled * normed, axis=1, keepdims=True)
        )

    context = context_in()
    inner_out = [inner(side, context[at], out_a_ref) for side, at in enumerate(sides)]
    out_in()
    attended = [
        mm(context[at], out_w[...]) + ADAPTER_SCALING * widened(side, inner_out[side], out_b_ref)
        for side, at in enumerate(sides)
    ]
    tokens_in()
    inverse_one = [None, None]
    inner_up = [None, None]

    def norm_one(side):
        at = sides[side]
        normed, inverse_one[side] = stats(tokens_ref[at] + attended[side])
        grad_one_ref[at] = normed
        hidden = normed * gain_one_ref[...]
        hidden_ref[at] = hidden
        low_ref[at] = hidden.astype(BF)
        inner_up[side] = inner(side, low_ref[at], up_a_ref)

    def activate(side, start):
        at = sides[side]
        columns = slice(start, start + chunk)
        pre = mm(low_ref[at], up_w[:, columns]) + ADAPTER_SCALING * widened(side, inner_up[side], up_b_ref, columns)
        below = 0.5 + 0.5 * lax.erf(pre * math.sqrt(0.5))
        act_ref[at, columns] = (pre * below).astype(BF)
        density = jnp.exp(pre * pre * -0.5) * (1.0 / math.sqrt(2.0 * math.pi))
        slope_ref[at, columns] = (below + pre * density).astype(BF)

    norm_one(0)
    up_in()
    activate(0, 0)
    norm_one(1)
    for start in range(chunk, ff, chunk):
        activate(0, start)
    for start in range(0, ff, chunk):
        activate(1, start)
    down_in()
    inner_down = [None, None]
    branch = [None, None]
    for side, at in enumerate(sides):
        inner_down[side] = inner(side, act_ref[at], down_a_ref)
        branch[side] = mm(act_ref[at], down_w[...]) + ADAPTER_SCALING * widened(side, inner_down[side], down_b_ref)
    cotangent_in()
    grad_two = [None, None]
    grad_inner = [None, None]

    def norm_two(side):
        at = sides[side]
        normed, inverse = stats(hidden_ref[at] + branch[side])
        layer_ref[at] = normed * gain_two_ref[...]
        work_ref[at] = back(normed, inverse, gain_two_ref[...], cotangent_ref[at])
        grad_two[side] = work_ref[at].astype(BF)
        grad_inner[side] = inner(side, grad_two[side], down_b_ref, ADAPTER_SCALING)

    def back_activate(side, start):
        at = sides[side]
        columns = slice(start, start + chunk)
        grad_act = mm(grad_two[side], down_w[columns, :], NT) + widened(side, grad_inner[side], down_a_ref, columns)
        slope_ref[at, columns] = (grad_act.astype(BF).astype(F32) * slope_ref[at, columns].astype(F32)).astype(BF)

    norm_two(0)
    back_activate(0, 0)
    norm_two(1)
    layer_out.copy.start()
    for start in range(chunk, ff, chunk):
        back_activate(0, start)
    all_two, all_inner, all_down = joined(grad_two), joined(grad_inner), joined(inner_down)
    for s in range(seqs):
        ff_ref[s, :, width + 2 * ff:] = ADAPTER_SCALING * factor_grad(all_down, all_two, s)
        ff_ref[s, :, width + ff:width + 2 * ff] = factor_grad(all_inner, act_ref, s)
    if shape is not None:
        pl.semaphore_wait(barrier, peers - 1)
        send(peers // 2)
    for start in range(0, ff, chunk):
        back_activate(1, start)
    grad_inner = [inner(side, slope_ref[at], up_b_ref, ADAPTER_SCALING) for side, at in enumerate(sides)]
    all_inner, all_up = joined(grad_inner), joined(inner_up)
    for s in range(seqs):
        ff_ref[s, :, width:width + ff] = ADAPTER_SCALING * factor_grad(all_up, slope_ref, s)
        ff_ref[s, :, :width] = factor_grad(all_inner, low_ref, s)
    send(0)
    grad_hidden = [
        mm(slope_ref[at], up_w[...], NT) + widened(side, grad_inner[side], up_a_ref) for side, at in enumerate(sides)
    ]
    grad_low = [None, None]
    for side, at in enumerate(sides):
        grad_one = back(grad_one_ref[at], inverse_one[side], gain_one_ref[...], grad_hidden[side] + work_ref[at])
        grad_one_ref[at] = grad_one
        grad_low[side] = grad_one.astype(BF)
        grad_inner[side] = inner(side, grad_low[side], out_b_ref, ADAPTER_SCALING)
        grad_context_ref[at] = (
            mm(grad_low[side], out_w[...], NT) + widened(side, grad_inner[side], out_a_ref)
        ).astype(BF)
    grad_one_out.copy.start()
    all_low, all_inner, all_out = joined(grad_low), joined(grad_inner), joined(inner_out)
    for s in range(seqs):
        out_gb_ref[s] = ADAPTER_SCALING * factor_grad(all_out, all_low, s)
        out_ga_ref[s] = factor_grad(all_inner, context, s)
    layer_out.wait()
    grad_one_out.wait()
    if shape is not None:
        ff_ref[0, :, : stage_ref.shape[2]] = stage_ref[me].astype(F32)

        def take(k):
            p = (me + peers - k) % peers
            remote(stage_ref.at[p], recv_ref.at[p], send_sems.at[p], recv_sems.at[p], place(p)).wait_recv()
            ff_ref[0, :, : stage_ref.shape[2]] += recv_ref[p].astype(F32)

        each(1, peers, take)
        result_ref[...] = ff_ref[0, :, : stage_ref.shape[2]].astype(BF)
        each(1, peers, lambda k: to_peer((me + k) % peers).wait_send())


def middle(context, tokens, cotangent, out_weight, up_weight, down_weight, factors, gain_one, gain_two, shape=None):
    seqs, share, width = tokens.shape
    rows = seqs * share
    ff = up_weight.shape[1]
    rank = factors[0].shape[1]
    vm = pl.BlockSpec(memory_space=pltpu.VMEM)
    hbm = pl.BlockSpec(memory_space=pltpu.HBM)
    wide = jax.ShapeDtypeStruct((rows, width), F32)
    factor = jax.ShapeDtypeStruct((seqs, rank, width), F32)
    columns = 2 * width + 2 * ff
    result = jax.ShapeDtypeStruct((seqs, rank, columns), F32)
    extra = []
    params = pltpu.CompilerParams(vmem_limit_bytes=VMEM)
    if shape is not None:
        peers = shape[0] * shape[1]
        result = jax.ShapeDtypeStruct((rank, columns // peers), BF)
        extra = [pltpu.VMEM((seqs, rank, columns), F32)] + [pltpu.VMEM((peers, rank, columns // peers), BF)] * 2
        extra += [pltpu.SemaphoreType.DMA((peers,))] * 2
        params = pltpu.CompilerParams(vmem_limit_bytes=VMEM, collective_id=1, has_side_effects=True)
    found = pl.pallas_call(
        partial(middle_kernel, seqs, shape),
        in_specs=[hbm] * 6 + [vm] * 8,
        out_specs=[hbm] * 2 + [vm] * 4,
        out_shape=[wide, wide, jax.ShapeDtypeStruct((rows, width), BF), factor, factor, result],
        scratch_shapes=[
            pltpu.VMEM(out_weight.shape, BF), pltpu.VMEM(up_weight.shape, BF), pltpu.VMEM(down_weight.shape, BF),
            pltpu.VMEM((rows, width), F32), pltpu.VMEM((rows, width), BF), pltpu.VMEM((rows, width), F32),
            pltpu.VMEM((rows, ff), BF), pltpu.VMEM((rows, ff), BF),
            pltpu.VMEM((rows, width), BF), *[pltpu.VMEM((rows, width), F32)] * 4, pltpu.SemaphoreType.DMA((8,)),
        ] + extra,
        compiler_params=params,
        cost_estimate=pl.CostEstimate(flops=36 * rows * width * width, bytes_accessed=24 * width * width, transcendentals=rows * ff),
        name="middle",
    )(context.reshape(rows, width), tokens.reshape(rows, width), cotangent.reshape(rows, width),
      out_weight, up_weight, down_weight, *factors, gain_one.reshape(1, width), gain_two.reshape(1, width))
    return [array.reshape(seqs, share, width) for array in found[:3]] + list(found[3:])


def shifted(value, axes, steps):
    count = math.prod(lax.axis_size(axis) for axis in axes)
    initial, last = (max(0, -steps), min(count, count - steps))
    return lax.ppermute(value, axes, [(source, source + steps) for source in range(initial, last)])


def bucket_of(offset, buckets, distance_cap):
    middle = buckets // 2
    sign_of = np.sign(offset)
    magnitude = np.where((offset < middle) & (offset > -middle), middle - 1, np.abs(offset))
    log_place = (
        np.ceil(np.log(magnitude / middle) / np.log((distance_cap - 1) / middle) * (middle - 1))
        + middle
    )
    return np.where(np.abs(offset) <= middle, offset, log_place * sign_of).astype(np.int32)


def offset_tables():
    place = np.arange(2 * HALF)

    def hot(distance, sign):
        clipped = np.clip(distance, 1 - HALF, HALF - 1)
        bucket = np.clip(BUCK + sign * bucket_of(clipped, BUCK, SPAN), 0, 2 * BUCK - 1)
        return np.eye(2 * BUCK, dtype=np.float32)[bucket]

    return hot(HALF - place, 1), hot(place - HALF, -1), hot(HALF - 1 - place, -1)


def segment_ids(lengths, positions):
    bounds = jnp.cumsum(lengths, axis=-1, dtype=jnp.int32)
    return jnp.sum(
        (bounds[..., None, :] <= positions[:, None]).astype(jnp.int32), axis=-1, dtype=jnp.int32
    )


def product(pattern, left_side, right_side):
    return jnp.einsum(pattern, left_side, right_side, preferred_element_type=F32)


def norm_stats(values):
    centered = values - jnp.mean(values, axis=-1, keepdims=True)
    inverse = lax.rsqrt(jnp.mean(centered * centered, axis=-1, keepdims=True) + EPSILON)
    return (centered * inverse, inverse)


def norm_back(normed, inverse, scale_gain, upstream):
    scaled = upstream * scale_gain
    return inverse * (
        scaled
        - jnp.mean(scaled, axis=-1, keepdims=True)
        - normed * jnp.mean(scaled * normed, axis=-1, keepdims=True)
    )


def adapter_forward(rows_in, weight, down, up):
    inner = product("sti,sir->str", rows_in, down).astype(BF)
    mapped = product("sti,io->sto", rows_in, weight) + ADAPTER_SCALING * product(
        "str,sro->sto", inner, up
    )
    return (mapped, inner)


def adapter_back(rows_in, inner, weight, down, up, gradient):
    grad_up = ADAPTER_SCALING * product("str,sto->sro", inner, gradient)
    grad_inner = (ADAPTER_SCALING * product("sto,sro->str", gradient, up)).astype(BF)
    grad_down = product("sti,str->sir", rows_in, grad_inner)
    grad_in = product("sto,io->sti", gradient, weight) + product("str,sir->sti", grad_inner, down)
    return (grad_in, grad_down, grad_up)


def body(
    tokens,
    cotangent,
    doc_lengths,
    adapter_ids,
    query_weight,
    key_weight,
    value_weight,
    output_weight,
    up_weight,
    down_weight,
    attention_gain,
    feedforward_gain,
    position_gain,
    position_table,
    attention_down,
    attention_up,
    expand_down,
    expand_up,
    reduce_down,
    reduce_up,
):
    seqs, row_count, width = tokens.shape
    head_groups = lax.axis_size("head")
    head_index = lax.axis_index("head")
    seq_index = lax.axis_index("seq")
    by_rows = seqs == 1 and row_count == HALF

    def turned(array):
        return jnp.swapaxes(array, -1, -2)

    token_low = lax.optimization_barrier(tokens.astype(BF))
    frozen = (query_weight, key_weight, value_weight)

    def columns(matrix):
        if by_rows:
            return matrix
        local = width // head_groups
        return lax.dynamic_slice_in_dim(matrix, head_index * local, local, matrix.ndim - 1)

    if by_rows:
        block_axes = ("seq", "head")
        block_index = seq_index * head_groups + head_index
        query_count = row_count
    else:
        block_axes = ("seq",)
        block_index = seq_index
        query_count = row_count * head_groups
    blocks = math.prod(lax.axis_size(axis) for axis in block_axes)

    first_place = block_index * query_count - HALF
    factors, query_seg, key_bias = prepare(
        adapter_ids,
        doc_lengths,
        jnp.stack([first_place, query_count * blocks]).astype(jnp.int32),
        [turned(attention_down), attention_up, turned(expand_down), expand_up, turned(reduce_down), reduce_up],
        query_count,
    )
    downs, att_up = factors[:4], factors[4:8]
    att_down = [turned(factor) for factor in downs]

    def halo(array):
        before = shifted(array[:, query_count - HALF :], block_axes, 1)
        after = shifted(array[:, :HALF], block_axes, -1)
        return before, after

    hots = [jnp.asarray(hot, BF) for hot in offset_tables()]
    if by_rows:
        before, after = halo(token_low)
        (query, key, value), (query_rel, query_back, key_rel), table_low, inners, position_inners = begin(
            token_low[0],
            position_table,
            position_gain,
            frozen,
            [down[0] for down in downs[:3]],
            [up[0] for up in att_up[:3]],
            hots,
        )
        queries, keys, values, key_rel, query_rel, query_back = (
            array[None] for array in (query, key, value, key_rel, query_rel, query_back)
        )
    else:
        projected = []
        inners = []
        for member in range(3):
            mapped, inner = adapter_forward(
                token_low, frozen[member], att_down[member], att_up[member]
            )
            projected.append(mapped.astype(BF))
            inners.append(inner)
        queries, keys, values = lax.all_to_all(
            jnp.stack(projected), "head", split_axis=3, concat_axis=2, tiled=True
        )
        keys_halo, values_halo = (jnp.concatenate(halo(array), axis=1) for array in (keys, values))
        table_low = (norm_stats(position_table)[0] * position_gain).astype(BF)
        position_inners = []
        tables = []
        for member in range(2):
            inner = product("pi,sir->spr", table_low, att_down[member]).astype(BF)
            mapped = product("pi,io->po", table_low, columns(frozen[member]))[
                None
            ] + ADAPTER_SCALING * product("spr,sro->spo", inner, columns(att_up[member]))
            position_inners.append(inner)
            tables.append(mapped.astype(BF))
        key_rel = product("cp,spo->sco", hots[0], tables[1]).astype(BF)
        query_rel = product("cp,spo->sco", hots[1], tables[0]).astype(BF)
        query_back = product("cp,spo->sco", hots[2], tables[0]).astype(BF)

    query_scores, key_scores = relative_scores(queries, keys, key_rel, query_rel)
    if by_rows:
        sides = (before[0], after[0], *frozen[1:], downs[1][0], downs[2][0], att_up[1][0], att_up[2][0])
    else:
        sides = (keys_halo, values_halo)
    context, probs, context_wide, inverse_total, *made = attention_forward(
        queries, keys, values, query_rel, query_seg, key_bias, query_scores, key_scores, sides
    )
    if by_rows:
        keys_halo, values_halo, *inners_halo = made
    if by_rows:
        context_rows = context
    else:
        context_rows = lax.all_to_all(context, "head", split_axis=1, concat_axis=2, tiled=True)

    ff_width = up_weight.shape[1]
    rank = attention_up.shape[2]
    peers = lax.axis_size("seq") * head_groups
    cores = lax.axis_size("batch")
    table_rows = position_table.shape[0]
    direct = by_rows and cores == 2 and table_rows == peers * cores * rank
    shape = (head_groups, peers // head_groups, cores, rank) if direct else None
    layer_output, grad_one, grad_context, grad_out_down, grad_out_up, grad_ff = middle(
        context_rows,
        tokens,
        cotangent,
        output_weight,
        up_weight,
        down_weight,
        (downs[3], att_up[3], *factors[8:]),
        attention_gain,
        feedforward_gain,
        shape,
    )
    if not by_rows:
        grad_context = lax.all_to_all(grad_context, "head", split_axis=2, concat_axis=1, tiled=True)

    group = ADAPTERS // head_groups
    def spread(array):
        chosen_by = select.reshape(select.shape + (1,) * (array.ndim - 1))
        return jnp.sum(chosen_by * array[:, None], axis=0)

    def unflat(array, widths):
        return jnp.split(array, np.cumsum(widths)[:-1].tolist(), axis=-1)

    *handed, grad_q, grad_k, grad_k_halo, grad_v, grad_v_halo, grad_key_rel, grad_query_rel = attention_backward(
        queries,
        keys,
        keys_halo,
        values,
        values_halo,
        key_rel,
        query_back,
        probs,
        grad_context,
        context_wide,
        inverse_total,
        *([layer_output] if direct else []),
    )
    if direct:
        layer_output = handed[0]

    def joined(total, from_above, from_below):
        if query_count == HALF:
            return total + from_above + from_below
        total = total.at[:, query_count - HALF :].add(from_above)
        return total.at[:, :HALF].add(from_below)

    def fold(total, halo_part):
        from_above = shifted(halo_part[:, :HALF], block_axes, -1).astype(F32)
        from_below = shifted(halo_part[:, HALF:], block_axes, 1).astype(F32)
        return joined(total.astype(F32), from_above, from_below)

    if direct:
        grad_tokens, table_total, late, both_ids, ff_total = finish(
            shape,
            key_halo=grad_k_halo[0],
            value_halo=grad_v_halo[0],
            key_w=key_weight,
            value_w=value_weight,
            back_hot=hots[2].T,
            query_rel_g=grad_query_rel[0],
            key_hot=hots[0].T,
            key_rel_g=grad_key_rel[0],
            query_w=query_weight,
            x=token_low[0],
            x_before=before[0],
            x_after=after[0],
            low=table_low,
            query_g=grad_q[0],
            key_g=grad_k[0],
            value_g=grad_v[0],
            grad_one=grad_one[0],
            query_a=downs[0][0],
            key_a=downs[1][0],
            value_a=downs[2][0],
            query_b=att_up[0][0],
            key_b=att_up[1][0],
            value_b=att_up[2][0],
            query_u=inners[0],
            key_u=inners[1],
            value_u=inners[2],
            key_uh=inners_halo[0],
            value_uh=inners_halo[1],
            query_pu=position_inners[0],
            key_pu=position_inners[1],
            own_id=jnp.broadcast_to(adapter_ids.astype(F32)[:, None], (8, TILE)),
            out_ga=grad_out_down[0],
            out_gb=grad_out_up[0],
            ff=grad_ff,
        )
        table_grad, down_grad, up_grad, *ff_grads, input_grad = spread_all(
            group,
            head_index.astype(jnp.int32).reshape(1),
            both_ids,
            late,
            ff_total,
            table_total,
            position_table,
            grad_tokens,
            position_gain,
            ff_width,
        )
        return (
            layer_output,
            input_grad[None],
            table_grad,
            turned(down_grad),
            up_grad,
            turned(ff_grads[0]),
            ff_grads[1],
            turned(ff_grads[2]),
            ff_grads[3],
        )
    else:
        ids = lax.all_gather(adapter_ids, "batch", axis=0, tiled=True)
        slots = head_index * group + jnp.arange(group, dtype=jnp.int32)
        select = (ids[:, None] == slots[None, :]).astype(F32)
        down_grads = []
        up_grads = []
        if by_rows:
            input_grad = grad_one
            grad_halo = 0.0
            rows_halo = jnp.concatenate([before, after], axis=1)
            for member, pieces in enumerate(
                (
                    ((token_low, inners[0][None], grad_q),),
                    ((token_low, inners[1][None], grad_k), (rows_halo, inners_halo[0][None], grad_k_halo)),
                    ((token_low, inners[2][None], grad_v), (rows_halo, inners_halo[1][None], grad_v_halo)),
                )
            ):
                found = [
                    adapter_back(rows, inner, frozen[member], att_down[member], att_up[member], gradient)
                    for rows, inner, gradient in pieces
                ]
                input_grad = input_grad + found[0][0]
                if member > 0:
                    grad_halo = grad_halo + found[1][0]
                down_grads.append(sum(turned(one[1]) for one in found))
                up_grads.append(sum(one[2] for one in found))
            input_grad = fold(input_grad, grad_halo.astype(BF))
            position_inners = [inner[None] for inner in position_inners]
        else:
            grad_qkv = jnp.stack(
                [grad_q, fold(grad_k, grad_k_halo).astype(BF), fold(grad_v, grad_v_halo).astype(BF)]
            )
            grad_qkv = lax.all_to_all(grad_qkv, "head", split_axis=2, concat_axis=3, tiled=True)
            input_grad = grad_one
            for member in range(3):
                grad_in, grad_dn, grad_upper = adapter_back(
                    token_low,
                    inners[member],
                    frozen[member],
                    att_down[member],
                    att_up[member],
                    grad_qkv[member],
                )
                input_grad = input_grad + grad_in
                down_grads.append(turned(grad_dn))
                up_grads.append(grad_upper)
        down_grads.append(grad_out_down)
        up_grads.append(grad_out_up)
        position_grads = (
            product("cb,soc->sbo", hots[2], grad_query_rel),
            product("cb,soc->sbo", hots[0], grad_key_rel),
        )
        grad_table_low = jnp.zeros(position_table.shape, F32)
        for member in range(2):
            gradient = position_grads[member].astype(BF)
            up = columns(att_up[member])
            grad_columns = ADAPTER_SCALING * product(
                "spr,spo->sro", position_inners[member], gradient
            )
            grad_inner = (ADAPTER_SCALING * product("spo,sro->spr", gradient, up)).astype(BF)
            grad_table_low = (
                grad_table_low
                + product("spo,io->pi", gradient, columns(frozen[member]))
                + product("spr,sir->pi", grad_inner, att_down[member])
            )
            down_grads[member] = down_grads[member] + product("spr,pi->sri", grad_inner, table_low)
            if not by_rows:
                grad_columns = lax.dynamic_update_slice_in_dim(
                    jnp.zeros_like(up_grads[member]),
                    grad_columns,
                    head_index * (width // head_groups),
                    2,
                )
            up_grads[member] = up_grads[member] + grad_columns
        late = jnp.concatenate(down_grads + up_grads, axis=-1)
        late = lax.all_gather(lax.psum(late, ("seq", "head")), "batch", axis=0, tiled=True)
        early = lax.all_gather(lax.psum(grad_ff, ("seq", "head")), "batch", axis=0, tiled=True)
        table_total = lax.psum(grad_table_low, ("seq", "batch"))
        table_total = lax.psum_scatter(table_total, "head", scatter_dimension=0, tiled=True)
    own_rows = table_rows // head_groups

    def head_rows(array):
        return lax.dynamic_slice_in_dim(array, head_index * own_rows, own_rows, 0)

    table_normed, table_inverse = norm_stats(head_rows(position_table))
    table_grad = norm_back(table_normed, table_inverse, position_gain, table_total)
    early = [spread(part) for part in unflat(early, [width, ff_width, ff_width, width])]
    late = [spread(part) for part in unflat(late, [width] * 8)]
    return (
        layer_output,
        input_grad,
        table_grad,
        jnp.stack([turned(part) for part in late[:4]]),
        jnp.stack(late[4:]),
        turned(early[0]),
        early[1],
        turned(early[2]),
        early[3],
    )


def solution(mesh):
    rows = P("batch", ("seq", "head"), None)
    return jax.shard_map(
        body,
        mesh=mesh,
        in_specs=(rows, rows, P("batch", None), P("batch")) + (P(),) * 16,
        out_specs=(
            rows,
            rows,
            P("head", None),
            P(None, "head", None, None),
            P(None, "head", None, None),
            P("head", None, None),
            P("head", None, None),
            P("head", None, None),
            P("head", None, None),
        ),
        check_vma=False,
    )
```

```python
from functools import partial
import math
from types import SimpleNamespace

import jax
import jax.numpy as jnp
import numpy as np
from jax import lax
from jax.experimental import pallas as pl
from jax.experimental.pallas import tpu as pltpu
from jax.sharding import PartitionSpec as P

HEADS = 16
HEAD_DIM = 64
BUCK = 256
SPAN = 512
ADAPTERS = 8
HALF = 512
DOCS = 8

EPSILON = 1e-07
ADAPTER_SCALING = 2.0
NEGATIVE = -1e30
PRECISE = lax.Precision.HIGHEST
TILE = 128
BF = jnp.bfloat16
F32 = jnp.float32
MESH = pl.DeviceIdType.MESH
VMEM = 63 * 2**20
NN = (((1,), (0,)), ((), ()))
NT = (((1,), (1,)), ((), ()))


def mm(a, b, dims=NN):
    return lax.dot_general(a, b, dims, preferred_element_type=F32)

def lanes(shape=(TILE, TILE)):
    return lax.broadcasted_iota(jnp.int32, shape, 1)

def rows(shape=(TILE, TILE)):
    return lax.broadcasted_iota(jnp.int32, shape, 0)

def skew(tile):
    return pltpu.roll(tile, 0, 1, stride=1, stride_axis=0)

def flip_matrix():
    return jnp.where(lanes() + rows() == TILE - 1, 1.0, 0.0).astype(BF)


class Loaded:
    def __init__(self, source, target, sem, start=True):
        self.target = target
        self.copy = pltpu.make_async_copy(source, target, sem)
        if start:
            self.copy.start()

    def __call__(self):
        if self.copy is not None:
            self.copy.wait()
            self.copy = None
        return self.target[...]


def with_halo(own_ref, halo_ref):
    return jnp.concatenate([halo_ref[0, :HALF], own_ref[0], halo_ref[0, HALF:]], axis=0)


class Stored:
    def __init__(self, target, buffer, sem):
        self.buffer = buffer
        self.copy = pltpu.make_async_copy(buffer, target, sem)

    def put(self, value):
        self.buffer[...] = value
        self.copy.start()

    def wait(self):
        self.copy.wait()


def prepare_kernel(seqs, ids_ref, lengths_ref, base_ref, *refs):
    stacks = [stack.at[member] for stack in refs[:2] for member in range(4)] + list(refs[2:6])
    count = len(stacks)
    refs = refs[6:]
    outs = refs[: count + 2]
    buffers = refs[count + 2 : 2 * count + 2]
    made = refs[2 * count + 2 : 3 * count + 4]
    sems, out_sems = refs[3 * count + 4 :]
    outs = [Stored(target, buffer, out_sems.at[i]) for i, (target, buffer) in enumerate(zip(outs, made))]
    query_seg_ref, key_bias_ref = made[count:]
    copies = []
    for s in range(seqs):
        for index, (stack, buffer) in enumerate(zip(stacks, buffers)):
            copy = pltpu.make_async_copy(stack.at[ids_ref[s]], buffer.at[s], sems.at[s, index])
            copy.start()
            copies.append(copy)
    rows_k = key_bias_ref.shape[1]
    rows_q = query_seg_ref.shape[1]
    place = base_ref[0] + rows((rows_k, TILE))
    slot = lanes((rows_k, TILE)) % HEAD_DIM
    inside = (place >= 0) & (place < base_ref[1])
    for s in range(seqs):
        segment = jnp.zeros((rows_k, TILE), jnp.int32)
        bound = jnp.int32(0)
        for document in range(DOCS):
            bound = bound + lengths_ref[s, document]
            segment += jnp.where(place >= bound, 1, 0)
        segment = jnp.where(inside, segment, DOCS)
        same = slot == segment
        query_seg_ref[s] = jnp.where(same, 1.0, 0.0)[HALF : HALF + rows_q].astype(BF)
        open_slot = (same & (segment < DOCS)) | (slot > DOCS)
        key_bias_ref[s] = jnp.where(open_slot, 0.0, NEGATIVE).astype(BF)
    for out in outs[count:]:
        out.copy.start()
    for copy in copies:
        copy.wait()
    for buffer, out in zip(buffers, outs):
        out.put(buffer[...].astype(BF))
    for out in outs:
        out.wait()


def prepare(adapter_ids, lengths, base, stacks, query_count):
    seqs = adapter_ids.shape[0]
    hbm = pl.BlockSpec(memory_space=pltpu.HBM)
    sm = pl.BlockSpec(memory_space=pltpu.SMEM)
    shapes = [(seqs,) + stack.shape[2:] for stack in stacks[:2] for _ in range(4)]
    shapes += [(seqs,) + stack.shape[1:] for stack in stacks[2:]]
    count = len(shapes)
    columns = [(seqs, query_count, TILE), (seqs, query_count + 2 * HALF, TILE)]
    found = pl.pallas_call(
        partial(prepare_kernel, seqs),
        in_specs=[sm] * 3 + [hbm] * len(stacks),
        out_specs=[hbm] * (count + 2),
        out_shape=[jax.ShapeDtypeStruct(shape, BF) for shape in shapes + columns],
        scratch_shapes=[pltpu.VMEM(shape, F32) for shape in shapes]
        + [pltpu.VMEM(shape, BF) for shape in shapes + columns]
        + [pltpu.SemaphoreType.DMA((seqs, count)), pltpu.SemaphoreType.DMA((count + 2,))],
        compiler_params=pltpu.CompilerParams(vmem_limit_bytes=VMEM),
        cost_estimate=pl.CostEstimate(flops=10**6, bytes_accessed=6 * 10**6, transcendentals=0),
        name="prepare",
    )(adapter_ids, lengths, base, *stacks)
    return found[:count], found[count], found[count + 1]


def adapted(x, weight, inner, up):
    return (mm(x, weight) + ADAPTER_SCALING * mm(inner, up)).astype(BF)


def begin_kernel(x_ref, table_ref, gain_ref, query_a, key_a, value_a, query_b, key_b, value_b,
                 query_w, key_w, value_w, query_hot, back_hot, key_hot,
                 query_out, key_out, value_out, query_rel_out, back_rel_out, key_rel_out, low_out,
                 query_u, key_u, value_u, query_pu, key_pu, *scratch):
    loaded = scratch[:6]
    stored = scratch[6:13]
    load_sems, store_sems = scratch[13:]
    query_w, key_w, value_w, query_hot, back_hot, key_hot = (
        Loaded(source, target, load_sems.at[index])
        for index, (source, target) in enumerate(zip((query_w, key_w, value_w, query_hot, back_hot, key_hot), loaded))
    )
    outs = [
        Stored(target, buffer, store_sems.at[index])
        for index, (target, buffer) in enumerate(
            zip((query_out, key_out, value_out, query_rel_out, back_rel_out, key_rel_out, low_out), stored)
        )
    ]
    x = x_ref[...]
    query_u[...] = mm(x, query_a[...], NT).astype(BF)
    key_u[...] = mm(x, key_a[...], NT).astype(BF)
    value_u[...] = mm(x, value_a[...], NT).astype(BF)
    values = table_ref[...]
    centered = values - jnp.mean(values, axis=1, keepdims=True)
    inverse = lax.rsqrt(jnp.mean(centered * centered, axis=1, keepdims=True) + EPSILON)
    low = (centered * inverse * gain_ref[...]).astype(BF)
    outs[6].put(low)
    query_pu[...] = mm(low, query_a[...], NT).astype(BF)
    key_pu[...] = mm(low, key_a[...], NT).astype(BF)
    outs[0].put(adapted(x, query_w(), query_u[...], query_b[...]))
    position_q = adapted(low, query_w(), query_pu[...], query_b[...])
    outs[1].put(adapted(x, key_w(), key_u[...], key_b[...]))
    position_k = adapted(low, key_w(), key_pu[...], key_b[...])
    outs[2].put(adapted(x, value_w(), value_u[...], value_b[...]))
    outs[3].put(mm(query_hot(), position_q).astype(BF))
    outs[4].put(mm(back_hot(), position_q).astype(BF))
    outs[5].put(mm(key_hot(), position_k).astype(BF))
    for out in outs:
        out.wait()


def begin(x, table, gain, weights, downs, ups, hots):
    rows_x, width = x.shape
    rank = ups[0].shape[0]
    places = table.shape[0]
    spans = hots[0].shape[0]
    vm = pl.BlockSpec(memory_space=pltpu.VMEM)
    hbm = pl.BlockSpec(memory_space=pltpu.HBM)
    large = [(rows_x, width)] * 3 + [(spans, width)] * 3 + [(places, width)]
    inner = jax.ShapeDtypeStruct((rows_x, rank), BF)
    position_inner = jax.ShapeDtypeStruct((places, rank), BF)
    sources = (*weights, hots[1], hots[2], hots[0])
    found = pl.pallas_call(
        begin_kernel,
        in_specs=[vm] * 9 + [hbm] * 6,
        out_specs=[hbm] * 7 + [vm] * 5,
        out_shape=[jax.ShapeDtypeStruct(shape, BF) for shape in large] + [inner] * 3 + [position_inner] * 2,
        scratch_shapes=[pltpu.VMEM(source.shape, BF) for source in sources]
        + [pltpu.VMEM(shape, BF) for shape in large]
        + [pltpu.SemaphoreType.DMA((6,)), pltpu.SemaphoreType.DMA((7,))],
        compiler_params=pltpu.CompilerParams(vmem_limit_bytes=VMEM),
        cost_estimate=pl.CostEstimate(
            flops=6 * rows_x * width * width + 10 * places * width * width,
            bytes_accessed=24 * places * width + 6 * width * width,
            transcendentals=0,
        ),
        name="begin",
    )(x, table, gain.reshape(1, width), *downs, *ups, *sources)
    return found[:3], found[3:6], found[6], found[7:10], found[10:]


def relative_kernel(q_ref, k_ref, pk_ref, pq_ref, qs_ref, ks_ref):
    tiles = HALF // TILE
    span = 2 * tiles
    below = lanes() + rows() < TILE
    column = lanes((HALF, TILE)) < HEAD_DIM
    for h in range(2):
        own = column if h == 0 else ~column
        km = jnp.where(own, k_ref[0], jnp.zeros_like(k_ref[0]))
        qm = jnp.where(own, q_ref[0], jnp.zeros_like(q_ref[0]))
        for d in range(1, span):
            pairs = [(t, d + t - tiles) for t in range(tiles) if 0 <= d + t - tiles < tiles]
            first, last = pairs[0][1], pairs[-1][1]
            key_rel = mm(
                km[first * TILE : (last + 1) * TILE], pq_ref[0, (span - 1 - d) * TILE : (span + 1 - d) * TILE, :], NT
            ).astype(BF)
            for t, j in pairs:
                part = key_rel[(j - first) * TILE : (j - first + 1) * TILE]
                ks_ref[0, h, t, :, j * TILE : (j + 1) * TILE] = skew(
                    jnp.where(below, part[:, TILE:], part[:, :TILE])
                ).T
        query_rel = mm(qm, pk_ref[0], NT).astype(BF)
        for t in range(tiles):
            part = query_rel[t * TILE : (t + 1) * TILE]
            for d in range(span + 1):
                here = part[:, min(d, span - 1) * TILE : (min(d, span - 1) + 1) * TILE]
                if 0 < d < span:
                    here = jnp.where(below, here, part[:, (d - 1) * TILE : d * TILE])
                qs_ref[0, h, t, :, d * TILE : (d + 1) * TILE] = skew(here)


def relative_scores(q, k, pk, pq):
    n, rq, width = q.shape
    pairs = width // TILE
    off = 2 * HALF
    tiles = rq // TILE
    return pl.pallas_call(
        relative_kernel,
        grid=(n, pairs),
        in_specs=[column_spec(rq), column_spec(rq), column_spec(off), column_spec(off)],
        out_specs=[head_spec(tiles, TILE, off + TILE), head_spec(tiles, TILE, HALF)],
        out_shape=[jax.ShapeDtypeStruct((n, 2 * pairs, tiles, TILE, off + TILE), BF),
                   jax.ShapeDtypeStruct((n, 2 * pairs, tiles, TILE, HALF), BF)],
        compiler_params=pltpu.CompilerParams(dimension_semantics=("arbitrary", "arbitrary"), vmem_limit_bytes=VMEM),
        cost_estimate=pl.CostEstimate(
            flops=16 * n * rq * off * width, bytes_accessed=60 * 10**6, transcendentals=0
        ),
        name="relative_scores",
    )(q, k, pk, pq)


def column_spec(r):
    return pl.BlockSpec((1, r, TILE), lambda s, p: (s, 0, p))


def head_spec(*shape):
    return pl.BlockSpec((1, 2) + shape, lambda s, p: (s, p) + (0,) * len(shape))


def forward_kernel(mapped, pairs, q_ref, k_ref, v_ref, pq_ref, qhot_ref, kbias_ref, qs_ref, ko_ref, *refs):
    if mapped:
        kh_ref, vh_ref, ctx_ref, p_ref, ctxf_ref, inv_ref = refs[:6]
    else:
        before, after, key_w, value_w, key_a, value_a, key_b, value_b = refs[:8]
        ctx_ref, p_ref, ctxf_ref, inv_ref, kh_ref, vh_ref, key_u, value_u = refs[8:16]
    prepared = (refs[-7:-4], refs[-4:-1])
    s_ref = refs[-1]
    step = pl.program_id(1)
    tiles = HALF // TILE
    span = 2 * tiles
    width = (span + 1) * TILE
    flip = flip_matrix()
    flips = jnp.concatenate([flip, flip], axis=1)
    factor = math.log2(math.e) / math.sqrt(3 * HEAD_DIM)
    below = lanes() + rows() < TILE
    place = lanes() + rows()
    tcol = lanes() < HEAD_DIM

    def halo_inners():
        for side, x in ((0, before), (1, after)):
            at = slice(side * HALF, (side + 1) * HALF)
            key_u[at] = mm(x[...], key_a[...], NT).astype(BF)
            value_u[at] = mm(x[...], value_a[...], NT).astype(BF)

    def halo_map(side):
        weights = jnp.concatenate([key_w[...], value_w[...]], axis=1)
        nothing = jnp.zeros_like(key_b[...])
        ups = jnp.concatenate(
            [jnp.concatenate([key_b[...], nothing], axis=1), jnp.concatenate([nothing, value_b[...]], axis=1)], axis=0
        )
        at = slice(side * HALF, (side + 1) * HALF)
        inner = jnp.concatenate([key_u[at], value_u[at]], axis=1)
        both = adapted((before, after)[side][...], weights, inner, ups)
        kh_ref[0, at] = both[:, :TILE]
        vh_ref[0, at] = both[:, TILE:]

    def prepare_head(h, target):
        kz_ref, vz_ref, ks_ref = target
        k = with_halo(k_ref, kh_ref)
        v = with_halo(v_ref, vh_ref)
        own = lanes(k.shape) < HEAD_DIM
        halo_own = lanes(kh_ref.shape[1:]) < HEAD_DIM
        if h == 1:
            own, halo_own = ~own, ~halo_own
        kz_ref[h] = jnp.where(own, k, kbias_ref[0])
        vz_ref[h] = jnp.where(own, v, jnp.ones_like(v))
        km = jnp.where(halo_own, kh_ref[0], jnp.zeros_like(kh_ref[0]))
        for d in range(span + 1):
            seen = [(t, d + t if d + t < tiles else d + t - tiles) for t in range(tiles) if not tiles <= d + t < 2 * tiles]
            if not seen:
                continue
            low = max(span - 1 - d, 0) * TILE
            high = min(span + 1 - d, span) * TILE
            first, last = seen[0][1], seen[-1][1]
            key_rel = mm(km[first * TILE : (last + 1) * TILE], pq_ref[0, low:high, :], NT).astype(BF)
            for t, j in seen:
                part = key_rel[(j - first) * TILE : (j - first + 1) * TILE]
                if 0 < d < span:
                    part = jnp.where(below, part[:, TILE:], part[:, :TILE])
                w = d if d < tiles else d - tiles
                ks_ref[h, t, :, w * TILE : (w + 1) * TILE] = skew(part).T

    def scores(t, h, source):
        kz_ref, _, ks_ref = source
        at = slice(t * TILE, (t + 1) * TILE)
        edge = (tiles - t) * TILE
        q_side = mm(flip, jnp.where(tcol if h == 0 else ~tcol, q_ref[0, at, :], qhot_ref[0, at, :])).astype(BF)
        key_side = jnp.concatenate([ks_ref[h, t, :, :edge], ko_ref[0, h, t], ks_ref[h, t, :, edge:]], axis=1)
        relative = jnp.concatenate([qs_ref[0, h, t], key_side], axis=0)
        s_ref[2 * (t % 2) + h] = mm(q_side, kz_ref[h, t * TILE : t * TILE + width, :], NT) + mm(flips, relative)

    def softmax(t, h, source):
        slot = 2 * (t % 2) + h
        at = slice(t * TILE, (t + 1) * TILE)
        own = tcol if h == 0 else ~tcol
        s_ref[slot, :, :TILE] = jnp.where(place > TILE - 1, s_ref[slot, :, :TILE], NEGATIVE)
        s_ref[slot, :, span * TILE :] = jnp.where(place < TILE - 1, s_ref[slot, :, span * TILE :], NEGATIVE)
        middle = s_ref[slot, :, tiles * TILE : (tiles + 1) * TILE]
        s_ref[slot, :, tiles * TILE : (tiles + 1) * TILE] = jnp.where(
            (place == TILE - 1) & (middle < 0.1 * NEGATIVE), 0.0, middle
        )
        top = s_ref[slot, :, :TILE]
        for d in range(1, span + 1):
            top = jnp.maximum(top, s_ref[slot, :, d * TILE : (d + 1) * TILE])
        peak = jnp.max(top, axis=1, keepdims=True)
        prob = jnp.exp2((s_ref[slot] - peak) * factor).astype(BF)
        a = t % 2
        row_at = slice(a * TILE, (a + 1) * TILE)
        p_ref[0, h, t // 2, row_at, a * TILE : a * TILE + width] = prob
        p_ref[0, h, t // 2, row_at, (1 - a) * width : (1 - a) * width + TILE] = jnp.zeros((TILE, TILE), BF)
        total = mm(prob, source[1][h, t * TILE : t * TILE + width, :])
        inv = 1.0 / jnp.where(own, pltpu.roll(total, HEAD_DIM, 1), total)
        inv_ref[0, h, at, :] = inv
        return total * inv

    @pl.when(step == 0)
    def _():
        if not mapped:
            halo_inners()
            halo_map(0)
            halo_map(1)
        for h in range(2):
            prepare_head(h, prepared[0])

    def both(target, source):
        between = []
        if target is not None:
            between = [lambda: prepare_head(0, target), lambda: prepare_head(1, target)]
        if target is not None and not mapped:
            between = [lambda: (halo_map(0), halo_map(1))] + between
        for h in range(2):
            scores(0, h, source)
        for t in range(tiles):
            outs = []
            for h in range(2):
                if t + 1 < tiles:
                    scores(t + 1, h, source)
                outs.append(softmax(t, h, source))
            if between:
                between.pop(0)()
            at = slice(t * TILE, (t + 1) * TILE)
            ctx = jnp.where(tcol, outs[0], outs[1])
            ctxf_ref[0, at, :] = ctx
            ctx_ref[0, at, :] = mm(flip, ctx.astype(BF)).astype(BF)

    for parity in range(2):

        @pl.when((step > 0) & (step < pairs) & (step % 2 == parity))
        def _():
            both(prepared[parity], prepared[1 - parity])

    @pl.when(step == pairs)
    def _():
        both(None, prepared[(pairs - 1) % 2])


def attention_forward(q, k, v, pq, qhot, kbias, query_scores, key_scores, halo):
    n, rq, width = q.shape
    off = 2 * HALF
    rk = rq + off
    pairs = width // TILE
    tiles = rq // TILE

    def coming(r):
        return pl.BlockSpec((1, r, TILE), lambda s, p: (s, 0, jnp.minimum(p, pairs - 1)))

    def current(r):
        return pl.BlockSpec((1, r, TILE), lambda s, p: (s, 0, jnp.maximum(p - 1, 0)))

    def current_heads(*shape):
        return pl.BlockSpec((1, 2) + shape, lambda s, p: (s, jnp.maximum(p - 1, 0)) + (0,) * len(shape))

    def whole(r):
        return pl.BlockSpec((1, r, TILE), lambda s, p: (s, 0, 0))

    mapped = len(halo) == 2
    in_specs = [current(rq), coming(rq), coming(rq), coming(off), whole(rq), whole(rk),
                current_heads(tiles, TILE, off + TILE), current_heads(tiles, TILE, HALF)]
    out_specs = [current(rq), current_heads(tiles // 2, 2 * TILE, off + 2 * TILE), current(rq), current_heads(rq, TILE)]
    out_shape = [jax.ShapeDtypeStruct((n, rq, width), BF),
                 jax.ShapeDtypeStruct((n, 2 * pairs, tiles // 2, 2 * TILE, off + 2 * TILE), BF),
                 jax.ShapeDtypeStruct((n, rq, width), F32),
                 jax.ShapeDtypeStruct((n, 2 * pairs, rq, TILE), F32)]
    if mapped:
        in_specs += [coming(off)] * 2
    else:
        rank = halo[4].shape[0]

        def once(*shape):
            return pl.BlockSpec(shape, lambda s, p: (0,) * len(shape))

        def columns(r):
            return pl.BlockSpec((r, TILE), lambda s, p: (0, jnp.minimum(p, pairs - 1)))

        in_specs += [once(HALF, width)] * 2 + [columns(width)] * 2 + [once(rank, width)] * 2 + [columns(rank)] * 2
        out_specs += [coming(off)] * 2 + [once(off, rank)] * 2
        out_shape += [jax.ShapeDtypeStruct((n, off, width), BF)] * 2 + [jax.ShapeDtypeStruct((off, rank), BF)] * 2
    return pl.pallas_call(
        partial(forward_kernel, mapped, pairs),
        grid=(n, pairs + 1),
        in_specs=in_specs,
        out_specs=out_specs,
        out_shape=out_shape,
        scratch_shapes=[pltpu.VMEM((2, rk, TILE), BF), pltpu.VMEM((2, rk, TILE), BF),
                        pltpu.VMEM((2, tiles, TILE, HALF + TILE), BF)] * 2
        + [pltpu.VMEM((4, TILE, off + TILE), F32)],
        compiler_params=pltpu.CompilerParams(dimension_semantics=("arbitrary", "arbitrary"), vmem_limit_bytes=VMEM),
        cost_estimate=pl.CostEstimate(
            flops=32 * n * rq * off * width, bytes_accessed=60 * 10**6, transcendentals=0
        ),
        name="attention_forward",
    )(q, k, v, pq, qhot, kbias, query_scores, key_scores, *halo)


def spread_kernel(group, head_ref, ids_ref, late_hbm, ff_hbm, table_hbm, places_hbm, grad_hbm, gain_ref,
                  table_out, down_out, up_out, expand_down, expand_up, reduce_down, reduce_up, grad_out,
                  late_ref, ff_ref, table_ref, places_ref, grad_ref, table_made, down_made, up_made,
                  expand_down_made, expand_up_made, reduce_down_made, reduce_up_made, sems, out_sems):
    cores, peers, rank, part = late_ref.shape
    late_in = Loaded(late_hbm, late_ref, sems.at[3])
    ff_in = Loaded(ff_hbm, ff_ref, sems.at[4])
    table_in = Loaded(table_hbm, table_ref, sems.at[5])
    grad_in = Loaded(grad_hbm, grad_ref, sems.at[1])
    grad_done = Stored(grad_out, grad_ref, sems.at[2])
    down_done = Stored(down_out, down_made, out_sems.at[0])
    up_done = Stored(up_out, up_made, out_sems.at[1])
    table_done = Stored(table_out, table_made, out_sems.at[2])
    ff_done = [
        Stored(target, made, out_sems.at[3 + index])
        for index, (target, made) in enumerate(
            (
                (expand_down, expand_down_made),
                (expand_up, expand_up_made),
                (reduce_down, reduce_down_made),
                (reduce_up, reduce_up_made),
            )
        )
    ]
    width = table_ref.shape[3]
    ff = expand_up_made.shape[2]
    rest = ff_ref.shape[3]
    own = places_ref.shape[0]
    fetch = pltpu.make_async_copy(places_hbm.at[pl.ds(pl.multiple_of(head_ref[0] * own, own), own)], places_ref, sems.at[0])
    fetch.start()
    first = head_ref[0] * group
    weights = [
        [jnp.where(ids_ref[s, :1, :1] == (first + a).astype(F32), 1.0, 0.0) for a in range(group)] for s in range(cores)
    ]

    def fill(out, a, source, pieces):
        for column, piece in pieces:
            value = sum(weights[s][a] * source[s, piece[0], :, piece[1]].astype(F32) for s in range(cores))
            out[:, column] = value

    per = width // part
    starts = (0, width, width + ff, width + 2 * ff)
    late_in()
    for member in range(8):
        for a in range(group):
            out = (down_made if member < 4 else up_made).at[member % 4, a]
            fill(out, a, late_ref, [
                (slice(half * part, (half + 1) * part), (member * per + half, slice(0, part))) for half in range(per)
            ])
        if member == 3:
            down_done.copy.start()
    up_done.copy.start()
    ff_in()
    for done, start in zip(ff_done, starts):
        count = done.buffer.shape[2]
        pieces = []
        at = start
        while at < start + count:
            peer, offset = at // rest, at % rest
            length = min(rest - offset, start + count - at)
            pieces.append((slice(at - start, at - start + length), (peer, slice(offset, offset + length))))
            at += length
        for a in range(group):
            fill(done.buffer.at[a], a, ff_ref, pieces)
        done.copy.start()
    table_in()
    grad_in()
    grad_done.copy.start()
    fetch.wait()
    values = places_ref[...]
    centered = values - jnp.mean(values, axis=1, keepdims=True)
    inverse = lax.rsqrt(jnp.mean(centered * centered, axis=1, keepdims=True) + EPSILON)
    normed = centered * inverse
    upstream = table_ref[...].reshape(values.shape).astype(F32) * gain_ref[...]
    table_made[...] = inverse * (
        upstream
        - jnp.mean(upstream, axis=1, keepdims=True)
        - normed * jnp.mean(upstream * normed, axis=1, keepdims=True)
    )
    table_done.copy.start()
    for done in (grad_done, down_done, up_done, table_done, *ff_done):
        done.wait()


def spread_all(group, head, ids, late, ff_late, table, places, grad, gain, ff):
    rank = late.shape[2]
    width = table.shape[3]
    own = (places.shape[0] * group // ADAPTERS, width)
    vm = pl.BlockSpec(memory_space=pltpu.VMEM)
    sm = pl.BlockSpec(memory_space=pltpu.SMEM)
    hbm = pl.BlockSpec(memory_space=pltpu.HBM)

    shapes = [own] + [(4, group, rank, width)] * 2
    shapes += [(group, rank, width), (group, rank, ff), (group, rank, ff), (group, rank, width)]

    def out(*shape):
        return jax.ShapeDtypeStruct(shape, F32)

    return pl.pallas_call(
        partial(spread_kernel, group),
        in_specs=[sm, vm] + [hbm] * 5 + [vm],
        out_specs=[hbm] * 8,
        out_shape=[out(*shape) for shape in shapes] + [out(*grad.shape)],
        scratch_shapes=[pltpu.VMEM(array.shape, BF) for array in (late, ff_late, table)]
        + [pltpu.VMEM(own, F32), pltpu.VMEM(grad.shape, F32)]
        + [pltpu.VMEM(shape, F32) for shape in shapes]
        + [pltpu.SemaphoreType.DMA((6,)), pltpu.SemaphoreType.DMA((7,))],
        compiler_params=pltpu.CompilerParams(vmem_limit_bytes=VMEM),
        name="spread_all",
    )(head, ids, late, ff_late, table, places, grad, gain.reshape(1, width))


def backward_kernel(handed, q_ref, k_ref, kh_ref, v_ref, vh_ref, pk_ref, pq_ref, p_ref, g_ref, ctxf_ref, inv_ref, *refs):
    if handed:
        layer_ref, layer_out, *refs = refs
        layer_out[...] = layer_ref[...]
    dq_ref, dk_ref, dkh_ref, dv_ref, dvh_ref, dpk_ref, dpq_ref, kx_ref, vx_ref = refs[:9]
    qr_ref, gr_ref, e_ref, gc_ref, gk_ref, dvt_ref, dkt_ref = refs[9:]
    rows_q = q_ref.shape[1]
    rows_k = kx_ref.shape[0]
    kx_ref[...] = with_halo(k_ref, kh_ref)
    vx_ref[...] = with_halo(v_ref, vh_ref)
    tiles = rows_q // TILE
    key_tiles = rows_k // TILE
    span = 2 * HALF // TILE
    wide = (span + 2) * TILE
    flip = flip_matrix()
    scale = 1.0 / math.sqrt(3 * HEAD_DIM)
    tcol = lanes() < HEAD_DIM
    qcol = lanes((rows_q, TILE)) < HEAD_DIM
    over = lanes() > rows()
    under = lanes() >= rows()

    @pl.when((pl.program_id(0) == 0) & (pl.program_id(1) == 0))
    def _():
        gk_ref[...] = jnp.zeros_like(gk_ref)

    for t in range(tiles):
        at = slice(t * TILE, (t + 1) * TILE)
        qr_ref[at] = mm(flip, q_ref[0, at]).astype(BF)
        gr_ref[at] = mm(flip, g_ref[0, at]).astype(BF)
    q_rev = qr_ref[...]
    g_rev = gr_ref[...]
    q_turned = q_rev.T
    k_turned = kx_ref[...].T
    product = g_rev.astype(F32) * ctxf_ref[0]
    dvt_ref[...] = jnp.zeros_like(dvt_ref)
    dkt_ref[...] = jnp.zeros_like(dkt_ref)
    zero = jnp.zeros((TILE, TILE), BF)
    dq_main = [[], []]
    dq_parts = [None, None]
    dk_tiles = [[], []]

    def of_head(h):
        own = qcol if h == 0 else ~qcol
        inv = inv_ref[0, h]
        delta = jnp.sum(jnp.where(own, product, 0.0), axis=1, keepdims=True) * inv
        g_turned = (g_rev.astype(F32) * inv).astype(BF).T[h * HEAD_DIM : (h + 1) * HEAD_DIM]
        return jnp.where(own, g_rev, jnp.zeros_like(g_rev)), inv, delta, g_turned

    heads = [of_head(h) for h in range(2)]

    def errors(h, u):
        g_masked, inv, delta, g_turned = heads[h]
        part = slice(h * HEAD_DIM, (h + 1) * HEAD_DIM)
        at = slice(u * 2 * TILE, (u + 1) * 2 * TILE)
        window = slice(u * 2 * TILE, u * 2 * TILE + wide)
        prob = p_ref[0, h, u]
        g_probs = mm(g_masked[at], vx_ref[window], NT)
        inv_u = jnp.concatenate([inv[at]] * (span + 2), axis=1)
        delta_u = jnp.concatenate([delta[at]] * (span + 2), axis=1)
        e = (prob.astype(F32) * (g_probs * inv_u - delta_u)).astype(BF)
        e_ref[h, u] = e
        dvt_ref[part, window] += mm(g_turned[:, at], prob)
        dkt_ref[part, window] += mm(q_turned[part, at], e)
        dq_main[h].append(mm(e, kx_ref[window]))

    def error(h, t, d):
        a = t % 2
        return e_ref[h, t // 2, a * TILE : (a + 1) * TILE, (a + d) * TILE : (a + d + 1) * TILE]

    def distances(h, t):
        here = None
        for d in range(span + 1):
            block = pltpu.roll(error(h, t, d), 1, 1, stride=1, stride_axis=0)
            if d > 0:
                gc_ref[h, t * TILE : (t + 1) * TILE, (d - 1) * TILE : d * TILE] = jnp.where(over, block, here)
            here = block

    def end_queries(h):
        part = slice(h * HEAD_DIM, (h + 1) * HEAD_DIM)
        dq_parts[h] = jnp.concatenate(dq_main[h], axis=0) + mm(gc_ref[h], pk_ref[0])
        dpk_ref[0, part, :] = (mm(q_turned[part], gc_ref[h]) * scale).astype(BF)

    def keys(h, j):
        spun = {j - t: skew(error(h, t, j - t).T) for t in range(tiles) if 0 <= j - t <= span}
        low = max(min(spun) - 1, 0)
        high = min(max(spun), span - 1)
        at = slice(j * TILE, (j + 1) * TILE)
        for c in range(low, high + 1):
            gk_ref[h, at, c * TILE : (c + 1) * TILE] = jnp.where(under, spun.get(c + 1, zero), spun.get(c, zero))
        cols = slice(low * TILE, (high + 1) * TILE)
        dk_tiles[h].append(mm(gk_ref[h, at, cols], pq_ref[0, cols]))

    def end_keys(h):
        part = slice(h * HEAD_DIM, (h + 1) * HEAD_DIM)
        for c in range(0, span, 2):
            near = slice(c * TILE, (c + tiles + 2) * TILE)
            cols = slice(c * TILE, (c + 2) * TILE)
            dpq_ref[0, part, cols] = (mm(k_turned[part, near], gk_ref[h, near, cols]) * scale).astype(BF)

    for h in range(2):
        for u in range(tiles // 2):
            errors(h, u)
            distances(h, 2 * u)
            distances(h, 2 * u + 1)
        end_queries(h)
        for j in range(key_tiles):
            keys(h, j)
        end_keys(h)
    dk_parts = [jnp.concatenate(found, axis=0) for found in dk_tiles]
    dq = (jnp.where(qcol, dq_parts[0], dq_parts[1]) * scale).astype(BF)
    for t in range(tiles):
        at = slice(t * TILE, (t + 1) * TILE)
        dq_ref[0, at] = mm(flip, dq[at]).astype(BF)
    kcol = lanes((rows_k, TILE)) < HEAD_DIM
    dk = ((dkt_ref[...].T + jnp.where(kcol, dk_parts[0], dk_parts[1])) * scale).astype(BF)
    dv = dvt_ref[...].astype(BF).T
    for whole, own_ref, halo_ref in ((dk, dk_ref, dkh_ref), (dv, dv_ref, dvh_ref)):
        halo_ref[0, :HALF] = whole[:HALF]
        own_ref[0] = whole[HALF : HALF + rows_q]
        halo_ref[0, HALF:] = whole[HALF + rows_q :]


def attention_backward(q, k, k_halo, v, v_halo, pk, pq, probs, g, ctxf, inv, *layer):
    n, rq, width = q.shape
    off = 2 * HALF
    rk = rq + off
    pairs = width // TILE
    wide = off + 2 * TILE
    def col(r):
        return pl.BlockSpec((1, r, TILE), lambda s, p: (s, 0, p))
    def row(r):
        return pl.BlockSpec((1, TILE, r), lambda s, p: (s, p, 0))
    return pl.pallas_call(
        partial(backward_kernel, len(layer) > 0),
        grid=(n, pairs),
        in_specs=[col(rq), col(rq), col(off), col(rq), col(off), col(off), col(off),
                  pl.BlockSpec((1, 2, rq // (2 * TILE), 2 * TILE, wide), lambda s, p: (s, p, 0, 0, 0)),
                  col(rq), col(rq),
                  pl.BlockSpec((1, 2, rq, TILE), lambda s, p: (s, p, 0, 0))] + [col(rq)] * len(layer),
        out_specs=[col(rq)] * len(layer) + [col(rq), col(rq), col(off), col(rq), col(off), row(off), row(off)],
        out_shape=[jax.ShapeDtypeStruct(array.shape, array.dtype) for array in layer]
        + [jax.ShapeDtypeStruct((n, rq, width), BF),
                   jax.ShapeDtypeStruct((n, rq, width), BF),
                   jax.ShapeDtypeStruct((n, off, width), BF),
                   jax.ShapeDtypeStruct((n, rq, width), BF),
                   jax.ShapeDtypeStruct((n, off, width), BF),
                   jax.ShapeDtypeStruct((n, width, off), BF),
                   jax.ShapeDtypeStruct((n, width, off), BF)],
        scratch_shapes=[pltpu.VMEM((rk, TILE), BF), pltpu.VMEM((rk, TILE), BF), pltpu.VMEM((rq, TILE), BF), pltpu.VMEM((rq, TILE), BF),
                        pltpu.VMEM((2, rq // (2 * TILE), 2 * TILE, wide), BF),
                        pltpu.VMEM((2, rq, off), BF),
                        pltpu.VMEM((2, rk, off), BF),
                        pltpu.VMEM((TILE, rk), F32), pltpu.VMEM((TILE, rk), F32)],
        compiler_params=pltpu.CompilerParams(dimension_semantics=("arbitrary", "arbitrary"), vmem_limit_bytes=VMEM),
        name="attention_backward",
    )(q, k, k_halo, v, v_halo, pk, pq, probs, g, ctxf, inv, *layer)


def gather_rows(left, right):
    return lax.dot_general(left, right, (((0,), (0,)), ((), ())), preferred_element_type=F32)


def whereabouts(shape):
    groups, blocks = shape[:2]
    seq, head, core = lax.axis_index("seq"), lax.axis_index("head"), lax.axis_index("batch")
    return blocks * groups, seq * groups + head, lambda p: (p // groups, p % groups, core), (seq, head, core)


def signal(barrier, device):
    pl.semaphore_signal(barrier, inc=1, device_id=device, device_id_type=MESH)


def remote(source, target, send_sem, recv_sem, device):
    return pltpu.make_async_remote_copy(
        src_ref=source, dst_ref=target, send_sem=send_sem, recv_sem=recv_sem, device_id=device, device_id_type=MESH
    )


def each(first, end, step):
    lax.fori_loop(first, end, lambda k, carry: (step(k), carry)[1], 0)


def finish_kernel(shape, names, *refs):
    groups, blocks, cores, rank = shape
    r = SimpleNamespace(**dict(zip(names, refs)))
    peers, me, place, (seq, head, core) = whereabouts(shape)
    partner = (seq, head, 1 - core)
    width = r.table_out.shape[3]

    held = SimpleNamespace()
    for index, name in enumerate(names[:LOADS]):
        target = refs[len(refs) - LOADS + index]
        setattr(held, name, Loaded(refs[index], target, r.load_sems.at[index], start=index < FIRST_LOADS))

    barrier = pltpu.get_barrier_semaphore()
    signal(barrier, partner)
    each(1, peers, lambda k: signal(barrier, place((me + k) % peers)))

    def inner_grad(gradient, up):
        return (ADAPTER_SCALING * mm(gradient, up[...], NT)).astype(BF)

    halo_buf, halo_recv, halo_sems = r.halo_buf, r.halo_recv, r.halo_sems
    half = HALF // 2

    def crossing(side, piece):
        there = place(jnp.maximum(me - 1, 0) if side == 0 else jnp.minimum(me + 1, peers - 1))
        return remote(
            halo_buf.at[side, piece], halo_recv.at[1 - side, piece],
            halo_sems.at[4 * side + 2 * piece], halo_sems.at[4 * side + 2 * piece + 1], there,
        )

    def start_crossing(side, piece):
        @pl.when(me > 0 if side == 0 else me < peers - 1)
        def _():
            crossing(side, piece).start()
    key_halo, value_halo = held.key_halo(), held.value_halo()
    key_hu, value_hu = inner_grad(key_halo, r.key_b), inner_grad(value_halo, r.value_b)
    key_w, value_w = held.key_w(), held.value_w()
    for name in names[FIRST_LOADS:LOADS]:
        getattr(held, name).copy.start()

    def map_piece(piece):
        for side in range(2):
            start = side * HALF + piece * half
            at = slice(start, start + half)
            halo_buf[side, piece] = (
                mm(key_halo[at], key_w, NT)
                + mm(value_halo[at], value_w, NT)
                + mm(key_hu[at], r.key_a[...])
                + mm(value_hu[at], r.value_a[...])
            ).astype(BF)
            if piece == 0 and side == 0:
                pl.semaphore_wait(barrier, peers)
            start_crossing(side, piece)

    map_piece(0)

    def give_f(p):
        return remote(r.ff, r.ff_out.at[core, me], r.spread_f.at[p], r.arrive_f.at[me], place(p))

    def on_f(p):
        return remote(r.ff_out.at[core, p], r.ff_out.at[core, p], r.pass_f.at[p], r.other_f.at[p], partner)

    def got_f(k):
        p = (me + peers - k) % peers
        remote(r.ff, r.ff_out.at[core, p], r.spread_f.at[p], r.arrive_f.at[p], place(p)).wait_recv()
        on_f(p).start()

    def end_f(k):
        p = k - 1
        remote(r.ff_out.at[1 - core, p], r.ff_out.at[1 - core, p], r.pass_f.at[p], r.other_f.at[p], partner).wait_recv()
        on_f(p).wait_send()

    r.ff_out[core, me] = r.ff[...]
    each(1, peers, lambda k: give_f((me + k) % peers).start())
    on_f(me).start()

    table_ref, stage_ref, recv_ref, sum_ref = r.table, r.stage, r.recv, r.sum
    core_ref, core_sems = r.core, r.core_sems
    position_q = mm(held.back_hot(), held.query_rel_g(), NT).astype(BF)
    position_k = mm(held.key_hot(), held.key_rel_g(), NT).astype(BF)
    query_pg, key_pg = inner_grad(position_q, r.query_b), inner_grad(position_k, r.key_b)
    query_w = held.query_w()
    table = (
        mm(position_q, query_w, NT)
        + mm(position_k, key_w, NT)
        + mm(query_pg, r.query_a[...])
        + mm(key_pg, r.key_a[...])
    ).astype(BF)
    for group in range(groups):
        for block in range(blocks):
            for side in range(cores):
                start = ((group * blocks + block) * cores + side) * rank
                table_ref[side, block * groups + group] = table[start : start + rank]
    swap = remote(table_ref.at[1 - core], core_ref, core_sems.at[0], core_sems.at[1], partner)
    swap.start()
    r.ids_out[core] = r.own_id[...]
    tell = remote(r.own_id, r.ids_out.at[core], core_sems.at[2], core_sems.at[3], partner)
    tell.start()

    x, x_before, x_after, low = held.x(), held.x_before(), held.x_after(), held.low()
    query_g, key_g, value_g = held.query_g(), held.key_g(), held.value_g()
    query_gu, key_gu, value_gu = inner_grad(query_g, r.query_b), inner_grad(key_g, r.key_b), inner_grad(value_g, r.value_b)
    def of_halo(inner):
        return gather_rows(inner[:HALF], x_before) + gather_rows(inner[HALF:], x_after)

    pieces = [
        gather_rows(query_gu, x) + gather_rows(query_pg, low),
        gather_rows(key_gu, x) + of_halo(key_hu) + gather_rows(key_pg, low),
        gather_rows(value_gu, x) + of_halo(value_hu),
        r.out_ga[...],
        ADAPTER_SCALING * (gather_rows(r.query_u[...], query_g) + gather_rows(r.query_pu[...], position_q)),
        ADAPTER_SCALING
        * (
            gather_rows(r.key_u[...], key_g)
            + gather_rows(r.key_uh[...], key_halo)
            + gather_rows(r.key_pu[...], position_k)
        ),
        ADAPTER_SCALING * (gather_rows(r.value_u[...], value_g) + gather_rows(r.value_uh[...], value_halo)),
        r.out_gb[...],
    ]
    part = len(pieces) * width // peers
    per = width // part
    for index, piece in enumerate(pieces):
        for cut in range(per):
            stage_ref[index * per + cut, :, width : width + part] = piece[:, cut * part : (cut + 1) * part].astype(BF)

    send_sems, recv_sems = r.send_sems, r.recv_sems
    swap.wait()

    def to_peer(p):
        return remote(stage_ref.at[p], recv_ref.at[me], send_sems.at[p], recv_sems.at[me], place(p))

    def send(k):
        p = (me + k) % peers
        stage_ref[p, :, :width] = (table_ref[core, p].astype(F32) + core_ref[p].astype(F32)).astype(BF)
        to_peer(p).start()

    each(1, peers, send)
    map_piece(1)
    each(1, peers, got_f)
    sum_ref[:, :width] = table_ref[core, me].astype(F32) + core_ref[me].astype(F32)
    sum_ref[:, width:] = stage_ref[me, :, width:].astype(F32)

    grad_ref = r.grad_made
    grad_done = Stored(r.grad_out, grad_ref, r.grad_sem.at[0])
    grad_ref[...] = (
        held.grad_one()
        + mm(query_g, query_w, NT)
        + mm(key_g, key_w, NT)
        + mm(value_g, value_w, NT)
        + mm(query_gu, r.query_a[...])
        + mm(key_gu, r.key_a[...])
        + mm(value_gu, r.value_a[...])
    )

    def take(k):
        p = (me + peers - k) % peers
        remote(stage_ref.at[p], recv_ref.at[p], send_sems.at[p], recv_sems.at[p], place(p)).wait_recv()
        sum_ref[...] += recv_ref[p].astype(F32)

    each(1, peers, take)
    mine_t, mine_l, table_out, late_out = r.mine_t, r.mine_l, r.table_out, r.late_out
    mine_t[...] = sum_ref[:, :width].astype(BF)
    mine_l[...] = sum_ref[:, width:].astype(BF)
    late_out[core, me] = mine_l[...]
    table_out[seq, core] = mine_t[...]

    def give_l(p):
        return remote(mine_l, late_out.at[core, me], r.spread_l.at[p], r.arrive_l.at[me], place(p))

    def give_t(s):
        return remote(mine_t, table_out.at[seq, core], r.spread_t.at[s], r.arrive_t.at[seq], (s, head, core))

    each(1, peers, lambda k: give_l((me + k) % peers).start())
    each(1, blocks, lambda k: give_t((seq + k) % blocks).start())

    def on_l(p):
        return remote(late_out.at[core, p], late_out.at[core, p], r.pass_l.at[p], r.other_l.at[p], partner)

    def on_t(s):
        return remote(table_out.at[s, core], table_out.at[s, core], r.pass_t.at[s], r.other_t.at[s], partner)

    on_l(me).start()
    on_t(seq).start()

    def got_l(k):
        p = (me + peers - k) % peers
        remote(mine_l, late_out.at[core, p], r.spread_l.at[p], r.arrive_l.at[p], place(p)).wait_recv()
        on_l(p).start()

    def got_t(k):
        s = (seq + blocks - k) % blocks
        remote(mine_t, table_out.at[s, core], r.spread_t.at[s], r.arrive_t.at[s], (s, head, core)).wait_recv()
        on_t(s).start()

    each(1, peers, got_l)
    each(1, blocks, got_t)

    @pl.when(me > 0)
    def _():
        for piece in range(2):
            crossing(0, piece).wait_send()
            crossing(1, piece).wait_recv()
        grad_ref[...] += halo_recv[0].astype(F32).reshape(HALF, width)

    @pl.when(me < peers - 1)
    def _():
        for piece in range(2):
            crossing(1, piece).wait_send()
            crossing(0, piece).wait_recv()
        grad_ref[...] += halo_recv[1].astype(F32).reshape(HALF, width)

    def end_l(k):
        p = k - 1
        remote(late_out.at[1 - core, p], late_out.at[1 - core, p], r.pass_l.at[p], r.other_l.at[p], partner).wait_recv()
        on_l(p).wait_send()

    def end_t(k):
        s = k - 1
        remote(table_out.at[s, 1 - core], table_out.at[s, 1 - core], r.pass_t.at[s], r.other_t.at[s], partner).wait_recv()
        on_t(s).wait_send()

    grad_done.copy.start()
    tell.wait()
    each(1, peers + 1, end_f)
    each(1, peers + 1, end_l)
    each(1, blocks + 1, end_t)

    def sent(k):
        p = (me + k) % peers
        to_peer(p).wait_send()
        give_l(p).wait_send()
        give_f(p).wait_send()

    each(1, peers, sent)
    each(1, blocks, lambda k: give_t((seq + k) % blocks).wait_send())
    grad_done.wait()


LOADS = 17
FIRST_LOADS = 4


def finish(shape, **arrays):
    groups, blocks, cores, rank = shape
    peers = groups * blocks
    rows, width = arrays[list(arrays)[LOADS - 1]].shape
    share = 8 * width // peers
    ff = arrays[list(arrays)[-1]]
    vm = pl.BlockSpec(memory_space=pltpu.VMEM)
    hbm = pl.BlockSpec(memory_space=pltpu.HBM)
    dma = pltpu.SemaphoreType.DMA
    outputs = dict(
        grad_out=jax.ShapeDtypeStruct((rows, width), F32),
        table_out=jax.ShapeDtypeStruct((blocks, cores, rank, width), BF),
        late_out=jax.ShapeDtypeStruct((cores, peers, rank, share), BF),
        ids_out=jax.ShapeDtypeStruct((cores, 8, TILE), F32),
        ff_out=jax.ShapeDtypeStruct((cores, peers) + ff.shape, BF),
    )
    scratch = dict(
        load_sems=dma((LOADS,)),
        grad_made=pltpu.VMEM((rows, width), F32),
        grad_sem=dma((1,)),
        halo_buf=pltpu.VMEM((2, 2, HALF // 2, width), BF),
        halo_recv=pltpu.VMEM((2, 2, HALF // 2, width), BF),
        halo_sems=dma((8,)),
        table=pltpu.VMEM((cores, peers, rank, width), BF),
        core=pltpu.VMEM((peers, rank, width), BF),
        stage=pltpu.VMEM((peers, rank, width + share), BF),
        recv=pltpu.VMEM((peers, rank, width + share), BF),
        sum=pltpu.VMEM((rank, width + share), F32),
        mine_t=pltpu.VMEM((rank, width), BF),
        mine_l=pltpu.VMEM((rank, share), BF),
        core_sems=dma((4,)),
        send_sems=dma((peers,)),
        recv_sems=dma((peers,)),
        spread_l=dma((peers,)),
        arrive_l=dma((peers,)),
        pass_l=dma((peers,)),
        other_l=dma((peers,)),
        spread_t=dma((blocks,)),
        arrive_t=dma((blocks,)),
        pass_t=dma((blocks,)),
        other_t=dma((blocks,)),
        spread_f=dma((peers,)),
        arrive_f=dma((peers,)),
        pass_f=dma((peers,)),
        other_f=dma((peers,)),
    )
    names = (*arrays, *outputs, *scratch)
    kept = [pltpu.VMEM(array.shape, array.dtype) for array in list(arrays.values())[:LOADS]]
    return pl.pallas_call(
        partial(finish_kernel, shape, names),
        in_specs=[hbm] * LOADS + [vm] * (len(arrays) - LOADS),
        out_specs=[hbm] + [vm] * (len(outputs) - 1),
        out_shape=list(outputs.values()),
        scratch_shapes=list(scratch.values()) + kept,
        compiler_params=pltpu.CompilerParams(
            collective_id=0, has_side_effects=True, vmem_limit_bytes=VMEM
        ),
        name="finish",
    )(*arrays.values())


def middle_kernel(seqs, shape, context_hbm, tokens_hbm, cotangent_hbm, out_w_hbm, up_w_hbm, down_w_hbm,
                  out_a_ref, out_b_ref, up_a_ref, up_b_ref, down_a_ref, down_b_ref, gain_one_ref, gain_two_ref,
                  layer_hbm, grad_one_hbm, grad_context_ref, out_ga_ref, out_gb_ref, result_ref,
                  out_w, up_w, down_w, hidden_ref, low_ref, work_ref, act_ref, slope_ref,
                  context_ref, tokens_ref, cotangent_ref, layer_ref, grad_one_ref, sems, *refs):
    if shape is None:
        ff_ref = result_ref
    else:
        ff_ref, stage_ref, recv_ref, send_sems, recv_sems = refs
        peers, me, place, _ = whereabouts(shape)
        barrier = pltpu.get_barrier_semaphore()
        each(1, peers, lambda k: signal(barrier, place((me + k) % peers)))

    def to_peer(p):
        return remote(stage_ref.at[p], recv_ref.at[me], send_sems.at[p], recv_sems.at[me], place(p))

    def send(first):
        if shape is None:
            return
        half = peers // 2
        part = stage_ref.shape[2]
        for p in range(first, first + half):
            stage_ref[p] = ff_ref[0, :, p * part : (p + 1) * part].astype(BF)

        def start(k):
            p = first + (me + k) % half

            @pl.when(p != me)
            def _():
                to_peer(p).start()

        each(0, half, start)

    rows, width = tokens_ref.shape
    ff = up_w.shape[1]
    share = rows // seqs
    chunk = 512
    context_in, out_in, tokens_in, up_in, down_in, cotangent_in = (
        Loaded(source, target, sems.at[index])
        for index, (source, target) in enumerate(
            (
                (context_hbm, context_ref),
                (out_w_hbm, out_w),
                (tokens_hbm, tokens_ref),
                (up_w_hbm, up_w),
                (down_w_hbm, down_w),
                (cotangent_hbm, cotangent_ref),
            )
        )
    )
    layer_out = Stored(layer_hbm, layer_ref, sems.at[6])
    grad_one_out = Stored(grad_one_hbm, grad_one_ref, sems.at[7])

    half = rows // 2
    sides = (slice(0, half), slice(half, rows))

    def parts(side, step):
        if seqs == 1:
            return step(0, slice(0, half))
        per = seqs // 2
        return jnp.concatenate(
            [step(side * per + s, slice(s * share, (s + 1) * share)) for s in range(per)], axis=0
        )

    def inner(side, values, factor_ref, scale=1.0):
        return parts(side, lambda s, at: (scale * mm(values[at], factor_ref[s], NT)).astype(BF))

    def widened(side, inner_values, factor_ref, columns=slice(None)):
        return parts(side, lambda s, at: mm(inner_values[at], factor_ref[s, :, columns]))

    def factor_grad(left, right, s):
        at = slice(s * share, (s + 1) * share)
        return gather_rows(left[at], right[at])

    def joined(pair):
        return jnp.concatenate(pair, axis=0)

    def stats(values):
        centered = values - jnp.mean(values, axis=1, keepdims=True)
        inverse = lax.rsqrt(jnp.mean(centered * centered, axis=1, keepdims=True) + EPSILON)
        return centered * inverse, inverse

    def back(normed, inverse, gain, upstream):
        scaled = upstream * gain
        return inverse * (
            scaled
            - jnp.mean(scaled, axis=1, keepdims=True)
            - normed * jnp.mean(scaled * normed, axis=1, keepdims=True)
        )

    context = context_in()
    inner_out = [inner(side, context[at], out_a_ref) for side, at in enumerate(sides)]
    out_in()
    attended = [
        mm(context[at], out_w[...]) + ADAPTER_SCALING * widened(side, inner_out[side], out_b_ref)
        for side, at in enumerate(sides)
    ]
    tokens_in()
    inverse_one = [None, None]
    inner_up = [None, None]

    def norm_one(side):
        at = sides[side]
        normed, inverse_one[side] = stats(tokens_ref[at] + attended[side])
        grad_one_ref[at] = normed
        hidden = normed * gain_one_ref[...]
        hidden_ref[at] = hidden
        low_ref[at] = hidden.astype(BF)
        inner_up[side] = inner(side, low_ref[at], up_a_ref)

    def activate(side, start):
        at = sides[side]
        columns = slice(start, start + chunk)
        pre = mm(low_ref[at], up_w[:, columns]) + ADAPTER_SCALING * widened(side, inner_up[side], up_b_ref, columns)
        below = 0.5 + 0.5 * lax.erf(pre * math.sqrt(0.5))
        act_ref[at, columns] = (pre * below).astype(BF)
        density = jnp.exp(pre * pre * -0.5) * (1.0 / math.sqrt(2.0 * math.pi))
        slope_ref[at, columns] = (below + pre * density).astype(BF)

    norm_one(0)
    up_in()
    activate(0, 0)
    norm_one(1)
    for start in range(chunk, ff, chunk):
        activate(0, start)
    for start in range(0, ff, chunk):
        activate(1, start)
    down_in()
    inner_down = [None, None]
    branch = [None, None]
    for side, at in enumerate(sides):
        inner_down[side] = inner(side, act_ref[at], down_a_ref)
        branch[side] = mm(act_ref[at], down_w[...]) + ADAPTER_SCALING * widened(side, inner_down[side], down_b_ref)
    cotangent_in()
    grad_two = [None, None]
    grad_inner = [None, None]

    def norm_two(side):
        at = sides[side]
        normed, inverse = stats(hidden_ref[at] + branch[side])
        layer_ref[at] = normed * gain_two_ref[...]
        work_ref[at] = back(normed, inverse, gain_two_ref[...], cotangent_ref[at])
        grad_two[side] = work_ref[at].astype(BF)
        grad_inner[side] = inner(side, grad_two[side], down_b_ref, ADAPTER_SCALING)

    def back_activate(side, start):
        at = sides[side]
        columns = slice(start, start + chunk)
        grad_act = mm(grad_two[side], down_w[columns, :], NT) + widened(side, grad_inner[side], down_a_ref, columns)
        slope_ref[at, columns] = (grad_act.astype(BF).astype(F32) * slope_ref[at, columns].astype(F32)).astype(BF)

    norm_two(0)
    back_activate(0, 0)
    norm_two(1)
    layer_out.copy.start()
    for start in range(chunk, ff, chunk):
        back_activate(0, start)
    all_two, all_inner, all_down = joined(grad_two), joined(grad_inner), joined(inner_down)
    for s in range(seqs):
        ff_ref[s, :, width + 2 * ff:] = ADAPTER_SCALING * factor_grad(all_down, all_two, s)
        ff_ref[s, :, width + ff:width + 2 * ff] = factor_grad(all_inner, act_ref, s)
    if shape is not None:
        pl.semaphore_wait(barrier, peers - 1)
        send(peers // 2)
    for start in range(0, ff, chunk):
        back_activate(1, start)
    grad_inner = [inner(side, slope_ref[at], up_b_ref, ADAPTER_SCALING) for side, at in enumerate(sides)]
    all_inner, all_up = joined(grad_inner), joined(inner_up)
    for s in range(seqs):
        ff_ref[s, :, width:width + ff] = ADAPTER_SCALING * factor_grad(all_up, slope_ref, s)
        ff_ref[s, :, :width] = factor_grad(all_inner, low_ref, s)
    send(0)
    grad_hidden = [
        mm(slope_ref[at], up_w[...], NT) + widened(side, grad_inner[side], up_a_ref) for side, at in enumerate(sides)
    ]
    grad_low = [None, None]
    for side, at in enumerate(sides):
        grad_one = back(grad_one_ref[at], inverse_one[side], gain_one_ref[...], grad_hidden[side] + work_ref[at])
        grad_one_ref[at] = grad_one
        grad_low[side] = grad_one.astype(BF)
        grad_inner[side] = inner(side, grad_low[side], out_b_ref, ADAPTER_SCALING)
        grad_context_ref[at] = (
            mm(grad_low[side], out_w[...], NT) + widened(side, grad_inner[side], out_a_ref)
        ).astype(BF)
    grad_one_out.copy.start()
    all_low, all_inner, all_out = joined(grad_low), joined(grad_inner), joined(inner_out)
    for s in range(seqs):
        out_gb_ref[s] = ADAPTER_SCALING * factor_grad(all_out, all_low, s)
        out_ga_ref[s] = factor_grad(all_inner, context, s)
    layer_out.wait()
    grad_one_out.wait()
    if shape is not None:
        ff_ref[0, :, : stage_ref.shape[2]] = stage_ref[me].astype(F32)

        def take(k):
            p = (me + peers - k) % peers
            remote(stage_ref.at[p], recv_ref.at[p], send_sems.at[p], recv_sems.at[p], place(p)).wait_recv()
            ff_ref[0, :, : stage_ref.shape[2]] += recv_ref[p].astype(F32)

        each(1, peers, take)
        result_ref[...] = ff_ref[0, :, : stage_ref.shape[2]].astype(BF)
        each(1, peers, lambda k: to_peer((me + k) % peers).wait_send())


def middle(context, tokens, cotangent, out_weight, up_weight, down_weight, factors, gain_one, gain_two, shape=None):
    seqs, share, width = tokens.shape
    rows = seqs * share
    ff = up_weight.shape[1]
    rank = factors[0].shape[1]
    vm = pl.BlockSpec(memory_space=pltpu.VMEM)
    hbm = pl.BlockSpec(memory_space=pltpu.HBM)
    wide = jax.ShapeDtypeStruct((rows, width), F32)
    factor = jax.ShapeDtypeStruct((seqs, rank, width), F32)
    columns = 2 * width + 2 * ff
    result = jax.ShapeDtypeStruct((seqs, rank, columns), F32)
    extra = []
    params = pltpu.CompilerParams(vmem_limit_bytes=VMEM)
    if shape is not None:
        peers = shape[0] * shape[1]
        result = jax.ShapeDtypeStruct((rank, columns // peers), BF)
        extra = [pltpu.VMEM((seqs, rank, columns), F32)] + [pltpu.VMEM((peers, rank, columns // peers), BF)] * 2
        extra += [pltpu.SemaphoreType.DMA((peers,))] * 2
        params = pltpu.CompilerParams(vmem_limit_bytes=VMEM, collective_id=1, has_side_effects=True)
    found = pl.pallas_call(
        partial(middle_kernel, seqs, shape),
        in_specs=[hbm] * 6 + [vm] * 8,
        out_specs=[hbm] * 2 + [vm] * 4,
        out_shape=[wide, wide, jax.ShapeDtypeStruct((rows, width), BF), factor, factor, result],
        scratch_shapes=[
            pltpu.VMEM(out_weight.shape, BF), pltpu.VMEM(up_weight.shape, BF), pltpu.VMEM(down_weight.shape, BF),
            pltpu.VMEM((rows, width), F32), pltpu.VMEM((rows, width), BF), pltpu.VMEM((rows, width), F32),
            pltpu.VMEM((rows, ff), BF), pltpu.VMEM((rows, ff), BF),
            pltpu.VMEM((rows, width), BF), *[pltpu.VMEM((rows, width), F32)] * 4, pltpu.SemaphoreType.DMA((8,)),
        ] + extra,
        compiler_params=params,
        cost_estimate=pl.CostEstimate(flops=36 * rows * width * width, bytes_accessed=24 * width * width, transcendentals=rows * ff),
        name="middle",
    )(context.reshape(rows, width), tokens.reshape(rows, width), cotangent.reshape(rows, width),
      out_weight, up_weight, down_weight, *factors, gain_one.reshape(1, width), gain_two.reshape(1, width))
    return [array.reshape(seqs, share, width) for array in found[:3]] + list(found[3:])


def shifted(value, axes, steps):
    count = math.prod(lax.axis_size(axis) for axis in axes)
    initial, last = (max(0, -steps), min(count, count - steps))
    return lax.ppermute(value, axes, [(source, source + steps) for source in range(initial, last)])


def bucket_of(offset, buckets, distance_cap):
    middle = buckets // 2
    sign_of = np.sign(offset)
    magnitude = np.where((offset < middle) & (offset > -middle), middle - 1, np.abs(offset))
    log_place = (
        np.ceil(np.log(magnitude / middle) / np.log((distance_cap - 1) / middle) * (middle - 1))
        + middle
    )
    return np.where(np.abs(offset) <= middle, offset, log_place * sign_of).astype(np.int32)


def offset_tables():
    place = np.arange(2 * HALF)

    def hot(distance, sign):
        clipped = np.clip(distance, 1 - HALF, HALF - 1)
        bucket = np.clip(BUCK + sign * bucket_of(clipped, BUCK, SPAN), 0, 2 * BUCK - 1)
        return np.eye(2 * BUCK, dtype=np.float32)[bucket]

    return hot(HALF - place, 1), hot(place - HALF, -1), hot(HALF - 1 - place, -1)


def segment_ids(lengths, positions):
    bounds = jnp.cumsum(lengths, axis=-1, dtype=jnp.int32)
    return jnp.sum(
        (bounds[..., None, :] <= positions[:, None]).astype(jnp.int32), axis=-1, dtype=jnp.int32
    )


def product(pattern, left_side, right_side):
    return jnp.einsum(pattern, left_side, right_side, preferred_element_type=F32)


def norm_stats(values):
    centered = values - jnp.mean(values, axis=-1, keepdims=True)
    inverse = lax.rsqrt(jnp.mean(centered * centered, axis=-1, keepdims=True) + EPSILON)
    return (centered * inverse, inverse)


def norm_back(normed, inverse, scale_gain, upstream):
    scaled = upstream * scale_gain
    return inverse * (
        scaled
        - jnp.mean(scaled, axis=-1, keepdims=True)
        - normed * jnp.mean(scaled * normed, axis=-1, keepdims=True)
    )


def adapter_forward(rows_in, weight, down, up):
    inner = product("sti,sir->str", rows_in, down).astype(BF)
    mapped = product("sti,io->sto", rows_in, weight) + ADAPTER_SCALING * product(
        "str,sro->sto", inner, up
    )
    return (mapped, inner)


def adapter_back(rows_in, inner, weight, down, up, gradient):
    grad_up = ADAPTER_SCALING * product("str,sto->sro", inner, gradient)
    grad_inner = (ADAPTER_SCALING * product("sto,sro->str", gradient, up)).astype(BF)
    grad_down = product("sti,str->sir", rows_in, grad_inner)
    grad_in = product("sto,io->sti", gradient, weight) + product("str,sir->sti", grad_inner, down)
    return (grad_in, grad_down, grad_up)


def body(
    tokens,
    cotangent,
    doc_lengths,
    adapter_ids,
    query_weight,
    key_weight,
    value_weight,
    output_weight,
    up_weight,
    down_weight,
    attention_gain,
    feedforward_gain,
    position_gain,
    position_table,
    attention_down,
    attention_up,
    expand_down,
    expand_up,
    reduce_down,
    reduce_up,
):
    seqs, row_count, width = tokens.shape
    head_groups = lax.axis_size("head")
    head_index = lax.axis_index("head")
    seq_index = lax.axis_index("seq")
    by_rows = seqs == 1 and row_count == HALF

    def turned(array):
        return jnp.swapaxes(array, -1, -2)

    token_low = lax.optimization_barrier(tokens.astype(BF))
    frozen = (query_weight, key_weight, value_weight)

    def columns(matrix):
        if by_rows:
            return matrix
        local = width // head_groups
        return lax.dynamic_slice_in_dim(matrix, head_index * local, local, matrix.ndim - 1)

    if by_rows:
        block_axes = ("seq", "head")
        block_index = seq_index * head_groups + head_index
        query_count = row_count
    else:
        block_axes = ("seq",)
        block_index = seq_index
        query_count = row_count * head_groups
    blocks = math.prod(lax.axis_size(axis) for axis in block_axes)

    first_place = block_index * query_count - HALF
    factors, query_seg, key_bias = prepare(
        adapter_ids,
        doc_lengths,
        jnp.stack([first_place, query_count * blocks]).astype(jnp.int32),
        [turned(attention_down), attention_up, turned(expand_down), expand_up, turned(reduce_down), reduce_up],
        query_count,
    )
    downs, att_up = factors[:4], factors[4:8]
    att_down = [turned(factor) for factor in downs]

    def halo(array):
        before = shifted(array[:, query_count - HALF :], block_axes, 1)
        after = shifted(array[:, :HALF], block_axes, -1)
        return before, after

    hots = [jnp.asarray(hot, BF) for hot in offset_tables()]
    if by_rows:
        before, after = halo(token_low)
        (query, key, value), (query_rel, query_back, key_rel), table_low, inners, position_inners = begin(
            token_low[0],
            position_table,
            position_gain,
            frozen,
            [down[0] for down in downs[:3]],
            [up[0] for up in att_up[:3]],
            hots,
        )
        queries, keys, values, key_rel, query_rel, query_back = (
            array[None] for array in (query, key, value, key_rel, query_rel, query_back)
        )
    else:
        projected = []
        inners = []
        for member in range(3):
            mapped, inner = adapter_forward(
                token_low, frozen[member], att_down[member], att_up[member]
            )
            projected.append(mapped.astype(BF))
            inners.append(inner)
        queries, keys, values = lax.all_to_all(
            jnp.stack(projected), "head", split_axis=3, concat_axis=2, tiled=True
        )
        keys_halo, values_halo = (jnp.concatenate(halo(array), axis=1) for array in (keys, values))
        table_low = (norm_stats(position_table)[0] * position_gain).astype(BF)
        position_inners = []
        tables = []
        for member in range(2):
            inner = product("pi,sir->spr", table_low, att_down[member]).astype(BF)
            mapped = product("pi,io->po", table_low, columns(frozen[member]))[
                None
            ] + ADAPTER_SCALING * product("spr,sro->spo", inner, columns(att_up[member]))
            position_inners.append(inner)
            tables.append(mapped.astype(BF))
        key_rel = product("cp,spo->sco", hots[0], tables[1]).astype(BF)
        query_rel = product("cp,spo->sco", hots[1], tables[0]).astype(BF)
        query_back = product("cp,spo->sco", hots[2], tables[0]).astype(BF)

    query_scores, key_scores = relative_scores(queries, keys, key_rel, query_rel)
    if by_rows:
        sides = (before[0], after[0], *frozen[1:], downs[1][0], downs[2][0], att_up[1][0], att_up[2][0])
    else:
        sides = (keys_halo, values_halo)
    context, probs, context_wide, inverse_total, *made = attention_forward(
        queries, keys, values, query_rel, query_seg, key_bias, query_scores, key_scores, sides
    )
    if by_rows:
        keys_halo, values_halo, *inners_halo = made
    if by_rows:
        context_rows = context
    else:
        context_rows = lax.all_to_all(context, "head", split_axis=1, concat_axis=2, tiled=True)

    ff_width = up_weight.shape[1]
    rank = attention_up.shape[2]
    peers = lax.axis_size("seq") * head_groups
    cores = lax.axis_size("batch")
    table_rows = position_table.shape[0]
    direct = by_rows and cores == 2 and table_rows == peers * cores * rank
    shape = (head_groups, peers // head_groups, cores, rank) if direct else None
    layer_output, grad_one, grad_context, grad_out_down, grad_out_up, grad_ff = middle(
        context_rows,
        tokens,
        cotangent,
        output_weight,
        up_weight,
        down_weight,
        (downs[3], att_up[3], *factors[8:]),
        attention_gain,
        feedforward_gain,
        shape,
    )
    if not by_rows:
        grad_context = lax.all_to_all(grad_context, "head", split_axis=2, concat_axis=1, tiled=True)

    group = ADAPTERS // head_groups
    def spread(array):
        chosen_by = select.reshape(select.shape + (1,) * (array.ndim - 1))
        return jnp.sum(chosen_by * array[:, None], axis=0)

    def unflat(array, widths):
        return jnp.split(array, np.cumsum(widths)[:-1].tolist(), axis=-1)

    *handed, grad_q, grad_k, grad_k_halo, grad_v, grad_v_halo, grad_key_rel, grad_query_rel = attention_backward(
        queries,
        keys,
        keys_halo,
        values,
        values_halo,
        key_rel,
        query_back,
        probs,
        grad_context,
        context_wide,
        inverse_total,
        *([layer_output] if direct else []),
    )
    if direct:
        layer_output = handed[0]

    def joined(total, from_above, from_below):
        if query_count == HALF:
            return total + from_above + from_below
        total = total.at[:, query_count - HALF :].add(from_above)
        return total.at[:, :HALF].add(from_below)

    def fold(total, halo_part):
        from_above = shifted(halo_part[:, :HALF], block_axes, -1).astype(F32)
        from_below = shifted(halo_part[:, HALF:], block_axes, 1).astype(F32)
        return joined(total.astype(F32), from_above, from_below)

    if direct:
        grad_tokens, table_total, late, both_ids, ff_total = finish(
            shape,
            key_halo=grad_k_halo[0],
            value_halo=grad_v_halo[0],
            key_w=key_weight,
            value_w=value_weight,
            back_hot=hots[2].T,
            query_rel_g=grad_query_rel[0],
            key_hot=hots[0].T,
            key_rel_g=grad_key_rel[0],
            query_w=query_weight,
            x=token_low[0],
            x_before=before[0],
            x_after=after[0],
            low=table_low,
            query_g=grad_q[0],
            key_g=grad_k[0],
            value_g=grad_v[0],
            grad_one=grad_one[0],
            query_a=downs[0][0],
            key_a=downs[1][0],
            value_a=downs[2][0],
            query_b=att_up[0][0],
            key_b=att_up[1][0],
            value_b=att_up[2][0],
            query_u=inners[0],
            key_u=inners[1],
            value_u=inners[2],
            key_uh=inners_halo[0],
            value_uh=inners_halo[1],
            query_pu=position_inners[0],
            key_pu=position_inners[1],
            own_id=jnp.broadcast_to(adapter_ids.astype(F32)[:, None], (8, TILE)),
            out_ga=grad_out_down[0],
            out_gb=grad_out_up[0],
            ff=grad_ff,
        )
        table_grad, down_grad, up_grad, *ff_grads, input_grad = spread_all(
            group,
            head_index.astype(jnp.int32).reshape(1),
            both_ids,
            late,
            ff_total,
            table_total,
            position_table,
            grad_tokens,
            position_gain,
            ff_width,
        )
        return (
            layer_output,
            input_grad[None],
            table_grad,
            turned(down_grad),
            up_grad,
            turned(ff_grads[0]),
            ff_grads[1],
            turned(ff_grads[2]),
            ff_grads[3],
        )
    else:
        ids = lax.all_gather(adapter_ids, "batch", axis=0, tiled=True)
        slots = head_index * group + jnp.arange(group, dtype=jnp.int32)
        select = (ids[:, None] == slots[None, :]).astype(F32)
        down_grads = []
        up_grads = []
        if by_rows:
            input_grad = grad_one
            grad_halo = 0.0
            rows_halo = jnp.concatenate([before, after], axis=1)
            for member, pieces in enumerate(
                (
                    ((token_low, inners[0][None], grad_q),),
                    ((token_low, inners[1][None], grad_k), (rows_halo, inners_halo[0][None], grad_k_halo)),
                    ((token_low, inners[2][None], grad_v), (rows_halo, inners_halo[1][None], grad_v_halo)),
                )
            ):
                found = [
                    adapter_back(rows, inner, frozen[member], att_down[member], att_up[member], gradient)
                    for rows, inner, gradient in pieces
                ]
                input_grad = input_grad + found[0][0]
                if member > 0:
                    grad_halo = grad_halo + found[1][0]
                down_grads.append(sum(turned(one[1]) for one in found))
                up_grads.append(sum(one[2] for one in found))
            input_grad = fold(input_grad, grad_halo.astype(BF))
            position_inners = [inner[None] for inner in position_inners]
        else:
            grad_qkv = jnp.stack(
                [grad_q, fold(grad_k, grad_k_halo).astype(BF), fold(grad_v, grad_v_halo).astype(BF)]
            )
            grad_qkv = lax.all_to_all(grad_qkv, "head", split_axis=2, concat_axis=3, tiled=True)
            input_grad = grad_one
            for member in range(3):
                grad_in, grad_dn, grad_upper = adapter_back(
                    token_low,
                    inners[member],
                    frozen[member],
                    att_down[member],
                    att_up[member],
                    grad_qkv[member],
                )
                input_grad = input_grad + grad_in
                down_grads.append(turned(grad_dn))
                up_grads.append(grad_upper)
        down_grads.append(grad_out_down)
        up_grads.append(grad_out_up)
        position_grads = (
            product("cb,soc->sbo", hots[2], grad_query_rel),
            product("cb,soc->sbo", hots[0], grad_key_rel),
        )
        grad_table_low = jnp.zeros(position_table.shape, F32)
        for member in range(2):
            gradient = position_grads[member].astype(BF)
            up = columns(att_up[member])
            grad_columns = ADAPTER_SCALING * product(
                "spr,spo->sro", position_inners[member], gradient
            )
            grad_inner = (ADAPTER_SCALING * product("spo,sro->spr", gradient, up)).astype(BF)
            grad_table_low = (
                grad_table_low
                + product("spo,io->pi", gradient, columns(frozen[member]))
                + product("spr,sir->pi", grad_inner, att_down[member])
            )
            down_grads[member] = down_grads[member] + product("spr,pi->sri", grad_inner, table_low)
            if not by_rows:
                grad_columns = lax.dynamic_update_slice_in_dim(
                    jnp.zeros_like(up_grads[member]),
                    grad_columns,
                    head_index * (width // head_groups),
                    2,
                )
            up_grads[member] = up_grads[member] + grad_columns
        late = jnp.concatenate(down_grads + up_grads, axis=-1)
        late = lax.all_gather(lax.psum(late, ("seq", "head")), "batch", axis=0, tiled=True)
        early = lax.all_gather(lax.psum(grad_ff, ("seq", "head")), "batch", axis=0, tiled=True)
        table_total = lax.psum(grad_table_low, ("seq", "batch"))
        table_total = lax.psum_scatter(table_total, "head", scatter_dimension=0, tiled=True)
    own_rows = table_rows // head_groups

    def head_rows(array):
        return lax.dynamic_slice_in_dim(array, head_index * own_rows, own_rows, 0)

    table_normed, table_inverse = norm_stats(head_rows(position_table))
    table_grad = norm_back(table_normed, table_inverse, position_gain, table_total)
    early = [spread(part) for part in unflat(early, [width, ff_width, ff_width, width])]
    late = [spread(part) for part in unflat(late, [width] * 8)]
    return (
        layer_output,
        input_grad,
        table_grad,
        jnp.stack([turned(part) for part in late[:4]]),
        jnp.stack(late[4:]),
        turned(early[0]),
        early[1],
        turned(early[2]),
        early[3],
    )


def solution(mesh):
    rows = P("batch", ("seq", "head"), None)
    return jax.shard_map(
        body,
        mesh=mesh,
        in_specs=(rows, rows, P("batch", None), P("batch")) + (P(),) * 16,
        out_specs=(
            rows,
            rows,
            P("head", None),
            P(None, "head", None, None),
            P(None, "head", None, None),
            P("head", None, None),
            P("head", None, None),
            P("head", None, None),
            P("head", None, None),
        ),
        check_vma=False,
    )
```
